32 devices in a mesh: fsdp: 16 (over z, y, x), rep: 2 (over core).
Axes of the slice: x: 2, y: 2, z: 4, core: 2. Of those that a mesh axis runs over, the one named last changes fastest.
Arguments:
- input_fine: bfloat16 [32, 48, 48, 256], P(('fsdp', 'rep')), may hold values from -6 to 6
- input_coarse: bfloat16 [32, 24, 24, 128], P(('fsdp', 'rep')), may hold values from -6 to 6
- upstream_fine: bfloat16 [32, 48, 48, 256], P(('fsdp', 'rep')), may hold values from -6 to 6
- upstream_coarse: bfloat16 [32, 24, 24, 128], P(('fsdp', 'rep')), may hold values from -6 to 6
- extents: int32 [32, 2], P(('fsdp', 'rep')), may hold values from 24 to 48
- master: float32 [1065728], P('fsdp'), may hold values from -5 to 5, as said below
- first_moment: float32 [1065728], P('fsdp'), may hold values from -0.0014648438 to 0.0014648438
- second_moment: float32 [1065728], P('fsdp'), may hold values from 9.383258e-10 to 3.753303e-09
- average: float32 [1065728], P('fsdp'), may hold values from -9 to 9, as said below
Outputs:
- out_fine: float32 [32, 48, 48, 256], P(('fsdp', 'rep'))
- out_coarse: float32 [32, 24, 24, 128], P(('fsdp', 'rep'))
- grad_input_fine: float32 [32, 48, 48, 256], P(('fsdp', 'rep'))
- grad_input_coarse: float32 [32, 24, 24, 128], P(('fsdp', 'rep'))
- grad_norm: float32 [], replicated
- new_master: float32 [1065728], P('fsdp')
- new_first: float32 [1065728], P('fsdp')
- new_second: float32 [1065728], P('fsdp')
- new_average: float32 [1065728], P('fsdp')
- norm_grads: float32 [768], replicated
The draws below stay inside these ranges and needn't reach their ends.
Inputs may be any that keep to these rules, and one draw needn't show every extreme that they name: `extents`: first column the valid height, second the valid width; the valid region is the top left corner of the padded image. `master`: the flat weight vector in the order of the steps. A running average of the flat weight vector.
All inputs are finite; a program needn't handle non-finite values.
Results may differ from the reference program's by a relative error of at most 0.024.
Values may be sent and summed in bfloat16 or wider, within the bound.
A program may use at most 64 MiB of HBM per device.

```python
import math
import jax
import jax.numpy as jnp
from jax import lax

C1 = 256
C2 = 128
GROUPS = 8
HEIGHT = 48
HALF = 24
ITERS = 12
STEP = 10
IMAGES = 32
RAW = 1065728
PARAMS = 1065728


def weights_from(key):
    keys = jax.random.split(key, 9)
    kernel_fine = jax.random.truncated_normal(keys[0], -3.0, 3.0, (9 * C1 * C1,), jnp.float32) / jnp.sqrt(9.0 * C1)
    kernel_down = jax.random.truncated_normal(keys[1], -3.0, 3.0, (9 * C1 * C2,), jnp.float32) / jnp.sqrt(9.0 * C1)
    kernel_coarse = jax.random.truncated_normal(keys[2], -3.0, 3.0, (9 * C2 * C2,), jnp.float32) / jnp.sqrt(9.0 * C2)
    kernel_up = jax.random.truncated_normal(keys[3], -3.0, 3.0, (C2 * C1,), jnp.float32) / jnp.sqrt(1.0 * C2)
    gain_fine = 0.5 * jnp.power(8.0, jnp.arange(C1, dtype=jnp.float32) / C1) * jax.random.uniform(keys[4], (C1,), jnp.float32, 0.8, 1.2)
    bias_fine = jax.random.uniform(keys[5], (C1,), jnp.float32, -0.5, 0.5)
    gain_coarse = 0.5 * jnp.power(8.0, jnp.arange(C2, dtype=jnp.float32) / C2) * jax.random.uniform(keys[6], (C2,), jnp.float32, 0.8, 1.2)
    bias_coarse = jax.random.uniform(keys[7], (C2,), jnp.float32, -0.5, 0.5)
    spare = 0.02 * jax.random.truncated_normal(keys[8], -3.0, 3.0, (PARAMS - RAW,), jnp.float32)
    return jnp.concatenate([kernel_fine, kernel_down, kernel_coarse, kernel_up, gain_fine, bias_fine, gain_coarse, bias_coarse, spare])


def draw_master(key, part):
    shared = weights_from(key)
    return shared


def draw_average(key, part):
    shared = weights_from(key)
    key = jax.random.fold_in(key, 2)
    return shared * jax.random.uniform(key, (PARAMS,), jnp.float32, 0.2, 1.8)


def touch_ends(values, key, smallest, high):
    longest = values.shape.index(max(values.shape))
    spots = []
    for shift in (0, 1):
        where = [jax.random.randint(jax.random.fold_in(key, axis), (), 0, length) for axis, length in enumerate(values.shape)]
        where[longest] = (where[longest] + shift) % values.shape[longest]
        spots.append(tuple(where))
    return values.at[spots[0]].set(smallest).at[spots[1]].set(high)


def level_of(rng, dims, shards, smallest, top_value):
    loudness = 1.0
    for dim, blocks in shards:
        draws = jax.random.uniform(jax.random.fold_in(jax.random.fold_in(rng, 6), dim), (blocks,), jnp.float32, smallest / len(shards), top_value / len(shards))
        loudness = loudness * jnp.repeat(jnp.exp(draws), dims[dim] // blocks).reshape((-1,) + (1,) * (len(dims) - 1 - dim))
    return loudness


def scatter_about(key, extent, scale, most, cuts=(), held_as=jnp.bfloat16):
    loudness = level_of(key, extent, cuts, -0.22, 0.18) if cuts else 1.0
    entries = jax.random.normal(key, extent, jnp.float32) * scale * loudness
    return jnp.minimum(jnp.maximum(entries, -most), most).astype(held_as)


def setup_inputs(seed: int = 0) -> dict:
    arg_keys = jax.random.split(jax.random.key(seed), 10)
    input_fine = scatter_about(arg_keys[0], (IMAGES, HEIGHT, HEIGHT, C1), 1.0, 6.0, ((0, 32),))
    input_coarse = scatter_about(arg_keys[1], (IMAGES, HALF, HALF, C2), 1.0, 6.0, ((0, 32),))
    upstream_fine = scatter_about(arg_keys[2], (IMAGES, HEIGHT, HEIGHT, C1), 1.0, 6.0, ((0, 32),))
    upstream_coarse = scatter_about(arg_keys[3], (IMAGES, HALF, HALF, C2), 1.0, 6.0, ((0, 32),))
    extents = touch_ends(jax.random.randint(arg_keys[4], (IMAGES, 2), HEIGHT // 2, HEIGHT + 1), jax.random.fold_in(arg_keys[4], 1), HEIGHT // 2, HEIGHT).astype(jnp.int32)
    master = draw_master(jax.random.fold_in(arg_keys[9], 71), 0)
    first_moment = scatter_about(arg_keys[6], (PARAMS,), (0.11 / PARAMS ** 0.5), 0.0014648438, ((0, 16),), jnp.float32)
    second_moment = jnp.clip(jnp.exp(math.log(3.753303001730046e-09) - 1.3862944 * jax.random.uniform(arg_keys[7], (PARAMS,), jnp.float32) ** level_of(arg_keys[7], (PARAMS,), ((0, 16),), -0.2, 0.2)), 9.383257504325115e-10, 3.753303001730046e-09)
    average = draw_average(jax.random.fold_in(arg_keys[9], 71), 0)
    return {"input_fine": input_fine, "input_coarse": input_coarse, "upstream_fine": upstream_fine, "upstream_coarse": upstream_coarse, "extents": extents, "master": master, "first_moment": first_moment, "second_moment": second_moment, "average": average}


@jax.custom_vjp
def low(v):
    return lax.optimization_barrier(v.astype(jnp.bfloat16)).astype(jnp.float32)

@jax.custom_vjp
def low_back(v):
    return v

def low_keep(v):
    return (low(v), None)

def low_pass(kept, grad):
    return (grad,)

def back_keep(v):
    return (v, None)

def back_low(kept, grad):
    return (low(grad),)
low.defvjp(low_keep, low_pass)
low_back.defvjp(back_keep, back_low)
highest = lax.Precision.HIGHEST
row_plan = ((1, -1), (0, 0), (1, 0))
clip_norm = 1.0
learn_rate = 0.02
beta_one = 0.9
beta_two = 0.999
adam_eps = 1e-08
decay_rate = 0.1

def shifted_field(values, down_by, right_by):
    height, breadth = (values.shape[1], values.shape[2])
    padded = jnp.pad(values, ((0, 0), (1, 1), (1, 1), (0, 0)))
    return padded[:, 1 + down_by:1 + down_by + height, 1 + right_by:1 + right_by + breadth, :]

def conv_same(values, kernel):
    summed = None
    for position in range(9):
        moved_values = shifted_field(values, position // 3 - 1, position % 3 - 1)
        product = jnp.einsum('bhwc,cd->bhwd', moved_values, kernel[:, position, :], precision=highest)
        summed = product if summed is None else summed + product
    return summed

def conv_down(values, kernel):
    images, height, breadth, channels = values.shape
    phases = values.reshape(images, height // 2, 2, breadth // 2, 2, channels)
    summed = None
    for position in range(9):
        row_phase, row_shift = row_plan[position // 3]
        col_phase, col_shift = row_plan[position % 3]
        moved_values = shifted_field(phases[:, :, row_phase, :, col_phase, :], row_shift, col_shift)
        product = jnp.einsum('bhwc,cd->bhwd', moved_values, kernel[:, position, :], precision=highest)
        summed = product if summed is None else summed + product
    return summed

def spread_up(values):
    images, height, breadth, channels = values.shape
    widened = jnp.broadcast_to(values[:, :, None, :, None, :], (images, height, 2, breadth, 2, channels))
    return widened.reshape(images, 2 * height, 2 * breadth, channels)

def normalize(values, validity):
    images, height, breadth, channels = values.shape
    grouped = values.reshape(images, height, breadth, GROUPS, channels // GROUPS)
    weights = validity[:, :, :, None, None]
    members = lax.optimization_barrier(jnp.sum(validity, axis=(1, 2))) * (channels // GROUPS)
    centre = lax.optimization_barrier(jnp.sum(grouped * weights, axis=(1, 2, 4))) / members[:, None]
    centered = grouped - centre[:, None, None, :, None]
    spread = lax.optimization_barrier(jnp.sum(centered * centered * weights, axis=(1, 2, 4))) / members[:, None]
    return (centered * lax.rsqrt(spread + 1e-05)[:, None, None, :, None]).reshape(values.shape)

def unpack(params):
    lengths = (9 * C1 * C1, 9 * C1 * C2, 9 * C2 * C2, C2 * C1, C1, C1, C2, C2)
    layouts = ((C1, 9, C1), (C1, 9, C2), (C2, 9, C2), (C2, C1), (C1,), (C1,), (C2,), (C2,))
    pieces = []
    offset = 0
    for length, layout in zip(lengths, layouts):
        pieces.append(params[offset:offset + length].reshape(layout))
        offset = offset + length
    return pieces

def masks_from(extents, height):
    row_index = jnp.arange(height).astype(jnp.int32)
    half_index = (2 * jnp.arange(height // 2)).astype(jnp.int32)
    heights_of = extents[:, 0][:, None, None]
    widths_of = extents[:, 1][:, None, None]
    mask_fine = ((row_index[None, :, None] < heights_of) & (row_index[None, None, :] < widths_of)).astype(jnp.float32)
    mask_coarse = ((half_index[None, :, None] < heights_of) & (half_index[None, None, :] < widths_of)).astype(jnp.float32)
    return (mask_fine, mask_coarse)

def layer_apply(params, input_fine, input_coarse, state_fine, state_coarse, mask_fine, mask_coarse):
    kernel_fine, kernel_down, kernel_coarse, kernel_up, gain_fine, bias_fine, gain_coarse, bias_coarse = unpack(params)
    conv_fine = low_back(conv_same(low(state_fine), kernel_fine))
    conv_coarse = low_back(conv_same(low(state_coarse), kernel_coarse))
    pre_fine = normalize(conv_fine, mask_fine) * gain_fine + bias_fine
    pre_coarse = normalize(conv_coarse, mask_coarse) * gain_coarse + bias_coarse
    branch_fine = low((jax.nn.silu(pre_fine) + input_fine) * mask_fine[..., None])
    branch_coarse = low((jax.nn.silu(pre_coarse) + input_coarse) * mask_coarse[..., None])
    lifted = low_back(jnp.einsum('bhwc,cd->bhwd', branch_coarse, kernel_up, precision=highest))
    lowered = low_back(conv_down(branch_fine, kernel_down))
    out_fine = (branch_fine + spread_up(lifted)) * mask_fine[..., None]
    out_coarse = (branch_coarse + lowered) * mask_coarse[..., None]
    return (out_fine, out_coarse)

def reference(input_fine, input_coarse, upstream_fine, upstream_coarse, extents, master, first_moment, second_moment, average):
    params = low(master)
    block_size = 8
    blocks = IMAGES // block_size

    def regroup(values):
        return values.reshape((blocks, block_size) + values.shape[1:])

    def one_block(grad_sum, block_items):
        fine_in, coarse_in, fine_up, coarse_up, sizes_here = block_items
        mask_fine, mask_coarse = masks_from(sizes_here, HEIGHT)
        fine_float = fine_in.astype(jnp.float32)
        coarse_float = coarse_in.astype(jnp.float32)

        def iterate(step_index, states):
            result = layer_apply(params, fine_float, coarse_float, states[0], states[1], mask_fine, mask_coarse)
            return (low(result[0]), low(result[1]))
        initial = (jnp.zeros(fine_float.shape, jnp.float32), jnp.zeros(coarse_float.shape, jnp.float32))
        states = lax.fori_loop(0, ITERS, iterate, initial)

        def apply_final(weight_values, fine_value, coarse_value):
            return layer_apply(weight_values, fine_value, coarse_value, states[0], states[1], mask_fine, mask_coarse)
        outputs, pullback = jax.vjp(apply_final, params, fine_float, coarse_float)
        gradients = pullback((fine_up.astype(jnp.float32), coarse_up.astype(jnp.float32)))
        return (grad_sum + gradients[0], (outputs[0], outputs[1], gradients[1], gradients[2]))
    grads, stacked = lax.scan(one_block, jnp.zeros((PARAMS,), jnp.float32), (regroup(input_fine), regroup(input_coarse), regroup(upstream_fine), regroup(upstream_coarse), regroup(extents)))
    out_fine = stacked[0].reshape(input_fine.shape)
    out_coarse = stacked[1].reshape(input_coarse.shape)
    grad_input_fine = stacked[2].reshape(input_fine.shape)
    grad_input_coarse = stacked[3].reshape(input_coarse.shape)
    grad_norm = jnp.sqrt(jnp.sum(grads * grads))
    factor = jnp.minimum(1.0, clip_norm / (grad_norm + 1e-06))
    clipped = grads * factor
    new_first = beta_one * first_moment + (1.0 - beta_one) * clipped
    new_second = beta_two * second_moment + (1.0 - beta_two) * clipped * clipped
    corrected_first = new_first / (1.0 - beta_one ** STEP)
    corrected_second = new_second / (1.0 - beta_two ** STEP)
    new_master = master - learn_rate * (corrected_first / (jnp.sqrt(corrected_second) + adam_eps) + decay_rate * master)
    ema_rate = min(0.999, (1.0 + STEP) / (10.0 + STEP))
    new_average = ema_rate * average + (1.0 - ema_rate) * new_master
    norm_grads = clipped[RAW - 2 * (C1 + C2):RAW]
    return (out_fine, out_coarse, grad_input_fine, grad_input_coarse, grad_norm, new_master, new_first, new_second, new_average, norm_grads)
```

```python
import functools

import jax
import jax.numpy as jnp
from jax import lax
from jax.experimental import pallas as pl
from jax.experimental.pallas import tpu as pltpu
from jax.sharding import PartitionSpec as P

F32, BF = jnp.float32, jnp.bfloat16
C1, C2, GROUPS, ITERS, STEP = 256, 128, 8, 12, 10
HEIGHT, HALF = 48, 24
PIX, CPIX = HEIGHT * HEIGHT, HALF * HALF
FLAT_ROWS = 8326
ROW_DOWN, ROW_COARSE, ROW_UP, ROW_VEC = 4608, 6912, 8064, 8320

clip_norm = 1.0
learn_rate = 0.02
beta_one = 0.9
beta_two = 0.999
adam_eps = 1e-08
decay_rate = 0.1


def dot(a, b):
    return jnp.dot(a, b, preferred_element_type=F32)


def dot_rows(a, b):
    return lax.dot_general(a, b, (((0,), (0,)), ((), ())), preferred_element_type=F32)


def run_sum(x, width):
    lane = lax.broadcasted_iota(jnp.int32, x.shape, 1)
    step = 1
    while step < width:
        up = pltpu.roll(x, 128 - step, 1)
        down = pltpu.roll(x, step, 1)
        x = x + jnp.where((lane & step) == 0, up, down)
        step *= 2
    return x


def shift_down(x):
    row = lax.broadcasted_iota(jnp.int32, x.shape, 0)
    return jnp.where(row == 0, 0.0, pltpu.roll(x, 1, 0))


def shift_up(x):
    last = x.shape[0] - 1
    row = lax.broadcasted_iota(jnp.int32, x.shape, 0)
    return jnp.where(row == last, 0.0, pltpu.roll(x, last, 0))


def tile_sum(x):
    total = x[0:8]
    for i in range(1, x.shape[0] // 8):
        total = total + x[8 * i : 8 * i + 8]
    return total


def twice(m):
    return jnp.concatenate([m, m], axis=1)


def interleave(ref, r, even, odd):
    for p in range(2):
        at = slice(128 * p, 128 * p + 128)
        ref[p, pl.ds(r * 48, 24, stride=2), :] = even[:, at]
        ref[p, pl.ds(r * 48 + 1, 24, stride=2), :] = odd[:, at]


def rows_of(r, count, unit):
    return pl.ds(pl.multiple_of(r * unit, unit if unit % 16 == 0 else 8), count)


def layer_kernel(
    ext_ref, inp_ref, inc_ref, upf_ref, upc_ref,
    wf_ref, wdo_ref, wde_ref, wdt_ref, wc01_ref, wc2_ref, wu_ref, wut_ref,
    gf_ref, bf_ref, gc_ref, bc_ref,
    outf_ref, outc_ref, gif_ref, gic_ref, grad_ref,
    s_ref, do_ref, de_ref, c_ref, x_ref, xc_ref, lift_ref, mf_ref, mc_ref, scf_ref, scc_ref,
    gl_ref, glo_ref, back_ref, gp_ref, g_ref, row_ref, stage_ref, sem_ref,
):
    hh, ww = ext_ref[0, 0], ext_ref[0, 1]
    pos = lax.broadcasted_iota(jnp.int32, (48, 128), 0)
    col = jnp.where(pos < 24, 2 * pos, 2 * pos - 47)
    colm = jnp.where(col < ww, 1.0, 0.0).astype(F32)

    def setup(r, _):
        at = rows_of(r, 48, 48)
        mf_ref[at, :] = jnp.where(r < hh, colm, 0.0)
        x_ref[at, :] = jnp.zeros((48, 256), F32)
        return 0

    lax.fori_loop(0, 48, setup, 0)

    def setup_coarse(r, _):
        mc_ref[rows_of(r, 24, 24), :] = jnp.where(2 * r < hh, colm[0:24], 0.0)
        return 0

    lax.fori_loop(0, 24, setup_coarse, 0)
    nf = (hh * ww).astype(F32) * (C1 // GROUPS)
    nc = (((hh + 1) // 2) * ((ww + 1) // 2)).astype(F32) * (C2 // GROUPS)
    s_ref[0:48, :] = jnp.zeros((48, 768), BF)
    s_ref[49 * 48 : 50 * 48, :] = jnp.zeros((48, 768), BF)
    xc_ref[...] = jnp.zeros((576, 128), F32)
    scf_ref[...] = jnp.zeros((8, 256), F32)
    scc_ref[...] = jnp.zeros((8, 128), F32)
    scf_ref[1:2, :] = 0.5 * bf_ref[...]
    scc_ref[1:2, :] = 0.5 * bc_ref[...]

    def coarse_branch():
        h = xc_ref[...] * scc_ref[0:1, :] + scc_ref[1:2, :]
        y = h * jnp.tanh(h) + h
        branch = ((y + inc_ref[...].astype(F32)) * mc_ref[...]).astype(BF)
        lift_ref[...] = dot(branch, wu_ref[...])
        return branch

    def fine_rows(g, final):
        scale, shift = scf_ref[0:1, :], scf_ref[1:2, :]
        pieces = ([], [])
        for j in range(4):
            r = 4 * g + j
            at = rows_of(r, 48, 48)
            m = twice(mf_ref[at, :])
            h = x_ref[at, :] * scale + shift
            y = h * jnp.tanh(h) + h
            branch = ((y + inp_ref[at, :].astype(F32)) * m).astype(BF).astype(F32)
            even, odd = branch[0:24], branch[24:48]
            pieces[j % 2].append((shift_down(odd), even, odd))
            lift = lift_ref[rows_of(2 * g + j // 2, 24, 24), :]
            z = (branch + jnp.concatenate([lift, lift], axis=0)) * m
            even, odd = z[0:24], z[24:48]
            if final:
                interleave(stage_ref.at[0], r, even, odd)
            else:
                to = pl.ds(pl.multiple_of(r * 48 + 48, 48), 48)
                s_ref[to, 0:256] = jnp.concatenate([shift_down(odd), even], axis=0).astype(BF)
                s_ref[to, 256:512] = z.astype(BF)
                s_ref[to, 512:768] = jnp.concatenate([odd, shift_up(even)], axis=0).astype(BF)
        at = rows_of(g, 48, 48)
        for ref, (p0, p1) in ((de_ref, pieces[0]), (do_ref, pieces[1])):
            for q in range(3):
                ref[at, 256 * q : 256 * q + 256] = jnp.concatenate([p0[q], p1[q]], axis=0).astype(BF)

    def lowered():
        po = dot(do_ref[...], wdo_ref[...])
        pe = dot(de_ref[...], wde_ref[...])
        return pe + po[:, 128:] + jnp.concatenate([jnp.zeros((24, 128), F32), po[:552, :128]], axis=0)

    def finish(s, q, width, n, gain, bias, to_ref):
        s, q = jnp.sum(s, axis=0, keepdims=True), jnp.sum(q, axis=0, keepdims=True)
        for p in range(s.shape[1] // 128):
            at = slice(128 * p, 128 * p + 128)
            mean = run_sum(s[:, at], width) / n
            var = jnp.maximum(run_sum(q[:, at], width) / n - mean * mean, 0.0)
            inv = lax.rsqrt(var + 1e-5)
            to_ref[0:1, at] = 0.5 * inv * gain[:, at]
            to_ref[1:2, at] = 0.5 * (bias[:, at] - mean * inv * gain[:, at])
            to_ref[2:3, at] = mean
            to_ref[3:4, at] = inv

    def iterate(t, _):
        branch_c = coarse_branch()

        def fine(g, _):
            fine_rows(g, False)
            return 0

        lax.fori_loop(0, 12, fine, 0)
        zc = (branch_c.astype(F32) + lowered()) * mc_ref[...]
        rows = [zc[24 * r : 24 * r + 24] for r in range(24)]
        c_ref[:, 0:128] = jnp.concatenate([shift_down(v) for v in rows], axis=0).astype(BF)
        c_ref[:, 128:256] = zc.astype(BF)
        c_ref[:, 256:384] = jnp.concatenate([shift_up(v) for v in rows], axis=0).astype(BF)
        p01 = dot(c_ref[...], wc01_ref[...])
        p2 = dot(c_ref[...], wc2_ref[...])
        none = jnp.zeros((24, 128), F32)
        xc = (
            p01[:, 128:]
            + jnp.concatenate([none, p01[:552, :128]], axis=0)
            + jnp.concatenate([p2[24:], none], axis=0)
        )
        xc_ref[...] = xc
        xcm = xc * mc_ref[...]
        sums_c = tile_sum(xcm), tile_sum(xcm * xcm)
        for b in range(4):
            at = 576 * b
            total = None
            for dy in range(3):
                p = dot(s_ref[at + 48 * dy : at + 48 * dy + 576, :], wf_ref[768 * dy : 768 * dy + 768, :])
                total = p if total is None else total + p
            x_ref[at : at + 576, :] = total

        def stats(r, carry):
            at = rows_of(r, 48, 48)
            xm = x_ref[at, :] * twice(mf_ref[at, :])
            return carry[0] + tile_sum(xm), carry[1] + tile_sum(xm * xm)

        none = jnp.zeros((8, 256), F32)
        sums_f = lax.fori_loop(0, 48, stats, (none, none), unroll=4)
        finish(*sums_f, C1 // GROUPS, nf, gf_ref[...], bf_ref[...], scf_ref)
        finish(*sums_c, C2 // GROUPS, nc, gc_ref[...], bc_ref[...], scc_ref)
        return 0

    lax.fori_loop(0, ITERS, iterate, 0)
    branch_c = coarse_branch()

    def fine_last(g, _):
        fine_rows(g, True)
        return 0

    lax.fori_loop(0, 12, fine_last, 0)
    sends = [
        pltpu.make_async_copy(stage_ref.at[i, p], ref.at[:, 128 * p : 128 * p + 128], sem_ref.at[i, p])
        for i, ref in enumerate((outf_ref, gif_ref))
        for p in range(2)
    ]
    sends[0].start()
    sends[1].start()
    outc_ref[...] = (branch_c.astype(F32) + lowered()) * mc_ref[...]

    seed_c = upc_ref[...].astype(F32) * mc_ref[...]
    none = jnp.zeros((24, 128), F32)
    rows = [seed_c[24 * r : 24 * r + 24] for r in range(24)]
    right = jnp.concatenate([shift_up(v) for v in rows], axis=0)
    glo_ref[:, 0:128] = seed_c.astype(BF)
    glo_ref[:, 128:256] = jnp.concatenate([seed_c[24:], none], axis=0).astype(BF)
    glo_ref[:, 256:384] = right.astype(BF)
    glo_ref[:, 384:512] = jnp.concatenate([right[24:], none], axis=0).astype(BF)

    def fold(g, _):
        both = []
        for i in range(2):
            total = None
            for j in range(2):
                at = rows_of(4 * g + 2 * i + j, 48, 48)
                seed = upf_ref[at, :].astype(F32) * twice(mf_ref[at, :])
                part = seed[0:24] + seed[24:48]
                total = part if total is None else total + part
            both.append(total)
        gl_ref[rows_of(g, 48, 48), :] = jnp.concatenate(both, axis=0).astype(BF)
        return 0

    lax.fori_loop(0, 12, fold, 0)
    up_grad = dot_rows(branch_c, gl_ref[...])
    for j in range(2):
        grad_ref[pl.ds(ROW_UP + j, 128, stride=2), :] = up_grad[:, 128 * j : 128 * j + 128]
    down_even = dot_rows(de_ref[...], glo_ref[:, 0:128])
    down_odd = dot_rows(do_ref[...], glo_ref[:, 0:256])
    for dx in range(3):
        at = slice(256 * dx, 256 * dx + 256)
        grad_ref[pl.ds(ROW_DOWN + dx, 256, stride=9), :] = down_odd[at, 128:256]
        grad_ref[pl.ds(ROW_DOWN + 3 + dx, 256, stride=9), :] = down_even[at]
        grad_ref[pl.ds(ROW_DOWN + 6 + dx, 256, stride=9), :] = down_odd[at, 0:128]

    back_c = (seed_c + dot(gl_ref[...], wut_ref[...])) * mc_ref[...]
    gic_ref[...] = back_c

    def pre_grad(gi, x, scale, shift, mean, inv):
        h = x * scale + shift
        t = jnp.tanh(h)
        sig = 0.5 * t + 0.5
        normed = (x - mean) * inv
        return gi * sig * (1.0 + 2.0 * h * (1.0 - sig)), normed

    def back_means(sum_bias, sum_gain, gain, width, n):
        return run_sum(sum_bias * gain, width) / n, run_sum(sum_gain * gain, width) / n

    gp_c, normed_c = pre_grad(
        back_c, xc_ref[...], scc_ref[0:1, :], scc_ref[1:2, :], scc_ref[2:3, :], scc_ref[3:4, :]
    )
    gain_c = jnp.sum(gp_c * normed_c, axis=0, keepdims=True)
    bias_c = jnp.sum(gp_c, axis=0, keepdims=True)
    grad_ref[ROW_VEC + 4 : ROW_VEC + 5, :] = gain_c
    grad_ref[ROW_VEC + 5 : ROW_VEC + 6, :] = bias_c
    grad_ref[ROW_VEC + 6 : ROW_VEC + 8, :] = jnp.zeros((2, 128), F32)
    mean_h, mean_hn = back_means(bias_c, gain_c, gc_ref[...], C2 // GROUPS, nc)
    gconv_c = (gp_c * gc_ref[...] - mean_h - normed_c * mean_hn) * scc_ref[3:4, :] * mc_ref[...]
    around = jnp.concatenate(
        [
            jnp.concatenate([gconv_c[24:], none], axis=0),
            gconv_c,
            jnp.concatenate([none, gconv_c[:552]], axis=0),
        ],
        axis=1,
    ).astype(BF)
    coarse_grad = dot_rows(c_ref[...], around)
    for dy in range(3):
        for dx in range(3):
            grad_ref[pl.ds(ROW_COARSE + 3 * dy + dx, 128, stride=9), :] = coarse_grad[
                128 * dx : 128 * dx + 128, 128 * dy : 128 * dy + 128
            ]

    back_ref[0] = dot(glo_ref[:, 0:128], wdt_ref[0:128, :])
    g00, g10, g01, g11 = (glo_ref[:, 128 * i : 128 * i + 128] for i in range(4))
    back_ref[1] = dot(jnp.concatenate([g00, g01], axis=1), wdt_ref[128:384, :])
    back_ref[2] = dot(jnp.concatenate([g00, g10], axis=1), wdt_ref[384:640, :])
    back_ref[3] = dot(jnp.concatenate([g00, g01, g10, g11], axis=1), wdt_ref[640:1152, :])

    def fine_back(i, carry):
        sums = list(carry)
        for j in range(2):
            r = 2 * i + j
            at = rows_of(r, 48, 48)
            half = rows_of(i, 24, 24)
            m = twice(mf_ref[at, :])
            back = jnp.concatenate([back_ref[2 * j, half, :], back_ref[2 * j + 1, half, :]], axis=0)
            gi = (upf_ref[at, :].astype(F32) + back) * m
            interleave(stage_ref.at[1], r, gi[0:24], gi[24:48])
            gp, normed = pre_grad(
                gi, x_ref[at, :], scf_ref[0:1, :], scf_ref[1:2, :], scf_ref[2:3, :], scf_ref[3:4, :]
            )
            gp_ref[at, :] = gp
            sums[0] = sums[0] + tile_sum(gp * normed)
            sums[1] = sums[1] + tile_sum(gp)
        return tuple(sums)

    none8 = jnp.zeros((8, 256), F32)
    gain_f, bias_f = lax.fori_loop(0, 24, fine_back, (none8, none8))
    sends[2].start()
    sends[3].start()
    gain_f = jnp.sum(gain_f, axis=0, keepdims=True)
    bias_f = jnp.sum(bias_f, axis=0, keepdims=True)
    mean_h, mean_hn = [], []
    for p in range(2):
        at = slice(128 * p, 128 * p + 128)
        grad_ref[ROW_VEC + p : ROW_VEC + p + 1, :] = gain_f[:, at]
        grad_ref[ROW_VEC + 2 + p : ROW_VEC + 3 + p, :] = bias_f[:, at]
        a, b = back_means(bias_f[:, at], gain_f[:, at], gf_ref[:, at], C1 // GROUPS, nf)
        mean_h.append(a)
        mean_hn.append(b)
    row_ref[0:1, :] = jnp.concatenate(mean_h, axis=1)
    row_ref[1:2, :] = jnp.concatenate(mean_hn, axis=1)
    g_ref[0:48, :] = jnp.zeros((48, 256), BF)
    g_ref[49 * 48 : 50 * 48, :] = jnp.zeros((48, 256), BF)

    def fine_conv_grad(r, _):
        at = rows_of(r, 48, 48)
        normed = (x_ref[at, :] - scf_ref[2:3, :]) * scf_ref[3:4, :]
        g = (gp_ref[at, :] * gf_ref[...] - row_ref[0:1, :] - normed * row_ref[1:2, :]) * scf_ref[3:4, :]
        g_ref[pl.ds(pl.multiple_of(r * 48 + 48, 48), 48), :] = (g * twice(mf_ref[at, :])).astype(BF)
        return 0

    lax.fori_loop(0, 48, fine_conv_grad, 0)
    for dx in range(3):
        states = s_ref[48:2352, 256 * dx : 256 * dx + 256]
        for dy in range(3):
            grad = dot_rows(states, g_ref[48 * (2 - dy) : 48 * (2 - dy) + 2304, :])
            for j in range(2):
                grad_ref[pl.ds(2 * (3 * dy + dx) + j, 256, stride=18), :] = grad[:, 128 * j : 128 * j + 128]
    for send in sends:
        send.wait()


def layer_call(*args):
    whole = pl.BlockSpec(memory_space=pltpu.VMEM)
    return pl.pallas_call(
        layer_kernel,
        out_shape=[
            jax.ShapeDtypeStruct((PIX, 256), F32),
            jax.ShapeDtypeStruct((CPIX, 128), F32),
            jax.ShapeDtypeStruct((PIX, 256), F32),
            jax.ShapeDtypeStruct((CPIX, 128), F32),
            jax.ShapeDtypeStruct((8328, 128), F32),
        ],
        in_specs=[pl.BlockSpec(memory_space=pltpu.SMEM)] + [whole] * 16,
        out_specs=[pl.BlockSpec(memory_space=pl.ANY), whole, pl.BlockSpec(memory_space=pl.ANY), whole, whole],
        scratch_shapes=[
            pltpu.VMEM((2400, 768), BF),
            pltpu.VMEM((576, 768), BF),
            pltpu.VMEM((576, 768), BF),
            pltpu.VMEM((576, 384), BF),
            pltpu.VMEM((PIX, 256), F32),
            pltpu.VMEM((CPIX, 128), F32),
            pltpu.VMEM((CPIX, 256), F32),
            pltpu.VMEM((PIX, 128), F32),
            pltpu.VMEM((CPIX, 128), F32),
            pltpu.VMEM((8, 256), F32),
            pltpu.VMEM((8, 128), F32),
            pltpu.VMEM((CPIX, 256), BF),
            pltpu.VMEM((CPIX, 512), BF),
            pltpu.VMEM((4, CPIX, 256), F32),
            pltpu.VMEM((PIX, 256), F32),
            pltpu.VMEM((2400, 256), BF),
            pltpu.VMEM((8, 256), F32),
            pltpu.VMEM((2, 2, PIX, 128), F32),
            pltpu.SemaphoreType.DMA((2, 2)),
        ],
        compiler_params=pltpu.CompilerParams(vmem_limit_bytes=62 * 2**20),
        name="layer",
    )(*args)


def by_parity(x):
    _, h, w, c = x.shape
    return x.reshape(h, w // 2, 2, c).transpose(0, 2, 1, 3).reshape(h * w, c)


def unpack(params):
    layouts = ((C1, 9, C1), (C1, 9, C2), (C2, 9, C2), (C2, C1), (1, C1), (1, C1), (1, C2), (1, C2))
    pieces = []
    offset = 0
    for layout in layouts:
        length = 1
        for size in layout:
            length *= size
        pieces.append(params[offset : offset + length].reshape(layout))
        offset = offset + length
    return pieces


def weight_forms(params):
    kf, kd, kc, ku, gf, bf, gc, bc = unpack(params)
    wf = kf.transpose(1, 0, 2).reshape(9 * C1, C1)
    kd = kd.transpose(1, 0, 2)
    turned = kd.transpose(0, 2, 1)
    wdt = jnp.concatenate([turned[t] for t in (4, 5, 3, 7, 1, 8, 6, 2, 0)], axis=0)
    kd = kd.reshape(3, 3 * C1, C2)
    kc = kc.transpose(1, 0, 2).reshape(3, 3 * C2, C2)
    return (
        wf,
        jnp.concatenate([kd[0], kd[2]], axis=1),
        kd[1],
        wdt,
        jnp.concatenate([kc[0], kc[1]], axis=1),
        kc[2],
        ku,
        ku.T,
        gf.astype(F32),
        bf.astype(F32),
        gc.astype(F32),
        bc.astype(F32),
    )


def per_device(
    input_fine, input_coarse, upstream_fine, upstream_coarse, extents, master, first_moment, second_moment, average
):
    resident = lax.all_gather(master.astype(BF), "fsdp", axis=0, tiled=True)
    out_fine, out_coarse, gi_fine, gi_coarse, grad = layer_call(
        extents,
        by_parity(input_fine),
        input_coarse.reshape(CPIX, C2),
        by_parity(upstream_fine),
        upstream_coarse.reshape(CPIX, C2),
        *weight_forms(resident),
    )
    flat_grad = grad[:FLAT_ROWS].reshape(-1)
    small_total = lax.psum(flat_grad[-2 * (C1 + C2) :], ("fsdp", "rep"))
    shard_grad = lax.psum_scatter(flat_grad, "fsdp", scatter_dimension=0, tiled=True)
    shard_grad = lax.psum(shard_grad.astype(BF), "rep").astype(F32)
    total_square = lax.psum(jnp.sum(shard_grad * shard_grad), "fsdp")
    grad_norm = jnp.sqrt(total_square)
    factor = jnp.minimum(1.0, clip_norm / (grad_norm + 1e-06))
    clipped = shard_grad * factor
    new_first = beta_one * first_moment + (1.0 - beta_one) * clipped
    new_second = beta_two * second_moment + (1.0 - beta_two) * clipped * clipped
    corrected_first = new_first / (1.0 - beta_one**STEP)
    corrected_second = new_second / (1.0 - beta_two**STEP)
    new_master = master - learn_rate * (
        corrected_first / (jnp.sqrt(corrected_second) + adam_eps) + decay_rate * master
    )
    ema_rate = min(0.999, (1.0 + STEP) / (10.0 + STEP))
    new_average = ema_rate * average + (1.0 - ema_rate) * new_master
    norm_grads = small_total * factor
    return (
        out_fine.reshape(input_fine.shape),
        out_coarse.reshape(input_coarse.shape),
        gi_fine.reshape(input_fine.shape),
        gi_coarse.reshape(input_coarse.shape),
        grad_norm,
        new_master,
        new_first,
        new_second,
        new_average,
        norm_grads,
    )


def solution(mesh):
    images = P(("fsdp", "rep"), None, None, None)
    flat = P("fsdp")
    in_specs = (images,) * 4 + (P(("fsdp", "rep"), None),) + (flat,) * 4
    out_specs = (images,) * 4 + (P(),) + (flat,) * 4 + (P(),)
    return jax.shard_map(per_device, mesh=mesh, in_specs=in_specs, out_specs=out_specs, check_vma=False)
```

```python
import functools

import jax
import jax.numpy as jnp
from jax import lax
from jax.experimental import pallas as pl
from jax.experimental.pallas import tpu as pltpu
from jax.sharding import PartitionSpec as P

F32, BF = jnp.float32, jnp.bfloat16
C1, C2, GROUPS, ITERS, STEP = 256, 128, 8, 12, 10
HEIGHT, HALF = 48, 24
PIX, CPIX = HEIGHT * HEIGHT, HALF * HALF
FLAT_ROWS = 8326
ROW_DOWN, ROW_COARSE, ROW_UP, ROW_VEC = 4608, 6912, 8064, 8320

clip_norm = 1.0
learn_rate = 0.02
beta_one = 0.9
beta_two = 0.999
adam_eps = 1e-08
decay_rate = 0.1


def dot(a, b):
    return jnp.dot(a, b, preferred_element_type=F32)


def dot_rows(a, b):
    return lax.dot_general(a, b, (((0,), (0,)), ((), ())), preferred_element_type=F32)


def dot_lanes(a, b):
    return lax.dot_general(a, b, (((1,), (1,)), ((), ())), preferred_element_type=F32)


def run_sum(x, width):
    lane = lax.broadcasted_iota(jnp.int32, x.shape, 1)
    step = 1
    while step < width:
        up = pltpu.roll(x, 128 - step, 1)
        down = pltpu.roll(x, step, 1)
        x = x + jnp.where((lane & step) == 0, up, down)
        step *= 2
    return x


def shift_down(x):
    row = lax.broadcasted_iota(jnp.int32, x.shape, 0)
    return jnp.where(row == 0, 0.0, pltpu.roll(x, 1, 0))


def shift_up(x):
    last = x.shape[0] - 1
    row = lax.broadcasted_iota(jnp.int32, x.shape, 0)
    return jnp.where(row == last, 0.0, pltpu.roll(x, last, 0))


def tile_sum(x):
    total = x[0:8]
    for i in range(1, x.shape[0] // 8):
        total = total + x[8 * i : 8 * i + 8]
    return total


def twice(m):
    return jnp.concatenate([m, m], axis=1)


def interleave(ref, r, even, odd):
    for p in range(2):
        at = slice(128 * p, 128 * p + 128)
        ref[p, pl.ds(r * 48, 24, stride=2), :] = even[:, at]
        ref[p, pl.ds(r * 48 + 1, 24, stride=2), :] = odd[:, at]


def rows_of(r, count, unit):
    return pl.ds(pl.multiple_of(r * unit, unit if unit % 16 == 0 else 8), count)


def layer_kernel(
    plan,
    ext_ref, inp_ref, upf_ref, inc_ref, upc_ref,
    wf_ref, wdo_ref, wde_ref, wdn_ref, wc01_ref, wc2_ref, wu_ref, vec_ref,
    outf_ref, outc_ref, gif_ref, gic_ref, blocks_ref,
    grad_ref, s_ref, do_ref, de_ref, c_ref, x_ref, xc_ref, lift_ref, mf_ref, mc_ref, scf_ref, scc_ref,
    gl_ref, glo_ref, back_ref, gp_ref, g_ref, row_ref, stage_ref, sem_ref,
):
    hh, ww = ext_ref[0, 0], ext_ref[0, 1]
    gain_f = jnp.concatenate([vec_ref[0:1, :], vec_ref[1:2, :]], axis=1)
    bias_f = jnp.concatenate([vec_ref[2:3, :], vec_ref[3:4, :]], axis=1)
    gain_c, bias_c = vec_ref[4:5, :], vec_ref[5:6, :]
    pos = lax.broadcasted_iota(jnp.int32, (48, 128), 0)
    col = jnp.where(pos < 24, 2 * pos, 2 * pos - 47)
    colm = jnp.where(col < ww, 1.0, 0.0).astype(F32)

    def setup(r, _):
        at = rows_of(r, 48, 48)
        mf_ref[at, :] = jnp.where(r < hh, colm, 0.0)
        x_ref[at, :] = jnp.zeros((48, 256), F32)
        return 0

    lax.fori_loop(0, 48, setup, 0)

    def setup_coarse(r, _):
        mc_ref[rows_of(r, 24, 24), :] = jnp.where(2 * r < hh, colm[0:24], 0.0)
        return 0

    lax.fori_loop(0, 24, setup_coarse, 0)
    nf = (hh * ww).astype(F32) * (C1 // GROUPS)
    nc = (((hh + 1) // 2) * ((ww + 1) // 2)).astype(F32) * (C2 // GROUPS)
    s_ref[0:48, :] = jnp.zeros((48, 768), BF)
    s_ref[49 * 48 : 50 * 48, :] = jnp.zeros((48, 768), BF)
    xc_ref[...] = jnp.zeros((576, 128), F32)
    scf_ref[...] = jnp.zeros((8, 256), F32)
    scc_ref[...] = jnp.zeros((8, 128), F32)
    scf_ref[1:2, :] = 0.5 * bias_f
    scc_ref[1:2, :] = 0.5 * bias_c

    def coarse_branch():
        h = xc_ref[...] * scc_ref[0:1, :] + scc_ref[1:2, :]
        y = h * jnp.tanh(h) + h
        branch = ((y + inc_ref[...].astype(F32)) * mc_ref[...]).astype(BF)
        lift_ref[...] = dot(branch, wu_ref[...])
        return branch

    def fine_rows(g, final):
        scale, shift = scf_ref[0:1, :], scf_ref[1:2, :]
        pieces = ([], [])
        for j in range(4):
            r = 4 * g + j
            at = rows_of(r, 48, 48)
            m = twice(mf_ref[at, :])
            h = x_ref[at, :] * scale + shift
            y = h * jnp.tanh(h) + h
            branch = ((y + inp_ref[at, :].astype(F32)) * m).astype(BF).astype(F32)
            even, odd = branch[0:24], branch[24:48]
            pieces[j % 2].append((shift_down(odd), even, odd))
            lift = lift_ref[rows_of(2 * g + j // 2, 24, 24), :]
            z = (branch + jnp.concatenate([lift, lift], axis=0)) * m
            even, odd = z[0:24], z[24:48]
            if final:
                interleave(stage_ref.at[0], r, even, odd)
            else:
                to = pl.ds(pl.multiple_of(r * 48 + 48, 48), 48)
                s_ref[to, 0:256] = jnp.concatenate([shift_down(odd), even], axis=0).astype(BF)
                s_ref[to, 256:512] = z.astype(BF)
                s_ref[to, 512:768] = jnp.concatenate([odd, shift_up(even)], axis=0).astype(BF)
        at = rows_of(g, 48, 48)
        for ref, (p0, p1) in ((de_ref, pieces[0]), (do_ref, pieces[1])):
            for q in range(3):
                ref[at, 256 * q : 256 * q + 256] = jnp.concatenate([p0[q], p1[q]], axis=0).astype(BF)

    def lowered():
        po = dot(do_ref[...], wdo_ref[...])
        pe = dot(de_ref[...], wde_ref[...])
        return pe + po[:, 128:] + jnp.concatenate([jnp.zeros((24, 128), F32), po[:552, :128]], axis=0)

    def finish(s, q, width, n, gain, bias, to_ref):
        s, q = jnp.sum(s, axis=0, keepdims=True), jnp.sum(q, axis=0, keepdims=True)
        for p in range(s.shape[1] // 128):
            at = slice(128 * p, 128 * p + 128)
            mean = run_sum(s[:, at], width) / n
            var = jnp.maximum(run_sum(q[:, at], width) / n - mean * mean, 0.0)
            inv = lax.rsqrt(var + 1e-5)
            to_ref[0:1, at] = 0.5 * inv * gain[:, at]
            to_ref[1:2, at] = 0.5 * (bias[:, at] - mean * inv * gain[:, at])
            to_ref[2:3, at] = mean
            to_ref[3:4, at] = inv

    def iterate(t, _):
        branch_c = coarse_branch()

        def fine(g, _):
            fine_rows(g, False)
            return 0

        lax.fori_loop(0, 12, fine, 0)
        zc = (branch_c.astype(F32) + lowered()) * mc_ref[...]
        rows = [zc[24 * r : 24 * r + 24] for r in range(24)]
        c_ref[:, 0:128] = jnp.concatenate([shift_down(v) for v in rows], axis=0).astype(BF)
        c_ref[:, 128:256] = zc.astype(BF)
        c_ref[:, 256:384] = jnp.concatenate([shift_up(v) for v in rows], axis=0).astype(BF)
        p01 = dot(c_ref[...], wc01_ref[...])
        p2 = dot(c_ref[...], wc2_ref[...])
        none = jnp.zeros((24, 128), F32)
        xc = (
            p01[:, 128:]
            + jnp.concatenate([none, p01[:552, :128]], axis=0)
            + jnp.concatenate([p2[24:], none], axis=0)
        )
        xc_ref[...] = xc
        xcm = xc * mc_ref[...]
        sums_c = tile_sum(xcm), tile_sum(xcm * xcm)
        for b in range(4):
            at = 576 * b
            total = None
            for dy in range(3):
                p = dot(s_ref[at + 48 * dy : at + 48 * dy + 576, :], wf_ref[768 * dy : 768 * dy + 768, :])
                total = p if total is None else total + p
            x_ref[at : at + 576, :] = total

        def stats(r, carry):
            at = rows_of(r, 48, 48)
            xm = x_ref[at, :] * twice(mf_ref[at, :])
            return carry[0] + tile_sum(xm), carry[1] + tile_sum(xm * xm)

        none = jnp.zeros((8, 256), F32)
        sums_f = lax.fori_loop(0, 48, stats, (none, none), unroll=4)
        finish(*sums_f, C1 // GROUPS, nf, gain_f, bias_f, scf_ref)
        finish(*sums_c, C2 // GROUPS, nc, gain_c, bias_c, scc_ref)
        return 0

    lax.fori_loop(0, ITERS, iterate, 0)
    branch_c = coarse_branch()

    def fine_last(g, _):
        fine_rows(g, True)
        return 0

    lax.fori_loop(0, 12, fine_last, 0)
    sends = [
        pltpu.make_async_copy(stage_ref.at[i, p], ref.at[:, 128 * p : 128 * p + 128], sem_ref.at[i, p])
        for i, ref in enumerate((outf_ref, gif_ref))
        for p in range(2)
    ]
    sends[0].start()
    sends[1].start()
    outc_ref[...] = (branch_c.astype(F32) + lowered()) * mc_ref[...]

    seed_c = upc_ref[...].astype(F32) * mc_ref[...]
    none = jnp.zeros((24, 128), F32)
    rows = [seed_c[24 * r : 24 * r + 24] for r in range(24)]
    right = jnp.concatenate([shift_up(v) for v in rows], axis=0)
    glo_ref[:, 0:128] = seed_c.astype(BF)
    glo_ref[:, 128:256] = jnp.concatenate([seed_c[24:], none], axis=0).astype(BF)
    glo_ref[:, 256:384] = right.astype(BF)
    glo_ref[:, 384:512] = jnp.concatenate([right[24:], none], axis=0).astype(BF)

    def fold(g, _):
        both = []
        for i in range(2):
            total = None
            for j in range(2):
                at = rows_of(4 * g + 2 * i + j, 48, 48)
                seed = upf_ref[at, :].astype(F32) * twice(mf_ref[at, :])
                part = seed[0:24] + seed[24:48]
                total = part if total is None else total + part
            both.append(total)
        gl_ref[rows_of(g, 48, 48), :] = jnp.concatenate(both, axis=0).astype(BF)
        return 0

    lax.fori_loop(0, 12, fold, 0)
    up_grad = dot_rows(branch_c, gl_ref[...])
    for j in range(2):
        grad_ref[pl.ds(ROW_UP + j, 128, stride=2), :] = up_grad[:, 128 * j : 128 * j + 128]
    down_even = dot_rows(de_ref[...], glo_ref[:, 0:128])
    down_odd = dot_rows(do_ref[...], glo_ref[:, 0:256])
    for dx in range(3):
        at = slice(256 * dx, 256 * dx + 256)
        grad_ref[pl.ds(ROW_DOWN + dx, 256, stride=9), :] = down_odd[at, 128:256]
        grad_ref[pl.ds(ROW_DOWN + 3 + dx, 256, stride=9), :] = down_even[at]
        grad_ref[pl.ds(ROW_DOWN + 6 + dx, 256, stride=9), :] = down_odd[at, 0:128]

    back_c = (seed_c + dot_lanes(gl_ref[...], wu_ref[...])) * mc_ref[...]
    gic_ref[...] = back_c

    def pre_grad(gi, x, scale, shift, mean, inv):
        h = x * scale + shift
        t = jnp.tanh(h)
        sig = 0.5 * t + 0.5
        normed = (x - mean) * inv
        return gi * sig * (1.0 + 2.0 * h * (1.0 - sig)), normed

    def back_means(sum_bias, sum_gain, gain, width, n):
        return run_sum(sum_bias * gain, width) / n, run_sum(sum_gain * gain, width) / n

    gp_c, normed_c = pre_grad(
        back_c, xc_ref[...], scc_ref[0:1, :], scc_ref[1:2, :], scc_ref[2:3, :], scc_ref[3:4, :]
    )
    sum_gain = jnp.sum(gp_c * normed_c, axis=0, keepdims=True)
    sum_bias = jnp.sum(gp_c, axis=0, keepdims=True)
    grad_ref[ROW_VEC + 4 : ROW_VEC + 5, :] = sum_gain
    grad_ref[ROW_VEC + 5 : ROW_VEC + 6, :] = sum_bias
    grad_ref[FLAT_ROWS:, :] = jnp.zeros((plan.tall - FLAT_ROWS, 128), F32)
    mean_h, mean_hn = back_means(sum_bias, sum_gain, gain_c, C2 // GROUPS, nc)
    gconv_c = (gp_c * gain_c - mean_h - normed_c * mean_hn) * scc_ref[3:4, :] * mc_ref[...]
    around = jnp.concatenate(
        [
            jnp.concatenate([gconv_c[24:], none], axis=0),
            gconv_c,
            jnp.concatenate([none, gconv_c[:552]], axis=0),
        ],
        axis=1,
    ).astype(BF)
    coarse_grad = dot_rows(c_ref[...], around)
    for dy in range(3):
        for dx in range(3):
            grad_ref[pl.ds(ROW_COARSE + 3 * dy + dx, 128, stride=9), :] = coarse_grad[
                128 * dx : 128 * dx + 128, 128 * dy : 128 * dy + 128
            ]

    back_ref[0] = dot_lanes(glo_ref[:, 0:128], wdn_ref[:, 0:128])
    g00, g10, g01, g11 = (glo_ref[:, 128 * i : 128 * i + 128] for i in range(4))
    back_ref[1] = dot_lanes(jnp.concatenate([g00, g01], axis=1), wdn_ref[:, 128:384])
    back_ref[2] = dot_lanes(jnp.concatenate([g00, g10], axis=1), wdn_ref[:, 384:640])
    back_ref[3] = dot_lanes(jnp.concatenate([g00, g01, g10, g11], axis=1), wdn_ref[:, 640:1152])

    def fine_back(i, carry):
        sums = list(carry)
        for j in range(2):
            r = 2 * i + j
            at = rows_of(r, 48, 48)
            half = rows_of(i, 24, 24)
            m = twice(mf_ref[at, :])
            back = jnp.concatenate([back_ref[2 * j, half, :], back_ref[2 * j + 1, half, :]], axis=0)
            gi = (upf_ref[at, :].astype(F32) + back) * m
            interleave(stage_ref.at[1], r, gi[0:24], gi[24:48])
            gp, normed = pre_grad(
                gi, x_ref[at, :], scf_ref[0:1, :], scf_ref[1:2, :], scf_ref[2:3, :], scf_ref[3:4, :]
            )
            gp_ref[at, :] = gp
            sums[0] = sums[0] + tile_sum(gp * normed)
            sums[1] = sums[1] + tile_sum(gp)
        return tuple(sums)

    none8 = jnp.zeros((8, 256), F32)
    sum_gain, sum_bias = lax.fori_loop(0, 24, fine_back, (none8, none8))
    sends[2].start()
    sends[3].start()
    sum_gain = jnp.sum(sum_gain, axis=0, keepdims=True)
    sum_bias = jnp.sum(sum_bias, axis=0, keepdims=True)
    mean_h, mean_hn = [], []
    for p in range(2):
        at = slice(128 * p, 128 * p + 128)
        grad_ref[ROW_VEC + p : ROW_VEC + p + 1, :] = sum_gain[:, at]
        grad_ref[ROW_VEC + 2 + p : ROW_VEC + 3 + p, :] = sum_bias[:, at]
        a, b = back_means(sum_bias[:, at], sum_gain[:, at], gain_f[:, at], C1 // GROUPS, nf)
        mean_h.append(a)
        mean_hn.append(b)
    row_ref[0:1, :] = jnp.concatenate(mean_h, axis=1)
    row_ref[1:2, :] = jnp.concatenate(mean_hn, axis=1)
    g_ref[0:48, :] = jnp.zeros((48, 256), BF)
    g_ref[49 * 48 : 50 * 48, :] = jnp.zeros((48, 256), BF)

    def fine_conv_grad(r, _):
        at = rows_of(r, 48, 48)
        normed = (x_ref[at, :] - scf_ref[2:3, :]) * scf_ref[3:4, :]
        g = (gp_ref[at, :] * gain_f - row_ref[0:1, :] - normed * row_ref[1:2, :]) * scf_ref[3:4, :]
        g_ref[pl.ds(pl.multiple_of(r * 48 + 48, 48), 48), :] = (g * twice(mf_ref[at, :])).astype(BF)
        return 0

    lax.fori_loop(0, 48, fine_conv_grad, 0)
    for dx in range(3):
        states = s_ref[48:2352, 256 * dx : 256 * dx + 256]
        for dy in range(3):
            grad = dot_rows(states, g_ref[48 * (2 - dy) : 48 * (2 - dy) + 2304, :])
            for j in range(2):
                grad_ref[pl.ds(2 * (3 * dy + dx) + j, 256, stride=18), :] = grad[:, 128 * j : 128 * j + 128]
    for n, first in enumerate(plan.first):
        blocks_ref[n] = grad_ref[first : first + plan.rows, :].astype(BF)
    for send in sends:
        send.wait()


def layer_call(plan, *args):
    whole = pl.BlockSpec(memory_space=pltpu.VMEM)
    return pl.pallas_call(
        functools.partial(layer_kernel, plan),
        out_shape=[
            jax.ShapeDtypeStruct((PIX, 256), F32),
            jax.ShapeDtypeStruct((CPIX, 128), F32),
            jax.ShapeDtypeStruct((PIX, 256), F32),
            jax.ShapeDtypeStruct((CPIX, 128), F32),
            jax.ShapeDtypeStruct((plan.n, plan.rows, 128), BF),
        ],
        in_specs=[pl.BlockSpec(memory_space=pltpu.SMEM)] + [whole] * 12,
        out_specs=[pl.BlockSpec(memory_space=pl.ANY), whole, pl.BlockSpec(memory_space=pl.ANY), whole, whole],
        scratch_shapes=[
            pltpu.VMEM((plan.tall, 128), F32),
            pltpu.VMEM((2400, 768), BF),
            pltpu.VMEM((576, 768), BF),
            pltpu.VMEM((576, 768), BF),
            pltpu.VMEM((576, 384), BF),
            pltpu.VMEM((PIX, 256), F32),
            pltpu.VMEM((CPIX, 128), F32),
            pltpu.VMEM((CPIX, 256), F32),
            pltpu.VMEM((PIX, 128), F32),
            pltpu.VMEM((CPIX, 128), F32),
            pltpu.VMEM((8, 256), F32),
            pltpu.VMEM((8, 128), F32),
            pltpu.VMEM((CPIX, 256), BF),
            pltpu.VMEM((CPIX, 512), BF),
            pltpu.VMEM((4, CPIX, 256), F32),
            pltpu.VMEM((PIX, 256), F32),
            pltpu.VMEM((2400, 256), BF),
            pltpu.VMEM((8, 256), F32),
            pltpu.VMEM((2, 2, PIX, 128), F32),
            pltpu.SemaphoreType.DMA((2, 2)),
        ],
        compiler_params=pltpu.CompilerParams(vmem_limit_bytes=62 * 2**20),
        name="layer",
    )(*args)


class Plan:
    def __init__(self, shards, length):
        self.dims = {16: (4, 2, 2), 128: (4, 8, 4)}.get(shards, (shards, 1, 1))
        self.n, self.length = shards, length
        self.first = [s * length // 128 for s in range(shards)]
        self.rows = -(-(length + 127) // 128)
        self.rows = -(-self.rows // 32) * 32
        self.part = self.rows // 2
        self.cut = -(-self.part // 32) * 16
        self.tall = -(-(self.first[-1] + self.rows) // 16) * 16

    def here(self):
        d0, d1, d2 = self.dims
        me = lax.axis_index("fsdp")
        return me, lax.axis_index("rep"), me // (d1 * d2), me // d2 % d1, me % d2

    def block(self, a, b, c):
        d0, d1, d2 = self.dims
        return (a * d1 + b) * d2 + c


def greet(plan, me, core, a, b, c):
    d0, d1, d2 = plan.dims
    barrier = pltpu.get_barrier_semaphore()
    others = [plan.block((a + k) % d0, b, c) for k in range(1, d0)]
    others += [plan.block(a, (b + k) % d1, c) for k in range(1, d1)]
    others += [plan.block(a, b, (c + k) % d2) for k in range(1, d2)]
    for other in others:
        pl.semaphore_signal(barrier, inc=1, device_id={"fsdp": other, "rep": core}, device_id_type=pl.DeviceIdType.MESH)
    pl.semaphore_signal(barrier, inc=1, device_id={"fsdp": me, "rep": 1 - core}, device_id_type=pl.DeviceIdType.MESH)
    pl.semaphore_wait(barrier, len(others) + 1)


def gather_kernel(plan, master_ref, inp_ref, upf_ref,
                  inpo_ref, upfo_ref, wf_ref, wdo_ref, wde_ref, wdn_ref, wc01_ref, wc2_ref, wu_ref, vec_ref,
                  g_ref, w_ref, tmp_ref, send_sem, recv_sem, sib_send, sib_recv, far_send):
    d0, d1, d2 = plan.dims
    me, core, a, b, c = plan.here()
    part, cut = plan.part, plan.cut
    off = (me * plan.length) % 128
    x = master_ref[...]
    x = pltpu.roll(x, off, 1)
    row = lax.broadcasted_iota(jnp.int32, x.shape, 0)
    lane = lax.broadcasted_iota(jnp.int32, x.shape, 1)
    above = jnp.where(row == 0, 0.0, pltpu.roll(x, 1, 0))
    g_ref[me] = jnp.where(lane < off, above, x).astype(BF)
    greet(plan, me, core, a, b, c)

    def span(half, which):
        start = which * part + (cut if half == 1 else 0)
        return pl.ds(pl.multiple_of(start, 16), part if half == 2 else (part - cut if half == 1 else cut))

    def copy(block, half, fsdp, rep, send, recv, which=core):
        at = g_ref.at[block, span(half, which)]
        return pltpu.make_async_remote_copy(src_ref=at, dst_ref=at, send_sem=send, recv_sem=recv,
            device_id={"fsdp": fsdp, "rep": rep}, device_id_type=pl.DeviceIdType.MESH)

    def far(k):
        return copy(me, 2, plan.block((a + d0 - k) % d0, b, c), core, far_send.at[k], recv_sem.at[me, 0])

    def along1(block, half, k):
        return copy(block, half, plan.block(a, (b + k) % d1, c), core, send_sem.at[block, half, k - 1], recv_sem.at[block, half])

    def along2(block, half, k):
        return copy(block, half, plan.block(a, b, (c + k) % d2), core, send_sem.at[block, half, d1 - 1 + k - 1], recv_sem.at[block, half])

    def beside(block, half):
        return copy(block, half, me, 1 - core, sib_send.at[block, half], sib_recv.at[block, half])

    def arrive(block, half, send_to):
        copy(block, half, me, core, far_send.at[0], recv_sem.at[block, half % 2]).wait_recv()

    sent = []
    def go(d):
        d.start()
        sent.append(d)

    for k in range(1, d0):
        go(far(k))

    def own_column(k):
        block = plan.block((a + k) % d0, b, c)
        if k:
            copy(block, 2, me, core, far_send.at[0], recv_sem.at[block, 0]).wait_recv()
        for half in (0, 1):
            for i in range(1, d2):
                go(along2(block, half, i))
            for i in range(1, d1):
                go(along1(block, half, i))
        if k:
            for half in (0, 1):
                go(beside(block, half))

    def near(k):
        a2 = (a + k) % d0
        for i in range(1, d2):
            block = plan.block(a2, b, (c + i) % d2)
            arrive(block, 0, None)
            for j in range(1, d1):
                go(along1(block, 0, j))
            go(beside(block, 0))
        for i in range(1, d1):
            block = plan.block(a2, (b + i) % d1, c)
            arrive(block, 1, None)
            for j in range(1, d2):
                go(along2(block, 1, j))
            go(beside(block, 1))
        for i in range(1, d2):
            block = plan.block(a2, b, (c + i) % d2)
            arrive(block, 1, None)
            go(beside(block, 1))
        for i in range(1, d1):
            block = plan.block(a2, (b + i) % d1, c)
            arrive(block, 0, None)
            go(beside(block, 0))

    def diagonal(k):
        a2 = (a + k) % d0
        for i in range(1, d1):
            for j in range(1, d2):
                block = plan.block(a2, (b + i) % d1, (c + j) % d2)
                for half in (0, 1):
                    arrive(block, half, None)
                    go(beside(block, half))

    def parity(src, dst):
        def one(r, _):
            at = pl.ds(pl.multiple_of(r * 48, 48), 48)
            v = src[at, :].astype(F32)
            for p in range(2):
                tmp_ref[p, at, :] = v[:, 128 * p:128 * p + 128]
            even = [tmp_ref[p, pl.ds(r * 48, 24, stride=2), :] for p in range(2)]
            odd = [tmp_ref[p, pl.ds(r * 48 + 1, 24, stride=2), :] for p in range(2)]
            both = jnp.concatenate([jnp.concatenate(even, axis=1), jnp.concatenate(odd, axis=1)], axis=0)
            dst[at, :] = both.astype(BF)
            return 0
        lax.fori_loop(0, 48, one, 0, unroll=4)

    own_column(0)
    parity(inp_ref, inpo_ref)
    parity(upf_ref, upfo_ref)
    for k in range(1, d0):
        own_column(k)
        near(k - 1)
        if k > 1:
            diagonal(k - 2)
    near(d0 - 1)
    if d0 > 1:
        diagonal(d0 - 2)
    diagonal(d0 - 1)
    for k in range(1, plan.n):
        block = (me + k) % plan.n
        for half in (0, 1):
            copy(block, half, me, core, far_send.at[0], sib_recv.at[block, half], which=1 - core).wait_recv()
    for d in sent:
        d.wait_send()

    for s in range(plan.n):
        v = g_ref[s].astype(F32)
        at = plan.first[s]
        if s:
            low = w_ref[at:at + 1, :] + v[0:1]
            w_ref[at:at + plan.rows, :] = v
            w_ref[at:at + 1, :] = low
        else:
            w_ref[0:plan.rows, :] = v
    for t in range(9):
        for h in range(2):
            wf_ref[256 * t:256 * t + 256, 128 * h:128 * h + 128] = w_ref[pl.ds(2 * t + h, 256, stride=18), :].astype(BF)
        d = w_ref[pl.ds(ROW_DOWN + t, 256, stride=9), :].astype(BF)
        dy, dx = t // 3, t % 3
        if dy == 1:
            wde_ref[256 * dx:256 * dx + 256, :] = d
        else:
            wdo_ref[256 * dx:256 * dx + 256, 64 * dy:64 * dy + 128] = d
        p = (4, 5, 3, 7, 1, 8, 6, 2, 0).index(t)
        wdn_ref[:, 128 * p:128 * p + 128] = d
        e = w_ref[pl.ds(ROW_COARSE + t, 128, stride=9), :].astype(BF)
        if dy < 2:
            wc01_ref[128 * dx:128 * dx + 128, 128 * dy:128 * dy + 128] = e
        else:
            wc2_ref[128 * dx:128 * dx + 128, :] = e
    for h in range(2):
        wu_ref[:, 128 * h:128 * h + 128] = w_ref[pl.ds(ROW_UP + h, 128, stride=2), :].astype(BF)
    vec_ref[...] = w_ref[ROW_VEC:ROW_VEC + 8, :]


def gather_call(plan, master, inp, upf):
    V = pl.BlockSpec(memory_space=pltpu.VMEM)
    sh = lambda *s: jax.ShapeDtypeStruct(s, BF)
    d0, d1, d2 = plan.dims
    D = pltpu.SemaphoreType.DMA
    return pl.pallas_call(functools.partial(gather_kernel, plan),
        out_shape=[sh(PIX, 256), sh(PIX, 256), sh(2304, 256), sh(768, 256), sh(768, 128), sh(256, 1152), sh(384, 256), sh(384, 128), sh(128, 256),
                   jax.ShapeDtypeStruct((8, 128), F32)],
        in_specs=[V] * 3, out_specs=[V] * 10,
        scratch_shapes=[pltpu.VMEM((plan.n, plan.rows, 128), BF), pltpu.VMEM((plan.tall, 128), F32), pltpu.VMEM((2, PIX, 128), F32),
            D((plan.n, 2, max(d1 + d2 - 2, 1))), D((plan.n, 2)), D((plan.n, 2)), D((plan.n, 2)), D((d0,))],
        compiler_params=pltpu.CompilerParams(collective_id=0, has_side_effects=True, vmem_limit_bytes=40 * 2**20),
        name="gather_weights")(master, inp, upf)


def reduce_kernel(plan, p_ref, out_ref, tile_ref,
                  q_ref, ua_ref, ub_ref, va_ref, vb_ref, z_ref, sa_ref, total_ref, n1_ref, n2_ref,
                  q_send, q_recv, s1_send, s1_recv, s2_send, s2_recv, s3_send, s3_recv, t_send, t_recv, n1_send, n1_recv, n2_send, n2_recv):
    d0, d1, d2 = plan.dims
    me, core, a, b, c = plan.here()
    part, cut = plan.part, plan.cut
    MESH = pl.DeviceIdType.MESH
    barrier = pltpu.get_barrier_semaphore()
    others = [({"fsdp": plan.block((a + k) % d0, b, c), "rep": core}) for k in range(1, d0)]
    plane = []
    for i in range(d1):
        for j in range(d2):
            for o in range(2):
                if i or j or o:
                    plane.append((i, j, o, {"fsdp": plan.block(a, (b + i) % d1, (c + j) % d2), "rep": (core + o) % 2}))
    others += [p[3] for p in plane]
    for other in others:
        pl.semaphore_signal(barrier, inc=1, device_id=other, device_id_type=MESH)
    pl.semaphore_wait(barrier, len(others))

    sent = []
    def go(src, dst, send, recv, to):
        d = pltpu.make_async_remote_copy(src_ref=src, dst_ref=dst, send_sem=send, recv_sem=recv, device_id=to, device_id_type=MESH)
        d.start()
        sent.append(d)

    def got(ref, recv):
        pltpu.make_async_copy(ref, ref, recv).wait()

    mine = pl.multiple_of(core * part, 16)
    theirs = pl.multiple_of((1 - core) * part, 16)
    halves = ((0, cut), (cut, part - cut))
    order = [(k + 1) % d0 for k in range(d0)]
    spots = []
    for k in order:
        for i in list(range(1, d1)) + [0]:
            for j in list(range(1, d2)) + [0]:
                spots.append((k, i, j))
    for k, i, j in spots:
        s = plan.block((a + k) % d0, (b + i) % d1, (c + j) % d2)
        go(p_ref.at[s, pl.ds(theirs, part)], q_ref.at[s], q_send.at[s], q_recv.at[s], {"fsdp": me, "rep": 1 - core})

    def pair(s, half):
        start, size = halves[half]
        x = p_ref[s, pl.ds(pl.multiple_of(mine + start, 16), size), :].astype(F32)
        return x + q_ref[s, start:start + size, :].astype(F32)

    def step1(k):
        a2 = (a + k) % d0
        for i in range(1, d1):
            for j in list(range(1, d2)) + [0]:
                s = plan.block(a2, (b + i) % d1, (c + j) % d2)
                got(q_ref.at[s], q_recv.at[s])
                sa_ref[s, 0:cut, :] = pair(s, 0).astype(BF)
                go(sa_ref.at[s, 0:cut], ua_ref.at[a2, (c + j) % d2, i - 1], s1_send.at[s, 0], s1_recv.at[0, a2, (c + j) % d2, i - 1],
                   {"fsdp": plan.block(a, (b + i) % d1, c), "rep": core})
                if j:
                    step1b(s, a2, i, j)
        for j in range(1, d2):
            s = plan.block(a2, b, (c + j) % d2)
            got(q_ref.at[s], q_recv.at[s])
            step1b(s, a2, 0, j)

    def step1b(s, a2, i, j):
        sa_ref[s, cut:part, :] = pair(s, 1).astype(BF)
        go(sa_ref.at[s, cut:part], ub_ref.at[a2, (b + i) % d1, j - 1], s1_send.at[s, 1], s1_recv.at[1, a2, (b + i) % d1, j - 1],
           {"fsdp": plan.block(a, b, (c + j) % d2), "rep": core})

    def from1(half, a2, other):
        ref = ua_ref if half == 0 else ub_ref
        total = None
        for i in range((d1 if half == 0 else d2) - 1):
            got(ref.at[a2, other, i], s1_recv.at[half, a2, other, i])
            v = ref[a2, other, i].astype(F32)
            total = v if total is None else total + v
        return total

    def plus(x, y):
        return x if y is None else x + y

    def step2(k):
        a2 = (a + k) % d0
        for j in range(1, d2):
            c2 = (c + j) % d2
            s = plan.block(a2, b, c2)
            sa_ref[s, 0:cut, :] = plus(pair(s, 0), from1(0, a2, c2)).astype(BF)
            go(sa_ref.at[s, 0:cut], va_ref.at[a2, j - 1], s2_send.at[0, a2, j - 1], s2_recv.at[0, a2, j - 1],
               {"fsdp": plan.block(a, b, c2), "rep": core})
        for i in range(1, d1):
            b2 = (b + i) % d1
            s = plan.block(a2, b2, c)
            sa_ref[s, cut:part, :] = plus(pair(s, 1), from1(1, a2, b2)).astype(BF)
            go(sa_ref.at[s, cut:part], vb_ref.at[a2, i - 1], s2_send.at[1, a2, i - 1], s2_recv.at[1, a2, i - 1],
               {"fsdp": plan.block(a, b2, c), "rep": core})

    def column(k):
        a2 = (a + k) % d0
        s = plan.block(a2, b, c)
        got(q_ref.at[s], q_recv.at[s])
        x = plus(pair(s, 0), from1(0, a2, c))
        for j in range(1, d2):
            got(va_ref.at[a2, j - 1], s2_recv.at[0, a2, j - 1])
            x = x + va_ref[a2, j - 1].astype(F32)
        y = plus(pair(s, 1), from1(1, a2, b))
        for i in range(1, d1):
            got(vb_ref.at[a2, i - 1], s2_recv.at[1, a2, i - 1])
            y = y + vb_ref[a2, i - 1].astype(F32)
        return s, x, y

    def step3(k):
        s, x, y = column(k)
        sa_ref[s, 0:cut, :] = x.astype(BF)
        sa_ref[s, cut:part, :] = y.astype(BF)
        go(sa_ref.at[s], z_ref.at[k - 1], s3_send.at[k - 1], s3_recv.at[k - 1], {"fsdp": plan.block((a + k) % d0, b, c), "rep": core})

    for n in range(d0 + 2):
        if n < d0:
            step1(order[n])
        if 0 <= n - 1 < d0:
            step2(order[n - 1])
        if 0 <= n - 2 < d0 - 1:
            step3(order[n - 2])
    _, x, y = column(0)
    total = jnp.concatenate([x, y], axis=0)
    for k in range(1, d0):
        got(z_ref.at[k - 1], s3_recv.at[k - 1])
        total = total + z_ref[k - 1].astype(F32)
    total_ref[pl.ds(mine, part), :] = total
    go(total_ref.at[pl.ds(mine, part)], total_ref.at[pl.ds(mine, part)], t_send.at[0], t_recv.at[0], {"fsdp": me, "rep": 1 - core})

    off = (me * plan.length) % 128
    row = lax.broadcasted_iota(jnp.int32, (part, 128), 0) + mine
    at = row * 128 + lax.broadcasted_iota(jnp.int32, (part, 128), 1)
    own = jnp.where((at >= off) & (at < off + plan.length), total, 0.0)
    last = me == plan.n - 1
    for i in range(6):
        spot = ROW_VEC - plan.first[-1] + i
        holds = last & (core == spot // part)
        n1_ref[a, i:i + 1, :] = jnp.where(holds, total[spot % part:spot % part + 1], 0.0)
    n1_ref[a, 6:7, :] = jnp.sum(own * own, axis=0, keepdims=True)
    n1_ref[a, 7:8, :] = jnp.zeros((1, 128), F32)
    for k in range(1, d0):
        go(n1_ref.at[a], n1_ref.at[a], n1_send.at[k], n1_recv.at[a], {"fsdp": plan.block((a + k) % d0, b, c), "rep": core})
    for k in range(1, d0):
        got(n1_ref.at[(a + k) % d0], n1_recv.at[(a + k) % d0])
    tile = n1_ref[0]
    for k in range(1, d0):
        tile = tile + n1_ref[k]
    slot = (b * d2 + c) * 2 + core
    n2_ref[slot] = tile
    for n, (i, j, o, to) in enumerate(plane):
        go(n2_ref.at[slot], n2_ref.at[slot], n2_send.at[n], n2_recv.at[slot], to)
    got(total_ref.at[pl.ds(theirs, part)], t_recv.at[0])
    x = pltpu.roll(total_ref[...], (128 - off) % 128, 1)
    below = pltpu.roll(x, plan.rows - 1, 0)
    lane = lax.broadcasted_iota(jnp.int32, x.shape, 1)
    out_ref[...] = jnp.where(lane + off >= 128, below, x)
    for n, (i, j, o, to) in enumerate(plane):
        other = (((b + i) % d1) * d2 + (c + j) % d2) * 2 + (core + o) % 2
        got(n2_ref.at[other], n2_recv.at[other])
    tile = n2_ref[0]
    for n in range(1, 2 * d1 * d2):
        tile = tile + n2_ref[n]
    tile_ref[...] = tile
    for d in sent:
        d.wait_send()


def reduce_call(plan, grads):
    V = pl.BlockSpec(memory_space=pltpu.VMEM)
    d0, d1, d2 = plan.dims
    D = pltpu.SemaphoreType.DMA
    b = lambda *s: pltpu.VMEM(s, BF)
    e1, e2 = max(d1 - 1, 1), max(d2 - 1, 1)
    return pl.pallas_call(functools.partial(reduce_kernel, plan),
        out_shape=[jax.ShapeDtypeStruct((plan.rows, 128), F32), jax.ShapeDtypeStruct((8, 128), F32)],
        in_specs=[V], out_specs=[V] * 2,
        scratch_shapes=[b(plan.n, plan.part, 128), b(d0, d2, e1, plan.cut, 128), b(d0, d1, e2, plan.part - plan.cut, 128),
            b(d0, e2, plan.cut, 128), b(d0, e1, plan.part - plan.cut, 128), b(max(d0 - 1, 1), plan.part, 128), b(plan.n, plan.part, 128),
            pltpu.VMEM((plan.rows, 128), F32), pltpu.VMEM((d0, 8, 128), F32), pltpu.VMEM((2 * d1 * d2, 8, 128), F32),
            D((plan.n,)), D((plan.n,)), D((plan.n, 2)), D((2, d0, max(d1, d2), max(e1, e2))), D((2, d0, max(e1, e2))), D((2, d0, max(e1, e2))),
            D((d0,)), D((d0,)), D((1,)), D((1,)), D((d0,)), D((d0,)), D((2 * d1 * d2,)), D((2 * d1 * d2,))],
        compiler_params=pltpu.CompilerParams(collective_id=1, has_side_effects=True, vmem_limit_bytes=40 * 2**20),
        name="reduce_gradients")(grads)


def per_device(
    input_fine, input_coarse, upstream_fine, upstream_coarse, extents, master, first_moment, second_moment, average
):
    plan = Plan(lax.axis_size("fsdp"), master.shape[0])
    padded = jnp.pad(master, (0, plan.rows * 128 - plan.length)).reshape(plan.rows, 128)
    inp, upf, *weights = gather_call(
        plan, padded, input_fine.reshape(PIX, C1), upstream_fine.reshape(PIX, C1)
    )
    out_fine, out_coarse, gi_fine, gi_coarse, blocks = layer_call(
        plan, extents, inp, upf, input_coarse.reshape(CPIX, C2), upstream_coarse.reshape(CPIX, C2), *weights
    )
    shard_grad, tile = reduce_call(plan, blocks)
    shard_grad = shard_grad.reshape(-1)[: plan.length]
    total_square = jnp.sum(tile[6])
    small_total = tile[:6].reshape(-1)
    grad_norm = jnp.sqrt(total_square)
    factor = jnp.minimum(1.0, clip_norm / (grad_norm + 1e-06))
    clipped = shard_grad * factor
    new_first = beta_one * first_moment + (1.0 - beta_one) * clipped
    new_second = beta_two * second_moment + (1.0 - beta_two) * clipped * clipped
    corrected_first = new_first / (1.0 - beta_one**STEP)
    corrected_second = new_second / (1.0 - beta_two**STEP)
    new_master = master - learn_rate * (
        corrected_first / (jnp.sqrt(corrected_second) + adam_eps) + decay_rate * master
    )
    ema_rate = min(0.999, (1.0 + STEP) / (10.0 + STEP))
    new_average = ema_rate * average + (1.0 - ema_rate) * new_master
    norm_grads = small_total * factor
    return (
        out_fine.reshape(input_fine.shape),
        out_coarse.reshape(input_coarse.shape),
        gi_fine.reshape(input_fine.shape),
        gi_coarse.reshape(input_coarse.shape),
        grad_norm,
        new_master,
        new_first,
        new_second,
        new_average,
        norm_grads,
    )


def solution(mesh):
    images = P(("fsdp", "rep"), None, None, None)
    flat = P("fsdp")
    in_specs = (images,) * 4 + (P(("fsdp", "rep"), None),) + (flat,) * 4
    out_specs = (images,) * 4 + (P(),) + (flat,) * 4 + (P(),)
    return jax.shard_map(per_device, mesh=mesh, in_specs=in_specs, out_specs=out_specs, check_vma=False)
```

```python
import functools

import jax
import jax.numpy as jnp
from jax import lax
from jax.experimental import pallas as pl
from jax.experimental.pallas import tpu as pltpu
from jax.sharding import PartitionSpec as P

F32, BF = jnp.float32, jnp.bfloat16
C1, C2, GROUPS, ITERS, STEP = 256, 128, 8, 12, 10
HEIGHT, HALF = 48, 24
PIX, CPIX = HEIGHT * HEIGHT, HALF * HALF
FLAT_ROWS = 8326
ROW_DOWN, ROW_COARSE, ROW_UP, ROW_VEC = 4608, 6912, 8064, 8320

clip_norm = 1.0
learn_rate = 0.02
beta_one = 0.9
beta_two = 0.999
adam_eps = 1e-08
decay_rate = 0.1


def dot(a, b):
    return jnp.dot(a, b, preferred_element_type=F32)


def dot_rows(a, b):
    return lax.dot_general(a, b, (((0,), (0,)), ((), ())), preferred_element_type=F32)


def dot_lanes(a, b):
    return lax.dot_general(a, b, (((1,), (1,)), ((), ())), preferred_element_type=F32)


def run_sum(x, width):
    lane = lax.broadcasted_iota(jnp.int32, x.shape, 1)
    step = 1
    while step < width:
        up = pltpu.roll(x, 128 - step, 1)
        down = pltpu.roll(x, step, 1)
        x = x + jnp.where((lane & step) == 0, up, down)
        step *= 2
    return x


def shift_down(x):
    count = x.shape[0] // 8
    top = lax.broadcasted_iota(jnp.int32, (8, x.shape[1]), 0) == 0
    turned = [pltpu.roll(x[8 * i : 8 * i + 8], 1, 0) for i in range(count)]
    return jnp.concatenate(
        [jnp.where(top, turned[i - 1] if i else 0.0, turned[i]) for i in range(count)], axis=0
    )


def shift_up(x):
    count = x.shape[0] // 8
    end = lax.broadcasted_iota(jnp.int32, (8, x.shape[1]), 0) == 7
    turned = [pltpu.roll(x[8 * i : 8 * i + 8], 7, 0) for i in range(count)]
    return jnp.concatenate(
        [jnp.where(end, turned[i + 1] if i < count - 1 else 0.0, turned[i]) for i in range(count)], axis=0
    )


def in_rows(x, change):
    return jnp.concatenate([change(x[24 * r : 24 * r + 24]) for r in range(24)], axis=0)


def row_down(x):
    return jnp.concatenate([jnp.zeros((24, x.shape[1]), F32), x[:552]], axis=0)


def row_up(x):
    return jnp.concatenate([x[24:], jnp.zeros((24, x.shape[1]), F32)], axis=0)


def tile_sum(x):
    total = x[0:8]
    for i in range(1, x.shape[0] // 8):
        total = total + x[8 * i : 8 * i + 8]
    return total


def twice(m):
    return jnp.concatenate([m, m], axis=1)


def interleave(ref, r, even, odd):
    for p in range(2):
        at = slice(128 * p, 128 * p + 128)
        ref[p, pl.ds(r * 48, 24, stride=2), :] = even[:, at]
        ref[p, pl.ds(r * 48 + 1, 24, stride=2), :] = odd[:, at]


def rows_of(r, count, unit):
    start = r * unit
    return pl.ds(start if isinstance(r, int) else pl.multiple_of(start, unit if unit % 16 == 0 else 8), count)


def layer_kernel(
    plan,
    ext_ref, vec_ref, inp_hbm, inc_hbm, wu_hbm, wdn_hbm, wc6_hbm, wf_hbm, upf_hbm, upc_hbm,
    outf_ref, outc_ref, gif_ref, gic_ref, blocks_ref,
    inp_ref, inc_ref, wu_ref, wdn_ref, wc6_ref, wf_ref, upf_ref, upc_ref,
    grad_ref, block_ref, s_ref, ph_ref, c_ref, x_ref, xc_ref, lift_ref, mf_ref, mc_ref, scf_ref, scc_ref,
    gl_ref, glo_ref, back_ref, gp_ref, g_ref, row_ref, stage_ref, small_ref, in_sem, out_sem, block_sem, small_sem,
):
    loads = [
        pltpu.make_async_copy(src, dst, in_sem.at[n])
        for n, (src, dst) in enumerate(
            (
                (inp_hbm, inp_ref), (inc_hbm, inc_ref), (wu_hbm, wu_ref), (wdn_hbm, wdn_ref),
                (wc6_hbm, wc6_ref), (wf_hbm, wf_ref), (upf_hbm, upf_ref), (upc_hbm, upc_ref),
            )
        )
    ]
    for load in loads:
        load.start()
    hh, ww = ext_ref[0, 0], ext_ref[0, 1]
    gain_f = jnp.concatenate([vec_ref[0:1, :], vec_ref[1:2, :]], axis=1)
    bias_f = jnp.concatenate([vec_ref[2:3, :], vec_ref[3:4, :]], axis=1)
    gain_c, bias_c = vec_ref[4:5, :], vec_ref[5:6, :]
    pos = lax.broadcasted_iota(jnp.int32, (48, 128), 0)
    col = jnp.where(pos < 24, 2 * pos, 2 * pos - 47)
    colm = jnp.where(col < ww, 1.0, 0.0).astype(F32)

    def setup(r, _):
        at = rows_of(r, 48, 48)
        mf_ref[at, :] = jnp.where(r < hh, colm, 0.0)
        x_ref[at, :] = jnp.zeros((48, 256), F32)
        return 0

    lax.fori_loop(0, 48, setup, 0)

    def setup_coarse(r, _):
        mc_ref[rows_of(r, 24, 24), :] = jnp.where(2 * r < hh, colm[0:24], 0.0)
        return 0

    lax.fori_loop(0, 24, setup_coarse, 0)
    nf = (hh * ww).astype(F32) * (C1 // GROUPS)
    nc = (((hh + 1) // 2) * ((ww + 1) // 2)).astype(F32) * (C2 // GROUPS)
    s_ref[0:48, :] = jnp.zeros((48, 768), BF)
    s_ref[49 * 48 : 50 * 48, :] = jnp.zeros((48, 768), BF)
    g_ref[0:48, :] = jnp.zeros((48, 256), BF)
    g_ref[49 * 48 : 50 * 48, :] = jnp.zeros((48, 256), BF)
    grad_ref[FLAT_ROWS:, :] = jnp.zeros((plan.tall - FLAT_ROWS, 128), F32)
    xc_ref[...] = jnp.zeros((576, 128), F32)
    scf_ref[...] = jnp.zeros((8, 256), F32)
    scc_ref[...] = jnp.zeros((8, 128), F32)
    scf_ref[1:2, :] = 0.5 * bias_f
    scc_ref[1:2, :] = 0.5 * bias_c
    for load in loads[:6]:
        load.wait()

    def coarse_branch():
        h = xc_ref[...] * scc_ref[0:1, :] + scc_ref[1:2, :]
        y = h * jnp.tanh(h) + h
        branch = ((y + inc_ref[...].astype(F32)) * mc_ref[...]).astype(BF)
        lift_ref[...] = dot(branch, wu_ref[...])
        return branch

    def fine_rows(g, final):
        scale, shift = scf_ref[0:1, :], scf_ref[1:2, :]
        pieces = ([], [])
        for j in range(4):
            r = 4 * g + j
            at = rows_of(r, 48, 48)
            m = twice(mf_ref[at, :])
            h = x_ref[at, :] * scale + shift
            y = h * jnp.tanh(h) + h
            lift = lift_ref[rows_of(2 * g + j // 2, 24, 24), :]
            lift = jnp.concatenate([lift, lift], axis=0)
            if final:
                low = ((y + inp_ref[at, :].astype(F32)) * m).astype(BF)
                branch = low.astype(F32)
                z = (branch + lift) * m
                interleave(stage_ref.at[0], r, z[0:24], z[24:48])
            else:
                m = m.astype(BF)
                low = (y.astype(BF) + inp_ref[at, :]) * m
                branch = low.astype(F32)
                z = ((low + lift.astype(BF)) * m).astype(F32)
                even, odd = z[0:24], z[24:48]
                to = rows_of(r + 1, 48, 48)
                s_ref[to, 0:256] = jnp.concatenate([shift_down(odd), even], axis=0).astype(BF)
                s_ref[to, 256:512] = z.astype(BF)
                s_ref[to, 512:768] = jnp.concatenate([odd, shift_up(even)], axis=0).astype(BF)
            pieces[j % 2].append(branch)
        at = rows_of(g, 48, 48)
        for i, (above, below) in enumerate(pieces):
            ph_ref[2 * i, at, :] = jnp.concatenate([above[0:24], below[0:24]], axis=0).astype(BF)
            ph_ref[2 * i + 1, at, :] = jnp.concatenate([above[24:48], below[24:48]], axis=0).astype(BF)

    def lowered():
        ee, eo, oe, oo = (ph_ref[i] for i in range(4))
        p = dot(eo, wdn_ref[:, 128:384]) + dot(oo, wdn_ref[:, 640:896])
        q = dot(oe, wdn_ref[:, 384:640])
        t = dot(oo, wdn_ref[:, 896:1152])
        here = p[:, :128] + q[:, :128] + dot(ee, wdn_ref[:, 0:128])
        return here + row_down(q[:, 128:] + t[:, :128]) + in_rows(p[:, 128:] + row_down(t[:, 128:]), shift_down)

    def coarse_step(branch):
        zc = (branch.astype(F32) + lowered()) * mc_ref[...]
        c_ref[:, 0:128] = in_rows(zc, shift_down).astype(BF)
        c_ref[:, 128:256] = zc.astype(BF)
        p = dot(c_ref[...], wc6_ref[...])
        t = [p[:, 128 * i : 128 * i + 128] for i in range(6)]
        xc = row_down(t[0]) + t[1] + row_up(t[2]) + in_rows(row_down(t[3]) + t[4] + row_up(t[5]), shift_up)
        xc_ref[...] = xc
        xm = xc * mc_ref[...]
        return tile_sum(xm), tile_sum(xm * xm)

    def conv_rows(first, last):
        total = None
        for dy in range(3):
            p = dot(s_ref[48 * (first + dy) : 48 * (last + dy), :], wf_ref[768 * dy : 768 * dy + 768, :])
            total = p if total is None else total + p
        x_ref[48 * first : 48 * last, :] = total
        xm = total * twice(mf_ref[48 * first : 48 * last, :])
        return tile_sum(xm), tile_sum(xm * xm)

    def finish(s, q, width, n, gain, bias, to_ref):
        s, q = jnp.sum(s, axis=0, keepdims=True), jnp.sum(q, axis=0, keepdims=True)
        for p in range(s.shape[1] // 128):
            at = slice(128 * p, 128 * p + 128)
            mean = run_sum(s[:, at], width) / n
            var = jnp.maximum(run_sum(q[:, at], width) / n - mean * mean, 0.0)
            inv = lax.rsqrt(var + 1e-5)
            to_ref[0:1, at] = 0.5 * inv * gain[:, at]
            to_ref[1:2, at] = 0.5 * (bias[:, at] - mean * inv * gain[:, at])
            to_ref[2:3, at] = mean
            to_ref[3:4, at] = inv

    def iterate(t, _):
        branch_c = coarse_branch()
        s = q = None
        for g in range(12):
            fine_rows(g, False)
            ds, dq = conv_rows(4 * g - 1 if g else 0, 4 * g + 3 if g < 11 else 48)
            s, q = (ds, dq) if s is None else (s + ds, q + dq)
        sums_c = coarse_step(branch_c)
        finish(s, q, C1 // GROUPS, nf, gain_f, bias_f, scf_ref)
        finish(*sums_c, C2 // GROUPS, nc, gain_c, bias_c, scc_ref)
        return 0

    lax.fori_loop(0, ITERS, iterate, 0)
    branch_c = coarse_branch()

    def fine_last(g, _):
        fine_rows(g, True)
        return 0

    lax.fori_loop(0, 12, fine_last, 0, unroll=2)
    sends = [
        pltpu.make_async_copy(stage_ref.at[i, p], ref.at[:, 128 * p : 128 * p + 128], out_sem.at[i, p])
        for i, ref in enumerate((outf_ref, gif_ref))
        for p in range(2)
    ]
    sends += [
        pltpu.make_async_copy(small_ref.at[i], ref, small_sem.at[i]) for i, ref in enumerate((outc_ref, gic_ref))
    ]
    sends[0].start()
    sends[1].start()
    small_ref[0] = (branch_c.astype(F32) + lowered()) * mc_ref[...]
    sends[4].start()
    for load in loads[6:]:
        load.wait()

    seed_c = upc_ref[...].astype(F32) * mc_ref[...]
    right = in_rows(seed_c, shift_up)
    glo_ref[:, 0:128] = seed_c.astype(BF)
    glo_ref[:, 128:256] = right.astype(BF)
    glo_ref[:, 256:384] = row_up(seed_c).astype(BF)
    glo_ref[:, 384:512] = row_up(right).astype(BF)

    def fold(g, _):
        both = []
        for i in range(2):
            total = None
            for j in range(2):
                at = rows_of(4 * g + 2 * i + j, 48, 48)
                seed = upf_ref[at, :].astype(F32) * twice(mf_ref[at, :])
                part = seed[0:24] + seed[24:48]
                total = part if total is None else total + part
            both.append(total)
        gl_ref[rows_of(g, 48, 48), :] = jnp.concatenate(both, axis=0).astype(BF)
        return 0

    lax.fori_loop(0, 12, fold, 0, unroll=2)
    up_grad = dot_rows(branch_c, gl_ref[...])
    for j in range(2):
        grad_ref[pl.ds(ROW_UP + j, 128, stride=2), :] = up_grad[:, 128 * j : 128 * j + 128]
    g00, g01, g10, g11 = (glo_ref[:, 128 * i : 128 * i + 128] for i in range(4))
    for i, (parts, taps) in enumerate(
        (((g00,), (4,)), ((g00, g01), (5, 3)), ((g00, g10), (7, 1)), ((g00, g01, g10, g11), (8, 6, 2, 0)))
    ):
        down = dot_rows(ph_ref[i], jnp.concatenate(parts, axis=1))
        for n, tap in enumerate(taps):
            grad_ref[pl.ds(ROW_DOWN + tap, 256, stride=9), :] = down[:, 128 * n : 128 * n + 128]

    back_c = (seed_c + dot_lanes(gl_ref[...], wu_ref[...])) * mc_ref[...]
    small_ref[1] = back_c
    sends[5].start()

    def pre_grad(gi, x, scale, shift, mean, inv):
        h = x * scale + shift
        t = jnp.tanh(h)
        sig = 0.5 * t + 0.5
        normed = (x - mean) * inv
        return gi * sig * (1.0 + 2.0 * h * (1.0 - sig)), normed

    def back_means(sum_bias, sum_gain, gain, width, n):
        return run_sum(sum_bias * gain, width) / n, run_sum(sum_gain * gain, width) / n

    gp_c, normed_c = pre_grad(
        back_c, xc_ref[...], scc_ref[0:1, :], scc_ref[1:2, :], scc_ref[2:3, :], scc_ref[3:4, :]
    )
    sum_gain = jnp.sum(gp_c * normed_c, axis=0, keepdims=True)
    sum_bias = jnp.sum(gp_c, axis=0, keepdims=True)
    grad_ref[ROW_VEC + 4 : ROW_VEC + 5, :] = sum_gain
    grad_ref[ROW_VEC + 5 : ROW_VEC + 6, :] = sum_bias
    mean_h, mean_hn = back_means(sum_bias, sum_gain, gain_c, C2 // GROUPS, nc)
    gconv = (gp_c * gain_c - mean_h - normed_c * mean_hn) * scc_ref[3:4, :] * mc_ref[...]
    around = jnp.concatenate([row_up(gconv), gconv, row_down(gconv)], axis=1)
    pair = dot_rows(c_ref[...], around.astype(BF))
    single = dot_rows(c_ref[:, 128:256], in_rows(around, shift_down).astype(BF))
    for dy in range(3):
        at = slice(128 * dy, 128 * dy + 128)
        grad_ref[pl.ds(ROW_COARSE + 3 * dy, 128, stride=9), :] = pair[0:128, at]
        grad_ref[pl.ds(ROW_COARSE + 3 * dy + 1, 128, stride=9), :] = pair[128:256, at]
        grad_ref[pl.ds(ROW_COARSE + 3 * dy + 2, 128, stride=9), :] = single[:, at]

    back_ref[0] = dot_lanes(g00, wdn_ref[:, 0:128])
    back_ref[1] = dot_lanes(jnp.concatenate([g00, g01], axis=1), wdn_ref[:, 128:384])
    back_ref[2] = dot_lanes(jnp.concatenate([g00, g10], axis=1), wdn_ref[:, 384:640])
    back_ref[3] = dot_lanes(glo_ref[...], wdn_ref[:, 640:1152])

    def fine_back(i, carry):
        sums = list(carry)
        for j in range(2):
            r = 2 * i + j
            at = rows_of(r, 48, 48)
            half = rows_of(i, 24, 24)
            m = twice(mf_ref[at, :])
            back = jnp.concatenate([back_ref[2 * j, half, :], back_ref[2 * j + 1, half, :]], axis=0)
            gi = (upf_ref[at, :].astype(F32) + back) * m
            interleave(stage_ref.at[1], r, gi[0:24], gi[24:48])
            gp, normed = pre_grad(
                gi, x_ref[at, :], scf_ref[0:1, :], scf_ref[1:2, :], scf_ref[2:3, :], scf_ref[3:4, :]
            )
            gp_ref[at, :] = gp
            sums[0] = sums[0] + tile_sum(gp * normed)
            sums[1] = sums[1] + tile_sum(gp)
        return tuple(sums)

    none8 = jnp.zeros((8, 256), F32)
    sum_gain, sum_bias = lax.fori_loop(0, 24, fine_back, (none8, none8), unroll=2)
    sends[2].start()
    sends[3].start()
    sum_gain = jnp.sum(sum_gain, axis=0, keepdims=True)
    sum_bias = jnp.sum(sum_bias, axis=0, keepdims=True)
    for p in range(2):
        at = slice(128 * p, 128 * p + 128)
        grad_ref[ROW_VEC + p : ROW_VEC + p + 1, :] = sum_gain[:, at]
        grad_ref[ROW_VEC + 2 + p : ROW_VEC + 3 + p, :] = sum_bias[:, at]
        row_ref[0:1, at], row_ref[1:2, at] = back_means(
            sum_bias[:, at], sum_gain[:, at], gain_f[:, at], C1 // GROUPS, nf
        )

    def fine_conv_grad(r, _):
        at = rows_of(r, 48, 48)
        normed = (x_ref[at, :] - scf_ref[2:3, :]) * scf_ref[3:4, :]
        g = (gp_ref[at, :] * gain_f - row_ref[0:1, :] - normed * row_ref[1:2, :]) * scf_ref[3:4, :]
        g_ref[rows_of(r + 1, 48, 48), :] = (g * twice(mf_ref[at, :])).astype(BF)
        return 0

    lax.fori_loop(0, 48, fine_conv_grad, 0, unroll=2)
    for dx in range(3):
        states = s_ref[48:2352, 256 * dx : 256 * dx + 256]
        for dy in range(3):
            grad = dot_rows(states, g_ref[48 * (2 - dy) : 48 * (2 - dy) + 2304, :])
            for j in range(2):
                grad_ref[pl.ds(2 * (3 * dy + dx) + j, 256, stride=18), :] = grad[:, 128 * j : 128 * j + 128]
    for n, first in enumerate(plan.first):
        block_ref[n] = grad_ref[first : first + plan.rows, :].astype(BF)
        send = pltpu.make_async_copy(block_ref.at[n], blocks_ref.at[n], block_sem.at[n])
        send.start()
        sends.append(send)
    for send in sends:
        send.wait()


def layer_call(plan, *args):
    there = pl.BlockSpec(memory_space=pltpu.HBM)
    low = lambda *shape: pltpu.VMEM(shape, BF)
    wide = lambda *shape: pltpu.VMEM(shape, F32)
    return pl.pallas_call(
        functools.partial(layer_kernel, plan),
        out_shape=[
            jax.ShapeDtypeStruct((PIX, 256), F32),
            jax.ShapeDtypeStruct((CPIX, 128), F32),
            jax.ShapeDtypeStruct((PIX, 256), F32),
            jax.ShapeDtypeStruct((CPIX, 128), F32),
            jax.ShapeDtypeStruct((plan.n, plan.rows, 128), BF),
        ],
        in_specs=[pl.BlockSpec(memory_space=pltpu.SMEM), pl.BlockSpec(memory_space=pltpu.VMEM)] + [there] * 8,
        out_specs=[there] * 5,
        scratch_shapes=[
            low(PIX, 256), low(CPIX, 128), low(128, 256), low(256, 1152), low(256, 768), low(9 * 256, 256),
            low(PIX, 256), low(CPIX, 128),
            wide(plan.tall, 128), low(plan.n, plan.rows, 128),
            low(2400, 768), low(4, CPIX, 256), low(CPIX, 256),
            wide(PIX, 256), wide(CPIX, 128), wide(CPIX, 256), wide(PIX, 128), wide(CPIX, 128),
            wide(8, 256), wide(8, 128),
            low(CPIX, 256), low(CPIX, 512), wide(4, CPIX, 256), wide(PIX, 256), low(2400, 256), wide(8, 256),
            wide(2, 2, PIX, 128), wide(2, CPIX, 128),
            pltpu.SemaphoreType.DMA((8,)),
            pltpu.SemaphoreType.DMA((2, 2)),
            pltpu.SemaphoreType.DMA((plan.n,)),
            pltpu.SemaphoreType.DMA((2,)),
        ],
        compiler_params=pltpu.CompilerParams(vmem_limit_bytes=62 * 2**20),
        name="layer",
    )(*args)


class Plan:
    def __init__(self, shards, length):
        self.dims = {16: (4, 2, 2), 128: (4, 8, 4)}.get(shards, (shards, 1, 1))
        self.n, self.length = shards, length
        self.first = [s * length // 128 for s in range(shards)]
        self.rows = -(-(length + 127) // 128)
        self.rows = -(-self.rows // 32) * 32
        self.part = self.rows // 2
        self.cut = -(-self.part // 32) * 16
        self.tall = -(-(self.first[-1] + self.rows) // 16) * 16

    def here(self):
        d0, d1, d2 = self.dims
        me = lax.axis_index("fsdp")
        return me, lax.axis_index("rep"), me // (d1 * d2), me // d2 % d1, me % d2

    def block(self, a, b, c):
        d0, d1, d2 = self.dims
        return (a * d1 + b) * d2 + c


def flip(a, k):
    bit = 1
    while bit <= k:
        if k & bit:
            a = a + bit - 2 * bit * (a // bit % 2)
        bit *= 2
    return a


def gather_kernel(
    plan,
    master_hbm, inp_hbm, upf_hbm,
    vec_hbm, inpo_hbm, upfo_hbm, wu_hbm, wdn_hbm, wc6_hbm, wf_hbm,
    master_ref, inp_ref, upf_ref, vec_ref, inpo_ref, upfo_ref, wu_ref, wdn_ref, wc6_ref, wf_ref,
    g_ref, w_ref, tmp_ref, in_sem, out_sem, send_sem, recv_sem, sib_send, sib_recv, far_send,
):
    d0, d1, d2 = plan.dims
    me, core, a, b, c = plan.here()
    part, cut = plan.part, plan.cut
    loads = [
        pltpu.make_async_copy(src, dst, in_sem.at[n])
        for n, (src, dst) in enumerate(((master_hbm, master_ref), (inp_hbm, inp_ref), (upf_hbm, upf_ref)))
    ]
    for load in loads:
        load.start()
    barrier = pltpu.get_barrier_semaphore()
    others = [plan.block((a + k) % d0, b, c) for k in range(1, d0)]
    others += [plan.block(a, (b + k) % d1, c) for k in range(1, d1)]
    others += [plan.block(a, b, (c + k) % d2) for k in range(1, d2)]
    others = [{"fsdp": other, "rep": core} for other in others] + [{"fsdp": me, "rep": 1 - core}]
    for other in others:
        pl.semaphore_signal(barrier, inc=1, device_id=other, device_id_type=pl.DeviceIdType.MESH)
    loads[0].wait()
    off = (me * plan.length) % 128
    x = pltpu.roll(master_ref[...], off, 1)
    row = lax.broadcasted_iota(jnp.int32, x.shape, 0)
    lane = lax.broadcasted_iota(jnp.int32, x.shape, 1)
    above = jnp.where(row == 0, 0.0, pltpu.roll(x, 1, 0))
    g_ref[me] = jnp.where(lane < off, above, x).astype(BF)
    pl.semaphore_wait(barrier, len(others))

    def span(half, which):
        start = which * part + (cut if half == 1 else 0)
        return pl.ds(pl.multiple_of(start, 16), (cut, part - cut)[half])

    def copy(block, half, fsdp, rep, send, recv, which):
        at = g_ref.at[block, span(half, which)]
        return pltpu.make_async_remote_copy(
            src_ref=at, dst_ref=at, send_sem=send, recv_sem=recv,
            device_id={"fsdp": fsdp, "rep": rep}, device_id_type=pl.DeviceIdType.MESH,
        )

    def arrive(block, half):
        copy(block, half, me, core, far_send.at[0, 0], recv_sem.at[block, half], core).wait_recv()

    sent = []

    def go(d):
        d.start()
        sent.append(d)

    def along1(block, half):
        for k in range(1, d1):
            go(copy(block, half, plan.block(a, (b + k) % d1, c), core,
                    send_sem.at[block, half, k - 1], recv_sem.at[block, half], core))

    def along2(block, half):
        for k in range(1, d2):
            go(copy(block, half, plan.block(a, b, (c + k) % d2), core,
                    send_sem.at[block, half, d1 + k - 2], recv_sem.at[block, half], core))

    def beside(block, half):
        go(copy(block, half, me, 1 - core, sib_send.at[block, half], sib_recv.at[block, half], core))

    def own_column(k):
        block = plan.block(flip(a, k), b, c)
        if k:
            arrive(block, 0)
        along2(block, 0)
        if k:
            arrive(block, 1)
        along1(block, 1)
        along2(block, 1)
        along1(block, 0)
        if k:
            beside(block, 0)
            beside(block, 1)

    def near(k):
        a2 = flip(a, k)
        ahead = [plan.block(a2, b, (c + i) % d2) for i in range(1, d2)]
        above = [plan.block(a2, (b + i) % d1, c) for i in range(1, d1)]
        for block in ahead:
            arrive(block, 0)
            along1(block, 0)
            beside(block, 0)
        for block in above:
            arrive(block, 1)
            along2(block, 1)
            beside(block, 1)
        for block in ahead:
            arrive(block, 1)
            beside(block, 1)
        for block in above:
            arrive(block, 0)
            beside(block, 0)

    def diagonal(k):
        a2 = flip(a, k)
        for i in range(1, d1):
            for j in range(1, d2):
                block = plan.block(a2, (b + i) % d1, (c + j) % d2)
                for half in (0, 1):
                    arrive(block, half)
                    beside(block, half)

    def parity(src, dst):
        def one(r, _):
            at = rows_of(r, 48, 48)
            v = src[at, :].astype(F32)
            for p in range(2):
                tmp_ref[p, at, :] = v[:, 128 * p : 128 * p + 128]
            even = [tmp_ref[p, pl.ds(r * 48, 24, stride=2), :] for p in range(2)]
            odd = [tmp_ref[p, pl.ds(r * 48 + 1, 24, stride=2), :] for p in range(2)]
            both = [jnp.concatenate(even, axis=1), jnp.concatenate(odd, axis=1)]
            dst[at, :] = jnp.concatenate(both, axis=0).astype(BF)
            return 0

        lax.fori_loop(0, 48, one, 0, unroll=4)

    outs = []

    def put(src, dst):
        copy_out = pltpu.make_async_copy(src, dst, out_sem.at[len(outs)])
        copy_out.start()
        outs.append(copy_out)

    for k in range(1, d0):
        for half in (0, 1):
            go(copy(me, half, plan.block(flip(a, k), b, c), core, far_send.at[k, half], recv_sem.at[me, half], core))
    own_column(0)
    loads[1].wait()
    parity(inp_ref, inpo_ref)
    put(inpo_ref, inpo_hbm)
    loads[2].wait()
    parity(upf_ref, upfo_ref)
    put(upfo_ref, upfo_hbm)
    for k in range(1, d0):
        own_column(k)
    for k in range(d0):
        near(k)
    for k in range(d0):
        diagonal(k)
    for k in range(1, plan.n):
        block = (me + k) % plan.n
        for half in (0, 1):
            copy(block, half, me, core, far_send.at[0, 0], sib_recv.at[block, half], 1 - core).wait_recv()

    for s in range(plan.n):
        v = g_ref[s].astype(F32)
        at = plan.first[s]
        if s:
            low = w_ref[at : at + 1, :] + v[0:1]
            w_ref[at : at + plan.rows, :] = v
            w_ref[at : at + 1, :] = low
        else:
            w_ref[0 : plan.rows, :] = v
    vec_ref[...] = w_ref[ROW_VEC : ROW_VEC + 8, :]
    put(vec_ref, vec_hbm)
    for t in range(9):
        at = slice(256 * t, 256 * t + 256)
        for h in range(2):
            wf_ref[at, 128 * h : 128 * h + 128] = w_ref[pl.ds(2 * t + h, 256, stride=18), :].astype(BF)
        put(wf_ref.at[at], wf_hbm.at[at])
    for h in range(2):
        wu_ref[:, 128 * h : 128 * h + 128] = w_ref[pl.ds(ROW_UP + h, 128, stride=2), :].astype(BF)
    put(wu_ref, wu_hbm)
    for t in range(9):
        p = (4, 5, 3, 7, 1, 8, 6, 2, 0).index(t)
        wdn_ref[:, 128 * p : 128 * p + 128] = w_ref[pl.ds(ROW_DOWN + t, 256, stride=9), :].astype(BF)
    put(wdn_ref, wdn_hbm)
    wc6_ref[0:128, 384:768] = jnp.zeros((128, 384), BF)
    for t in range(9):
        dy, dx = t // 3, t % 3
        at, p = 128 * (dx + 1) // 2 // 128 * 128, dy + 3 * (dx // 2)
        wc6_ref[at : at + 128, 128 * p : 128 * p + 128] = w_ref[pl.ds(ROW_COARSE + t, 128, stride=9), :].astype(BF)
    put(wc6_ref, wc6_hbm)
    for d in sent:
        d.wait_send()
    for d in outs:
        d.wait()


def gather_call(plan, master, inp, upf):
    there = pl.BlockSpec(memory_space=pltpu.HBM)
    low = lambda *shape: jax.ShapeDtypeStruct(shape, BF)
    outs = [
        jax.ShapeDtypeStruct((8, 128), F32), low(PIX, 256), low(PIX, 256), low(128, 256), low(256, 1152),
        low(256, 768), low(9 * 256, 256),
    ]
    d0, d1, d2 = plan.dims
    sems = pltpu.SemaphoreType.DMA
    return pl.pallas_call(
        functools.partial(gather_kernel, plan),
        out_shape=[pltpu.HBM(o.shape, o.dtype) for o in outs],
        in_specs=[there] * 3,
        out_specs=[there] * 7,
        scratch_shapes=[pltpu.VMEM((plan.rows, 128), F32), pltpu.VMEM((PIX, 256), BF), pltpu.VMEM((PIX, 256), BF)]
        + [pltpu.VMEM(o.shape, o.dtype) for o in outs]
        + [
            pltpu.VMEM((plan.n, plan.rows, 128), BF), pltpu.VMEM((plan.tall, 128), F32), pltpu.VMEM((2, PIX, 128), F32),
            sems((3,)), sems((15,)), sems((plan.n, 2, max(d1 + d2 - 2, 1))), sems((plan.n, 2)), sems((plan.n, 2)),
            sems((plan.n, 2)), sems((d0, 2)),
        ],
        compiler_params=pltpu.CompilerParams(collective_id=0, has_side_effects=True, vmem_limit_bytes=32 * 2**20),
        name="gather_weights",
    )(*(pltpu.with_memory_space_constraint(x, pltpu.HBM) for x in (master, inp, upf)))


def reduce_kernel(plan, p_hbm, out_ref, tile_ref,
                  p_ref, q_ref, ua_ref, ub_ref, va_ref, vb_ref, z_ref, sa_ref, total_ref, n1_ref, n2_ref,
                  q_send, q_recv, s1_send, s1_recv, s2_send, s2_recv, s3_send, s3_recv, t_send, t_recv, n1_send, n1_recv, n2_send, n2_recv, own_sem):
    d0, d1, d2 = plan.dims
    me, core, a, b, c = plan.here()
    part, cut = plan.part, plan.cut
    MESH = pl.DeviceIdType.MESH
    mine = pl.multiple_of(core * part, 16)
    theirs = pl.multiple_of((1 - core) * part, 16)
    load = pltpu.make_async_copy(p_hbm.at[:, pl.ds(mine, part)], p_ref, own_sem.at[0])
    load.start()
    barrier = pltpu.get_barrier_semaphore()
    others = [({"fsdp": plan.block((a + k) % d0, b, c), "rep": core}) for k in range(1, d0)]
    plane = []
    for i in range(d1):
        for j in range(d2):
            for o in range(2):
                if i or j or o:
                    plane.append((i, j, o, {"fsdp": plan.block(a, (b + i) % d1, (c + j) % d2), "rep": (core + o) % 2}))
    others += [p[3] for p in plane]
    for other in others:
        pl.semaphore_signal(barrier, inc=1, device_id=other, device_id_type=MESH)
    pl.semaphore_wait(barrier, len(others))

    sent = []
    def go(src, dst, send, recv, to):
        d = pltpu.make_async_remote_copy(src_ref=src, dst_ref=dst, send_sem=send, recv_sem=recv, device_id=to, device_id_type=MESH)
        d.start()
        sent.append(d)

    def got(ref, recv):
        pltpu.make_async_copy(ref, ref, recv).wait()

    halves = ((0, cut), (cut, part - cut))
    order = [(k + 1) % d0 for k in range(d0)]
    spots = []
    for k in order:
        for i in list(range(1, d1)) + [0]:
            for j in list(range(1, d2)) + [0]:
                spots.append((k, i, j))
    for k, i, j in spots:
        s = plan.block((a + k) % d0, (b + i) % d1, (c + j) % d2)
        go(p_hbm.at[s, pl.ds(theirs, part)], q_ref.at[s], q_send.at[s], q_recv.at[s], {"fsdp": me, "rep": 1 - core})

    load.wait()

    def pair(s, half):
        start, size = halves[half]
        x = p_ref[s, start:start + size, :].astype(F32)
        return x + q_ref[s, start:start + size, :].astype(F32)

    def step1(k):
        a2 = (a + k) % d0
        for i in range(1, d1):
            for j in list(range(1, d2)) + [0]:
                s = plan.block(a2, (b + i) % d1, (c + j) % d2)
                got(q_ref.at[s], q_recv.at[s])
                sa_ref[s, 0:cut, :] = pair(s, 0).astype(BF)
                go(sa_ref.at[s, 0:cut], ua_ref.at[a2, (c + j) % d2, i - 1], s1_send.at[s, 0], s1_recv.at[0, a2, (c + j) % d2, i - 1],
                   {"fsdp": plan.block(a, (b + i) % d1, c), "rep": core})
                if j:
                    step1b(s, a2, i, j)
        for j in range(1, d2):
            s = plan.block(a2, b, (c + j) % d2)
            got(q_ref.at[s], q_recv.at[s])
            step1b(s, a2, 0, j)

    def step1b(s, a2, i, j):
        sa_ref[s, cut:part, :] = pair(s, 1).astype(BF)
        go(sa_ref.at[s, cut:part], ub_ref.at[a2, (b + i) % d1, j - 1], s1_send.at[s, 1], s1_recv.at[1, a2, (b + i) % d1, j - 1],
           {"fsdp": plan.block(a, b, (c + j) % d2), "rep": core})

    def from1(half, a2, other):
        ref = ua_ref if half == 0 else ub_ref
        total = None
        for i in range((d1 if half == 0 else d2) - 1):
            got(ref.at[a2, other, i], s1_recv.at[half, a2, other, i])
            v = ref[a2, other, i].astype(F32)
            total = v if total is None else total + v
        return total

    def plus(x, y):
        return x if y is None else x + y

    def step2(k):
        a2 = (a + k) % d0
        for j in range(1, d2):
            c2 = (c + j) % d2
            s = plan.block(a2, b, c2)
            sa_ref[s, 0:cut, :] = plus(pair(s, 0), from1(0, a2, c2)).astype(BF)
            go(sa_ref.at[s, 0:cut], va_ref.at[a2, j - 1], s2_send.at[0, a2, j - 1], s2_recv.at[0, a2, j - 1],
               {"fsdp": plan.block(a, b, c2), "rep": core})
        for i in range(1, d1):
            b2 = (b + i) % d1
            s = plan.block(a2, b2, c)
            sa_ref[s, cut:part, :] = plus(pair(s, 1), from1(1, a2, b2)).astype(BF)
            go(sa_ref.at[s, cut:part], vb_ref.at[a2, i - 1], s2_send.at[1, a2, i - 1], s2_recv.at[1, a2, i - 1],
               {"fsdp": plan.block(a, b2, c), "rep": core})

    def column(k):
        a2 = (a + k) % d0
        s = plan.block(a2, b, c)
        got(q_ref.at[s], q_recv.at[s])
        x = plus(pair(s, 0), from1(0, a2, c))
        for j in range(1, d2):
            got(va_ref.at[a2, j - 1], s2_recv.at[0, a2, j - 1])
            x = x + va_ref[a2, j - 1].astype(F32)
        y = plus(pair(s, 1), from1(1, a2, b))
        for i in range(1, d1):
            got(vb_ref.at[a2, i - 1], s2_recv.at[1, a2, i - 1])
            y = y + vb_ref[a2, i - 1].astype(F32)
        return s, x, y

    def step3(k):
        s, x, y = column(k)
        sa_ref[s, 0:cut, :] = x.astype(BF)
        sa_ref[s, cut:part, :] = y.astype(BF)
        go(sa_ref.at[s], z_ref.at[k - 1], s3_send.at[k - 1], s3_recv.at[k - 1], {"fsdp": plan.block((a + k) % d0, b, c), "rep": core})

    for n in range(d0 + 2):
        if n < d0:
            step1(order[n])
        if 0 <= n - 1 < d0:
            step2(order[n - 1])
        if 0 <= n - 2 < d0 - 1:
            step3(order[n - 2])
    _, x, y = column(0)
    total = jnp.concatenate([x, y], axis=0)
    for k in range(1, d0):
        got(z_ref.at[k - 1], s3_recv.at[k - 1])
        total = total + z_ref[k - 1].astype(F32)
    total_ref[pl.ds(mine, part), :] = total
    go(total_ref.at[pl.ds(mine, part)], total_ref.at[pl.ds(mine, part)], t_send.at[0], t_recv.at[0], {"fsdp": me, "rep": 1 - core})

    off = (me * plan.length) % 128
    row = lax.broadcasted_iota(jnp.int32, (part, 128), 0) + mine
    at = row * 128 + lax.broadcasted_iota(jnp.int32, (part, 128), 1)
    own = jnp.where((at >= off) & (at < off + plan.length), total, 0.0)
    last = me == plan.n - 1
    for i in range(6):
        spot = ROW_VEC - plan.first[-1] + i
        holds = last & (core == spot // part)
        n1_ref[a, i:i + 1, :] = jnp.where(holds, total[spot % part:spot % part + 1], 0.0)
    n1_ref[a, 6:7, :] = jnp.sum(own * own, axis=0, keepdims=True)
    n1_ref[a, 7:8, :] = jnp.zeros((1, 128), F32)
    for k in range(1, d0):
        go(n1_ref.at[a], n1_ref.at[a], n1_send.at[k], n1_recv.at[a], {"fsdp": plan.block((a + k) % d0, b, c), "rep": core})
    for k in range(1, d0):
        got(n1_ref.at[(a + k) % d0], n1_recv.at[(a + k) % d0])
    tile = n1_ref[0]
    for k in range(1, d0):
        tile = tile + n1_ref[k]
    slot = (b * d2 + c) * 2 + core
    n2_ref[slot] = tile
    for n, (i, j, o, to) in enumerate(plane):
        go(n2_ref.at[slot], n2_ref.at[slot], n2_send.at[n], n2_recv.at[slot], to)
    got(total_ref.at[pl.ds(theirs, part)], t_recv.at[0])
    x = pltpu.roll(total_ref[...], (128 - off) % 128, 1)
    below = pltpu.roll(x, plan.rows - 1, 0)
    lane = lax.broadcasted_iota(jnp.int32, x.shape, 1)
    moved = jnp.where(lane + off >= 128, below, x)
    for n, (i, j, o, to) in enumerate(plane):
        other = (((b + i) % d1) * d2 + (c + j) % d2) * 2 + (core + o) % 2
        got(n2_ref.at[other], n2_recv.at[other])
    tile = n2_ref[0]
    for n in range(1, 2 * d1 * d2):
        tile = tile + n2_ref[n]
    grad_norm = jnp.sqrt(jnp.sum(tile[6:7], axis=1, keepdims=True))
    factor = jnp.minimum(1.0, clip_norm / (grad_norm + 1e-06))
    out_ref[...] = moved * factor
    tile_ref[0:6, :] = tile[0:6] * factor
    tile_ref[6:8, :] = jnp.broadcast_to(grad_norm, (2, 128))
    for d in sent:
        d.wait_send()


def reduce_call(plan, grads):
    V = pl.BlockSpec(memory_space=pltpu.VMEM)
    d0, d1, d2 = plan.dims
    D = pltpu.SemaphoreType.DMA
    b = lambda *s: pltpu.VMEM(s, BF)
    e1, e2 = max(d1 - 1, 1), max(d2 - 1, 1)
    return pl.pallas_call(functools.partial(reduce_kernel, plan),
        out_shape=[jax.ShapeDtypeStruct((plan.rows, 128), F32), jax.ShapeDtypeStruct((8, 128), F32)],
        in_specs=[pl.BlockSpec(memory_space=pltpu.HBM)], out_specs=[V] * 2,
        scratch_shapes=[b(plan.n, plan.part, 128), b(plan.n, plan.part, 128), b(d0, d2, e1, plan.cut, 128), b(d0, d1, e2, plan.part - plan.cut, 128),
            b(d0, e2, plan.cut, 128), b(d0, e1, plan.part - plan.cut, 128), b(max(d0 - 1, 1), plan.part, 128), b(plan.n, plan.part, 128),
            pltpu.VMEM((plan.rows, 128), F32), pltpu.VMEM((d0, 8, 128), F32), pltpu.VMEM((2 * d1 * d2, 8, 128), F32),
            D((plan.n,)), D((plan.n,)), D((plan.n, 2)), D((2, d0, max(d1, d2), max(e1, e2))), D((2, d0, max(e1, e2))), D((2, d0, max(e1, e2))),
            D((d0,)), D((d0,)), D((1,)), D((1,)), D((d0,)), D((d0,)), D((2 * d1 * d2,)), D((2 * d1 * d2,)), D((1,))],
        compiler_params=pltpu.CompilerParams(collective_id=1, has_side_effects=True, vmem_limit_bytes=32 * 2**20),
        name="reduce_gradients")(pltpu.with_memory_space_constraint(grads, pltpu.HBM))


def per_device(
    input_fine, input_coarse, upstream_fine, upstream_coarse, extents, master, first_moment, second_moment, average
):
    plan = Plan(lax.axis_size("fsdp"), master.shape[0])
    padded = jnp.pad(master, (0, plan.rows * 128 - plan.length)).reshape(plan.rows, 128)
    vec, inp, upf, wu, wdn, wc6, wf = gather_call(
        plan, padded, input_fine.reshape(PIX, C1), upstream_fine.reshape(PIX, C1)
    )
    out_fine, out_coarse, gi_fine, gi_coarse, blocks = layer_call(
        plan, extents, vec, inp, input_coarse.reshape(CPIX, C2), wu, wdn, wc6, wf, upf,
        upstream_coarse.reshape(CPIX, C2),
    )
    clipped, tile = reduce_call(plan, blocks)
    clipped = clipped.reshape(-1)[: plan.length]
    grad_norm = tile[6, 0]
    norm_grads = tile[:6].reshape(-1)
    new_first = beta_one * first_moment + (1.0 - beta_one) * clipped
    new_second = beta_two * second_moment + (1.0 - beta_two) * clipped * clipped
    corrected_first = new_first / (1.0 - beta_one**STEP)
    corrected_second = new_second / (1.0 - beta_two**STEP)
    new_master = master - learn_rate * (
        corrected_first / (jnp.sqrt(corrected_second) + adam_eps) + decay_rate * master
    )
    ema_rate = min(0.999, (1.0 + STEP) / (10.0 + STEP))
    new_average = ema_rate * average + (1.0 - ema_rate) * new_master
    return (
        out_fine.reshape(input_fine.shape),
        out_coarse.reshape(input_coarse.shape),
        gi_fine.reshape(input_fine.shape),
        gi_coarse.reshape(input_coarse.shape),
        grad_norm,
        new_master,
        new_first,
        new_second,
        new_average,
        norm_grads,
    )


def solution(mesh):
    images = P(("fsdp", "rep"), None, None, None)
    flat = P("fsdp")
    in_specs = (images,) * 4 + (P(("fsdp", "rep"), None),) + (flat,) * 4
    out_specs = (images,) * 4 + (P(),) + (flat,) * 4 + (P(),)
    return jax.shard_map(per_device, mesh=mesh, in_specs=in_specs, out_specs=out_specs, check_vma=False)
```

```python
import functools

import jax
import jax.numpy as jnp
from jax import lax
from jax.experimental import pallas as pl
from jax.experimental.pallas import tpu as pltpu
from jax.sharding import PartitionSpec as P

F32, BF = jnp.float32, jnp.bfloat16
C1, C2, GROUPS, ITERS, STEP = 256, 128, 8, 12, 10
HEIGHT, HALF = 48, 24
PIX, CPIX = HEIGHT * HEIGHT, HALF * HALF
FLAT_ROWS = 8326
ROW_DOWN, ROW_COARSE, ROW_UP, ROW_VEC = 4608, 6912, 8064, 8320

clip_norm = 1.0
learn_rate = 0.02
beta_one = 0.9
beta_two = 0.999
adam_eps = 1e-08
decay_rate = 0.1


def dot(a, b):
    return jnp.dot(a, b, preferred_element_type=F32)


def dot_rows(a, b):
    return lax.dot_general(a, b, (((0,), (0,)), ((), ())), preferred_element_type=F32)


def dot_lanes(a, b):
    return lax.dot_general(a, b, (((1,), (1,)), ((), ())), preferred_element_type=F32)


def run_sum(x, width):
    lane = lax.broadcasted_iota(jnp.int32, x.shape, 1)
    step = 1
    while step < width:
        up = pltpu.roll(x, 128 - step, 1)
        down = pltpu.roll(x, step, 1)
        x = x + jnp.where((lane & step) == 0, up, down)
        step *= 2
    return x


def shift_down(x):
    count = x.shape[0] // 8
    top = lax.broadcasted_iota(jnp.int32, (8, x.shape[1]), 0) == 0
    turned = [pltpu.roll(x[8 * i : 8 * i + 8], 1, 0) for i in range(count)]
    return jnp.concatenate(
        [jnp.where(top, turned[i - 1] if i else 0.0, turned[i]) for i in range(count)], axis=0
    )


def shift_up(x):
    count = x.shape[0] // 8
    end = lax.broadcasted_iota(jnp.int32, (8, x.shape[1]), 0) == 7
    turned = [pltpu.roll(x[8 * i : 8 * i + 8], 7, 0) for i in range(count)]
    return jnp.concatenate(
        [jnp.where(end, turned[i + 1] if i < count - 1 else 0.0, turned[i]) for i in range(count)], axis=0
    )


def rows_out(x):
    parts = [x[24 * i : 24 * i + 24] for i in range(24)]
    return parts[0::2] + parts[1::2]


def pair_order(rows):
    return jnp.concatenate([rows[i // 2 + 12 * (i % 2)] for i in range(24)], axis=0)


def image_order(x):
    return jnp.concatenate(rows_out(x), axis=0)


def in_rows(x, change):
    return jnp.concatenate([change(x[24 * r : 24 * r + 24]) for r in range(24)], axis=0)


def row_down(x):
    rows = rows_out(x)
    return pair_order([jnp.zeros_like(rows[0])] + rows[:-1])


def row_up(x):
    rows = rows_out(x)
    return pair_order(rows[1:] + [jnp.zeros_like(rows[0])])


def tile_sum(x):
    total = x[0:8]
    for i in range(1, x.shape[0] // 8):
        total = total + x[8 * i : 8 * i + 8]
    return total


def twice(m):
    return jnp.concatenate([m, m], axis=1)


def interleave(ref, r, even, odd):
    for p in range(2):
        at = slice(128 * p, 128 * p + 128)
        ref[p, pl.ds(r * 48, 24, stride=2), :] = even[:, at]
        ref[p, pl.ds(r * 48 + 1, 24, stride=2), :] = odd[:, at]


def rows_of(r, count, unit):
    start = r * unit
    return pl.ds(start if isinstance(r, int) else pl.multiple_of(start, unit if unit % 16 == 0 else 8), count)


STEPS = "E0 E1 E2 C0 E3 E4 E5 C1 E6 E7 E8 C2 E9 E10 E11 C3 L C4 Z K C5 S F B"


def layer_kernel(
    plan,
    ext_ref, vec_ref, inp_hbm, inc_hbm, wu_hbm, wdn_hbm, wc6_hbm, wf_hbm, upf_hbm, upc_hbm,
    outf_ref, outc_ref, gif_ref, gic_ref, blocks_ref,
    inp_ref, inc_in, wu_ref, wdn_ref, wc6_ref, wf_ref, upf_ref, upc_ref,
    grad_ref, block_ref, u_ref, ph_ref, c_ref, x_ref, xc_ref, inc_ref, branch_ref, lift_ref, mf_ref, mb_ref, mc_ref,
    scf_ref, scc_ref, gl_ref, glo_ref, back_ref, gp_ref, g_ref, row_ref, stage_ref, small_ref,
    in_sem, out_sem, block_sem, small_sem,
):
    loads = [
        pltpu.make_async_copy(src, dst, in_sem.at[n])
        for n, (src, dst) in enumerate(
            (
                (inc_hbm, inc_in), (inp_hbm, inp_ref), (wu_hbm, wu_ref), (wdn_hbm, wdn_ref),
                (wc6_hbm, wc6_ref), (wf_hbm, wf_ref), (upf_hbm, upf_ref), (upc_hbm, upc_ref),
            )
        )
    ]
    for load in loads:
        load.start()
    hh, ww = ext_ref[0, 0], ext_ref[0, 1]
    gain_f = jnp.concatenate([vec_ref[0:1, :], vec_ref[1:2, :]], axis=1)
    bias_f = jnp.concatenate([vec_ref[2:3, :], vec_ref[3:4, :]], axis=1)
    gain_c, bias_c = vec_ref[4:5, :], vec_ref[5:6, :]
    pos = lax.broadcasted_iota(jnp.int32, (24, 128), 0)
    even = jnp.where(2 * pos < ww, 1.0, 0.0).astype(F32)
    odd = jnp.where(2 * pos + 1 < ww, 1.0, 0.0).astype(F32)

    def setup(r, _):
        at = rows_of(r, 96, 96)
        low, high = r < hh, r + 24 < hh
        m = [jnp.where(here, v, 0.0) for v in (even, odd) for here in (low, high)]
        m = jnp.concatenate(m, axis=0)
        mf_ref[at, :] = m
        mb_ref[at, :] = m.astype(BF)
        x_ref[at, :] = jnp.zeros((96, 256), F32)
        return 0

    lax.fori_loop(0, 24, setup, 0)

    def setup_coarse(r, _):
        m = [jnp.where(2 * r < hh, even, 0.0), jnp.where(2 * r + 24 < hh, even, 0.0)]
        mc_ref[rows_of(r, 48, 48), :] = jnp.concatenate(m, axis=0)
        return 0

    lax.fori_loop(0, 12, setup_coarse, 0)
    nf = (hh * ww).astype(F32) * (C1 // GROUPS)
    nc = (((hh + 1) // 2) * ((ww + 1) // 2)).astype(F32) * (C2 // GROUPS)
    g_ref[:, 0:96, :] = jnp.zeros((4, 96, 256), BF)
    g_ref[:, 26 * 48 : 28 * 48, :] = jnp.zeros((4, 96, 256), BF)
    grad_ref[FLAT_ROWS:, :] = jnp.zeros((plan.tall - FLAT_ROWS, 128), F32)
    xc_ref[...] = jnp.zeros((576, 128), F32)
    scf_ref[...] = jnp.zeros((8, 256), F32)
    scc_ref[...] = jnp.zeros((8, 128), F32)
    scf_ref[1:2, :] = 0.5 * bias_f
    scc_ref[1:2, :] = 0.5 * bias_c
    loads[0].wait()
    v = inc_in[...].astype(F32)
    inc_ref[...] = pair_order([v[24 * r : 24 * r + 24] for r in range(24)])
    for load in loads[1:6]:
        load.wait()

    def coarse_branch():
        h = xc_ref[...] * scc_ref[0:1, :] + scc_ref[1:2, :]
        y = h * jnp.tanh(h) + h
        branch = ((y + inc_ref[...]) * mc_ref[...]).astype(BF)
        branch_ref[...] = branch
        lift_ref[...] = dot(branch, wu_ref[...])

    def unit(r, final):
        scale, shift = scf_ref[0:1, :], scf_ref[1:2, :]
        half = rows_of(r // 2, 48, 48)
        lift = lift_ref[half, :]
        lift_low = lift.astype(BF)
        z = []
        for p in range(2):
            at = rows_of(2 * r + p, 48, 48)
            h = x_ref[at, :] * scale + shift
            y = h * jnp.tanh(h) + h
            if final:
                m = twice(mf_ref[at, :])
                low = ((y + inp_ref[at, :].astype(F32)) * m).astype(BF)
                z.append((low.astype(F32) + lift) * m)
            else:
                m = twice(mb_ref[at, :])
                low = (y.astype(BF) + inp_ref[at, :]) * m
                z.append((low + lift_low) * m)
            ph_ref[2 * (r % 2) + p, half, :] = low
        even, odd = z
        if final:
            for i in range(2):
                at = slice(24 * i, 24 * i + 24)
                interleave(stage_ref.at[0], r + 24 * i, even[at], odd[at])
            return
        wide = odd.astype(F32)
        left = jnp.concatenate([shift_down(wide[0:24]), shift_down(wide[24:48])], axis=0).astype(BF)
        wide = even.astype(F32)
        right = jnp.concatenate([shift_up(wide[0:24]), shift_up(wide[24:48])], axis=0).astype(BF)
        for i, u in enumerate((left - odd, even + odd, odd - even, even - right)):
            u_ref[i, rows_of(r + 1, 48, 48), :] = u
            if r == 0:
                w = u.astype(F32)
                u_ref[i, 25 * 48 : 26 * 48, :] = jnp.concatenate([w[24:48], jnp.zeros_like(w[0:24])], axis=0).astype(BF)
            if r == 23:
                w = u.astype(F32)
                u_ref[i, 0:48, :] = jnp.concatenate([jnp.zeros_like(w[0:24]), w[0:24]], axis=0).astype(BF)

    def lowered_parts():
        ee, eo, oe, oo = (ph_ref[i] for i in range(4))
        p = dot(eo, wdn_ref[:, 128:384]) + dot(oo, wdn_ref[:, 640:896])
        q = dot(oe, wdn_ref[:, 384:640])
        t = dot(oo, wdn_ref[:, 896:1152])
        return p, q, t, dot(ee, wdn_ref[:, 0:128])

    def lowered(parts):
        p, q, t, e = parts
        here = p[:, :128] + q[:, :128] + e
        return here + row_down(q[:, 128:] + t[:, :128]) + in_rows(p[:, 128:] + row_down(t[:, 128:]), shift_down)

    def coarse_state(parts):
        zc = (branch_ref[...].astype(F32) + lowered(parts)) * mc_ref[...]
        c_ref[:, 0:128] = in_rows(zc, shift_down).astype(BF)
        c_ref[:, 128:256] = zc.astype(BF)

    def coarse_sums(p):
        t = [p[:, 128 * i : 128 * i + 128] for i in range(6)]
        xc = row_down(t[0]) + t[1] + row_up(t[2]) + in_rows(row_down(t[3]) + t[4] + row_up(t[5]), shift_up)
        xc_ref[...] = xc
        xm = xc * mc_ref[...]
        return tile_sum(xm), tile_sum(xm * xm)

    def conv_units(units):
        products = []
        for i in range(4):
            total = None
            for dy in range(3):
                rows = [u_ref[i, 48 * (first + dy) : 48 * (last + dy), :] for first, last in units]
                rows = rows[0] if len(rows) == 1 else jnp.concatenate(rows, axis=0)
                at = 768 * i + 256 * dy
                p = dot(rows, wf_ref[at : at + 256, :])
                total = p if total is None else total + p
            products.append(total)
        m0, m1, m2, m3 = products
        even, odd = m0 + m1 + m2, m1 - m2 - m3
        s = q = None
        for n, r in enumerate(r for first, last in units for r in range(first, last)):
            for p, y in enumerate((even, odd)):
                y = y[48 * n : 48 * n + 48]
                at = slice(96 * r + 48 * p, 96 * r + 48 * p + 48)
                x_ref[at, :] = y
                ym = y * twice(mf_ref[at, :])
                ds, dq = tile_sum(ym), tile_sum(ym * ym)
                s, q = (ds, dq) if s is None else (s + ds, q + dq)
        return s, q

    def finish(s, q, width, n, gain, bias, to_ref):
        s, q = jnp.sum(s, axis=0, keepdims=True), jnp.sum(q, axis=0, keepdims=True)
        for p in range(s.shape[1] // 128):
            at = slice(128 * p, 128 * p + 128)
            mean = run_sum(s[:, at], width) / n
            var = jnp.maximum(run_sum(q[:, at], width) / n - mean * mean, 0.0)
            inv = lax.rsqrt(var + 1e-5)
            to_ref[0:1, at] = 0.5 * inv * gain[:, at]
            to_ref[1:2, at] = 0.5 * (bias[:, at] - mean * inv * gain[:, at])
            to_ref[2:3, at] = mean
            to_ref[3:4, at] = inv

    def iterate(t, _):
        s = q = parts = conv_c = sums_c = None
        for step in STEPS.split():
            n = int(step[1:] or 0)
            if step[0] == "E":
                unit(2 * n, False)
                unit(2 * n + 1, False)
            elif step[0] == "C":
                units = ((4 * n + 1, 4 * n + 5),) if n < 5 else ((21, 24), (0, 1))
                ds, dq = conv_units(units)
                s, q = (ds, dq) if s is None else (s + ds, q + dq)
            elif step == "L":
                parts = lowered_parts()
            elif step == "Z":
                coarse_state(parts)
            elif step == "K":
                conv_c = dot(c_ref[...], wc6_ref[...])
            elif step == "S":
                sums_c = coarse_sums(conv_c)
            elif step == "F":
                finish(*sums_c, C2 // GROUPS, nc, gain_c, bias_c, scc_ref)
            elif step == "B":
                coarse_branch()
        finish(s, q, C1 // GROUPS, nf, gain_f, bias_f, scf_ref)
        return 0

    coarse_branch()
    lax.fori_loop(0, ITERS, iterate, 0)

    def last_rows(r, _):
        unit(2 * r, True)
        unit(2 * r + 1, True)
        return 0

    lax.fori_loop(0, 12, last_rows, 0)
    sends = [
        pltpu.make_async_copy(stage_ref.at[i, p], ref.at[:, 128 * p : 128 * p + 128], out_sem.at[i, p])
        for i, ref in enumerate((outf_ref, gif_ref))
        for p in range(2)
    ]
    sends += [
        pltpu.make_async_copy(small_ref.at[i], ref, small_sem.at[i]) for i, ref in enumerate((outc_ref, gic_ref))
    ]
    sends[0].start()
    sends[1].start()
    small_ref[0] = image_order((branch_ref[...].astype(F32) + lowered(lowered_parts())) * mc_ref[...])
    sends[4].start()
    for load in loads[6:]:
        load.wait()

    v = upc_ref[...].astype(F32)
    seed_c = pair_order([v[24 * r : 24 * r + 24] for r in range(24)]) * mc_ref[...]
    right = in_rows(seed_c, shift_up)
    glo_ref[:, 0:128] = seed_c.astype(BF)
    glo_ref[:, 128:256] = right.astype(BF)
    glo_ref[:, 256:384] = row_up(seed_c).astype(BF)
    glo_ref[:, 384:512] = row_up(right).astype(BF)

    def fold(j, _):
        total = None
        for i in range(4):
            at = rows_of(4 * j + i, 48, 48)
            seed = upf_ref[at, :].astype(F32) * twice(mf_ref[at, :])
            total = seed if total is None else total + seed
        gl_ref[rows_of(j, 48, 48), :] = total.astype(BF)
        return 0

    lax.fori_loop(0, 12, fold, 0, unroll=2)
    up_grad = dot_rows(branch_ref[...], gl_ref[...])
    for j in range(2):
        grad_ref[pl.ds(ROW_UP + j, 128, stride=2), :] = up_grad[:, 128 * j : 128 * j + 128]
    g00, g01, g10, g11 = (glo_ref[:, 128 * i : 128 * i + 128] for i in range(4))
    for i, (parts, taps) in enumerate(
        (((g00,), (4,)), ((g00, g01), (5, 3)), ((g00, g10), (7, 1)), ((g00, g01, g10, g11), (8, 6, 2, 0)))
    ):
        down = dot_rows(ph_ref[i], jnp.concatenate(parts, axis=1))
        for n, tap in enumerate(taps):
            grad_ref[pl.ds(ROW_DOWN + tap, 256, stride=9), :] = down[:, 128 * n : 128 * n + 128]

    back_c = (seed_c + dot_lanes(gl_ref[...], wu_ref[...])) * mc_ref[...]
    small_ref[1] = image_order(back_c)
    sends[5].start()

    def pre_grad(gi, x, scale, shift, mean, inv):
        h = x * scale + shift
        t = jnp.tanh(h)
        sig = 0.5 * t + 0.5
        normed = (x - mean) * inv
        return gi * sig * (1.0 + 2.0 * h * (1.0 - sig)), normed

    def back_means(sum_bias, sum_gain, gain, width, n):
        return run_sum(sum_bias * gain, width) / n, run_sum(sum_gain * gain, width) / n

    gp_c, normed_c = pre_grad(
        back_c, xc_ref[...], scc_ref[0:1, :], scc_ref[1:2, :], scc_ref[2:3, :], scc_ref[3:4, :]
    )
    sum_gain = jnp.sum(gp_c * normed_c, axis=0, keepdims=True)
    sum_bias = jnp.sum(gp_c, axis=0, keepdims=True)
    grad_ref[ROW_VEC + 4 : ROW_VEC + 5, :] = sum_gain
    grad_ref[ROW_VEC + 5 : ROW_VEC + 6, :] = sum_bias
    mean_h, mean_hn = back_means(sum_bias, sum_gain, gain_c, C2 // GROUPS, nc)
    gconv = (gp_c * gain_c - mean_h - normed_c * mean_hn) * scc_ref[3:4, :] * mc_ref[...]
    around = jnp.concatenate([row_up(gconv), gconv, row_down(gconv)], axis=1)
    pair = dot_rows(c_ref[...], around.astype(BF))
    single = dot_rows(c_ref[:, 128:256], in_rows(around, shift_down).astype(BF))
    for dy in range(3):
        at = slice(128 * dy, 128 * dy + 128)
        grad_ref[pl.ds(ROW_COARSE + 3 * dy, 128, stride=9), :] = pair[0:128, at]
        grad_ref[pl.ds(ROW_COARSE + 3 * dy + 1, 128, stride=9), :] = pair[128:256, at]
        grad_ref[pl.ds(ROW_COARSE + 3 * dy + 2, 128, stride=9), :] = single[:, at]

    back_ref[0] = dot_lanes(g00, wdn_ref[:, 0:128])
    back_ref[1] = dot_lanes(jnp.concatenate([g00, g01], axis=1), wdn_ref[:, 128:384])
    back_ref[2] = dot_lanes(jnp.concatenate([g00, g10], axis=1), wdn_ref[:, 384:640])
    back_ref[3] = dot_lanes(glo_ref[...], wdn_ref[:, 640:1152])

    def fine_back(j, carry):
        sums = list(carry)
        for i in range(2):
            gi = []
            for p in range(2):
                at = rows_of(4 * j + 2 * i + p, 48, 48)
                back = back_ref[2 * i + p, rows_of(j, 48, 48), :]
                gi.append((upf_ref[at, :].astype(F32) + back) * twice(mf_ref[at, :]))
                gp, normed = pre_grad(
                    gi[p], x_ref[at, :], scf_ref[0:1, :], scf_ref[1:2, :], scf_ref[2:3, :], scf_ref[3:4, :]
                )
                gp_ref[at, :] = gp
                sums[0] = sums[0] + tile_sum(gp * normed)
                sums[1] = sums[1] + tile_sum(gp)
            for n in range(2):
                half = slice(24 * n, 24 * n + 24)
                interleave(stage_ref.at[1], 2 * j + i + 24 * n, gi[0][half], gi[1][half])
        return tuple(sums)

    none8 = jnp.zeros((8, 256), F32)
    sum_gain, sum_bias = lax.fori_loop(0, 12, fine_back, (none8, none8))
    sends[2].start()
    sends[3].start()
    sum_gain = jnp.sum(sum_gain, axis=0, keepdims=True)
    sum_bias = jnp.sum(sum_bias, axis=0, keepdims=True)
    for p in range(2):
        at = slice(128 * p, 128 * p + 128)
        grad_ref[ROW_VEC + p : ROW_VEC + p + 1, :] = sum_gain[:, at]
        grad_ref[ROW_VEC + 2 + p : ROW_VEC + 3 + p, :] = sum_bias[:, at]
        row_ref[0:1, at], row_ref[1:2, at] = back_means(
            sum_bias[:, at], sum_gain[:, at], gain_f[:, at], C1 // GROUPS, nf
        )

    def fine_conv_grad(r, _):
        g = []
        for p in range(2):
            at = rows_of(2 * r + p, 48, 48)
            normed = (x_ref[at, :] - scf_ref[2:3, :]) * scf_ref[3:4, :]
            v = (gp_ref[at, :] * gain_f - row_ref[0:1, :] - normed * row_ref[1:2, :]) * scf_ref[3:4, :]
            g.append(v * twice(mf_ref[at, :]))
        even, odd = g
        for i, v in enumerate((even, even + odd, even - odd, -odd)):
            g_ref[i, rows_of(r + 2, 48, 48), :] = v.astype(BF)
        return 0

    lax.fori_loop(0, 24, fine_conv_grad, 0, unroll=2)
    products = []
    for i in range(4):
        shifted = [g_ref[i, 48 * (2 - dy) : 48 * (2 - dy) + 26 * 48, :] for dy in range(3)]
        products.append(dot_rows(u_ref[i], jnp.concatenate(shifted, axis=1)))
    p0, p1, p2, p3 = products
    both, apart = 0.5 * (p1 + p2), 0.5 * (p1 - p2)
    for dx, grad in enumerate((p0 + both, apart, both + p3)):
        for dy in range(3):
            for j in range(2):
                at = 256 * dy + 128 * j
                grad_ref[pl.ds(2 * (3 * dy + dx) + j, 256, stride=18), :] = grad[:, at : at + 128]
    for n, first in enumerate(plan.first):
        block_ref[n] = grad_ref[first : first + plan.rows, :].astype(BF)
        send = pltpu.make_async_copy(block_ref.at[n], blocks_ref.at[n], block_sem.at[n])
        send.start()
        sends.append(send)
    for send in sends:
        send.wait()


def layer_call(plan, *args):
    there = pl.BlockSpec(memory_space=pltpu.HBM)
    low = lambda *shape: pltpu.VMEM(shape, BF)
    wide = lambda *shape: pltpu.VMEM(shape, F32)
    return pl.pallas_call(
        functools.partial(layer_kernel, plan),
        out_shape=[
            jax.ShapeDtypeStruct((PIX, 256), F32),
            jax.ShapeDtypeStruct((CPIX, 128), F32),
            jax.ShapeDtypeStruct((PIX, 256), F32),
            jax.ShapeDtypeStruct((CPIX, 128), F32),
            jax.ShapeDtypeStruct((plan.n, plan.rows, 128), BF),
        ],
        in_specs=[pl.BlockSpec(memory_space=pltpu.SMEM), pl.BlockSpec(memory_space=pltpu.VMEM)] + [there] * 8,
        out_specs=[there] * 5,
        scratch_shapes=[
            low(PIX, 256), low(CPIX, 128), low(128, 256), low(256, 1152), low(256, 768), low(12 * 256, 256),
            low(PIX, 256), low(CPIX, 128),
            wide(plan.tall, 128), low(plan.n, plan.rows, 128),
            low(4, 26 * 48, 256), low(4, CPIX, 256), low(CPIX, 256),
            wide(PIX, 256), wide(CPIX, 128), wide(CPIX, 128), low(CPIX, 128), wide(CPIX, 256),
            wide(PIX, 128), low(PIX, 128), wide(CPIX, 128),
            wide(8, 256), wide(8, 128),
            low(CPIX, 256), low(CPIX, 512), wide(4, CPIX, 256), wide(PIX, 256), low(4, 28 * 48, 256), wide(8, 256),
            wide(2, 2, PIX, 128), wide(2, CPIX, 128),
            pltpu.SemaphoreType.DMA((8,)),
            pltpu.SemaphoreType.DMA((2, 2)),
            pltpu.SemaphoreType.DMA((plan.n,)),
            pltpu.SemaphoreType.DMA((2,)),
        ],
        compiler_params=pltpu.CompilerParams(vmem_limit_bytes=62 * 2**20),
        name="layer",
    )(*args)


class Plan:
    def __init__(self, shards, length):
        self.dims = {16: (4, 2, 2), 128: (4, 8, 4)}.get(shards, (shards, 1, 1))
        self.n, self.length = shards, length
        self.first = [s * length // 128 for s in range(shards)]
        self.rows = -(-(length + 127) // 128)
        self.rows = -(-self.rows // 32) * 32
        self.part = self.rows // 2
        self.cut = -(-self.part // 32) * 16
        self.tall = -(-(self.first[-1] + self.rows) // 16) * 16

    def here(self):
        d0, d1, d2 = self.dims
        me = lax.axis_index("fsdp")
        return me, lax.axis_index("rep"), me // (d1 * d2), me // d2 % d1, me % d2

    def block(self, a, b, c):
        d0, d1, d2 = self.dims
        return (a * d1 + b) * d2 + c


def flip(a, k):
    bit = 1
    while bit <= k:
        if k & bit:
            a = a + bit - 2 * bit * (a // bit % 2)
        bit *= 2
    return a


def gather_kernel(
    plan,
    master_hbm, inp_hbm, upf_hbm,
    vec_hbm, inpo_hbm, upfo_hbm, wu_hbm, wdn_hbm, wc6_hbm, wf_hbm,
    master_ref, inp_ref, upf_ref, vec_ref, inpo_ref, upfo_ref, wu_ref, wdn_ref, wc6_ref, wf_ref,
    g_ref, w_ref, tmp_ref, in_sem, out_sem, send_sem, recv_sem, sib_send, sib_recv, far_send,
):
    d0, d1, d2 = plan.dims
    me, core, a, b, c = plan.here()
    part, cut = plan.part, plan.cut
    loads = [
        pltpu.make_async_copy(src, dst, in_sem.at[n])
        for n, (src, dst) in enumerate(((master_hbm, master_ref), (inp_hbm, inp_ref), (upf_hbm, upf_ref)))
    ]
    for load in loads:
        load.start()
    barrier = pltpu.get_barrier_semaphore()
    others = [plan.block((a + k) % d0, b, c) for k in range(1, d0)]
    others += [plan.block(a, (b + k) % d1, c) for k in range(1, d1)]
    others += [plan.block(a, b, (c + k) % d2) for k in range(1, d2)]
    others = [{"fsdp": other, "rep": core} for other in others] + [{"fsdp": me, "rep": 1 - core}]
    for other in others:
        pl.semaphore_signal(barrier, inc=1, device_id=other, device_id_type=pl.DeviceIdType.MESH)
    loads[0].wait()
    off = (me * plan.length) % 128
    x = pltpu.roll(master_ref[...], off, 1)
    row = lax.broadcasted_iota(jnp.int32, x.shape, 0)
    lane = lax.broadcasted_iota(jnp.int32, x.shape, 1)
    above = jnp.where(row == 0, 0.0, pltpu.roll(x, 1, 0))
    g_ref[me] = jnp.where(lane < off, above, x).astype(BF)
    pl.semaphore_wait(barrier, len(others))

    def span(half, which):
        start = which * part + (cut if half == 1 else 0)
        return pl.ds(pl.multiple_of(start, 16), (cut, part - cut)[half])

    def copy(block, half, fsdp, rep, send, recv, which):
        at = g_ref.at[block, span(half, which)]
        return pltpu.make_async_remote_copy(
            src_ref=at, dst_ref=at, send_sem=send, recv_sem=recv,
            device_id={"fsdp": fsdp, "rep": rep}, device_id_type=pl.DeviceIdType.MESH,
        )

    def arrive(block, half):
        copy(block, half, me, core, far_send.at[0, 0], recv_sem.at[block, half], core).wait_recv()

    sent = []

    def go(d):
        d.start()
        sent.append(d)

    def along1(block, half):
        for k in range(1, d1):
            go(copy(block, half, plan.block(a, (b + k) % d1, c), core,
                    send_sem.at[block, half, k - 1], recv_sem.at[block, half], core))

    def along2(block, half):
        for k in range(1, d2):
            go(copy(block, half, plan.block(a, b, (c + k) % d2), core,
                    send_sem.at[block, half, d1 + k - 2], recv_sem.at[block, half], core))

    def beside(block, half):
        go(copy(block, half, me, 1 - core, sib_send.at[block, half], sib_recv.at[block, half], core))

    def own_column(k):
        block = plan.block(flip(a, k), b, c)
        if k:
            arrive(block, 0)
        along2(block, 0)
        if k:
            arrive(block, 1)
        along1(block, 1)
        along2(block, 1)
        along1(block, 0)
        if k:
            beside(block, 0)
            beside(block, 1)

    def near(k):
        a2 = flip(a, k)
        ahead = [plan.block(a2, b, (c + i) % d2) for i in range(1, d2)]
        above = [plan.block(a2, (b + i) % d1, c) for i in range(1, d1)]
        for block in ahead:
            arrive(block, 0)
            along1(block, 0)
            beside(block, 0)
        for block in above:
            arrive(block, 1)
            along2(block, 1)
            beside(block, 1)
        for block in ahead:
            arrive(block, 1)
            beside(block, 1)
        for block in above:
            arrive(block, 0)
            beside(block, 0)

    def diagonal(k):
        a2 = flip(a, k)
        for i in range(1, d1):
            for j in range(1, d2):
                block = plan.block(a2, (b + i) % d1, (c + j) % d2)
                for half in (0, 1):
                    arrive(block, half)
                    beside(block, half)

    def parity(src, dst):
        def one(r, _):
            parts = []
            for n in range(2):
                at = rows_of(r + 24 * n, 48, 48)
                v = src[at, :].astype(F32)
                for p in range(2):
                    tmp_ref[p, at, :] = v[:, 128 * p : 128 * p + 128]
            for first in range(2):
                for n in range(2):
                    at = pl.ds((r + 24 * n) * 48 + first, 24, stride=2)
                    parts.append(jnp.concatenate([tmp_ref[p, at, :] for p in range(2)], axis=1))
            dst[rows_of(r, 96, 96), :] = jnp.concatenate(parts, axis=0).astype(BF)
            return 0

        lax.fori_loop(0, 24, one, 0, unroll=2)

    outs = []

    def put(src, dst):
        copy_out = pltpu.make_async_copy(src, dst, out_sem.at[len(outs)])
        copy_out.start()
        outs.append(copy_out)

    for k in range(1, d0):
        for half in (0, 1):
            go(copy(me, half, plan.block(flip(a, k), b, c), core, far_send.at[k, half], recv_sem.at[me, half], core))
    own_column(0)
    loads[1].wait()
    parity(inp_ref, inpo_ref)
    put(inpo_ref, inpo_hbm)
    loads[2].wait()
    parity(upf_ref, upfo_ref)
    put(upfo_ref, upfo_hbm)
    for k in range(1, d0):
        own_column(k)
    for k in range(d0):
        near(k)
    for k in range(d0):
        diagonal(k)
    for k in range(1, plan.n):
        block = (me + k) % plan.n
        for half in (0, 1):
            copy(block, half, me, core, far_send.at[0, 0], sib_recv.at[block, half], 1 - core).wait_recv()

    for s in range(plan.n):
        v = g_ref[s].astype(F32)
        at = plan.first[s]
        if s:
            low = w_ref[at : at + 1, :] + v[0:1]
            w_ref[at : at + plan.rows, :] = v
            w_ref[at : at + 1, :] = low
        else:
            w_ref[0 : plan.rows, :] = v
    vec_ref[...] = w_ref[ROW_VEC : ROW_VEC + 8, :]
    put(vec_ref, vec_hbm)
    for dy in range(3):
        for h in range(2):
            g0, g1, g2 = (w_ref[pl.ds(2 * (3 * dy + dx) + h, 256, stride=18), :] for dx in range(3))
            outer = g0 + g2
            for i, v in enumerate((g0, 0.5 * (outer + g1), 0.5 * (outer - g1), g2)):
                at = 768 * i + 256 * dy
                wf_ref[at : at + 256, 128 * h : 128 * h + 128] = v.astype(BF)
    put(wf_ref, wf_hbm)
    for h in range(2):
        wu_ref[:, 128 * h : 128 * h + 128] = w_ref[pl.ds(ROW_UP + h, 128, stride=2), :].astype(BF)
    put(wu_ref, wu_hbm)
    for t in range(9):
        p = (4, 5, 3, 7, 1, 8, 6, 2, 0).index(t)
        wdn_ref[:, 128 * p : 128 * p + 128] = w_ref[pl.ds(ROW_DOWN + t, 256, stride=9), :].astype(BF)
    put(wdn_ref, wdn_hbm)
    wc6_ref[0:128, 384:768] = jnp.zeros((128, 384), BF)
    for t in range(9):
        dy, dx = t // 3, t % 3
        at, p = 128 * (dx + 1) // 2 // 128 * 128, dy + 3 * (dx // 2)
        wc6_ref[at : at + 128, 128 * p : 128 * p + 128] = w_ref[pl.ds(ROW_COARSE + t, 128, stride=9), :].astype(BF)
    put(wc6_ref, wc6_hbm)
    for d in sent:
        d.wait_send()
    for d in outs:
        d.wait()


def gather_call(plan, master, inp, upf):
    there = pl.BlockSpec(memory_space=pltpu.HBM)
    low = lambda *shape: jax.ShapeDtypeStruct(shape, BF)
    outs = [
        jax.ShapeDtypeStruct((8, 128), F32), low(PIX, 256), low(PIX, 256), low(128, 256), low(256, 1152),
        low(256, 768), low(12 * 256, 256),
    ]
    d0, d1, d2 = plan.dims
    sems = pltpu.SemaphoreType.DMA
    return pl.pallas_call(
        functools.partial(gather_kernel, plan),
        out_shape=[pltpu.HBM(o.shape, o.dtype) for o in outs],
        in_specs=[there] * 3,
        out_specs=[there] * 7,
        scratch_shapes=[pltpu.VMEM((plan.rows, 128), F32), pltpu.VMEM((PIX, 256), BF), pltpu.VMEM((PIX, 256), BF)]
        + [pltpu.VMEM(o.shape, o.dtype) for o in outs]
        + [
            pltpu.VMEM((plan.n, plan.rows, 128), BF), pltpu.VMEM((plan.tall, 128), F32), pltpu.VMEM((2, PIX, 128), F32),
            sems((3,)), sems((15,)), sems((plan.n, 2, max(d1 + d2 - 2, 1))), sems((plan.n, 2)), sems((plan.n, 2)),
            sems((plan.n, 2)), sems((d0, 2)),
        ],
        compiler_params=pltpu.CompilerParams(collective_id=0, has_side_effects=True, vmem_limit_bytes=32 * 2**20),
        name="gather_weights",
    )(*(pltpu.with_memory_space_constraint(x, pltpu.HBM) for x in (master, inp, upf)))


def reduce_kernel(plan, p_hbm, out_ref, tile_ref,
                  p_ref, q_ref, ua_ref, ub_ref, va_ref, vb_ref, z_ref, sa_ref, total_ref, n1_ref, n2_ref,
                  q_send, q_recv, s1_send, s1_recv, s2_send, s2_recv, s3_send, s3_recv, t_send, t_recv, n1_send, n1_recv, n2_send, n2_recv, own_sem):
    d0, d1, d2 = plan.dims
    me, core, a, b, c = plan.here()
    part, cut = plan.part, plan.cut
    MESH = pl.DeviceIdType.MESH
    mine = pl.multiple_of(core * part, 16)
    theirs = pl.multiple_of((1 - core) * part, 16)
    load = pltpu.make_async_copy(p_hbm.at[:, pl.ds(mine, part)], p_ref, own_sem.at[0])
    load.start()
    barrier = pltpu.get_barrier_semaphore()
    others = [({"fsdp": plan.block((a + k) % d0, b, c), "rep": core}) for k in range(1, d0)]
    plane = []
    for i in range(d1):
        for j in range(d2):
            for o in range(2):
                if i or j or o:
                    plane.append((i, j, o, {"fsdp": plan.block(a, (b + i) % d1, (c + j) % d2), "rep": (core + o) % 2}))
    others += [p[3] for p in plane]
    for other in others:
        pl.semaphore_signal(barrier, inc=1, device_id=other, device_id_type=MESH)
    pl.semaphore_wait(barrier, len(others))

    sent = []
    def go(src, dst, send, recv, to):
        d = pltpu.make_async_remote_copy(src_ref=src, dst_ref=dst, send_sem=send, recv_sem=recv, device_id=to, device_id_type=MESH)
        d.start()
        sent.append(d)

    def got(ref, recv):
        pltpu.make_async_copy(ref, ref, recv).wait()

    halves = ((0, cut), (cut, part - cut))
    order = [(k + 1) % d0 for k in range(d0)]
    spots = []
    for k in order:
        for i in list(range(1, d1)) + [0]:
            for j in list(range(1, d2)) + [0]:
                spots.append((k, i, j))
    for k, i, j in spots:
        s = plan.block((a + k) % d0, (b + i) % d1, (c + j) % d2)
        go(p_hbm.at[s, pl.ds(theirs, part)], q_ref.at[s], q_send.at[s], q_recv.at[s], {"fsdp": me, "rep": 1 - core})

    load.wait()

    def pair(s, half):
        start, size = halves[half]
        x = p_ref[s, start:start + size, :].astype(F32)
        return x + q_ref[s, start:start + size, :].astype(F32)

    def step1(k):
        a2 = (a + k) % d0
        for i in range(1, d1):
            for j in list(range(1, d2)) + [0]:
                s = plan.block(a2, (b + i) % d1, (c + j) % d2)
                got(q_ref.at[s], q_recv.at[s])
                sa_ref[s, 0:cut, :] = pair(s, 0).astype(BF)
                go(sa_ref.at[s, 0:cut], ua_ref.at[a2, (c + j) % d2, i - 1], s1_send.at[s, 0], s1_recv.at[0, a2, (c + j) % d2, i - 1],
                   {"fsdp": plan.block(a, (b + i) % d1, c), "rep": core})
                if j:
                    step1b(s, a2, i, j)
        for j in range(1, d2):
            s = plan.block(a2, b, (c + j) % d2)
            got(q_ref.at[s], q_recv.at[s])
            step1b(s, a2, 0, j)

    def step1b(s, a2, i, j):
        sa_ref[s, cut:part, :] = pair(s, 1).astype(BF)
        go(sa_ref.at[s, cut:part], ub_ref.at[a2, (b + i) % d1, j - 1], s1_send.at[s, 1], s1_recv.at[1, a2, (b + i) % d1, j - 1],
           {"fsdp": plan.block(a, b, (c + j) % d2), "rep": core})

    def from1(half, a2, other):
        ref = ua_ref if half == 0 else ub_ref
        total = None
        for i in range((d1 if half == 0 else d2) - 1):
            got(ref.at[a2, other, i], s1_recv.at[half, a2, other, i])
            v = ref[a2, other, i].astype(F32)
            total = v if total is None else total + v
        return total

    def plus(x, y):
        return x if y is None else x + y

    def step2(k):
        a2 = (a + k) % d0
        for j in range(1, d2):
            c2 = (c + j) % d2
            s = plan.block(a2, b, c2)
            sa_ref[s, 0:cut, :] = plus(pair(s, 0), from1(0, a2, c2)).astype(BF)
            go(sa_ref.at[s, 0:cut], va_ref.at[a2, j - 1], s2_send.at[0, a2, j - 1], s2_recv.at[0, a2, j - 1],
               {"fsdp": plan.block(a, b, c2), "rep": core})
        for i in range(1, d1):
            b2 = (b + i) % d1
            s = plan.block(a2, b2, c)
            sa_ref[s, cut:part, :] = plus(pair(s, 1), from1(1, a2, b2)).astype(BF)
            go(sa_ref.at[s, cut:part], vb_ref.at[a2, i - 1], s2_send.at[1, a2, i - 1], s2_recv.at[1, a2, i - 1],
               {"fsdp": plan.block(a, b2, c), "rep": core})

    def column(k):
        a2 = (a + k) % d0
        s = plan.block(a2, b, c)
        got(q_ref.at[s], q_recv.at[s])
        x = plus(pair(s, 0), from1(0, a2, c))
        for j in range(1, d2):
            got(va_ref.at[a2, j - 1], s2_recv.at[0, a2, j - 1])
            x = x + va_ref[a2, j - 1].astype(F32)
        y = plus(pair(s, 1), from1(1, a2, b))
        for i in range(1, d1):
            got(vb_ref.at[a2, i - 1], s2_recv.at[1, a2, i - 1])
            y = y + vb_ref[a2, i - 1].astype(F32)
        return s, x, y

    def step3(k):
        s, x, y = column(k)
        sa_ref[s, 0:cut, :] = x.astype(BF)
        sa_ref[s, cut:part, :] = y.astype(BF)
        go(sa_ref.at[s], z_ref.at[k - 1], s3_send.at[k - 1], s3_recv.at[k - 1], {"fsdp": plan.block((a + k) % d0, b, c), "rep": core})

    for n in range(d0 + 2):
        if n < d0:
            step1(order[n])
        if 0 <= n - 1 < d0:
            step2(order[n - 1])
        if 0 <= n - 2 < d0 - 1:
            step3(order[n - 2])
    _, x, y = column(0)
    total = jnp.concatenate([x, y], axis=0)
    for k in range(1, d0):
        got(z_ref.at[k - 1], s3_recv.at[k - 1])
        total = total + z_ref[k - 1].astype(F32)
    total_ref[pl.ds(mine, part), :] = total
    go(total_ref.at[pl.ds(mine, part)], total_ref.at[pl.ds(mine, part)], t_send.at[0], t_recv.at[0], {"fsdp": me, "rep": 1 - core})

    off = (me * plan.length) % 128
    row = lax.broadcasted_iota(jnp.int32, (part, 128), 0) + mine
    at = row * 128 + lax.broadcasted_iota(jnp.int32, (part, 128), 1)
    own = jnp.where((at >= off) & (at < off + plan.length), total, 0.0)
    last = me == plan.n - 1
    for i in range(6):
        spot = ROW_VEC - plan.first[-1] + i
        holds = last & (core == spot // part)
        n1_ref[a, i:i + 1, :] = jnp.where(holds, total[spot % part:spot % part + 1], 0.0)
    n1_ref[a, 6:7, :] = jnp.sum(own * own, axis=0, keepdims=True)
    n1_ref[a, 7:8, :] = jnp.zeros((1, 128), F32)
    for k in range(1, d0):
        go(n1_ref.at[a], n1_ref.at[a], n1_send.at[k], n1_recv.at[a], {"fsdp": plan.block((a + k) % d0, b, c), "rep": core})
    for k in range(1, d0):
        got(n1_ref.at[(a + k) % d0], n1_recv.at[(a + k) % d0])
    tile = n1_ref[0]
    for k in range(1, d0):
        tile = tile + n1_ref[k]
    slot = (b * d2 + c) * 2 + core
    n2_ref[slot] = tile
    for n, (i, j, o, to) in enumerate(plane):
        go(n2_ref.at[slot], n2_ref.at[slot], n2_send.at[n], n2_recv.at[slot], to)
    got(total_ref.at[pl.ds(theirs, part)], t_recv.at[0])
    x = pltpu.roll(total_ref[...], (128 - off) % 128, 1)
    below = pltpu.roll(x, plan.rows - 1, 0)
    lane = lax.broadcasted_iota(jnp.int32, x.shape, 1)
    moved = jnp.where(lane + off >= 128, below, x)
    for n, (i, j, o, to) in enumerate(plane):
        other = (((b + i) % d1) * d2 + (c + j) % d2) * 2 + (core + o) % 2
        got(n2_ref.at[other], n2_recv.at[other])
    tile = n2_ref[0]
    for n in range(1, 2 * d1 * d2):
        tile = tile + n2_ref[n]
    grad_norm = jnp.sqrt(jnp.sum(tile[6:7], axis=1, keepdims=True))
    factor = jnp.minimum(1.0, clip_norm / (grad_norm + 1e-06))
    out_ref[...] = moved * factor
    tile_ref[0:6, :] = tile[0:6] * factor
    tile_ref[6:8, :] = jnp.broadcast_to(grad_norm, (2, 128))
    for d in sent:
        d.wait_send()


def reduce_call(plan, grads):
    V = pl.BlockSpec(memory_space=pltpu.VMEM)
    d0, d1, d2 = plan.dims
    D = pltpu.SemaphoreType.DMA
    b = lambda *s: pltpu.VMEM(s, BF)
    e1, e2 = max(d1 - 1, 1), max(d2 - 1, 1)
    return pl.pallas_call(functools.partial(reduce_kernel, plan),
        out_shape=[jax.ShapeDtypeStruct((plan.rows, 128), F32), jax.ShapeDtypeStruct((8, 128), F32)],
        in_specs=[pl.BlockSpec(memory_space=pltpu.HBM)], out_specs=[V] * 2,
        scratch_shapes=[b(plan.n, plan.part, 128), b(plan.n, plan.part, 128), b(d0, d2, e1, plan.cut, 128), b(d0, d1, e2, plan.part - plan.cut, 128),
            b(d0, e2, plan.cut, 128), b(d0, e1, plan.part - plan.cut, 128), b(max(d0 - 1, 1), plan.part, 128), b(plan.n, plan.part, 128),
            pltpu.VMEM((plan.rows, 128), F32), pltpu.VMEM((d0, 8, 128), F32), pltpu.VMEM((2 * d1 * d2, 8, 128), F32),
            D((plan.n,)), D((plan.n,)), D((plan.n, 2)), D((2, d0, max(d1, d2), max(e1, e2))), D((2, d0, max(e1, e2))), D((2, d0, max(e1, e2))),
            D((d0,)), D((d0,)), D((1,)), D((1,)), D((d0,)), D((d0,)), D((2 * d1 * d2,)), D((2 * d1 * d2,)), D((1,))],
        compiler_params=pltpu.CompilerParams(collective_id=1, has_side_effects=True, vmem_limit_bytes=32 * 2**20),
        name="reduce_gradients")(pltpu.with_memory_space_constraint(grads, pltpu.HBM))


def per_device(
    input_fine, input_coarse, upstream_fine, upstream_coarse, extents, master, first_moment, second_moment, average
):
    plan = Plan(lax.axis_size("fsdp"), master.shape[0])
    padded = jnp.pad(master, (0, plan.rows * 128 - plan.length)).reshape(plan.rows, 128)
    vec, inp, upf, wu, wdn, wc6, wf = gather_call(
        plan, padded, input_fine.reshape(PIX, C1), upstream_fine.reshape(PIX, C1)
    )
    out_fine, out_coarse, gi_fine, gi_coarse, blocks = layer_call(
        plan, extents, vec, inp, input_coarse.reshape(CPIX, C2), wu, wdn, wc6, wf, upf,
        upstream_coarse.reshape(CPIX, C2),
    )
    clipped, tile = reduce_call(plan, blocks)
    clipped = clipped.reshape(-1)[: plan.length]
    grad_norm = tile[6, 0]
    norm_grads = tile[:6].reshape(-1)
    new_first = beta_one * first_moment + (1.0 - beta_one) * clipped
    new_second = beta_two * second_moment + (1.0 - beta_two) * clipped * clipped
    corrected_first = new_first / (1.0 - beta_one**STEP)
    corrected_second = new_second / (1.0 - beta_two**STEP)
    new_master = master - learn_rate * (
        corrected_first / (jnp.sqrt(corrected_second) + adam_eps) + decay_rate * master
    )
    ema_rate = min(0.999, (1.0 + STEP) / (10.0 + STEP))
    new_average = ema_rate * average + (1.0 - ema_rate) * new_master
    return (
        out_fine.reshape(input_fine.shape),
        out_coarse.reshape(input_coarse.shape),
        gi_fine.reshape(input_fine.shape),
        gi_coarse.reshape(input_coarse.shape),
        grad_norm,
        new_master,
        new_first,
        new_second,
        new_average,
        norm_grads,
    )


def solution(mesh):
    images = P(("fsdp", "rep"), None, None, None)
    flat = P("fsdp")
    in_specs = (images,) * 4 + (P(("fsdp", "rep"), None),) + (flat,) * 4
    out_specs = (images,) * 4 + (P(),) + (flat,) * 4 + (P(),)
    return jax.shard_map(per_device, mesh=mesh, in_specs=in_specs, out_specs=out_specs, check_vma=False)
```

```python
import functools

import jax
import jax.numpy as jnp
from jax import lax
from jax.experimental import pallas as pl
from jax.experimental.pallas import tpu as pltpu
from jax.sharding import PartitionSpec as P

F32, BF = jnp.float32, jnp.bfloat16
C1, C2, GROUPS, ITERS, STEP = 256, 128, 8, 12, 10
HEIGHT, HALF = 48, 24
PIX, CPIX = HEIGHT * HEIGHT, HALF * HALF
FLAT_ROWS = 8326
ROW_DOWN, ROW_COARSE, ROW_UP, ROW_VEC = 4608, 6912, 8064, 8320

clip_norm = 1.0
learn_rate = 0.02
beta_one = 0.9
beta_two = 0.999
adam_eps = 1e-08
decay_rate = 0.1


def dot(a, b):
    return jnp.dot(a, b, preferred_element_type=F32)


def dot_rows(a, b):
    return lax.dot_general(a, b, (((0,), (0,)), ((), ())), preferred_element_type=F32)


def dot_lanes(a, b):
    return lax.dot_general(a, b, (((1,), (1,)), ((), ())), preferred_element_type=F32)


def run_sum(x, width):
    lane = lax.broadcasted_iota(jnp.int32, x.shape, 1)
    step = 1
    while step < width:
        up = pltpu.roll(x, 128 - step, 1)
        down = pltpu.roll(x, step, 1)
        x = x + jnp.where((lane & step) == 0, up, down)
        step *= 2
    return x


def shift_down(x):
    count = x.shape[0] // 8
    top = lax.broadcasted_iota(jnp.int32, (8, x.shape[1]), 0) == 0
    turned = [pltpu.roll(x[8 * i : 8 * i + 8], 1, 0) for i in range(count)]
    return jnp.concatenate(
        [jnp.where(top, turned[i - 1] if i else 0.0, turned[i]) for i in range(count)], axis=0
    )


def shift_up(x):
    count = x.shape[0] // 8
    end = lax.broadcasted_iota(jnp.int32, (8, x.shape[1]), 0) == 7
    turned = [pltpu.roll(x[8 * i : 8 * i + 8], 7, 0) for i in range(count)]
    return jnp.concatenate(
        [jnp.where(end, turned[i + 1] if i < count - 1 else 0.0, turned[i]) for i in range(count)], axis=0
    )


def rows_out(x):
    parts = [x[24 * i : 24 * i + 24] for i in range(24)]
    return parts[0::2] + parts[1::2]


def pair_order(rows):
    return jnp.concatenate([rows[i // 2 + 12 * (i % 2)] for i in range(24)], axis=0)


def image_order(x):
    return jnp.concatenate(rows_out(x), axis=0)


def in_rows(x, change):
    return jnp.concatenate([change(x[24 * r : 24 * r + 24]) for r in range(24)], axis=0)


def row_down(x):
    rows = rows_out(x)
    return pair_order([jnp.zeros_like(rows[0])] + rows[:-1])


def row_up(x):
    rows = rows_out(x)
    return pair_order(rows[1:] + [jnp.zeros_like(rows[0])])


def tile_sum(x):
    total = x[0:8]
    for i in range(1, x.shape[0] // 8):
        total = total + x[8 * i : 8 * i + 8]
    return total


def twice(m):
    return jnp.concatenate([m, m], axis=1)


def interleave(ref, r, even, odd):
    for p in range(2):
        at = slice(128 * p, 128 * p + 128)
        ref[p, pl.ds(r * 48, 24, stride=2), :] = even[:, at]
        ref[p, pl.ds(r * 48 + 1, 24, stride=2), :] = odd[:, at]


def rows_of(r, count, unit):
    start = r * unit
    return pl.ds(start if isinstance(r, int) else pl.multiple_of(start, unit if unit % 16 == 0 else 8), count)


STEPS = "E0 E1 E2 E3 C1-7 E4 E5 E6 C7-13 E7 E8 E9 E10 E11 C13-17 L C17-21 Z K C21-24,0-1 S F B"


def layer_kernel(
    plan,
    ext_ref, vec_ref, inp_hbm, inc_hbm, wu_hbm, wdn_hbm, wc6_hbm, wf_hbm, upf_hbm, upc_hbm,
    outf_ref, outc_ref, gif_ref, gic_ref, uo_ref, go_ref, join_ref, blocks_ref,
    inp_ref, inc_in, wu_ref, wdn_ref, wc6_ref, wf_ref, upf_ref, upc_ref,
    grad_ref, block_ref, u_ref, ph_ref, c_ref, x_ref, xc_ref, inc_ref, branch_ref, lift_ref, mf_ref, mb_ref, mc_ref,
    scf_ref, scc_ref, gl_ref, glo_ref, back_ref, gp_ref, g_ref, row_ref, stage_ref, small_ref,
    in_sem, out_sem, hand_sem, small_sem,
):
    loads = [
        pltpu.make_async_copy(src, dst, in_sem.at[n])
        for n, (src, dst) in enumerate(
            (
                (inc_hbm, inc_in), (inp_hbm, inp_ref), (wu_hbm, wu_ref), (wdn_hbm, wdn_ref),
                (wc6_hbm, wc6_ref), (wf_hbm, wf_ref), (upf_hbm, upf_ref), (upc_hbm, upc_ref),
            )
        )
    ]
    for load in loads:
        load.start()
    hh, ww = ext_ref[0, 0], ext_ref[0, 1]
    gain_f = jnp.concatenate([vec_ref[0:1, :], vec_ref[1:2, :]], axis=1)
    bias_f = jnp.concatenate([vec_ref[2:3, :], vec_ref[3:4, :]], axis=1)
    gain_c, bias_c = vec_ref[4:5, :], vec_ref[5:6, :]
    pos = lax.broadcasted_iota(jnp.int32, (24, 128), 0)
    even = jnp.where(2 * pos < ww, 1.0, 0.0).astype(F32)
    odd = jnp.where(2 * pos + 1 < ww, 1.0, 0.0).astype(F32)

    def setup(r, _):
        at = rows_of(r, 96, 96)
        low, high = r < hh, r + 24 < hh
        m = [jnp.where(here, v, 0.0) for v in (even, odd) for here in (low, high)]
        m = jnp.concatenate(m, axis=0)
        mf_ref[at, :] = m
        mb_ref[at, :] = m.astype(BF)
        x_ref[at, :] = jnp.zeros((96, 256), F32)
        return 0

    lax.fori_loop(0, 24, setup, 0)

    def setup_coarse(r, _):
        m = [jnp.where(2 * r < hh, even, 0.0), jnp.where(2 * r + 24 < hh, even, 0.0)]
        mc_ref[rows_of(r, 48, 48), :] = jnp.concatenate(m, axis=0)
        return 0

    lax.fori_loop(0, 12, setup_coarse, 0)
    nf = (hh * ww).astype(F32) * (C1 // GROUPS)
    nc = (((hh + 1) // 2) * ((ww + 1) // 2)).astype(F32) * (C2 // GROUPS)
    g_ref[:, 0:96, :] = jnp.zeros((2, 96, 256), BF)
    g_ref[:, 26 * 48 : 28 * 48, :] = jnp.zeros((2, 96, 256), BF)
    grad_ref[FLAT_ROWS:, :] = jnp.zeros((plan.tall - FLAT_ROWS, 128), F32)
    xc_ref[...] = jnp.zeros((576, 128), F32)
    scf_ref[...] = jnp.zeros((8, 256), F32)
    scc_ref[...] = jnp.zeros((8, 128), F32)
    scf_ref[1:2, :] = 0.5 * bias_f
    scc_ref[1:2, :] = 0.5 * bias_c
    loads[0].wait()
    v = inc_in[...].astype(F32)
    inc_ref[...] = pair_order([v[24 * r : 24 * r + 24] for r in range(24)])
    for load in loads[1:6]:
        load.wait()

    def coarse_branch():
        h = xc_ref[...] * scc_ref[0:1, :] + scc_ref[1:2, :]
        y = h * jnp.tanh(h) + h
        branch = ((y + inc_ref[...]) * mc_ref[...]).astype(BF)
        branch_ref[...] = branch
        lift_ref[...] = dot(branch, wu_ref[...])

    def unit(r, final):
        scale, shift = scf_ref[0:1, :], scf_ref[1:2, :]
        half = rows_of(r // 2, 48, 48)
        lift = lift_ref[half, :]
        lift_low = lift.astype(BF)
        z = []
        for p in range(2):
            at = rows_of(2 * r + p, 48, 48)
            h = x_ref[at, :] * scale + shift
            y = h * jnp.tanh(h) + h
            if final:
                m = twice(mf_ref[at, :])
                low = ((y + inp_ref[at, :].astype(F32)) * m).astype(BF)
                z.append((low.astype(F32) + lift) * m)
            else:
                m = twice(mb_ref[at, :])
                low = (y.astype(BF) + inp_ref[at, :]) * m
                z.append((low + lift_low) * m)
            ph_ref[2 * (r % 2) + p, half, :] = low
        even, odd = z
        if final:
            for i in range(2):
                at = slice(24 * i, 24 * i + 24)
                interleave(stage_ref.at[0], r + 24 * i, even[at], odd[at])
            return
        wide = odd.astype(F32)
        left = jnp.concatenate([shift_down(wide[0:24]), shift_down(wide[24:48])], axis=0).astype(BF)
        wide = even.astype(F32)
        right = jnp.concatenate([shift_up(wide[0:24]), shift_up(wide[24:48])], axis=0).astype(BF)
        for i, u in enumerate((left - odd, even + odd, odd - even, even - right)):
            u_ref[i, rows_of(r + 1, 48, 48), :] = u
            if r == 0:
                w = u.astype(F32)
                u_ref[i, 25 * 48 : 26 * 48, :] = jnp.concatenate([w[24:48], jnp.zeros_like(w[0:24])], axis=0).astype(BF)
            if r == 23:
                w = u.astype(F32)
                u_ref[i, 0:48, :] = jnp.concatenate([jnp.zeros_like(w[0:24]), w[0:24]], axis=0).astype(BF)

    def lowered_parts(first=0, last=CPIX):
        ee, eo, oe, oo = (ph_ref[i, first:last, :] for i in range(4))
        p = dot(eo, wdn_ref[:, 128:384]) + dot(oo, wdn_ref[:, 640:896])
        q = dot(oe, wdn_ref[:, 384:640])
        t = dot(oo, wdn_ref[:, 896:1152])
        return p, q, t, dot(ee, wdn_ref[:, 0:128])

    def lowered(parts):
        p, q, t, e = parts
        here = p[:, :128] + q[:, :128] + e
        return here + row_down(q[:, 128:] + t[:, :128]) + in_rows(p[:, 128:] + row_down(t[:, 128:]), shift_down)

    def coarse_state(parts):
        zc = (branch_ref[...].astype(F32) + lowered(parts)) * mc_ref[...]
        c_ref[:, 0:128] = in_rows(zc, shift_down).astype(BF)
        c_ref[:, 128:256] = zc.astype(BF)

    def coarse_sums(p):
        t = [p[:, 128 * i : 128 * i + 128] for i in range(6)]
        xc = row_down(t[0]) + t[1] + row_up(t[2]) + in_rows(row_down(t[3]) + t[4] + row_up(t[5]), shift_up)
        xc_ref[...] = xc
        xm = xc * mc_ref[...]
        return tile_sum(xm), tile_sum(xm * xm)

    def conv_units(units):
        products = []
        for i in range(4):
            total = None
            for dy in range(3):
                rows = [u_ref[i, 48 * (first + dy) : 48 * (last + dy), :] for first, last in units]
                rows = rows[0] if len(rows) == 1 else jnp.concatenate(rows, axis=0)
                at = 768 * i + 256 * dy
                p = dot(rows, wf_ref[at : at + 256, :])
                total = p if total is None else total + p
            products.append(total)
        m0, m1, m2, m3 = products
        even, odd = m0 + m1 + m2, m1 - m2 - m3
        s = q = None
        for n, r in enumerate(r for first, last in units for r in range(first, last)):
            for p, y in enumerate((even, odd)):
                y = y[48 * n : 48 * n + 48]
                at = slice(96 * r + 48 * p, 96 * r + 48 * p + 48)
                x_ref[at, :] = y
                ym = y * twice(mf_ref[at, :])
                ds, dq = tile_sum(ym), tile_sum(ym * ym)
                s, q = (ds, dq) if s is None else (s + ds, q + dq)
        return s, q

    def finish(s, q, width, n, gain, bias, to_ref):
        s, q = jnp.sum(s, axis=0, keepdims=True), jnp.sum(q, axis=0, keepdims=True)
        for p in range(s.shape[1] // 128):
            at = slice(128 * p, 128 * p + 128)
            mean = run_sum(s[:, at], width) / n
            var = jnp.maximum(run_sum(q[:, at], width) / n - mean * mean, 0.0)
            inv = lax.rsqrt(var + 1e-5)
            to_ref[0:1, at] = 0.5 * inv * gain[:, at]
            to_ref[1:2, at] = 0.5 * (bias[:, at] - mean * inv * gain[:, at])
            to_ref[2:3, at] = mean
            to_ref[3:4, at] = inv

    def iterate(t, _):
        s = q = parts = conv_c = sums_c = None
        for step in STEPS.split():
            if step[0] == "E":
                unit(2 * int(step[1:]), False)
                unit(2 * int(step[1:]) + 1, False)
            elif step[0] == "C":
                ds, dq = conv_units([tuple(map(int, piece.split("-"))) for piece in step[1:].split(",")])
                s, q = (ds, dq) if s is None else (s + ds, q + dq)
            elif step == "L":
                parts = lowered_parts()
            elif step == "L0":
                parts = lowered_parts(0, 288)
            elif step == "L1":
                parts = [jnp.concatenate(both, axis=0) for both in zip(parts, lowered_parts(288, 576))]
            elif step == "Z":
                coarse_state(parts)
            elif step == "K":
                conv_c = dot(c_ref[...], wc6_ref[...])
            elif step == "S":
                sums_c = coarse_sums(conv_c)
            elif step == "F":
                finish(*sums_c, C2 // GROUPS, nc, gain_c, bias_c, scc_ref)
            elif step == "B":
                coarse_branch()
        finish(s, q, C1 // GROUPS, nf, gain_f, bias_f, scf_ref)
        return 0

    coarse_branch()
    lax.fori_loop(0, ITERS, iterate, 0)

    def last_rows(r, _):
        unit(2 * r, True)
        unit(2 * r + 1, True)
        return 0

    lax.fori_loop(0, 12, last_rows, 0)
    sends = [
        pltpu.make_async_copy(stage_ref.at[i, p], ref.at[:, 128 * p : 128 * p + 128], out_sem.at[i, p])
        for i, ref in enumerate((outf_ref, gif_ref))
        for p in range(2)
    ]
    sends += [
        pltpu.make_async_copy(small_ref.at[i], ref, small_sem.at[i]) for i, ref in enumerate((outc_ref, gic_ref))
    ]
    sends[0].start()
    sends[1].start()

    def hand(src, dst):
        send = pltpu.make_async_copy(src, dst, hand_sem.at[len(sends) - 6])
        send.start()
        sends.append(send)

    hand(u_ref, uo_ref)
    small_ref[0] = image_order((branch_ref[...].astype(F32) + lowered(lowered_parts())) * mc_ref[...])
    sends[4].start()
    for load in loads[6:]:
        load.wait()

    v = upc_ref[...].astype(F32)
    seed_c = pair_order([v[24 * r : 24 * r + 24] for r in range(24)]) * mc_ref[...]
    right = in_rows(seed_c, shift_up)
    glo_ref[:, 0:128] = seed_c.astype(BF)
    glo_ref[:, 128:256] = right.astype(BF)
    glo_ref[:, 256:384] = row_up(seed_c).astype(BF)
    glo_ref[:, 384:512] = row_up(right).astype(BF)

    def fold(j, _):
        total = None
        for i in range(4):
            at = rows_of(4 * j + i, 48, 48)
            seed = upf_ref[at, :].astype(F32) * twice(mf_ref[at, :])
            total = seed if total is None else total + seed
        gl_ref[rows_of(j, 48, 48), :] = total.astype(BF)
        return 0

    lax.fori_loop(0, 12, fold, 0, unroll=2)
    up_grad = dot_rows(branch_ref[...], gl_ref[...])
    for j in range(2):
        grad_ref[pl.ds(ROW_UP + j, 128, stride=2), :] = up_grad[:, 128 * j : 128 * j + 128]
    g00, g01, g10, g11 = (glo_ref[:, 128 * i : 128 * i + 128] for i in range(4))
    for i, (parts, taps) in enumerate(
        (((g00,), (4,)), ((g00, g01), (5, 3)), ((g00, g10), (7, 1)), ((g00, g01, g10, g11), (8, 6, 2, 0)))
    ):
        down = dot_rows(ph_ref[i], jnp.concatenate(parts, axis=1))
        for n, tap in enumerate(taps):
            grad_ref[pl.ds(ROW_DOWN + tap, 256, stride=9), :] = down[:, 128 * n : 128 * n + 128]

    back_c = (seed_c + dot_lanes(gl_ref[...], wu_ref[...])) * mc_ref[...]
    small_ref[1] = image_order(back_c)
    sends[5].start()

    def pre_grad(gi, x, scale, shift, mean, inv):
        h = x * scale + shift
        t = jnp.tanh(h)
        sig = 0.5 * t + 0.5
        normed = (x - mean) * inv
        return gi * sig * (1.0 + 2.0 * h * (1.0 - sig)), normed

    def back_means(sum_bias, sum_gain, gain, width, n):
        return run_sum(sum_bias * gain, width) / n, run_sum(sum_gain * gain, width) / n

    gp_c, normed_c = pre_grad(
        back_c, xc_ref[...], scc_ref[0:1, :], scc_ref[1:2, :], scc_ref[2:3, :], scc_ref[3:4, :]
    )
    sum_gain = jnp.sum(gp_c * normed_c, axis=0, keepdims=True)
    sum_bias = jnp.sum(gp_c, axis=0, keepdims=True)
    grad_ref[ROW_VEC + 4 : ROW_VEC + 5, :] = sum_gain
    grad_ref[ROW_VEC + 5 : ROW_VEC + 6, :] = sum_bias
    mean_h, mean_hn = back_means(sum_bias, sum_gain, gain_c, C2 // GROUPS, nc)
    gconv = (gp_c * gain_c - mean_h - normed_c * mean_hn) * scc_ref[3:4, :] * mc_ref[...]
    around = jnp.concatenate([row_up(gconv), gconv, row_down(gconv)], axis=1)
    pair = dot_rows(c_ref[...], around.astype(BF))
    single = dot_rows(c_ref[:, 128:256], in_rows(around, shift_down).astype(BF))
    for dy in range(3):
        at = slice(128 * dy, 128 * dy + 128)
        grad_ref[pl.ds(ROW_COARSE + 3 * dy, 128, stride=9), :] = pair[0:128, at]
        grad_ref[pl.ds(ROW_COARSE + 3 * dy + 1, 128, stride=9), :] = pair[128:256, at]
        grad_ref[pl.ds(ROW_COARSE + 3 * dy + 2, 128, stride=9), :] = single[:, at]

    back_ref[0] = dot_lanes(g00, wdn_ref[:, 0:128])
    back_ref[1] = dot_lanes(jnp.concatenate([g00, g01], axis=1), wdn_ref[:, 128:384])
    back_ref[2] = dot_lanes(jnp.concatenate([g00, g10], axis=1), wdn_ref[:, 384:640])
    back_ref[3] = dot_lanes(glo_ref[...], wdn_ref[:, 640:1152])

    def fine_back(j, carry):
        sums = list(carry)
        for i in range(2):
            gi = []
            for p in range(2):
                at = rows_of(4 * j + 2 * i + p, 48, 48)
                back = back_ref[2 * i + p, rows_of(j, 48, 48), :]
                gi.append((upf_ref[at, :].astype(F32) + back) * twice(mf_ref[at, :]))
                gp, normed = pre_grad(
                    gi[p], x_ref[at, :], scf_ref[0:1, :], scf_ref[1:2, :], scf_ref[2:3, :], scf_ref[3:4, :]
                )
                gp_ref[at, :] = gp
                sums[0] = sums[0] + tile_sum(gp * normed)
                sums[1] = sums[1] + tile_sum(gp)
            for n in range(2):
                half = slice(24 * n, 24 * n + 24)
                interleave(stage_ref.at[1], 2 * j + i + 24 * n, gi[0][half], gi[1][half])
        return tuple(sums)

    none8 = jnp.zeros((8, 256), F32)
    sum_gain, sum_bias = lax.fori_loop(0, 12, fine_back, (none8, none8))
    sends[2].start()
    sends[3].start()
    sum_gain = jnp.sum(sum_gain, axis=0, keepdims=True)
    sum_bias = jnp.sum(sum_bias, axis=0, keepdims=True)
    for p in range(2):
        at = slice(128 * p, 128 * p + 128)
        grad_ref[ROW_VEC + p : ROW_VEC + p + 1, :] = sum_gain[:, at]
        grad_ref[ROW_VEC + 2 + p : ROW_VEC + 3 + p, :] = sum_bias[:, at]
        row_ref[0:1, at], row_ref[1:2, at] = back_means(
            sum_bias[:, at], sum_gain[:, at], gain_f[:, at], C1 // GROUPS, nf
        )

    def fine_conv_grad(r, _):
        g = []
        for p in range(2):
            at = rows_of(2 * r + p, 48, 48)
            normed = (x_ref[at, :] - scf_ref[2:3, :]) * scf_ref[3:4, :]
            v = (gp_ref[at, :] * gain_f - row_ref[0:1, :] - normed * row_ref[1:2, :]) * scf_ref[3:4, :]
            g.append(v * twice(mf_ref[at, :]))
        for p in range(2):
            g_ref[p, rows_of(r + 2, 48, 48), :] = g[p].astype(BF)
        return 0

    for n in range(2):
        lax.fori_loop(12 * n, 12 * n + 12, fine_conv_grad, 0, unroll=2)
        at = pl.ds(14 * 48 * n, 14 * 48)
        hand(g_ref.at[:, at], go_ref.at[:, at])
    hand(grad_ref.at[pl.ds(ROW_DOWN, plan.rows)], join_ref)
    for n, s in enumerate(plan.early):
        first = plan.first[s]
        block_ref[n] = grad_ref[first : first + plan.rows, :].astype(BF)
        hand(block_ref.at[n], blocks_ref.at[n])
    for send in sends:
        send.wait()


def layer_call(plan, *args):
    there = pl.BlockSpec(memory_space=pltpu.HBM)
    low = lambda *shape: pltpu.VMEM(shape, BF)
    wide = lambda *shape: pltpu.VMEM(shape, F32)
    return pl.pallas_call(
        functools.partial(layer_kernel, plan),
        out_shape=[
            jax.ShapeDtypeStruct((PIX, 256), F32),
            jax.ShapeDtypeStruct((CPIX, 128), F32),
            jax.ShapeDtypeStruct((PIX, 256), F32),
            jax.ShapeDtypeStruct((CPIX, 128), F32),
            *(pltpu.HBM(shape, dtype) for shape, dtype in plan.handed),
        ],
        in_specs=[pl.BlockSpec(memory_space=pltpu.SMEM), pl.BlockSpec(memory_space=pltpu.VMEM)] + [there] * 8,
        out_specs=[there] * 8,
        scratch_shapes=[
            low(PIX, 256), low(CPIX, 128), low(128, 256), low(256, 1152), low(256, 768), low(12 * 256, 256),
            low(PIX, 256), low(CPIX, 128),
            wide(plan.tall, 128), low(len(plan.early), plan.rows, 128),
            low(4, 26 * 48, 256), low(4, CPIX, 256), low(CPIX, 256),
            wide(PIX, 256), wide(CPIX, 128), wide(CPIX, 128), low(CPIX, 128), wide(CPIX, 256),
            wide(PIX, 128), low(PIX, 128), wide(CPIX, 128),
            wide(8, 256), wide(8, 128),
            low(CPIX, 256), low(CPIX, 512), wide(4, CPIX, 256), wide(PIX, 256), low(2, 28 * 48, 256), wide(8, 256),
            wide(2, 2, PIX, 128), wide(2, CPIX, 128),
            pltpu.SemaphoreType.DMA((8,)),
            pltpu.SemaphoreType.DMA((2, 2)),
            pltpu.SemaphoreType.DMA((plan.n + 4,)),
            pltpu.SemaphoreType.DMA((2,)),
        ],
        compiler_params=pltpu.CompilerParams(vmem_limit_bytes=62 * 2**20),
        name="layer",
    )(*args)


class Plan:
    def __init__(self, shards, length):
        self.dims = {16: (4, 2, 2), 128: (4, 8, 4)}.get(shards, (shards, 1, 1))
        self.n, self.length = shards, length
        self.first = [s * length // 128 for s in range(shards)]
        self.rows = -(-(length + 127) // 128)
        self.rows = -(-self.rows // 32) * 32
        self.part = self.rows // 2
        self.cut = -(-self.part // 32) * 16
        self.tall = -(-(self.first[-1] + self.rows) // 16) * 16
        self.early = [s for s in range(shards) if self.first[s] >= ROW_DOWN]
        self.handed = (
            ((4, 26 * 48, 256), BF), ((2, 28 * 48, 256), BF), ((self.rows, 128), F32),
            ((len(self.early), self.rows, 128), BF),
        )

    def here(self):
        d0, d1, d2 = self.dims
        me = lax.axis_index("fsdp")
        return me, lax.axis_index("rep"), me // (d1 * d2), me // d2 % d1, me % d2

    def block(self, a, b, c):
        d0, d1, d2 = self.dims
        return (a * d1 + b) * d2 + c


def flip(a, k):
    bit = 1
    while bit <= k:
        if k & bit:
            a = a + bit - 2 * bit * (a // bit % 2)
        bit *= 2
    return a


def to_rows(plan, ref):
    full = plan.length // 128
    left = plan.length - 128 * full
    parts = [ref[pl.ds(0, 128 * full)].reshape(full, 128)]
    if left:
        tail = ref[pl.ds(128 * full, left)].reshape(1, left)
        parts.append(jnp.concatenate([tail, jnp.zeros((1, 128 - left), F32)], axis=1))
    have = full + (left > 0)
    parts.append(jnp.zeros((plan.rows - have, 128), F32))
    return jnp.concatenate(parts, axis=0)


def gather_kernel(
    plan,
    master_ref, inp_hbm, upf_hbm,
    vec_hbm, inpo_hbm, upfo_hbm, wu_hbm, wdn_hbm, wc6_hbm, wf_hbm,
    inp_ref, upf_ref, vec_ref, inpo_ref, upfo_ref, wu_ref, wdn_ref, wc6_ref, wf_ref,
    g_ref, w_ref, tmp_ref, in_sem, out_sem, send_sem, recv_sem, sib_send, sib_recv, far_send,
):
    d0, d1, d2 = plan.dims
    me, core, a, b, c = plan.here()
    part, cut = plan.part, plan.cut
    loads = [
        pltpu.make_async_copy(src, dst, in_sem.at[n])
        for n, (src, dst) in enumerate(((inp_hbm, inp_ref), (upf_hbm, upf_ref)))
    ]
    for load in loads:
        load.start()
    barrier = pltpu.get_barrier_semaphore()
    others = [plan.block((a + k) % d0, b, c) for k in range(1, d0)]
    others += [plan.block(a, (b + k) % d1, c) for k in range(1, d1)]
    others += [plan.block(a, b, (c + k) % d2) for k in range(1, d2)]
    others = [{"fsdp": other, "rep": core} for other in others] + [{"fsdp": me, "rep": 1 - core}]
    for other in others:
        pl.semaphore_signal(barrier, inc=1, device_id=other, device_id_type=pl.DeviceIdType.MESH)
    off = (me * plan.length) % 128
    x = pltpu.roll(to_rows(plan, master_ref), off, 1)
    row = lax.broadcasted_iota(jnp.int32, x.shape, 0)
    lane = lax.broadcasted_iota(jnp.int32, x.shape, 1)
    above = jnp.where(row == 0, 0.0, pltpu.roll(x, 1, 0))
    g_ref[me] = jnp.where(lane < off, above, x).astype(BF)
    pl.semaphore_wait(barrier, len(others))

    def span(half, which):
        start = which * part + (cut if half == 1 else 0)
        return pl.ds(pl.multiple_of(start, 16), (cut, part - cut)[half])

    def copy(block, half, fsdp, rep, send, recv, which):
        at = g_ref.at[block, span(half, which)]
        return pltpu.make_async_remote_copy(
            src_ref=at, dst_ref=at, send_sem=send, recv_sem=recv,
            device_id={"fsdp": fsdp, "rep": rep}, device_id_type=pl.DeviceIdType.MESH,
        )

    def arrive(block, half):
        copy(block, half, me, core, far_send.at[0, 0], recv_sem.at[block, half], core).wait_recv()

    sent = []

    def go(d):
        d.start()
        sent.append(d)

    def along1(block, half):
        for k in range(1, d1):
            go(copy(block, half, plan.block(a, (b + k) % d1, c), core,
                    send_sem.at[block, half, k - 1], recv_sem.at[block, half], core))

    def along2(block, half):
        for k in range(1, d2):
            go(copy(block, half, plan.block(a, b, (c + k) % d2), core,
                    send_sem.at[block, half, d1 + k - 2], recv_sem.at[block, half], core))

    def beside(block, half):
        go(copy(block, half, me, 1 - core, sib_send.at[block, half], sib_recv.at[block, half], core))

    def own_column(k):
        block = plan.block(flip(a, k), b, c)
        if k:
            arrive(block, 0)
        along2(block, 0)
        if k:
            arrive(block, 1)
        along1(block, 1)
        along2(block, 1)
        along1(block, 0)
        if k:
            beside(block, 0)
            beside(block, 1)

    def near(k):
        a2 = flip(a, k)
        ahead = [plan.block(a2, b, (c + i) % d2) for i in range(1, d2)]
        above = [plan.block(a2, (b + i) % d1, c) for i in range(1, d1)]
        for block in ahead:
            arrive(block, 0)
            along1(block, 0)
            beside(block, 0)
        for block in above:
            arrive(block, 1)
            along2(block, 1)
            beside(block, 1)
        for block in ahead:
            arrive(block, 1)
            beside(block, 1)
        for block in above:
            arrive(block, 0)
            beside(block, 0)

    def diagonal(k):
        a2 = flip(a, k)
        for i in range(1, d1):
            for j in range(1, d2):
                block = plan.block(a2, (b + i) % d1, (c + j) % d2)
                for half in (0, 1):
                    arrive(block, half)
                    beside(block, half)

    def parity(src, dst):
        def one(r, _):
            parts = []
            for n in range(2):
                at = rows_of(r + 24 * n, 48, 48)
                v = src[at, :].astype(F32)
                for p in range(2):
                    tmp_ref[p, at, :] = v[:, 128 * p : 128 * p + 128]
            for first in range(2):
                for n in range(2):
                    at = pl.ds((r + 24 * n) * 48 + first, 24, stride=2)
                    parts.append(jnp.concatenate([tmp_ref[p, at, :] for p in range(2)], axis=1))
            dst[rows_of(r, 96, 96), :] = jnp.concatenate(parts, axis=0).astype(BF)
            return 0

        lax.fori_loop(0, 24, one, 0, unroll=2)

    outs = []

    def put(src, dst):
        copy_out = pltpu.make_async_copy(src, dst, out_sem.at[len(outs)])
        copy_out.start()
        outs.append(copy_out)

    for k in range(1, d0):
        for half in (0, 1):
            go(copy(me, half, plan.block(flip(a, k), b, c), core, far_send.at[k, half], recv_sem.at[me, half], core))
    own_column(0)
    loads[0].wait()
    parity(inp_ref, inpo_ref)
    put(inpo_ref, inpo_hbm)
    loads[1].wait()
    parity(upf_ref, upfo_ref)
    put(upfo_ref, upfo_hbm)
    for k in range(1, d0):
        own_column(k)
    for k in range(d0):
        near(k)
    for k in range(d0):
        diagonal(k)
    for k in range(1, plan.n):
        block = (me + k) % plan.n
        for half in (0, 1):
            copy(block, half, me, core, far_send.at[0, 0], sib_recv.at[block, half], 1 - core).wait_recv()

    for s in range(plan.n):
        v = g_ref[s].astype(F32)
        at = plan.first[s]
        if s:
            low = w_ref[at : at + 1, :] + v[0:1]
            w_ref[at : at + plan.rows, :] = v
            w_ref[at : at + 1, :] = low
        else:
            w_ref[0 : plan.rows, :] = v
    vec_ref[...] = w_ref[ROW_VEC : ROW_VEC + 8, :]
    put(vec_ref, vec_hbm)
    for dy in range(3):
        for h in range(2):
            g0, g1, g2 = (w_ref[pl.ds(2 * (3 * dy + dx) + h, 256, stride=18), :] for dx in range(3))
            outer = g0 + g2
            for i, v in enumerate((g0, 0.5 * (outer + g1), 0.5 * (outer - g1), g2)):
                at = 768 * i + 256 * dy
                wf_ref[at : at + 256, 128 * h : 128 * h + 128] = v.astype(BF)
    put(wf_ref, wf_hbm)
    for h in range(2):
        wu_ref[:, 128 * h : 128 * h + 128] = w_ref[pl.ds(ROW_UP + h, 128, stride=2), :].astype(BF)
    put(wu_ref, wu_hbm)
    for t in range(9):
        p = (4, 5, 3, 7, 1, 8, 6, 2, 0).index(t)
        wdn_ref[:, 128 * p : 128 * p + 128] = w_ref[pl.ds(ROW_DOWN + t, 256, stride=9), :].astype(BF)
    put(wdn_ref, wdn_hbm)
    wc6_ref[0:128, 384:768] = jnp.zeros((128, 384), BF)
    for t in range(9):
        dy, dx = t // 3, t % 3
        at, p = 128 * (dx + 1) // 2 // 128 * 128, dy + 3 * (dx // 2)
        wc6_ref[at : at + 128, 128 * p : 128 * p + 128] = w_ref[pl.ds(ROW_COARSE + t, 128, stride=9), :].astype(BF)
    put(wc6_ref, wc6_hbm)
    for d in sent:
        d.wait_send()
    for d in outs:
        d.wait()


def gather_call(plan, master, inp, upf):
    there = pl.BlockSpec(memory_space=pltpu.HBM)
    low = lambda *shape: jax.ShapeDtypeStruct(shape, BF)
    outs = [
        jax.ShapeDtypeStruct((8, 128), F32), low(PIX, 256), low(PIX, 256), low(128, 256), low(256, 1152),
        low(256, 768), low(12 * 256, 256),
    ]
    d0, d1, d2 = plan.dims
    sems = pltpu.SemaphoreType.DMA
    return pl.pallas_call(
        functools.partial(gather_kernel, plan),
        out_shape=[pltpu.HBM(o.shape, o.dtype) for o in outs],
        in_specs=[pl.BlockSpec(memory_space=pltpu.VMEM), there, there],
        out_specs=[there] * 7,
        scratch_shapes=[pltpu.VMEM((PIX, 256), BF), pltpu.VMEM((PIX, 256), BF)]
        + [pltpu.VMEM(o.shape, o.dtype) for o in outs]
        + [
            pltpu.VMEM((plan.n, plan.rows, 128), BF), pltpu.VMEM((plan.tall, 128), F32), pltpu.VMEM((2, PIX, 128), F32),
            sems((2,)), sems((15,)), sems((plan.n, 2, max(d1 + d2 - 2, 1))), sems((plan.n, 2)), sems((plan.n, 2)),
            sems((plan.n, 2)), sems((d0, 2)),
        ],
        compiler_params=pltpu.CompilerParams(collective_id=0, has_side_effects=True, vmem_limit_bytes=32 * 2**20),
        name="gather_weights",
    )(master, *(pltpu.with_memory_space_constraint(x, pltpu.HBM) for x in (inp, upf)))


def reduce_kernel(
    plan,
    u_hbm, g_hbm, join_hbm, blocks_hbm,
    out_ref, tile_ref,
    u_ref, g_ref, sums_ref, grad_ref, p_ref, q_ref, ua_ref, ub_ref, va_ref, vb_ref, z_ref, sa_ref, total_ref,
    n1_ref, n2_ref,
    in_sem, q_send, q_recv, s1_send, s1_recv, s2_send, s2_recv, s3_send, s3_recv, t_send, t_recv,
    n1_send, n1_recv, n2_send, n2_recv,
):
    d0, d1, d2 = plan.dims
    me, core, a, b, c = plan.here()
    part, cut = plan.part, plan.cut
    MESH = pl.DeviceIdType.MESH
    barrier = pltpu.get_barrier_semaphore()
    others = [{"fsdp": plan.block((a + k) % d0, b, c), "rep": core} for k in range(1, d0)]
    plane = []
    for i in range(d1):
        for j in range(d2):
            for o in range(2):
                if i or j or o:
                    plane.append((i, j, o, {"fsdp": plan.block(a, (b + i) % d1, (c + j) % d2), "rep": (core + o) % 2}))
    others += [p[3] for p in plane]
    for other in others:
        pl.semaphore_signal(barrier, inc=1, device_id=other, device_id_type=MESH)
    loads = [pltpu.make_async_copy(g_hbm, g_ref, in_sem.at[0])]
    loads += [pltpu.make_async_copy(u_hbm.at[i], u_ref.at[i], in_sem.at[1 + i]) for i in range(4)]
    loads.append(pltpu.make_async_copy(join_hbm, grad_ref.at[pl.ds(ROW_DOWN, plan.rows)], in_sem.at[5]))
    count = len(plan.early)
    loads.append(pltpu.make_async_copy(blocks_hbm, p_ref.at[pl.ds(plan.n - count, count)], in_sem.at[6]))
    for load in loads:
        load.start()

    loads[0].wait()
    even, odd = g_ref[0], g_ref[1]
    sums_ref[0] = even + odd
    sums_ref[1] = even - odd
    products = []
    for i, ref in enumerate((g_ref.at[0], sums_ref.at[0], sums_ref.at[1], g_ref.at[1])):
        shifted = [ref[48 * (2 - dy) : 48 * (2 - dy) + 26 * 48, :] for dy in range(3)]
        loads[1 + i].wait()
        products.append(dot_rows(u_ref[i], jnp.concatenate(shifted, axis=1)))
    p0, p1, p2, p3 = products
    both, apart = 0.5 * (p1 + p2), 0.5 * (p1 - p2)
    for dx, grad in enumerate((p0 + both, apart, both - p3)):
        for dy in range(3):
            for j in range(2):
                at = 256 * dy + 128 * j
                grad_ref[pl.ds(2 * (3 * dy + dx) + j, 256, stride=18), :] = grad[:, at : at + 128]
    loads[5].wait()
    for s in range(plan.n - count):
        first = plan.first[s]
        p_ref[s] = grad_ref[first : first + plan.rows, :].astype(BF)
    loads[6].wait()
    pl.semaphore_wait(barrier, len(others))

    sent = []

    def go(src, dst, send, recv, to):
        d = pltpu.make_async_remote_copy(
            src_ref=src, dst_ref=dst, send_sem=send, recv_sem=recv, device_id=to, device_id_type=MESH
        )
        d.start()
        sent.append(d)

    def got(ref, recv):
        pltpu.make_async_copy(ref, ref, recv).wait()

    mine = pl.multiple_of(core * part, 16)
    theirs = pl.multiple_of((1 - core) * part, 16)
    halves = ((0, cut), (cut, part - cut))
    order = [(k + 1) % d0 for k in range(d0)]
    for k in order:
        for i in list(range(1, d1)) + [0]:
            for j in list(range(1, d2)) + [0]:
                s = plan.block((a + k) % d0, (b + i) % d1, (c + j) % d2)
                go(
                    p_ref.at[s, pl.ds(theirs, part)], q_ref.at[s], q_send.at[s], q_recv.at[s],
                    {"fsdp": me, "rep": 1 - core},
                )

    def pair(s, half):
        start, size = halves[half]
        x = p_ref[s, pl.ds(pl.multiple_of(mine + start, 16), size), :].astype(F32)
        return x + q_ref[s, start : start + size, :].astype(F32)

    def step1(k):
        a2 = (a + k) % d0
        for i in range(1, d1):
            for j in list(range(1, d2)) + [0]:
                s = plan.block(a2, (b + i) % d1, (c + j) % d2)
                got(q_ref.at[s], q_recv.at[s])
                sa_ref[s, 0:cut, :] = pair(s, 0).astype(BF)
                go(sa_ref.at[s, 0:cut], ua_ref.at[a2, (c + j) % d2, i - 1], s1_send.at[s, 0], s1_recv.at[0, a2, (c + j) % d2, i - 1],
                   {"fsdp": plan.block(a, (b + i) % d1, c), "rep": core})
                if j:
                    step1b(s, a2, i, j)
        for j in range(1, d2):
            s = plan.block(a2, b, (c + j) % d2)
            got(q_ref.at[s], q_recv.at[s])
            step1b(s, a2, 0, j)

    def step1b(s, a2, i, j):
        sa_ref[s, cut:part, :] = pair(s, 1).astype(BF)
        go(sa_ref.at[s, cut:part], ub_ref.at[a2, (b + i) % d1, j - 1], s1_send.at[s, 1], s1_recv.at[1, a2, (b + i) % d1, j - 1],
           {"fsdp": plan.block(a, b, (c + j) % d2), "rep": core})

    def from1(half, a2, other):
        ref = ua_ref if half == 0 else ub_ref
        total = None
        for i in range((d1 if half == 0 else d2) - 1):
            got(ref.at[a2, other, i], s1_recv.at[half, a2, other, i])
            v = ref[a2, other, i].astype(F32)
            total = v if total is None else total + v
        return total

    def plus(x, y):
        return x if y is None else x + y

    def step2(k):
        a2 = (a + k) % d0
        for j in range(1, d2):
            c2 = (c + j) % d2
            s = plan.block(a2, b, c2)
            sa_ref[s, 0:cut, :] = plus(pair(s, 0), from1(0, a2, c2)).astype(BF)
            go(sa_ref.at[s, 0:cut], va_ref.at[a2, j - 1], s2_send.at[0, a2, j - 1], s2_recv.at[0, a2, j - 1],
               {"fsdp": plan.block(a, b, c2), "rep": core})
        for i in range(1, d1):
            b2 = (b + i) % d1
            s = plan.block(a2, b2, c)
            sa_ref[s, cut:part, :] = plus(pair(s, 1), from1(1, a2, b2)).astype(BF)
            go(sa_ref.at[s, cut:part], vb_ref.at[a2, i - 1], s2_send.at[1, a2, i - 1], s2_recv.at[1, a2, i - 1],
               {"fsdp": plan.block(a, b2, c), "rep": core})

    def column(k):
        a2 = (a + k) % d0
        s = plan.block(a2, b, c)
        got(q_ref.at[s], q_recv.at[s])
        x = plus(pair(s, 0), from1(0, a2, c))
        for j in range(1, d2):
            got(va_ref.at[a2, j - 1], s2_recv.at[0, a2, j - 1])
            x = x + va_ref[a2, j - 1].astype(F32)
        y = plus(pair(s, 1), from1(1, a2, b))
        for i in range(1, d1):
            got(vb_ref.at[a2, i - 1], s2_recv.at[1, a2, i - 1])
            y = y + vb_ref[a2, i - 1].astype(F32)
        return s, x, y

    def step3(k):
        s, x, y = column(k)
        sa_ref[s, 0:cut, :] = x.astype(BF)
        sa_ref[s, cut:part, :] = y.astype(BF)
        go(sa_ref.at[s], z_ref.at[k - 1], s3_send.at[k - 1], s3_recv.at[k - 1], {"fsdp": plan.block((a + k) % d0, b, c), "rep": core})

    for n in range(d0 + 2):
        if n < d0:
            step1(order[n])
        if 0 <= n - 1 < d0:
            step2(order[n - 1])
        if 0 <= n - 2 < d0 - 1:
            step3(order[n - 2])
    _, x, y = column(0)
    total = jnp.concatenate([x, y], axis=0)
    for k in range(1, d0):
        got(z_ref.at[k - 1], s3_recv.at[k - 1])
        total = total + z_ref[k - 1].astype(F32)
    total_ref[pl.ds(mine, part), :] = total
    go(total_ref.at[pl.ds(mine, part)], total_ref.at[pl.ds(mine, part)], t_send.at[0], t_recv.at[0], {"fsdp": me, "rep": 1 - core})

    off = (me * plan.length) % 128
    row = lax.broadcasted_iota(jnp.int32, (part, 128), 0) + mine
    at = row * 128 + lax.broadcasted_iota(jnp.int32, (part, 128), 1)
    own = jnp.where((at >= off) & (at < off + plan.length), total, 0.0)
    last = me == plan.n - 1
    for i in range(6):
        spot = ROW_VEC - plan.first[-1] + i
        holds = last & (core == spot // part)
        n1_ref[a, i:i + 1, :] = jnp.where(holds, total[spot % part:spot % part + 1], 0.0)
    n1_ref[a, 6:7, :] = jnp.sum(own * own, axis=0, keepdims=True)
    n1_ref[a, 7:8, :] = jnp.zeros((1, 128), F32)
    for k in range(1, d0):
        go(n1_ref.at[a], n1_ref.at[a], n1_send.at[k], n1_recv.at[a], {"fsdp": plan.block((a + k) % d0, b, c), "rep": core})
    for k in range(1, d0):
        got(n1_ref.at[(a + k) % d0], n1_recv.at[(a + k) % d0])
    tile = n1_ref[0]
    for k in range(1, d0):
        tile = tile + n1_ref[k]
    slot = (b * d2 + c) * 2 + core
    n2_ref[slot] = tile
    for n, (i, j, o, to) in enumerate(plane):
        go(n2_ref.at[slot], n2_ref.at[slot], n2_send.at[n], n2_recv.at[slot], to)
    got(total_ref.at[pl.ds(theirs, part)], t_recv.at[0])
    x = pltpu.roll(total_ref[...], (128 - off) % 128, 1)
    below = pltpu.roll(x, plan.rows - 1, 0)
    lane = lax.broadcasted_iota(jnp.int32, x.shape, 1)
    out_ref[...] = jnp.where(lane + off >= 128, below, x)
    for n, (i, j, o, to) in enumerate(plane):
        other = (((b + i) % d1) * d2 + (c + j) % d2) * 2 + (core + o) % 2
        got(n2_ref.at[other], n2_recv.at[other])
    tile = n2_ref[0]
    for n in range(1, 2 * d1 * d2):
        tile = tile + n2_ref[n]
    tile_ref[...] = tile
    for d in sent:
        d.wait_send()


def reduce_call(plan, *handed):
    whole = pl.BlockSpec(memory_space=pltpu.VMEM)
    d0, d1, d2 = plan.dims
    sems = pltpu.SemaphoreType.DMA
    low = lambda *shape: pltpu.VMEM(shape, BF)
    wide = lambda *shape: pltpu.VMEM(shape, F32)
    e1, e2 = max(d1 - 1, 1), max(d2 - 1, 1)
    rest = plan.part - plan.cut
    return pl.pallas_call(
        functools.partial(reduce_kernel, plan),
        out_shape=[jax.ShapeDtypeStruct((plan.rows, 128), F32), jax.ShapeDtypeStruct((8, 128), F32)],
        in_specs=[pl.BlockSpec(memory_space=pltpu.HBM)] * 4,
        out_specs=[whole] * 2,
        scratch_shapes=[
            low(4, 26 * 48, 256), low(2, 28 * 48, 256), low(2, 28 * 48, 256), wide(ROW_DOWN + plan.rows, 128),
            low(plan.n, plan.rows, 128), low(plan.n, plan.part, 128),
            low(d0, d2, e1, plan.cut, 128), low(d0, d1, e2, rest, 128),
            low(d0, e2, plan.cut, 128), low(d0, e1, rest, 128), low(max(d0 - 1, 1), plan.part, 128),
            low(plan.n, plan.part, 128),
            wide(plan.rows, 128), wide(d0, 8, 128), wide(2 * d1 * d2, 8, 128),
            sems((7,)), sems((plan.n,)), sems((plan.n,)), sems((plan.n, 2)),
            sems((2, d0, max(d1, d2), max(e1, e2))), sems((2, d0, max(e1, e2))), sems((2, d0, max(e1, e2))),
            sems((d0,)), sems((d0,)), sems((1,)), sems((1,)),
            sems((d0,)), sems((d0,)), sems((2 * d1 * d2,)), sems((2 * d1 * d2,)),
        ],
        compiler_params=pltpu.CompilerParams(collective_id=1, has_side_effects=True, vmem_limit_bytes=40 * 2**20),
        name="reduce_gradients",
    )(*(pltpu.with_memory_space_constraint(x, pltpu.HBM) for x in handed))


def update_kernel(
    plan,
    grad_ref, tile_ref, master_ref, first_ref, second_ref, average_ref,
    norm_ref, new_master_ref, new_first_ref, new_second_ref, new_average_ref, small_ref,
):
    grad_norm = jnp.sqrt(jnp.sum(tile_ref[6:7, :], axis=1, keepdims=True))
    factor = jnp.minimum(1.0, clip_norm / (grad_norm + 1e-06))
    norm_ref[...] = grad_norm
    for i in range(6):
        small_ref[pl.ds(128 * i, 128)] = (tile_ref[i : i + 1, :] * factor).reshape(128)
    full = plan.length // 128
    left = plan.length - 128 * full
    ema_rate = min(0.999, (1.0 + STEP) / (10.0 + STEP))

    def update(row, rows, lanes):
        at = pl.ds(128 * row, 128 * (rows - 1) + lanes)
        shape = (rows, lanes)
        clipped = grad_ref[row : row + rows, 0:lanes] * factor
        new_first = beta_one * first_ref[at].reshape(shape) + (1.0 - beta_one) * clipped
        new_second = beta_two * second_ref[at].reshape(shape) + (1.0 - beta_two) * clipped * clipped
        corrected_first = new_first / (1.0 - beta_one**STEP)
        corrected_second = new_second / (1.0 - beta_two**STEP)
        master = master_ref[at].reshape(shape)
        new_master = master - learn_rate * (
            corrected_first / (jnp.sqrt(corrected_second) + adam_eps) + decay_rate * master
        )
        new_average = ema_rate * average_ref[at].reshape(shape) + (1.0 - ema_rate) * new_master
        size = 128 * (rows - 1) + lanes
        new_master_ref[at] = new_master.reshape(size)
        new_first_ref[at] = new_first.reshape(size)
        new_second_ref[at] = new_second.reshape(size)
        new_average_ref[at] = new_average.reshape(size)

    update(0, full, 128)
    if left:
        update(full, 1, left)


def update_call(plan, *args):
    whole = pl.BlockSpec(memory_space=pltpu.VMEM)
    flat = jax.ShapeDtypeStruct((plan.length,), F32)
    return pl.pallas_call(
        functools.partial(update_kernel, plan),
        out_shape=[jax.ShapeDtypeStruct((1, 1), F32), flat, flat, flat, flat, jax.ShapeDtypeStruct((768,), F32)],
        in_specs=[whole] * 6,
        out_specs=[whole] * 6,
        compiler_params=pltpu.CompilerParams(vmem_limit_bytes=16 * 2**20),
        name="update",
    )(*args)


def per_device(
    input_fine, input_coarse, upstream_fine, upstream_coarse, extents, master, first_moment, second_moment, average
):
    plan = Plan(lax.axis_size("fsdp"), master.shape[0])
    vec, inp, upf, wu, wdn, wc6, wf = gather_call(
        plan, master, input_fine.reshape(PIX, C1), upstream_fine.reshape(PIX, C1)
    )
    out_fine, out_coarse, gi_fine, gi_coarse, *handed = layer_call(
        plan, extents, vec, inp, input_coarse.reshape(CPIX, C2), wu, wdn, wc6, wf, upf,
        upstream_coarse.reshape(CPIX, C2),
    )
    grad, tile = reduce_call(plan, *handed)
    grad_norm, new_master, new_first, new_second, new_average, norm_grads = update_call(
        plan, grad, tile, master, first_moment, second_moment, average
    )
    grad_norm = grad_norm.reshape(())
    return (
        out_fine.reshape(input_fine.shape),
        out_coarse.reshape(input_coarse.shape),
        gi_fine.reshape(input_fine.shape),
        gi_coarse.reshape(input_coarse.shape),
        grad_norm,
        new_master,
        new_first,
        new_second,
        new_average,
        norm_grads,
    )


def solution(mesh):
    images = P(("fsdp", "rep"), None, None, None)
    flat = P("fsdp")
    in_specs = (images,) * 4 + (P(("fsdp", "rep"), None),) + (flat,) * 4
    out_specs = (images,) * 4 + (P(),) + (flat,) * 4 + (P(),)
    return jax.shard_map(per_device, mesh=mesh, in_specs=in_specs, out_specs=out_specs, check_vma=False)
```

```python
import functools

import jax
import jax.numpy as jnp
from jax import lax
from jax.experimental import pallas as pl
from jax.experimental.pallas import tpu as pltpu
from jax.sharding import PartitionSpec as P

F32, BF = jnp.float32, jnp.bfloat16
C1, C2, GROUPS, ITERS, STEP = 256, 128, 8, 12, 10
HEIGHT, HALF = 48, 24
PIX, CPIX = HEIGHT * HEIGHT, HALF * HALF
FLAT_ROWS = 8326
ROW_DOWN, ROW_COARSE, ROW_UP, ROW_VEC = 4608, 6912, 8064, 8320

clip_norm = 1.0
learn_rate = 0.02
beta_one = 0.9
beta_two = 0.999
adam_eps = 1e-08
decay_rate = 0.1


def dot(a, b):
    return jnp.dot(a, b, preferred_element_type=F32)


def dot_rows(a, b):
    return lax.dot_general(a, b, (((0,), (0,)), ((), ())), preferred_element_type=F32)


def dot_lanes(a, b):
    return lax.dot_general(a, b, (((1,), (1,)), ((), ())), preferred_element_type=F32)


def run_sum(x, width):
    lane = lax.broadcasted_iota(jnp.int32, x.shape, 1)
    step = 1
    while step < width:
        up = pltpu.roll(x, 128 - step, 1)
        down = pltpu.roll(x, step, 1)
        x = x + jnp.where((lane & step) == 0, up, down)
        step *= 2
    return x


def shift_down(x):
    count = x.shape[0] // 8
    top = lax.broadcasted_iota(jnp.int32, (8, x.shape[1]), 0) == 0
    turned = [pltpu.roll(x[8 * i : 8 * i + 8], 1, 0) for i in range(count)]
    return jnp.concatenate(
        [jnp.where(top, turned[i - 1] if i else 0.0, turned[i]) for i in range(count)], axis=0
    )


def shift_up(x):
    count = x.shape[0] // 8
    end = lax.broadcasted_iota(jnp.int32, (8, x.shape[1]), 0) == 7
    turned = [pltpu.roll(x[8 * i : 8 * i + 8], 7, 0) for i in range(count)]
    return jnp.concatenate(
        [jnp.where(end, turned[i + 1] if i < count - 1 else 0.0, turned[i]) for i in range(count)], axis=0
    )


def rows_out(x):
    parts = [x[24 * i : 24 * i + 24] for i in range(24)]
    return parts[0::2] + parts[1::2]


def pair_order(rows):
    return jnp.concatenate([rows[i // 2 + 12 * (i % 2)] for i in range(24)], axis=0)


def image_order(x):
    return jnp.concatenate(rows_out(x), axis=0)


def in_rows(x, change):
    return jnp.concatenate([change(x[24 * r : 24 * r + 24]) for r in range(24)], axis=0)


def row_down(x):
    rows = rows_out(x)
    return pair_order([jnp.zeros_like(rows[0])] + rows[:-1])


def row_up(x):
    rows = rows_out(x)
    return pair_order(rows[1:] + [jnp.zeros_like(rows[0])])


def tile_sum(x):
    total = x[0:8]
    for i in range(1, x.shape[0] // 8):
        total = total + x[8 * i : 8 * i + 8]
    return total


def twice(m):
    return jnp.concatenate([m, m], axis=1)


def interleave(ref, r, even, odd):
    for p in range(2):
        at = slice(128 * p, 128 * p + 128)
        ref[p, pl.ds(r * 48, 24, stride=2), :] = even[:, at]
        ref[p, pl.ds(r * 48 + 1, 24, stride=2), :] = odd[:, at]


def rows_of(r, count, unit):
    start = r * unit
    return pl.ds(start if isinstance(r, int) else pl.multiple_of(start, unit if unit % 16 == 0 else 8), count)


STEPS = "E0 E1 E2 E3 C1-7 E4 E5 E6 C7-13 E7 E8 E9 E10 E11 C13-17 L C17-21 Z K C21-24,0-1 S F B"


def layer_kernel(
    plan,
    ext_ref, vec_ref, inp_in, wu_in, wdn_in, wc6_in, wf_in, upf_ref, inc_hbm, upc_hbm,
    outf_ref, outc_ref, gif_ref, gic_ref, u_ref, g_ref, join_ref, blocks_ref,
    inp_ref, wu_ref, wdn_ref, wc6_ref, wf_ref, inc_in, upc_ref, grad_ref, ph_ref, c_ref, x_ref, xc_ref, inc_ref, branch_ref, lift_ref, mf_ref, mb_ref, mc_ref,
    scf_ref, scc_ref, gl_ref, glo_ref, back_ref, gp_ref, row_ref, stage_ref, small_ref,
    in_sem, out_sem, small_sem,
):
    loads = [
        pltpu.make_async_copy(src, dst, in_sem.at[n])
        for n, (src, dst) in enumerate(
            ((inc_hbm, inc_in), (upc_hbm, upc_ref))
        )
    ]
    for load in loads:
        load.start()
    hh, ww = ext_ref[0, 0], ext_ref[0, 1]
    gain_f = jnp.concatenate([vec_ref[0:1, :], vec_ref[1:2, :]], axis=1)
    bias_f = jnp.concatenate([vec_ref[2:3, :], vec_ref[3:4, :]], axis=1)
    gain_c, bias_c = vec_ref[4:5, :], vec_ref[5:6, :]
    pos = lax.broadcasted_iota(jnp.int32, (24, 128), 0)
    even = jnp.where(2 * pos < ww, 1.0, 0.0).astype(F32)
    odd = jnp.where(2 * pos + 1 < ww, 1.0, 0.0).astype(F32)

    def setup(r, _):
        at = rows_of(r, 96, 96)
        low, high = r < hh, r + 24 < hh
        m = [jnp.where(here, v, 0.0) for v in (even, odd) for here in (low, high)]
        m = jnp.concatenate(m, axis=0)
        mf_ref[at, :] = m
        mb_ref[at, :] = m.astype(BF)
        x_ref[at, :] = jnp.zeros((96, 256), F32)
        return 0

    lax.fori_loop(0, 24, setup, 0)

    def setup_coarse(r, _):
        m = [jnp.where(2 * r < hh, even, 0.0), jnp.where(2 * r + 24 < hh, even, 0.0)]
        mc_ref[rows_of(r, 48, 48), :] = jnp.concatenate(m, axis=0)
        return 0

    lax.fori_loop(0, 12, setup_coarse, 0)
    nf = (hh * ww).astype(F32) * (C1 // GROUPS)
    nc = (((hh + 1) // 2) * ((ww + 1) // 2)).astype(F32) * (C2 // GROUPS)
    g_ref[:, 0:96, :] = jnp.zeros((2, 96, 256), BF)
    g_ref[:, 26 * 48 : 28 * 48, :] = jnp.zeros((2, 96, 256), BF)
    grad_ref[FLAT_ROWS:, :] = jnp.zeros((plan.tall - FLAT_ROWS, 128), F32)
    xc_ref[...] = jnp.zeros((576, 128), F32)
    scf_ref[...] = jnp.zeros((8, 256), F32)
    scc_ref[...] = jnp.zeros((8, 128), F32)
    scf_ref[1:2, :] = 0.5 * bias_f
    scc_ref[1:2, :] = 0.5 * bias_c
    for src, dst in (
        (inp_in, inp_ref), (wu_in, wu_ref), (wdn_in, wdn_ref), (wc6_in, wc6_ref), (wf_in, wf_ref)
    ):
        dst[...] = src[...]
    loads[0].wait()
    v = inc_in[...].astype(F32)
    inc_ref[...] = pair_order([v[24 * r : 24 * r + 24] for r in range(24)])

    def coarse_branch():
        h = xc_ref[...] * scc_ref[0:1, :] + scc_ref[1:2, :]
        y = h * jnp.tanh(h) + h
        branch = ((y + inc_ref[...]) * mc_ref[...]).astype(BF)
        branch_ref[...] = branch
        lift_ref[...] = dot(branch, wu_ref[...])

    def unit(r, final):
        scale, shift = scf_ref[0:1, :], scf_ref[1:2, :]
        half = rows_of(r // 2, 48, 48)
        lift = lift_ref[half, :]
        lift_low = lift.astype(BF)
        z = []
        for p in range(2):
            at = rows_of(2 * r + p, 48, 48)
            h = x_ref[at, :] * scale + shift
            y = h * jnp.tanh(h) + h
            if final:
                m = twice(mf_ref[at, :])
                low = ((y + inp_ref[at, :].astype(F32)) * m).astype(BF)
                z.append((low.astype(F32) + lift) * m)
            else:
                m = twice(mb_ref[at, :])
                low = (y.astype(BF) + inp_ref[at, :]) * m
                z.append((low + lift_low) * m)
            ph_ref[2 * (r % 2) + p, half, :] = low
        even, odd = z
        if final:
            for i in range(2):
                at = slice(24 * i, 24 * i + 24)
                interleave(stage_ref.at[0], r + 24 * i, even[at], odd[at])
            return
        wide = odd.astype(F32)
        left = jnp.concatenate([shift_down(wide[0:24]), shift_down(wide[24:48])], axis=0).astype(BF)
        wide = even.astype(F32)
        right = jnp.concatenate([shift_up(wide[0:24]), shift_up(wide[24:48])], axis=0).astype(BF)
        for i, u in enumerate((left - odd, even + odd, odd - even, even - right)):
            u_ref[i, rows_of(r + 1, 48, 48), :] = u
            if r == 0:
                w = u.astype(F32)
                u_ref[i, 25 * 48 : 26 * 48, :] = jnp.concatenate([w[24:48], jnp.zeros_like(w[0:24])], axis=0).astype(BF)
            if r == 23:
                w = u.astype(F32)
                u_ref[i, 0:48, :] = jnp.concatenate([jnp.zeros_like(w[0:24]), w[0:24]], axis=0).astype(BF)

    def lowered_parts(first=0, last=CPIX):
        ee, eo, oe, oo = (ph_ref[i, first:last, :] for i in range(4))
        p = dot(eo, wdn_ref[:, 128:384]) + dot(oo, wdn_ref[:, 640:896])
        q = dot(oe, wdn_ref[:, 384:640])
        t = dot(oo, wdn_ref[:, 896:1152])
        return p, q, t, dot(ee, wdn_ref[:, 0:128])

    def lowered(parts):
        p, q, t, e = parts
        here = p[:, :128] + q[:, :128] + e
        return here + row_down(q[:, 128:] + t[:, :128]) + in_rows(p[:, 128:] + row_down(t[:, 128:]), shift_down)

    def coarse_state(parts):
        zc = (branch_ref[...].astype(F32) + lowered(parts)) * mc_ref[...]
        c_ref[:, 0:128] = in_rows(zc, shift_down).astype(BF)
        c_ref[:, 128:256] = zc.astype(BF)

    def coarse_sums(p):
        t = [p[:, 128 * i : 128 * i + 128] for i in range(6)]
        xc = row_down(t[0]) + t[1] + row_up(t[2]) + in_rows(row_down(t[3]) + t[4] + row_up(t[5]), shift_up)
        xc_ref[...] = xc
        xm = xc * mc_ref[...]
        return tile_sum(xm), tile_sum(xm * xm)

    def conv_units(units):
        products = []
        for i in range(4):
            total = None
            for dy in range(3):
                rows = [u_ref[i, 48 * (first + dy) : 48 * (last + dy), :] for first, last in units]
                rows = rows[0] if len(rows) == 1 else jnp.concatenate(rows, axis=0)
                at = 768 * i + 256 * dy
                p = dot(rows, wf_ref[at : at + 256, :])
                total = p if total is None else total + p
            products.append(total)
        m0, m1, m2, m3 = products
        even, odd = m0 + m1 + m2, m1 - m2 - m3
        s = q = None
        for n, r in enumerate(r for first, last in units for r in range(first, last)):
            for p, y in enumerate((even, odd)):
                y = y[48 * n : 48 * n + 48]
                at = slice(96 * r + 48 * p, 96 * r + 48 * p + 48)
                x_ref[at, :] = y
                ym = y * twice(mf_ref[at, :])
                ds, dq = tile_sum(ym), tile_sum(ym * ym)
                s, q = (ds, dq) if s is None else (s + ds, q + dq)
        return s, q

    def finish(s, q, width, n, gain, bias, to_ref):
        s, q = jnp.sum(s, axis=0, keepdims=True), jnp.sum(q, axis=0, keepdims=True)
        for p in range(s.shape[1] // 128):
            at = slice(128 * p, 128 * p + 128)
            mean = run_sum(s[:, at], width) / n
            var = jnp.maximum(run_sum(q[:, at], width) / n - mean * mean, 0.0)
            inv = lax.rsqrt(var + 1e-5)
            to_ref[0:1, at] = 0.5 * inv * gain[:, at]
            to_ref[1:2, at] = 0.5 * (bias[:, at] - mean * inv * gain[:, at])
            to_ref[2:3, at] = mean
            to_ref[3:4, at] = inv

    def iterate(t, _):
        s = q = parts = conv_c = sums_c = None
        for step in STEPS.split():
            if step[0] == "E":
                unit(2 * int(step[1:]), False)
                unit(2 * int(step[1:]) + 1, False)
            elif step[0] == "C":
                ds, dq = conv_units([tuple(map(int, piece.split("-"))) for piece in step[1:].split(",")])
                s, q = (ds, dq) if s is None else (s + ds, q + dq)
            elif step == "L":
                parts = lowered_parts()
            elif step == "L0":
                parts = lowered_parts(0, 288)
            elif step == "L1":
                parts = [jnp.concatenate(both, axis=0) for both in zip(parts, lowered_parts(288, 576))]
            elif step == "Z":
                coarse_state(parts)
            elif step == "K":
                conv_c = dot(c_ref[...], wc6_ref[...])
            elif step == "S":
                sums_c = coarse_sums(conv_c)
            elif step == "F":
                finish(*sums_c, C2 // GROUPS, nc, gain_c, bias_c, scc_ref)
            elif step == "B":
                coarse_branch()
        finish(s, q, C1 // GROUPS, nf, gain_f, bias_f, scf_ref)
        return 0

    coarse_branch()
    lax.fori_loop(0, ITERS, iterate, 0)

    def last_rows(r, _):
        unit(2 * r, True)
        unit(2 * r + 1, True)
        return 0

    lax.fori_loop(0, 12, last_rows, 0)
    sends = [
        pltpu.make_async_copy(stage_ref.at[i, p], ref.at[:, 128 * p : 128 * p + 128], out_sem.at[i, p])
        for i, ref in enumerate((outf_ref, gif_ref))
        for p in range(2)
    ]
    sends += [
        pltpu.make_async_copy(small_ref.at[i], ref, small_sem.at[i]) for i, ref in enumerate((outc_ref, gic_ref))
    ]
    sends[0].start()
    sends[1].start()
    small_ref[0] = image_order((branch_ref[...].astype(F32) + lowered(lowered_parts())) * mc_ref[...])
    sends[4].start()
    loads[1].wait()

    v = upc_ref[...].astype(F32)
    seed_c = pair_order([v[24 * r : 24 * r + 24] for r in range(24)]) * mc_ref[...]
    right = in_rows(seed_c, shift_up)
    glo_ref[:, 0:128] = seed_c.astype(BF)
    glo_ref[:, 128:256] = right.astype(BF)
    glo_ref[:, 256:384] = row_up(seed_c).astype(BF)
    glo_ref[:, 384:512] = row_up(right).astype(BF)

    def fold(j, _):
        total = None
        for i in range(4):
            at = rows_of(4 * j + i, 48, 48)
            seed = upf_ref[at, :].astype(F32) * twice(mf_ref[at, :])
            total = seed if total is None else total + seed
        gl_ref[rows_of(j, 48, 48), :] = total.astype(BF)
        return 0

    lax.fori_loop(0, 12, fold, 0, unroll=2)
    up_grad = dot_rows(branch_ref[...], gl_ref[...])
    for j in range(2):
        grad_ref[pl.ds(ROW_UP + j, 128, stride=2), :] = up_grad[:, 128 * j : 128 * j + 128]
    g00, g01, g10, g11 = (glo_ref[:, 128 * i : 128 * i + 128] for i in range(4))
    for i, (parts, taps) in enumerate(
        (((g00,), (4,)), ((g00, g01), (5, 3)), ((g00, g10), (7, 1)), ((g00, g01, g10, g11), (8, 6, 2, 0)))
    ):
        down = dot_rows(ph_ref[i], jnp.concatenate(parts, axis=1))
        for n, tap in enumerate(taps):
            grad_ref[pl.ds(ROW_DOWN + tap, 256, stride=9), :] = down[:, 128 * n : 128 * n + 128]

    back_c = (seed_c + dot_lanes(gl_ref[...], wu_ref[...])) * mc_ref[...]
    small_ref[1] = image_order(back_c)
    sends[5].start()

    def pre_grad(gi, x, scale, shift, mean, inv):
        h = x * scale + shift
        t = jnp.tanh(h)
        sig = 0.5 * t + 0.5
        normed = (x - mean) * inv
        return gi * sig * (1.0 + 2.0 * h * (1.0 - sig)), normed

    def back_means(sum_bias, sum_gain, gain, width, n):
        return run_sum(sum_bias * gain, width) / n, run_sum(sum_gain * gain, width) / n

    gp_c, normed_c = pre_grad(
        back_c, xc_ref[...], scc_ref[0:1, :], scc_ref[1:2, :], scc_ref[2:3, :], scc_ref[3:4, :]
    )
    sum_gain = jnp.sum(gp_c * normed_c, axis=0, keepdims=True)
    sum_bias = jnp.sum(gp_c, axis=0, keepdims=True)
    grad_ref[ROW_VEC + 4 : ROW_VEC + 5, :] = sum_gain
    grad_ref[ROW_VEC + 5 : ROW_VEC + 6, :] = sum_bias
    mean_h, mean_hn = back_means(sum_bias, sum_gain, gain_c, C2 // GROUPS, nc)
    gconv = (gp_c * gain_c - mean_h - normed_c * mean_hn) * scc_ref[3:4, :] * mc_ref[...]
    around = jnp.concatenate([row_up(gconv), gconv, row_down(gconv)], axis=1)
    pair = dot_rows(c_ref[...], around.astype(BF))
    single = dot_rows(c_ref[:, 128:256], in_rows(around, shift_down).astype(BF))
    for dy in range(3):
        at = slice(128 * dy, 128 * dy + 128)
        grad_ref[pl.ds(ROW_COARSE + 3 * dy, 128, stride=9), :] = pair[0:128, at]
        grad_ref[pl.ds(ROW_COARSE + 3 * dy + 1, 128, stride=9), :] = pair[128:256, at]
        grad_ref[pl.ds(ROW_COARSE + 3 * dy + 2, 128, stride=9), :] = single[:, at]

    back_ref[0] = dot_lanes(g00, wdn_ref[:, 0:128])
    back_ref[1] = dot_lanes(jnp.concatenate([g00, g01], axis=1), wdn_ref[:, 128:384])
    back_ref[2] = dot_lanes(jnp.concatenate([g00, g10], axis=1), wdn_ref[:, 384:640])
    back_ref[3] = dot_lanes(glo_ref[...], wdn_ref[:, 640:1152])

    def fine_back(j, carry):
        sums = list(carry)
        for i in range(2):
            gi = []
            for p in range(2):
                at = rows_of(4 * j + 2 * i + p, 48, 48)
                back = back_ref[2 * i + p, rows_of(j, 48, 48), :]
                gi.append((upf_ref[at, :].astype(F32) + back) * twice(mf_ref[at, :]))
                gp, normed = pre_grad(
                    gi[p], x_ref[at, :], scf_ref[0:1, :], scf_ref[1:2, :], scf_ref[2:3, :], scf_ref[3:4, :]
                )
                gp_ref[at, :] = gp
                sums[0] = sums[0] + tile_sum(gp * normed)
                sums[1] = sums[1] + tile_sum(gp)
            for n in range(2):
                half = slice(24 * n, 24 * n + 24)
                interleave(stage_ref.at[1], 2 * j + i + 24 * n, gi[0][half], gi[1][half])
        return tuple(sums)

    none8 = jnp.zeros((8, 256), F32)
    sum_gain, sum_bias = lax.fori_loop(0, 12, fine_back, (none8, none8))
    sends[2].start()
    sends[3].start()
    sum_gain = jnp.sum(sum_gain, axis=0, keepdims=True)
    sum_bias = jnp.sum(sum_bias, axis=0, keepdims=True)
    for p in range(2):
        at = slice(128 * p, 128 * p + 128)
        grad_ref[ROW_VEC + p : ROW_VEC + p + 1, :] = sum_gain[:, at]
        grad_ref[ROW_VEC + 2 + p : ROW_VEC + 3 + p, :] = sum_bias[:, at]
        row_ref[0:1, at], row_ref[1:2, at] = back_means(
            sum_bias[:, at], sum_gain[:, at], gain_f[:, at], C1 // GROUPS, nf
        )

    def fine_conv_grad(r, _):
        g = []
        for p in range(2):
            at = rows_of(2 * r + p, 48, 48)
            normed = (x_ref[at, :] - scf_ref[2:3, :]) * scf_ref[3:4, :]
            v = (gp_ref[at, :] * gain_f - row_ref[0:1, :] - normed * row_ref[1:2, :]) * scf_ref[3:4, :]
            g.append(v * twice(mf_ref[at, :]))
        for p in range(2):
            g_ref[p, rows_of(r + 2, 48, 48), :] = g[p].astype(BF)
        return 0

    lax.fori_loop(0, 24, fine_conv_grad, 0, unroll=2)
    join_ref[...] = grad_ref[ROW_DOWN : ROW_DOWN + plan.rows, :]
    for n, s in enumerate(plan.early):
        first = plan.first[s]
        blocks_ref[n] = grad_ref[first : first + plan.rows, :].astype(BF)
    for send in sends:
        send.wait()


def layer_call(plan, *args):
    there = pl.BlockSpec(memory_space=pltpu.HBM)
    whole = pl.BlockSpec(memory_space=pltpu.VMEM)
    low = lambda *shape: pltpu.VMEM(shape, BF)
    wide = lambda *shape: pltpu.VMEM(shape, F32)
    return pl.pallas_call(
        functools.partial(layer_kernel, plan),
        out_shape=[
            jax.ShapeDtypeStruct((PIX, 256), F32),
            jax.ShapeDtypeStruct((CPIX, 128), F32),
            jax.ShapeDtypeStruct((PIX, 256), F32),
            jax.ShapeDtypeStruct((CPIX, 128), F32),
            *(jax.ShapeDtypeStruct(shape, dtype) for shape, dtype in plan.handed),
        ],
        in_specs=[pl.BlockSpec(memory_space=pltpu.SMEM)] + [whole] * 7 + [there] * 2,
        out_specs=[there] * 4 + [whole] * 4,
        scratch_shapes=[
            low(PIX, 256), low(128, 256), low(256, 1152), low(256, 768), low(12 * 256, 256),
            low(CPIX, 128), low(CPIX, 128),
            wide(plan.tall, 128), low(4, CPIX, 256), low(CPIX, 256),
            wide(PIX, 256), wide(CPIX, 128), wide(CPIX, 128), low(CPIX, 128), wide(CPIX, 256),
            wide(PIX, 128), low(PIX, 128), wide(CPIX, 128),
            wide(8, 256), wide(8, 128),
            low(CPIX, 256), low(CPIX, 512), wide(4, CPIX, 256), wide(PIX, 256), wide(8, 256),
            wide(2, 2, PIX, 128), wide(2, CPIX, 128),
            pltpu.SemaphoreType.DMA((2,)),
            pltpu.SemaphoreType.DMA((2, 2)),
            pltpu.SemaphoreType.DMA((2,)),
        ],
        compiler_params=pltpu.CompilerParams(vmem_limit_bytes=38 * 2**20),
        name="layer",
    )(*args)


class Plan:
    def __init__(self, shards, length):
        self.dims = {16: (4, 2, 2), 128: (4, 8, 4)}.get(shards, (shards, 1, 1))
        self.n, self.length = shards, length
        self.first = [s * length // 128 for s in range(shards)]
        self.rows = -(-(length + 127) // 128)
        self.rows = -(-self.rows // 32) * 32
        self.part = self.rows // 2
        self.cut = -(-self.part // 32) * 16
        self.tall = -(-(self.first[-1] + self.rows) // 16) * 16
        self.early = [s for s in range(shards) if self.first[s] >= ROW_DOWN]
        self.handed = (
            ((4, 26 * 48, 256), BF), ((2, 28 * 48, 256), BF), ((self.rows, 128), F32),
            ((len(self.early), self.rows, 128), BF),
        )

    def here(self):
        d0, d1, d2 = self.dims
        me = lax.axis_index("fsdp")
        return me, lax.axis_index("rep"), me // (d1 * d2), me // d2 % d1, me % d2

    def block(self, a, b, c):
        d0, d1, d2 = self.dims
        return (a * d1 + b) * d2 + c


def flip(a, k):
    bit = 1
    while bit <= k:
        if k & bit:
            a = a + bit - 2 * bit * (a // bit % 2)
        bit *= 2
    return a


def to_rows(plan, ref):
    full = plan.length // 128
    left = plan.length - 128 * full
    parts = [ref[pl.ds(0, 128 * full)].reshape(full, 128)]
    if left:
        tail = ref[pl.ds(128 * full, left)].reshape(1, left)
        parts.append(jnp.concatenate([tail, jnp.zeros((1, 128 - left), F32)], axis=1))
    have = full + (left > 0)
    parts.append(jnp.zeros((plan.rows - have, 128), F32))
    return jnp.concatenate(parts, axis=0)


def gather_kernel(
    plan,
    master_ref, inp_hbm, upf_hbm,
    vec_ref, inpo_ref, upfo_ref, wu_ref, wdn_ref, wc6_ref, wf_ref,
    inp_ref, upf_ref, g_ref, w_ref, tmp_ref, in_sem, send_sem, recv_sem, sib_send, sib_recv, far_send,
):
    d0, d1, d2 = plan.dims
    me, core, a, b, c = plan.here()
    part, cut = plan.part, plan.cut
    loads = [
        pltpu.make_async_copy(src, dst, in_sem.at[n])
        for n, (src, dst) in enumerate(((inp_hbm, inp_ref), (upf_hbm, upf_ref)))
    ]
    for load in loads:
        load.start()
    barrier = pltpu.get_barrier_semaphore()
    others = [plan.block((a + k) % d0, b, c) for k in range(1, d0)]
    others += [plan.block(a, (b + k) % d1, c) for k in range(1, d1)]
    others += [plan.block(a, b, (c + k) % d2) for k in range(1, d2)]
    others = [{"fsdp": other, "rep": core} for other in others] + [{"fsdp": me, "rep": 1 - core}]
    for other in others:
        pl.semaphore_signal(barrier, inc=1, device_id=other, device_id_type=pl.DeviceIdType.MESH)
    off = (me * plan.length) % 128
    x = pltpu.roll(to_rows(plan, master_ref), off, 1)
    row = lax.broadcasted_iota(jnp.int32, x.shape, 0)
    lane = lax.broadcasted_iota(jnp.int32, x.shape, 1)
    above = jnp.where(row == 0, 0.0, pltpu.roll(x, 1, 0))
    g_ref[me] = jnp.where(lane < off, above, x).astype(BF)
    pl.semaphore_wait(barrier, len(others))

    def span(half, which):
        start = which * part + (cut if half == 1 else 0)
        return pl.ds(pl.multiple_of(start, 16), (cut, part - cut)[half])

    def copy(block, half, fsdp, rep, send, recv, which):
        at = g_ref.at[block, span(half, which)]
        return pltpu.make_async_remote_copy(
            src_ref=at, dst_ref=at, send_sem=send, recv_sem=recv,
            device_id={"fsdp": fsdp, "rep": rep}, device_id_type=pl.DeviceIdType.MESH,
        )

    def arrive(block, half):
        copy(block, half, me, core, far_send.at[0, 0], recv_sem.at[block, half], core).wait_recv()

    sent = []

    def go(d):
        d.start()
        sent.append(d)

    def along1(block, half):
        for k in range(1, d1):
            go(copy(block, half, plan.block(a, (b + k) % d1, c), core,
                    send_sem.at[block, half, k - 1], recv_sem.at[block, half], core))

    def along2(block, half):
        for k in range(1, d2):
            go(copy(block, half, plan.block(a, b, (c + k) % d2), core,
                    send_sem.at[block, half, d1 + k - 2], recv_sem.at[block, half], core))

    def beside(block, half):
        go(copy(block, half, me, 1 - core, sib_send.at[block, half], sib_recv.at[block, half], core))

    def own_column(k):
        block = plan.block(flip(a, k), b, c)
        if k:
            arrive(block, 0)
        along2(block, 0)
        if k:
            arrive(block, 1)
        along1(block, 1)
        along2(block, 1)
        along1(block, 0)
        if k:
            beside(block, 0)
            beside(block, 1)

    def near(k):
        a2 = flip(a, k)
        ahead = [plan.block(a2, b, (c + i) % d2) for i in range(1, d2)]
        above = [plan.block(a2, (b + i) % d1, c) for i in range(1, d1)]
        for block in ahead:
            arrive(block, 0)
            along1(block, 0)
            beside(block, 0)
        for block in above:
            arrive(block, 1)
            along2(block, 1)
            beside(block, 1)
        for block in ahead:
            arrive(block, 1)
            beside(block, 1)
        for block in above:
            arrive(block, 0)
            beside(block, 0)

    def diagonal(k):
        a2 = flip(a, k)
        for i in range(1, d1):
            for j in range(1, d2):
                block = plan.block(a2, (b + i) % d1, (c + j) % d2)
                for half in (0, 1):
                    arrive(block, half)
                    beside(block, half)

    def parity(src, dst):
        def one(r, _):
            parts = []
            for n in range(2):
                at = rows_of(r + 24 * n, 48, 48)
                v = src[at, :].astype(F32)
                for p in range(2):
                    tmp_ref[p, at, :] = v[:, 128 * p : 128 * p + 128]
            for first in range(2):
                for n in range(2):
                    at = pl.ds((r + 24 * n) * 48 + first, 24, stride=2)
                    parts.append(jnp.concatenate([tmp_ref[p, at, :] for p in range(2)], axis=1))
            dst[rows_of(r, 96, 96), :] = jnp.concatenate(parts, axis=0).astype(BF)
            return 0

        lax.fori_loop(0, 24, one, 0, unroll=2)

    for k in range(1, d0):
        for half in (0, 1):
            go(copy(me, half, plan.block(flip(a, k), b, c), core, far_send.at[k, half], recv_sem.at[me, half], core))
    own_column(0)
    loads[0].wait()
    parity(inp_ref, inpo_ref)
    loads[1].wait()
    parity(upf_ref, upfo_ref)
    for k in range(1, d0):
        own_column(k)
    for k in range(d0):
        near(k)
    for k in range(d0):
        diagonal(k)
    for k in range(1, plan.n):
        block = (me + k) % plan.n
        for half in (0, 1):
            copy(block, half, me, core, far_send.at[0, 0], sib_recv.at[block, half], 1 - core).wait_recv()

    for s in range(plan.n):
        v = g_ref[s].astype(F32)
        at = plan.first[s]
        if s:
            low = w_ref[at : at + 1, :] + v[0:1]
            w_ref[at : at + plan.rows, :] = v
            w_ref[at : at + 1, :] = low
        else:
            w_ref[0 : plan.rows, :] = v
    vec_ref[...] = w_ref[ROW_VEC : ROW_VEC + 8, :]
    for dy in range(3):
        for h in range(2):
            g0, g1, g2 = (w_ref[pl.ds(2 * (3 * dy + dx) + h, 256, stride=18), :] for dx in range(3))
            outer = g0 + g2
            for i, v in enumerate((g0, 0.5 * (outer + g1), 0.5 * (outer - g1), g2)):
                at = 768 * i + 256 * dy
                wf_ref[at : at + 256, 128 * h : 128 * h + 128] = v.astype(BF)
    for h in range(2):
        wu_ref[:, 128 * h : 128 * h + 128] = w_ref[pl.ds(ROW_UP + h, 128, stride=2), :].astype(BF)
    for t in range(9):
        p = (4, 5, 3, 7, 1, 8, 6, 2, 0).index(t)
        wdn_ref[:, 128 * p : 128 * p + 128] = w_ref[pl.ds(ROW_DOWN + t, 256, stride=9), :].astype(BF)
    wc6_ref[0:128, 384:768] = jnp.zeros((128, 384), BF)
    for t in range(9):
        dy, dx = t // 3, t % 3
        at, p = 128 * (dx + 1) // 2 // 128 * 128, dy + 3 * (dx // 2)
        wc6_ref[at : at + 128, 128 * p : 128 * p + 128] = w_ref[pl.ds(ROW_COARSE + t, 128, stride=9), :].astype(BF)
    for d in sent:
        d.wait_send()


def gather_call(plan, master, inp, upf):
    there = pl.BlockSpec(memory_space=pltpu.HBM)
    whole = pl.BlockSpec(memory_space=pltpu.VMEM)
    low = lambda *shape: jax.ShapeDtypeStruct(shape, BF)
    outs = [
        jax.ShapeDtypeStruct((8, 128), F32), low(PIX, 256), low(PIX, 256), low(128, 256), low(256, 1152),
        low(256, 768), low(12 * 256, 256),
    ]
    d0, d1, d2 = plan.dims
    sems = pltpu.SemaphoreType.DMA
    return pl.pallas_call(
        functools.partial(gather_kernel, plan),
        out_shape=outs,
        in_specs=[whole, there, there],
        out_specs=[whole] * 7,
        scratch_shapes=[
            pltpu.VMEM((PIX, 256), BF), pltpu.VMEM((PIX, 256), BF),
            pltpu.VMEM((plan.n, plan.rows, 128), BF), pltpu.VMEM((plan.tall, 128), F32), pltpu.VMEM((2, PIX, 128), F32),
            sems((2,)), sems((plan.n, 2, max(d1 + d2 - 2, 1))), sems((plan.n, 2)), sems((plan.n, 2)),
            sems((plan.n, 2)), sems((d0, 2)),
        ],
        compiler_params=pltpu.CompilerParams(collective_id=0, has_side_effects=True, vmem_limit_bytes=20 * 2**20),
        name="gather_weights",
    )(master, *(pltpu.with_memory_space_constraint(x, pltpu.HBM) for x in (inp, upf)))


def reduce_kernel(
    plan,
    u_ref, g_ref, join_ref, blocks_ref,
    out_ref, tile_ref,
    sums_ref, grad_ref, p_ref, q_ref, ua_ref, ub_ref, va_ref, vb_ref, z_ref, sa_ref, total_ref,
    n1_ref, n2_ref,
    q_send, q_recv, s1_send, s1_recv, s2_send, s2_recv, s3_send, s3_recv, t_send, t_recv,
    n1_send, n1_recv, n2_send, n2_recv,
):
    d0, d1, d2 = plan.dims
    me, core, a, b, c = plan.here()
    part, cut = plan.part, plan.cut
    MESH = pl.DeviceIdType.MESH
    barrier = pltpu.get_barrier_semaphore()
    others = [{"fsdp": plan.block((a + k) % d0, b, c), "rep": core} for k in range(1, d0)]
    plane = []
    for i in range(d1):
        for j in range(d2):
            for o in range(2):
                if i or j or o:
                    plane.append((i, j, o, {"fsdp": plan.block(a, (b + i) % d1, (c + j) % d2), "rep": (core + o) % 2}))
    others += [p[3] for p in plane]
    for other in others:
        pl.semaphore_signal(barrier, inc=1, device_id=other, device_id_type=MESH)
    even, odd = g_ref[0], g_ref[1]
    sums_ref[0] = even + odd
    sums_ref[1] = even - odd
    products = []
    for i, ref in enumerate((g_ref.at[0], sums_ref.at[0], sums_ref.at[1], g_ref.at[1])):
        shifted = [ref[48 * (2 - dy) : 48 * (2 - dy) + 26 * 48, :] for dy in range(3)]
        products.append(dot_rows(u_ref[i], jnp.concatenate(shifted, axis=1)))
    p0, p1, p2, p3 = products
    both, apart = 0.5 * (p1 + p2), 0.5 * (p1 - p2)
    for dx, grad in enumerate((p0 + both, apart, both - p3)):
        for dy in range(3):
            for j in range(2):
                at = 256 * dy + 128 * j
                grad_ref[pl.ds(2 * (3 * dy + dx) + j, 256, stride=18), :] = grad[:, at : at + 128]
    count = len(plan.early)
    grad_ref[ROW_DOWN:, :] = join_ref[...]
    for s in range(plan.n - count):
        first = plan.first[s]
        p_ref[s] = grad_ref[first : first + plan.rows, :].astype(BF)
    p_ref[plan.n - count :] = blocks_ref[...]
    pl.semaphore_wait(barrier, len(others))

    sent = []

    def go(src, dst, send, recv, to):
        d = pltpu.make_async_remote_copy(
            src_ref=src, dst_ref=dst, send_sem=send, recv_sem=recv, device_id=to, device_id_type=MESH
        )
        d.start()
        sent.append(d)

    def got(ref, recv):
        pltpu.make_async_copy(ref, ref, recv).wait()

    mine = pl.multiple_of(core * part, 16)
    theirs = pl.multiple_of((1 - core) * part, 16)
    halves = ((0, cut), (cut, part - cut))
    order = [(k + 1) % d0 for k in range(d0)]
    for k in order:
        for i in list(range(1, d1)) + [0]:
            for j in list(range(1, d2)) + [0]:
                s = plan.block((a + k) % d0, (b + i) % d1, (c + j) % d2)
                go(
                    p_ref.at[s, pl.ds(theirs, part)], q_ref.at[s], q_send.at[s], q_recv.at[s],
                    {"fsdp": me, "rep": 1 - core},
                )

    def pair(s, half):
        start, size = halves[half]
        x = p_ref[s, pl.ds(pl.multiple_of(mine + start, 16), size), :].astype(F32)
        return x + q_ref[s, start : start + size, :].astype(F32)

    def step1(k):
        a2 = (a + k) % d0
        for i in range(1, d1):
            for j in list(range(1, d2)) + [0]:
                s = plan.block(a2, (b + i) % d1, (c + j) % d2)
                got(q_ref.at[s], q_recv.at[s])
                sa_ref[s, 0:cut, :] = pair(s, 0).astype(BF)
                go(sa_ref.at[s, 0:cut], ua_ref.at[a2, (c + j) % d2, i - 1], s1_send.at[s, 0], s1_recv.at[0, a2, (c + j) % d2, i - 1],
                   {"fsdp": plan.block(a, (b + i) % d1, c), "rep": core})
                if j:
                    step1b(s, a2, i, j)
        for j in range(1, d2):
            s = plan.block(a2, b, (c + j) % d2)
            got(q_ref.at[s], q_recv.at[s])
            step1b(s, a2, 0, j)

    def step1b(s, a2, i, j):
        sa_ref[s, cut:part, :] = pair(s, 1).astype(BF)
        go(sa_ref.at[s, cut:part], ub_ref.at[a2, (b + i) % d1, j - 1], s1_send.at[s, 1], s1_recv.at[1, a2, (b + i) % d1, j - 1],
           {"fsdp": plan.block(a, b, (c + j) % d2), "rep": core})

    def from1(half, a2, other):
        ref = ua_ref if half == 0 else ub_ref
        total = None
        for i in range((d1 if half == 0 else d2) - 1):
            got(ref.at[a2, other, i], s1_recv.at[half, a2, other, i])
            v = ref[a2, other, i].astype(F32)
            total = v if total is None else total + v
        return total

    def plus(x, y):
        return x if y is None else x + y

    def step2(k):
        a2 = (a + k) % d0
        for j in range(1, d2):
            c2 = (c + j) % d2
            s = plan.block(a2, b, c2)
            sa_ref[s, 0:cut, :] = plus(pair(s, 0), from1(0, a2, c2)).astype(BF)
            go(sa_ref.at[s, 0:cut], va_ref.at[a2, j - 1], s2_send.at[0, a2, j - 1], s2_recv.at[0, a2, j - 1],
               {"fsdp": plan.block(a, b, c2), "rep": core})
        for i in range(1, d1):
            b2 = (b + i) % d1
            s = plan.block(a2, b2, c)
            sa_ref[s, cut:part, :] = plus(pair(s, 1), from1(1, a2, b2)).astype(BF)
            go(sa_ref.at[s, cut:part], vb_ref.at[a2, i - 1], s2_send.at[1, a2, i - 1], s2_recv.at[1, a2, i - 1],
               {"fsdp": plan.block(a, b2, c), "rep": core})

    def column(k):
        a2 = (a + k) % d0
        s = plan.block(a2, b, c)
        got(q_ref.at[s], q_recv.at[s])
        x = plus(pair(s, 0), from1(0, a2, c))
        for j in range(1, d2):
            got(va_ref.at[a2, j - 1], s2_recv.at[0, a2, j - 1])
            x = x + va_ref[a2, j - 1].astype(F32)
        y = plus(pair(s, 1), from1(1, a2, b))
        for i in range(1, d1):
            got(vb_ref.at[a2, i - 1], s2_recv.at[1, a2, i - 1])
            y = y + vb_ref[a2, i - 1].astype(F32)
        return s, x, y

    def step3(k):
        s, x, y = column(k)
        sa_ref[s, 0:cut, :] = x.astype(BF)
        sa_ref[s, cut:part, :] = y.astype(BF)
        go(sa_ref.at[s], z_ref.at[k - 1], s3_send.at[k - 1], s3_recv.at[k - 1], {"fsdp": plan.block((a + k) % d0, b, c), "rep": core})

    for n in range(d0 + 2):
        if n < d0:
            step1(order[n])
        if 0 <= n - 1 < d0:
            step2(order[n - 1])
        if 0 <= n - 2 < d0 - 1:
            step3(order[n - 2])
    _, x, y = column(0)
    total = jnp.concatenate([x, y], axis=0)
    for k in range(1, d0):
        got(z_ref.at[k - 1], s3_recv.at[k - 1])
        total = total + z_ref[k - 1].astype(F32)
    total_ref[pl.ds(mine, part), :] = total
    go(total_ref.at[pl.ds(mine, part)], total_ref.at[pl.ds(mine, part)], t_send.at[0], t_recv.at[0], {"fsdp": me, "rep": 1 - core})

    off = (me * plan.length) % 128
    row = lax.broadcasted_iota(jnp.int32, (part, 128), 0) + mine
    at = row * 128 + lax.broadcasted_iota(jnp.int32, (part, 128), 1)
    own = jnp.where((at >= off) & (at < off + plan.length), total, 0.0)
    last = me == plan.n - 1
    for i in range(6):
        spot = ROW_VEC - plan.first[-1] + i
        holds = last & (core == spot // part)
        n1_ref[a, i:i + 1, :] = jnp.where(holds, total[spot % part:spot % part + 1], 0.0)
    n1_ref[a, 6:7, :] = jnp.sum(own * own, axis=0, keepdims=True)
    n1_ref[a, 7:8, :] = jnp.zeros((1, 128), F32)
    for k in range(1, d0):
        go(n1_ref.at[a], n1_ref.at[a], n1_send.at[k], n1_recv.at[a], {"fsdp": plan.block((a + k) % d0, b, c), "rep": core})
    for k in range(1, d0):
        got(n1_ref.at[(a + k) % d0], n1_recv.at[(a + k) % d0])
    tile = n1_ref[0]
    for k in range(1, d0):
        tile = tile + n1_ref[k]
    slot = (b * d2 + c) * 2 + core
    n2_ref[slot] = tile
    for n, (i, j, o, to) in enumerate(plane):
        go(n2_ref.at[slot], n2_ref.at[slot], n2_send.at[n], n2_recv.at[slot], to)
    got(total_ref.at[pl.ds(theirs, part)], t_recv.at[0])
    x = pltpu.roll(total_ref[...], (128 - off) % 128, 1)
    below = pltpu.roll(x, plan.rows - 1, 0)
    lane = lax.broadcasted_iota(jnp.int32, x.shape, 1)
    out_ref[...] = jnp.where(lane + off >= 128, below, x)
    for n, (i, j, o, to) in enumerate(plane):
        other = (((b + i) % d1) * d2 + (c + j) % d2) * 2 + (core + o) % 2
        got(n2_ref.at[other], n2_recv.at[other])
    tile = n2_ref[0]
    for n in range(1, 2 * d1 * d2):
        tile = tile + n2_ref[n]
    tile_ref[...] = tile
    for d in sent:
        d.wait_send()


def reduce_call(plan, *handed):
    whole = pl.BlockSpec(memory_space=pltpu.VMEM)
    d0, d1, d2 = plan.dims
    sems = pltpu.SemaphoreType.DMA
    low = lambda *shape: pltpu.VMEM(shape, BF)
    wide = lambda *shape: pltpu.VMEM(shape, F32)
    e1, e2 = max(d1 - 1, 1), max(d2 - 1, 1)
    rest = plan.part - plan.cut
    return pl.pallas_call(
        functools.partial(reduce_kernel, plan),
        out_shape=[jax.ShapeDtypeStruct((plan.rows, 128), F32), jax.ShapeDtypeStruct((8, 128), F32)],
        in_specs=[whole] * 4,
        out_specs=[whole] * 2,
        scratch_shapes=[
            low(2, 28 * 48, 256), wide(ROW_DOWN + plan.rows, 128),
            low(plan.n, plan.rows, 128), low(plan.n, plan.part, 128),
            low(d0, d2, e1, plan.cut, 128), low(d0, d1, e2, rest, 128),
            low(d0, e2, plan.cut, 128), low(d0, e1, rest, 128), low(max(d0 - 1, 1), plan.part, 128),
            low(plan.n, plan.part, 128),
            wide(plan.rows, 128), wide(d0, 8, 128), wide(2 * d1 * d2, 8, 128),
            sems((plan.n,)), sems((plan.n,)), sems((plan.n, 2)),
            sems((2, d0, max(d1, d2), max(e1, e2))), sems((2, d0, max(e1, e2))), sems((2, d0, max(e1, e2))),
            sems((d0,)), sems((d0,)), sems((1,)), sems((1,)),
            sems((d0,)), sems((d0,)), sems((2 * d1 * d2,)), sems((2 * d1 * d2,)),
        ],
        compiler_params=pltpu.CompilerParams(collective_id=1, has_side_effects=True, vmem_limit_bytes=20 * 2**20),
        name="reduce_gradients",
    )(*handed)


def update_kernel(
    plan,
    grad_ref, tile_ref, master_ref, first_ref, second_ref, average_ref,
    norm_ref, new_master_ref, new_first_ref, new_second_ref, new_average_ref, small_ref,
):
    grad_norm = jnp.sqrt(jnp.sum(tile_ref[6:7, :], axis=1, keepdims=True))
    factor = jnp.minimum(1.0, clip_norm / (grad_norm + 1e-06))
    norm_ref[...] = grad_norm
    for i in range(6):
        small_ref[pl.ds(128 * i, 128)] = (tile_ref[i : i + 1, :] * factor).reshape(128)
    full = plan.length // 128
    left = plan.length - 128 * full
    ema_rate = min(0.999, (1.0 + STEP) / (10.0 + STEP))

    def update(row, rows, lanes):
        at = pl.ds(128 * row, 128 * (rows - 1) + lanes)
        shape = (rows, lanes)
        clipped = grad_ref[row : row + rows, 0:lanes] * factor
        new_first = beta_one * first_ref[at].reshape(shape) + (1.0 - beta_one) * clipped
        new_second = beta_two * second_ref[at].reshape(shape) + (1.0 - beta_two) * clipped * clipped
        corrected_first = new_first / (1.0 - beta_one**STEP)
        corrected_second = new_second / (1.0 - beta_two**STEP)
        master = master_ref[at].reshape(shape)
        new_master = master - learn_rate * (
            corrected_first / (jnp.sqrt(corrected_second) + adam_eps) + decay_rate * master
        )
        new_average = ema_rate * average_ref[at].reshape(shape) + (1.0 - ema_rate) * new_master
        size = 128 * (rows - 1) + lanes
        new_master_ref[at] = new_master.reshape(size)
        new_first_ref[at] = new_first.reshape(size)
        new_second_ref[at] = new_second.reshape(size)
        new_average_ref[at] = new_average.reshape(size)

    update(0, full, 128)
    if left:
        update(full, 1, left)


def update_call(plan, *args):
    whole = pl.BlockSpec(memory_space=pltpu.VMEM)
    flat = jax.ShapeDtypeStruct((plan.length,), F32)
    return pl.pallas_call(
        functools.partial(update_kernel, plan),
        out_shape=[jax.ShapeDtypeStruct((1, 1), F32), flat, flat, flat, flat, jax.ShapeDtypeStruct((768,), F32)],
        in_specs=[whole] * 6,
        out_specs=[whole] * 6,
        compiler_params=pltpu.CompilerParams(vmem_limit_bytes=16 * 2**20),
        name="update",
    )(*args)


def per_device(
    input_fine, input_coarse, upstream_fine, upstream_coarse, extents, master, first_moment, second_moment, average
):
    plan = Plan(lax.axis_size("fsdp"), master.shape[0])
    vec, inp, upf, wu, wdn, wc6, wf = gather_call(
        plan, master, input_fine.reshape(PIX, C1), upstream_fine.reshape(PIX, C1)
    )
    out_fine, out_coarse, gi_fine, gi_coarse, *handed = layer_call(
        plan, extents, vec, inp, wu, wdn, wc6, wf, upf,
        input_coarse.reshape(CPIX, C2), upstream_coarse.reshape(CPIX, C2),
    )
    grad, tile = reduce_call(plan, *handed)
    grad_norm, new_master, new_first, new_second, new_average, norm_grads = update_call(
        plan, grad, tile, master, first_moment, second_moment, average
    )
    grad_norm = grad_norm.reshape(())
    return (
        out_fine.reshape(input_fine.shape),
        out_coarse.reshape(input_coarse.shape),
        gi_fine.reshape(input_fine.shape),
        gi_coarse.reshape(input_coarse.shape),
        grad_norm,
        new_master,
        new_first,
        new_second,
        new_average,
        norm_grads,
    )


def solution(mesh):
    images = P(("fsdp", "rep"), None, None, None)
    flat = P("fsdp")
    in_specs = (images,) * 4 + (P(("fsdp", "rep"), None),) + (flat,) * 4
    out_specs = (images,) * 4 + (P(),) + (flat,) * 4 + (P(),)
    return jax.shard_map(per_device, mesh=mesh, in_specs=in_specs, out_specs=out_specs, check_vma=False)
```

```python
import functools

import jax
import jax.numpy as jnp
from jax import lax
from jax.experimental import pallas as pl
from jax.experimental.pallas import tpu as pltpu
from jax.sharding import PartitionSpec as P

F32, BF = jnp.float32, jnp.bfloat16
C1, C2, GROUPS, ITERS, STEP = 256, 128, 8, 12, 10
HEIGHT, HALF = 48, 24
PIX, CPIX = HEIGHT * HEIGHT, HALF * HALF
FLAT_ROWS = 8326
ROW_DOWN, ROW_COARSE, ROW_UP, ROW_VEC = 4608, 6912, 8064, 8320

clip_norm = 1.0
learn_rate = 0.02
beta_one = 0.9
beta_two = 0.999
adam_eps = 1e-08
decay_rate = 0.1


def dot(a, b):
    return jnp.dot(a, b, preferred_element_type=F32)


def dot_rows(a, b):
    return lax.dot_general(a, b, (((0,), (0,)), ((), ())), preferred_element_type=F32)


def dot_lanes(a, b):
    return lax.dot_general(a, b, (((1,), (1,)), ((), ())), preferred_element_type=F32)


def run_sum(x, width):
    lane = lax.broadcasted_iota(jnp.int32, x.shape, 1)
    step = 1
    while step < width:
        up = pltpu.roll(x, 128 - step, 1)
        down = pltpu.roll(x, step, 1)
        x = x + jnp.where((lane & step) == 0, up, down)
        step *= 2
    return x


def shift_down(x):
    count = x.shape[0] // 8
    top = lax.broadcasted_iota(jnp.int32, (8, x.shape[1]), 0) == 0
    turned = [pltpu.roll(x[8 * i : 8 * i + 8], 1, 0) for i in range(count)]
    return jnp.concatenate(
        [jnp.where(top, turned[i - 1] if i else 0.0, turned[i]) for i in range(count)], axis=0
    )


def shift_up(x):
    count = x.shape[0] // 8
    end = lax.broadcasted_iota(jnp.int32, (8, x.shape[1]), 0) == 7
    turned = [pltpu.roll(x[8 * i : 8 * i + 8], 7, 0) for i in range(count)]
    return jnp.concatenate(
        [jnp.where(end, turned[i + 1] if i < count - 1 else 0.0, turned[i]) for i in range(count)], axis=0
    )


def rows_out(x):
    parts = [x[24 * i : 24 * i + 24] for i in range(24)]
    return parts[0::2] + parts[1::2]


def pair_order(rows):
    return jnp.concatenate([rows[i // 2 + 12 * (i % 2)] for i in range(24)], axis=0)


def image_order(x):
    return jnp.concatenate(rows_out(x), axis=0)


def in_rows(x, change):
    return jnp.concatenate([change(x[24 * r : 24 * r + 24]) for r in range(24)], axis=0)


def row_down(x):
    rows = rows_out(x)
    return pair_order([jnp.zeros_like(rows[0])] + rows[:-1])


def row_up(x):
    rows = rows_out(x)
    return pair_order(rows[1:] + [jnp.zeros_like(rows[0])])


def tile_sum(x):
    total = x[0:8]
    for i in range(1, x.shape[0] // 8):
        total = total + x[8 * i : 8 * i + 8]
    return total


def twice(m):
    return jnp.concatenate([m, m], axis=1)


def interleave(ref, r, even, odd):
    for p in range(2):
        at = slice(128 * p, 128 * p + 128)
        ref[p, pl.ds(r * 48, 24, stride=2), :] = even[:, at]
        ref[p, pl.ds(r * 48 + 1, 24, stride=2), :] = odd[:, at]


def rows_of(r, count, unit):
    start = r * unit
    return pl.ds(start if isinstance(r, int) else pl.multiple_of(start, unit if unit % 16 == 0 else 8), count)


STEPS = "E0 E1 E2 E3 C1-7 E4 E5 E6 C7-13 E7 E8 E9 E10 E11 C13-17 L C17-21 Z K C21-24,0-1 S F B"


def layer_kernel(
    plan,
    ext_ref, vec_ref, inp_in, wu_in, wdn_in, wc6_in, wf_in, upf_ref, inc_hbm, upc_hbm,
    outf_ref, outc_ref, gif_ref, gic_ref, u_ref, g_ref, join_ref, blocks_ref,
    inp_ref, wu_ref, wdn_ref, wc6_ref, wf_ref, inc_in, upc_ref, grad_ref, ph_ref, c_ref, x_ref, xc_ref, inc_ref, branch_ref, lift_ref, mf_ref, mb_ref, mc_ref,
    scf_ref, scc_ref, gl_ref, glo_ref, back_ref, gp_ref, row_ref, stage_ref, small_ref,
    in_sem, out_sem, small_sem,
):
    loads = [
        pltpu.make_async_copy(src, dst, in_sem.at[n])
        for n, (src, dst) in enumerate(
            ((inc_hbm, inc_in), (upc_hbm, upc_ref))
        )
    ]
    for load in loads:
        load.start()
    hh, ww = ext_ref[0, 0], ext_ref[0, 1]
    gain_f = jnp.concatenate([vec_ref[0:1, :], vec_ref[1:2, :]], axis=1)
    bias_f = jnp.concatenate([vec_ref[2:3, :], vec_ref[3:4, :]], axis=1)
    gain_c, bias_c = vec_ref[4:5, :], vec_ref[5:6, :]
    pos = lax.broadcasted_iota(jnp.int32, (24, 128), 0)
    even = jnp.where(2 * pos < ww, 1.0, 0.0).astype(F32)
    odd = jnp.where(2 * pos + 1 < ww, 1.0, 0.0).astype(F32)

    def setup(r, _):
        at = rows_of(r, 96, 96)
        low, high = r < hh, r + 24 < hh
        m = [jnp.where(here, v, 0.0) for v in (even, odd) for here in (low, high)]
        m = jnp.concatenate(m, axis=0)
        mf_ref[at, :] = m
        mb_ref[at, :] = m.astype(BF)
        x_ref[at, :] = jnp.zeros((96, 256), F32)
        return 0

    lax.fori_loop(0, 24, setup, 0)

    def setup_coarse(r, _):
        m = [jnp.where(2 * r < hh, even, 0.0), jnp.where(2 * r + 24 < hh, even, 0.0)]
        mc_ref[rows_of(r, 48, 48), :] = jnp.concatenate(m, axis=0)
        return 0

    lax.fori_loop(0, 12, setup_coarse, 0)
    nf = (hh * ww).astype(F32) * (C1 // GROUPS)
    nc = (((hh + 1) // 2) * ((ww + 1) // 2)).astype(F32) * (C2 // GROUPS)
    g_ref[:, 0:96, :] = jnp.zeros((2, 96, 256), BF)
    g_ref[:, 26 * 48 : 28 * 48, :] = jnp.zeros((2, 96, 256), BF)
    grad_ref[FLAT_ROWS:, :] = jnp.zeros((plan.tall - FLAT_ROWS, 128), F32)
    xc_ref[...] = jnp.zeros((576, 128), F32)
    scf_ref[...] = jnp.zeros((8, 256), F32)
    scc_ref[...] = jnp.zeros((8, 128), F32)
    scf_ref[1:2, :] = 0.5 * bias_f
    scc_ref[1:2, :] = 0.5 * bias_c
    for src, dst in (
        (inp_in, inp_ref), (wu_in, wu_ref), (wdn_in, wdn_ref), (wc6_in, wc6_ref), (wf_in, wf_ref)
    ):
        dst[...] = src[...]
    loads[0].wait()
    v = inc_in[...].astype(F32)
    inc_ref[...] = pair_order([v[24 * r : 24 * r + 24] for r in range(24)])

    def coarse_branch():
        h = xc_ref[...] * scc_ref[0:1, :] + scc_ref[1:2, :]
        y = h * jnp.tanh(h) + h
        branch = ((y + inc_ref[...]) * mc_ref[...]).astype(BF)
        branch_ref[...] = branch
        lift_ref[...] = dot(branch, wu_ref[...])

    def unit(r, final):
        scale, shift = scf_ref[0:1, :], scf_ref[1:2, :]
        half = rows_of(r // 2, 48, 48)
        lift = lift_ref[half, :]
        lift_low = lift.astype(BF)
        z = []
        for p in range(2):
            at = rows_of(2 * r + p, 48, 48)
            h = x_ref[at, :] * scale + shift
            if final:
                y = h * jnp.tanh(h) + h
            else:
                h = h.astype(BF)
                y = h * jnp.tanh(h) + h
            if final:
                m = twice(mf_ref[at, :])
                low = ((y + inp_ref[at, :].astype(F32)) * m).astype(BF)
                z.append((low.astype(F32) + lift) * m)
            else:
                m = twice(mb_ref[at, :])
                low = (y.astype(BF) + inp_ref[at, :]) * m
                z.append((low + lift_low) * m)
            ph_ref[2 * (r % 2) + p, half, :] = low
        even, odd = z
        if final:
            for i in range(2):
                at = slice(24 * i, 24 * i + 24)
                interleave(stage_ref.at[0], r + 24 * i, even[at], odd[at])
            return
        wide = odd.astype(F32)
        left = jnp.concatenate([shift_down(wide[0:24]), shift_down(wide[24:48])], axis=0).astype(BF)
        wide = even.astype(F32)
        right = jnp.concatenate([shift_up(wide[0:24]), shift_up(wide[24:48])], axis=0).astype(BF)
        for i, u in enumerate((left - odd, even + odd, odd - even, even - right)):
            u_ref[i, rows_of(r + 1, 48, 48), :] = u
            if r == 0:
                w = u.astype(F32)
                u_ref[i, 25 * 48 : 26 * 48, :] = jnp.concatenate([w[24:48], jnp.zeros_like(w[0:24])], axis=0).astype(BF)
            if r == 23:
                w = u.astype(F32)
                u_ref[i, 0:48, :] = jnp.concatenate([jnp.zeros_like(w[0:24]), w[0:24]], axis=0).astype(BF)

    def lowered_parts(first=0, last=CPIX):
        ee, eo, oe, oo = (ph_ref[i, first:last, :] for i in range(4))
        p = dot(eo, wdn_ref[:, 128:384]) + dot(oo, wdn_ref[:, 640:896])
        q = dot(oe, wdn_ref[:, 384:640])
        t = dot(oo, wdn_ref[:, 896:1152])
        return p, q, t, dot(ee, wdn_ref[:, 0:128])

    def lowered(parts):
        p, q, t, e = parts
        here = p[:, :128] + q[:, :128] + e
        return here + row_down(q[:, 128:] + t[:, :128]) + in_rows(p[:, 128:] + row_down(t[:, 128:]), shift_down)

    def coarse_state(parts):
        zc = (branch_ref[...].astype(F32) + lowered(parts)) * mc_ref[...]
        c_ref[:, 0:128] = in_rows(zc, shift_down).astype(BF)
        c_ref[:, 128:256] = zc.astype(BF)

    def coarse_sums(p):
        t = [p[:, 128 * i : 128 * i + 128] for i in range(6)]
        xc = row_down(t[0]) + t[1] + row_up(t[2]) + in_rows(row_down(t[3]) + t[4] + row_up(t[5]), shift_up)
        xc_ref[...] = xc
        xm = xc * mc_ref[...]
        return tile_sum(xm), tile_sum(xm * xm)

    def conv_units(units):
        products = []
        for i in range(4):
            total = None
            for dy in range(3):
                rows = [u_ref[i, 48 * (first + dy) : 48 * (last + dy), :] for first, last in units]
                rows = rows[0] if len(rows) == 1 else jnp.concatenate(rows, axis=0)
                at = 768 * i + 256 * dy
                p = dot(rows, wf_ref[at : at + 256, :])
                total = p if total is None else total + p
            products.append(total)
        m0, m1, m2, m3 = products
        even, odd = m0 + m1 + m2, m1 - m2 - m3
        s = q = None
        for n, r in enumerate(r for first, last in units for r in range(first, last)):
            for p, y in enumerate((even, odd)):
                y = y[48 * n : 48 * n + 48]
                at = slice(96 * r + 48 * p, 96 * r + 48 * p + 48)
                x_ref[at, :] = y
                ym = y * twice(mf_ref[at, :])
                ds, dq = tile_sum(ym), tile_sum(ym * ym)
                s, q = (ds, dq) if s is None else (s + ds, q + dq)
        return s, q

    def finish(s, q, width, n, gain, bias, to_ref):
        s, q = jnp.sum(s, axis=0, keepdims=True), jnp.sum(q, axis=0, keepdims=True)
        for p in range(s.shape[1] // 128):
            at = slice(128 * p, 128 * p + 128)
            mean = run_sum(s[:, at], width) / n
            var = jnp.maximum(run_sum(q[:, at], width) / n - mean * mean, 0.0)
            inv = lax.rsqrt(var + 1e-5)
            to_ref[0:1, at] = 0.5 * inv * gain[:, at]
            to_ref[1:2, at] = 0.5 * (bias[:, at] - mean * inv * gain[:, at])
            to_ref[2:3, at] = mean
            to_ref[3:4, at] = inv

    def iterate(t, _):
        s = q = parts = conv_c = sums_c = None
        for step in STEPS.split():
            if step[0] == "E":
                unit(2 * int(step[1:]), False)
                unit(2 * int(step[1:]) + 1, False)
            elif step[0] == "C":
                ds, dq = conv_units([tuple(map(int, piece.split("-"))) for piece in step[1:].split(",")])
                s, q = (ds, dq) if s is None else (s + ds, q + dq)
            elif step == "L":
                parts = lowered_parts()
            elif step == "L0":
                parts = lowered_parts(0, 288)
            elif step == "L1":
                parts = [jnp.concatenate(both, axis=0) for both in zip(parts, lowered_parts(288, 576))]
            elif step == "Z":
                coarse_state(parts)
            elif step == "K":
                conv_c = dot(c_ref[...], wc6_ref[...])
            elif step == "S":
                sums_c = coarse_sums(conv_c)
            elif step == "F":
                finish(*sums_c, C2 // GROUPS, nc, gain_c, bias_c, scc_ref)
            elif step == "B":
                coarse_branch()
        finish(s, q, C1 // GROUPS, nf, gain_f, bias_f, scf_ref)
        return 0

    coarse_branch()
    lax.fori_loop(0, ITERS, iterate, 0)

    sends = []

    def put(i, ref, half):
        for n in range(2):
            for p in range(2):
                at = pl.ds(48 * (12 * half + 24 * n), 576)
                send = pltpu.make_async_copy(
                    stage_ref.at[i, p, at], ref.at[at, 128 * p : 128 * p + 128], out_sem.at[i, half, n, p]
                )
                send.start()
                sends.append(send)

    def put_small(i, ref):
        send = pltpu.make_async_copy(small_ref.at[i], ref, small_sem.at[i])
        send.start()
        sends.append(send)

    for r in range(24):
        unit(r, True)
    put(0, outf_ref, 0)
    put(0, outf_ref, 1)
    small_ref[0] = image_order((branch_ref[...].astype(F32) + lowered(lowered_parts())) * mc_ref[...])
    put_small(0, outc_ref)
    loads[1].wait()

    v = upc_ref[...].astype(F32)
    seed_c = pair_order([v[24 * r : 24 * r + 24] for r in range(24)]) * mc_ref[...]
    right = in_rows(seed_c, shift_up)
    glo_ref[:, 0:128] = seed_c.astype(BF)
    glo_ref[:, 128:256] = right.astype(BF)
    glo_ref[:, 256:384] = row_up(seed_c).astype(BF)
    glo_ref[:, 384:512] = row_up(right).astype(BF)

    for j in range(12):
        total = None
        for i in range(4):
            at = rows_of(4 * j + i, 48, 48)
            seed = upf_ref[at, :].astype(F32) * twice(mf_ref[at, :])
            total = seed if total is None else total + seed
        gl_ref[rows_of(j, 48, 48), :] = total.astype(BF)
    g00, g01, g10, g11 = (glo_ref[:, 128 * i : 128 * i + 128] for i in range(4))

    back_c = (seed_c + dot_lanes(gl_ref[...], wu_ref[...])) * mc_ref[...]
    small_ref[1] = image_order(back_c)
    put_small(1, gic_ref)

    def pre_grad(gi, x, scale, shift, mean, inv):
        h = x * scale + shift
        t = jnp.tanh(h)
        sig = 0.5 * t + 0.5
        normed = (x - mean) * inv
        return gi * sig * (1.0 + 2.0 * h * (1.0 - sig)), normed

    def back_means(sum_bias, sum_gain, gain, width, n):
        return run_sum(sum_bias * gain, width) / n, run_sum(sum_gain * gain, width) / n

    gp_c, normed_c = pre_grad(
        back_c, xc_ref[...], scc_ref[0:1, :], scc_ref[1:2, :], scc_ref[2:3, :], scc_ref[3:4, :]
    )
    sum_gain = jnp.sum(gp_c * normed_c, axis=0, keepdims=True)
    sum_bias = jnp.sum(gp_c, axis=0, keepdims=True)
    grad_ref[ROW_VEC + 4 : ROW_VEC + 5, :] = sum_gain
    grad_ref[ROW_VEC + 5 : ROW_VEC + 6, :] = sum_bias
    mean_h, mean_hn = back_means(sum_bias, sum_gain, gain_c, C2 // GROUPS, nc)
    gconv = (gp_c * gain_c - mean_h - normed_c * mean_hn) * scc_ref[3:4, :] * mc_ref[...]
    around = jnp.concatenate([row_up(gconv), gconv, row_down(gconv)], axis=1)
    pair = dot_rows(c_ref[...], around.astype(BF))
    single = dot_rows(c_ref[:, 128:256], in_rows(around, shift_down).astype(BF))
    for dy in range(3):
        at = slice(128 * dy, 128 * dy + 128)
        grad_ref[pl.ds(ROW_COARSE + 3 * dy, 128, stride=9), :] = pair[0:128, at]
        grad_ref[pl.ds(ROW_COARSE + 3 * dy + 1, 128, stride=9), :] = pair[128:256, at]
        grad_ref[pl.ds(ROW_COARSE + 3 * dy + 2, 128, stride=9), :] = single[:, at]

    back_ref[0] = dot_lanes(g00, wdn_ref[:, 0:128])
    back_ref[1] = dot_lanes(jnp.concatenate([g00, g01], axis=1), wdn_ref[:, 128:384])
    back_ref[2] = dot_lanes(jnp.concatenate([g00, g10], axis=1), wdn_ref[:, 384:640])
    back_ref[3] = dot_lanes(glo_ref[...], wdn_ref[:, 640:1152])

    none8 = jnp.zeros((8, 256), F32)
    sums = [none8, none8]
    for j in range(12):
        for i in range(2):
            gi = []
            for p in range(2):
                at = rows_of(4 * j + 2 * i + p, 48, 48)
                back = back_ref[2 * i + p, rows_of(j, 48, 48), :]
                gi.append((upf_ref[at, :].astype(F32) + back) * twice(mf_ref[at, :]))
                gp, normed = pre_grad(
                    gi[p], x_ref[at, :], scf_ref[0:1, :], scf_ref[1:2, :], scf_ref[2:3, :], scf_ref[3:4, :]
                )
                gp_ref[at, :] = gp
                sums[0] = sums[0] + tile_sum(gp * normed)
                sums[1] = sums[1] + tile_sum(gp)
            for n in range(2):
                half = slice(24 * n, 24 * n + 24)
                interleave(stage_ref.at[1], 2 * j + i + 24 * n, gi[0][half], gi[1][half])
        if j % 6 == 5:
            put(1, gif_ref, j // 6)
    up_grad = dot_rows(branch_ref[...], gl_ref[...])
    for j in range(2):
        grad_ref[pl.ds(ROW_UP + j, 128, stride=2), :] = up_grad[:, 128 * j : 128 * j + 128]
    for i, (parts, taps) in enumerate(
        (((g00,), (4,)), ((g00, g01), (5, 3)), ((g00, g10), (7, 1)), ((g00, g01, g10, g11), (8, 6, 2, 0)))
    ):
        down = dot_rows(ph_ref[i], jnp.concatenate(parts, axis=1))
        for n, tap in enumerate(taps):
            grad_ref[pl.ds(ROW_DOWN + tap, 256, stride=9), :] = down[:, 128 * n : 128 * n + 128]
    sum_gain, sum_bias = (jnp.sum(v, axis=0, keepdims=True) for v in sums)
    for p in range(2):
        at = slice(128 * p, 128 * p + 128)
        grad_ref[ROW_VEC + p : ROW_VEC + p + 1, :] = sum_gain[:, at]
        grad_ref[ROW_VEC + 2 + p : ROW_VEC + 3 + p, :] = sum_bias[:, at]
        row_ref[0:1, at], row_ref[1:2, at] = back_means(
            sum_bias[:, at], sum_gain[:, at], gain_f[:, at], C1 // GROUPS, nf
        )

    for r in range(24):
        g = []
        for p in range(2):
            at = rows_of(2 * r + p, 48, 48)
            normed = (x_ref[at, :] - scf_ref[2:3, :]) * scf_ref[3:4, :]
            v = (gp_ref[at, :] * gain_f - row_ref[0:1, :] - normed * row_ref[1:2, :]) * scf_ref[3:4, :]
            g.append(v * twice(mf_ref[at, :]))
        for p in range(2):
            g_ref[p, rows_of(r + 2, 48, 48), :] = g[p].astype(BF)
    join_ref[...] = grad_ref[ROW_DOWN : ROW_DOWN + plan.rows, :]
    for n, s in enumerate(plan.early):
        first = plan.first[s]
        blocks_ref[n] = grad_ref[first : first + plan.rows, :].astype(BF)
    for send in sends:
        send.wait()


def layer_call(plan, *args):
    there = pl.BlockSpec(memory_space=pltpu.HBM)
    whole = pl.BlockSpec(memory_space=pltpu.VMEM)
    low = lambda *shape: pltpu.VMEM(shape, BF)
    wide = lambda *shape: pltpu.VMEM(shape, F32)
    return pl.pallas_call(
        functools.partial(layer_kernel, plan),
        out_shape=[
            jax.ShapeDtypeStruct((PIX, 256), F32),
            jax.ShapeDtypeStruct((CPIX, 128), F32),
            jax.ShapeDtypeStruct((PIX, 256), F32),
            jax.ShapeDtypeStruct((CPIX, 128), F32),
            *(jax.ShapeDtypeStruct(shape, dtype) for shape, dtype in plan.handed),
        ],
        in_specs=[pl.BlockSpec(memory_space=pltpu.SMEM)] + [whole] * 7 + [there] * 2,
        out_specs=[there] * 4 + [whole] * 4,
        scratch_shapes=[
            low(PIX, 256), low(128, 256), low(256, 1152), low(256, 768), low(12 * 256, 256),
            low(CPIX, 128), low(CPIX, 128),
            wide(plan.tall, 128), low(4, CPIX, 256), low(CPIX, 256),
            wide(PIX, 256), wide(CPIX, 128), wide(CPIX, 128), low(CPIX, 128), wide(CPIX, 256),
            wide(PIX, 128), low(PIX, 128), wide(CPIX, 128),
            wide(8, 256), wide(8, 128),
            low(CPIX, 256), low(CPIX, 512), wide(4, CPIX, 256), wide(PIX, 256), wide(8, 256),
            wide(2, 2, PIX, 128), wide(2, CPIX, 128),
            pltpu.SemaphoreType.DMA((2,)),
            pltpu.SemaphoreType.DMA((2, 2, 2, 2)),
            pltpu.SemaphoreType.DMA((2,)),
        ],
        compiler_params=pltpu.CompilerParams(vmem_limit_bytes=38 * 2**20),
        name="layer",
    )(*args)


class Plan:
    def __init__(self, shards, length):
        self.dims = {16: (4, 2, 2), 128: (4, 8, 4)}.get(shards, (shards, 1, 1))
        self.n, self.length = shards, length
        self.first = [s * length // 128 for s in range(shards)]
        self.rows = -(-(length + 127) // 128)
        self.rows = -(-self.rows // 32) * 32
        self.part = self.rows // 2
        self.cut = -(-self.part // 32) * 16
        self.tall = -(-(self.first[-1] + self.rows) // 16) * 16
        self.early = [s for s in range(shards) if self.first[s] >= ROW_DOWN]
        self.handed = (
            ((4, 26 * 48, 256), BF), ((2, 28 * 48, 256), BF), ((self.rows, 128), F32),
            ((len(self.early), self.rows, 128), BF),
        )

    def here(self):
        d0, d1, d2 = self.dims
        me = lax.axis_index("fsdp")
        return me, lax.axis_index("rep"), me // (d1 * d2), me // d2 % d1, me % d2

    def block(self, a, b, c):
        d0, d1, d2 = self.dims
        return (a * d1 + b) * d2 + c


def flip(a, k):
    bit = 1
    while bit <= k:
        if k & bit:
            a = a + bit - 2 * bit * (a // bit % 2)
        bit *= 2
    return a


def to_rows(plan, ref):
    full = plan.length // 128
    left = plan.length - 128 * full
    parts = [ref[pl.ds(0, 128 * full)].reshape(full, 128)]
    if left:
        tail = ref[pl.ds(128 * full, left)].reshape(1, left)
        parts.append(jnp.concatenate([tail, jnp.zeros((1, 128 - left), F32)], axis=1))
    have = full + (left > 0)
    parts.append(jnp.zeros((plan.rows - have, 128), F32))
    return jnp.concatenate(parts, axis=0)


def gather_kernel(
    plan,
    master_ref, inp_hbm, upf_hbm,
    vec_ref, inpo_ref, upfo_ref, wu_ref, wdn_ref, wc6_ref, wf_ref,
    inp_ref, upf_ref, g_ref, w_ref, tmp_ref, in_sem, send_sem, recv_sem, sib_send, sib_recv, far_send,
):
    d0, d1, d2 = plan.dims
    me, core, a, b, c = plan.here()
    part, cut = plan.part, plan.cut
    loads = [
        pltpu.make_async_copy(src, dst, in_sem.at[n])
        for n, (src, dst) in enumerate(((inp_hbm, inp_ref), (upf_hbm, upf_ref)))
    ]
    for load in loads:
        load.start()
    barrier = pltpu.get_barrier_semaphore()
    others = [plan.block((a + k) % d0, b, c) for k in range(1, d0)]
    others += [plan.block(a, (b + k) % d1, c) for k in range(1, d1)]
    others += [plan.block(a, b, (c + k) % d2) for k in range(1, d2)]
    others = [{"fsdp": other, "rep": core} for other in others] + [{"fsdp": me, "rep": 1 - core}]
    for other in others:
        pl.semaphore_signal(barrier, inc=1, device_id=other, device_id_type=pl.DeviceIdType.MESH)
    off = (me * plan.length) % 128
    x = pltpu.roll(to_rows(plan, master_ref), off, 1)
    row = lax.broadcasted_iota(jnp.int32, x.shape, 0)
    lane = lax.broadcasted_iota(jnp.int32, x.shape, 1)
    above = jnp.where(row == 0, 0.0, pltpu.roll(x, 1, 0))
    g_ref[me] = jnp.where(lane < off, above, x).astype(BF)
    pl.semaphore_wait(barrier, len(others))

    def span(half, which):
        start = which * part + (cut if half == 1 else 0)
        return pl.ds(pl.multiple_of(start, 16), (cut, part - cut)[half])

    def copy(block, half, fsdp, rep, send, recv, which):
        at = g_ref.at[block, span(half, which)]
        return pltpu.make_async_remote_copy(
            src_ref=at, dst_ref=at, send_sem=send, recv_sem=recv,
            device_id={"fsdp": fsdp, "rep": rep}, device_id_type=pl.DeviceIdType.MESH,
        )

    def arrive(block, half):
        copy(block, half, me, core, far_send.at[0, 0], recv_sem.at[block, half], core).wait_recv()

    sent = []

    def go(d):
        d.start()
        sent.append(d)

    def along1(block, half):
        for k in range(1, d1):
            go(copy(block, half, plan.block(a, (b + k) % d1, c), core,
                    send_sem.at[block, half, k - 1], recv_sem.at[block, half], core))

    def along2(block, half):
        for k in range(1, d2):
            go(copy(block, half, plan.block(a, b, (c + k) % d2), core,
                    send_sem.at[block, half, d1 + k - 2], recv_sem.at[block, half], core))

    def beside(block, half):
        go(copy(block, half, me, 1 - core, sib_send.at[block, half], sib_recv.at[block, half], core))

    def own_column(k):
        block = plan.block(flip(a, k), b, c)
        if k:
            arrive(block, 0)
        along2(block, 0)
        if k:
            arrive(block, 1)
        along1(block, 1)
        along2(block, 1)
        along1(block, 0)
        if k:
            beside(block, 0)
            beside(block, 1)

    def near(k):
        a2 = flip(a, k)
        ahead = [plan.block(a2, b, (c + i) % d2) for i in range(1, d2)]
        above = [plan.block(a2, (b + i) % d1, c) for i in range(1, d1)]
        for block in ahead:
            arrive(block, 0)
            along1(block, 0)
            beside(block, 0)
        for block in above:
            arrive(block, 1)
            along2(block, 1)
            beside(block, 1)
        for block in ahead:
            arrive(block, 1)
            beside(block, 1)
        for block in above:
            arrive(block, 0)
            beside(block, 0)

    def diagonal(k):
        a2 = flip(a, k)
        for i in range(1, d1):
            for j in range(1, d2):
                block = plan.block(a2, (b + i) % d1, (c + j) % d2)
                for half in (0, 1):
                    arrive(block, half)
                    beside(block, half)

    def parity(src, dst):
        def one(r, _):
            parts = []
            for n in range(2):
                at = rows_of(r + 24 * n, 48, 48)
                v = src[at, :].astype(F32)
                for p in range(2):
                    tmp_ref[p, at, :] = v[:, 128 * p : 128 * p + 128]
            for first in range(2):
                for n in range(2):
                    at = pl.ds((r + 24 * n) * 48 + first, 24, stride=2)
                    parts.append(jnp.concatenate([tmp_ref[p, at, :] for p in range(2)], axis=1))
            dst[rows_of(r, 96, 96), :] = jnp.concatenate(parts, axis=0).astype(BF)
            return 0

        lax.fori_loop(0, 24, one, 0, unroll=2)

    for k in range(1, d0):
        for half in (0, 1):
            go(copy(me, half, plan.block(flip(a, k), b, c), core, far_send.at[k, half], recv_sem.at[me, half], core))
    own_column(0)
    loads[0].wait()
    parity(inp_ref, inpo_ref)
    loads[1].wait()
    parity(upf_ref, upfo_ref)
    for k in range(1, d0):
        own_column(k)
    for k in range(d0):
        near(k)
    for k in range(d0):
        diagonal(k)
    for k in range(1, plan.n):
        block = (me + k) % plan.n
        for half in (0, 1):
            copy(block, half, me, core, far_send.at[0, 0], sib_recv.at[block, half], 1 - core).wait_recv()

    for s in range(plan.n):
        v = g_ref[s].astype(F32)
        at = plan.first[s]
        if s:
            low = w_ref[at : at + 1, :] + v[0:1]
            w_ref[at : at + plan.rows, :] = v
            w_ref[at : at + 1, :] = low
        else:
            w_ref[0 : plan.rows, :] = v
    vec_ref[...] = w_ref[ROW_VEC : ROW_VEC + 8, :]
    for dy in range(3):
        for h in range(2):
            g0, g1, g2 = (w_ref[pl.ds(2 * (3 * dy + dx) + h, 256, stride=18), :] for dx in range(3))
            outer = g0 + g2
            for i, v in enumerate((g0, 0.5 * (outer + g1), 0.5 * (outer - g1), g2)):
                at = 768 * i + 256 * dy
                wf_ref[at : at + 256, 128 * h : 128 * h + 128] = v.astype(BF)
    for h in range(2):
        wu_ref[:, 128 * h : 128 * h + 128] = w_ref[pl.ds(ROW_UP + h, 128, stride=2), :].astype(BF)
    for t in range(9):
        p = (4, 5, 3, 7, 1, 8, 6, 2, 0).index(t)
        wdn_ref[:, 128 * p : 128 * p + 128] = w_ref[pl.ds(ROW_DOWN + t, 256, stride=9), :].astype(BF)
    wc6_ref[0:128, 384:768] = jnp.zeros((128, 384), BF)
    for t in range(9):
        dy, dx = t // 3, t % 3
        at, p = 128 * (dx + 1) // 2 // 128 * 128, dy + 3 * (dx // 2)
        wc6_ref[at : at + 128, 128 * p : 128 * p + 128] = w_ref[pl.ds(ROW_COARSE + t, 128, stride=9), :].astype(BF)
    for d in sent:
        d.wait_send()


def gather_call(plan, master, inp, upf):
    there = pl.BlockSpec(memory_space=pltpu.HBM)
    whole = pl.BlockSpec(memory_space=pltpu.VMEM)
    low = lambda *shape: jax.ShapeDtypeStruct(shape, BF)
    outs = [
        jax.ShapeDtypeStruct((8, 128), F32), low(PIX, 256), low(PIX, 256), low(128, 256), low(256, 1152),
        low(256, 768), low(12 * 256, 256),
    ]
    d0, d1, d2 = plan.dims
    sems = pltpu.SemaphoreType.DMA
    return pl.pallas_call(
        functools.partial(gather_kernel, plan),
        out_shape=outs,
        in_specs=[whole, there, there],
        out_specs=[whole] * 7,
        scratch_shapes=[
            pltpu.VMEM((PIX, 256), BF), pltpu.VMEM((PIX, 256), BF),
            pltpu.VMEM((plan.n, plan.rows, 128), BF), pltpu.VMEM((plan.tall, 128), F32), pltpu.VMEM((2, PIX, 128), F32),
            sems((2,)), sems((plan.n, 2, max(d1 + d2 - 2, 1))), sems((plan.n, 2)), sems((plan.n, 2)),
            sems((plan.n, 2)), sems((d0, 2)),
        ],
        compiler_params=pltpu.CompilerParams(collective_id=0, has_side_effects=True, vmem_limit_bytes=20 * 2**20),
        name="gather_weights",
    )(master, *(pltpu.with_memory_space_constraint(x, pltpu.HBM) for x in (inp, upf)))


def reduce_kernel(
    plan,
    u_ref, g_ref, join_ref, blocks_ref,
    out_ref, tile_ref,
    sums_ref, grad_ref, p_ref, q_ref, ua_ref, ub_ref, va_ref, vb_ref, z_ref, sa_ref, total_ref,
    n1_ref, n2_ref,
    q_send, q_recv, s1_send, s1_recv, s2_send, s2_recv, s3_send, s3_recv, t_send, t_recv,
    n1_send, n1_recv, n2_send, n2_recv,
):
    d0, d1, d2 = plan.dims
    me, core, a, b, c = plan.here()
    part, cut = plan.part, plan.cut
    MESH = pl.DeviceIdType.MESH
    barrier = pltpu.get_barrier_semaphore()
    others = [{"fsdp": plan.block((a + k) % d0, b, c), "rep": core} for k in range(1, d0)]
    plane = []
    for i in range(d1):
        for j in range(d2):
            for o in range(2):
                if i or j or o:
                    plane.append((i, j, o, {"fsdp": plan.block(a, (b + i) % d1, (c + j) % d2), "rep": (core + o) % 2}))
    others += [p[3] for p in plane]
    for other in others:
        pl.semaphore_signal(barrier, inc=1, device_id=other, device_id_type=MESH)
    even, odd = g_ref[0], g_ref[1]
    sums_ref[0] = even + odd
    sums_ref[1] = even - odd
    products = []
    for i, ref in enumerate((g_ref.at[0], sums_ref.at[0], sums_ref.at[1], g_ref.at[1])):
        shifted = [ref[48 * (2 - dy) : 48 * (2 - dy) + 26 * 48, :] for dy in range(3)]
        products.append(dot_rows(u_ref[i], jnp.concatenate(shifted, axis=1)))
    p0, p1, p2, p3 = products
    both, apart = 0.5 * (p1 + p2), 0.5 * (p1 - p2)
    for dx, grad in enumerate((p0 + both, apart, both - p3)):
        for dy in range(3):
            for j in range(2):
                at = 256 * dy + 128 * j
                grad_ref[pl.ds(2 * (3 * dy + dx) + j, 256, stride=18), :] = grad[:, at : at + 128]
    count = len(plan.early)
    grad_ref[ROW_DOWN:, :] = join_ref[...]
    for s in range(plan.n - count):
        first = plan.first[s]
        p_ref[s] = grad_ref[first : first + plan.rows, :].astype(BF)
    p_ref[plan.n - count :] = blocks_ref[...]
    pl.semaphore_wait(barrier, len(others))

    sent = []

    def go(src, dst, send, recv, to):
        d = pltpu.make_async_remote_copy(
            src_ref=src, dst_ref=dst, send_sem=send, recv_sem=recv, device_id=to, device_id_type=MESH
        )
        d.start()
        sent.append(d)

    def got(ref, recv):
        pltpu.make_async_copy(ref, ref, recv).wait()

    mine = pl.multiple_of(core * part, 16)
    theirs = pl.multiple_of((1 - core) * part, 16)
    halves = ((0, cut), (cut, part - cut))
    order = [(k + 1) % d0 for k in range(d0)]
    for k in order:
        for i in list(range(1, d1)) + [0]:
            for j in list(range(1, d2)) + [0]:
                s = plan.block((a + k) % d0, (b + i) % d1, (c + j) % d2)
                go(
                    p_ref.at[s, pl.ds(theirs, part)], q_ref.at[s], q_send.at[s], q_recv.at[s],
                    {"fsdp": me, "rep": 1 - core},
                )

    def pair(s, half):
        start, size = halves[half]
        x = p_ref[s, pl.ds(pl.multiple_of(mine + start, 16), size), :].astype(F32)
        return x + q_ref[s, start : start + size, :].astype(F32)

    def step1(k):
        a2 = (a + k) % d0
        for i in range(1, d1):
            for j in list(range(1, d2)) + [0]:
                s = plan.block(a2, (b + i) % d1, (c + j) % d2)
                got(q_ref.at[s], q_recv.at[s])
                sa_ref[s, 0:cut, :] = pair(s, 0).astype(BF)
                go(sa_ref.at[s, 0:cut], ua_ref.at[a2, (c + j) % d2, i - 1], s1_send.at[s, 0], s1_recv.at[0, a2, (c + j) % d2, i - 1],
                   {"fsdp": plan.block(a, (b + i) % d1, c), "rep": core})
                if j:
                    step1b(s, a2, i, j)
        for j in range(1, d2):
            s = plan.block(a2, b, (c + j) % d2)
            got(q_ref.at[s], q_recv.at[s])
            step1b(s, a2, 0, j)

    def step1b(s, a2, i, j):
        sa_ref[s, cut:part, :] = pair(s, 1).astype(BF)
        go(sa_ref.at[s, cut:part], ub_ref.at[a2, (b + i) % d1, j - 1], s1_send.at[s, 1], s1_recv.at[1, a2, (b + i) % d1, j - 1],
           {"fsdp": plan.block(a, b, (c + j) % d2), "rep": core})

    def from1(half, a2, other):
        ref = ua_ref if half == 0 else ub_ref
        total = None
        for i in range((d1 if half == 0 else d2) - 1):
            got(ref.at[a2, other, i], s1_recv.at[half, a2, other, i])
            v = ref[a2, other, i].astype(F32)
            total = v if total is None else total + v
        return total

    def plus(x, y):
        return x if y is None else x + y

    def step2(k):
        a2 = (a + k) % d0
        for j in range(1, d2):
            c2 = (c + j) % d2
            s = plan.block(a2, b, c2)
            sa_ref[s, 0:cut, :] = plus(pair(s, 0), from1(0, a2, c2)).astype(BF)
            go(sa_ref.at[s, 0:cut], va_ref.at[a2, j - 1], s2_send.at[0, a2, j - 1], s2_recv.at[0, a2, j - 1],
               {"fsdp": plan.block(a, b, c2), "rep": core})
        for i in range(1, d1):
            b2 = (b + i) % d1
            s = plan.block(a2, b2, c)
            sa_ref[s, cut:part, :] = plus(pair(s, 1), from1(1, a2, b2)).astype(BF)
            go(sa_ref.at[s, cut:part], vb_ref.at[a2, i - 1], s2_send.at[1, a2, i - 1], s2_recv.at[1, a2, i - 1],
               {"fsdp": plan.block(a, b2, c), "rep": core})

    def column(k):
        a2 = (a + k) % d0
        s = plan.block(a2, b, c)
        got(q_ref.at[s], q_recv.at[s])
        x = plus(pair(s, 0), from1(0, a2, c))
        for j in range(1, d2):
            got(va_ref.at[a2, j - 1], s2_recv.at[0, a2, j - 1])
            x = x + va_ref[a2, j - 1].astype(F32)
        y = plus(pair(s, 1), from1(1, a2, b))
        for i in range(1, d1):
            got(vb_ref.at[a2, i - 1], s2_recv.at[1, a2, i - 1])
            y = y + vb_ref[a2, i - 1].astype(F32)
        return s, x, y

    def step3(k):
        s, x, y = column(k)
        sa_ref[s, 0:cut, :] = x.astype(BF)
        sa_ref[s, cut:part, :] = y.astype(BF)
        go(sa_ref.at[s], z_ref.at[k - 1], s3_send.at[k - 1], s3_recv.at[k - 1], {"fsdp": plan.block((a + k) % d0, b, c), "rep": core})

    for n in range(d0 + 2):
        if n < d0:
            step1(order[n])
        if 0 <= n - 1 < d0:
            step2(order[n - 1])
        if 0 <= n - 2 < d0 - 1:
            step3(order[n - 2])
    _, x, y = column(0)
    total = jnp.concatenate([x, y], axis=0)
    for k in range(1, d0):
        got(z_ref.at[k - 1], s3_recv.at[k - 1])
        total = total + z_ref[k - 1].astype(F32)
    total_ref[pl.ds(mine, part), :] = total
    go(total_ref.at[pl.ds(mine, part)], total_ref.at[pl.ds(mine, part)], t_send.at[0], t_recv.at[0], {"fsdp": me, "rep": 1 - core})

    off = (me * plan.length) % 128
    row = lax.broadcasted_iota(jnp.int32, (part, 128), 0) + mine
    at = row * 128 + lax.broadcasted_iota(jnp.int32, (part, 128), 1)
    own = jnp.where((at >= off) & (at < off + plan.length), total, 0.0)
    last = me == plan.n - 1
    for i in range(6):
        spot = ROW_VEC - plan.first[-1] + i
        holds = last & (core == spot // part)
        n1_ref[a, i:i + 1, :] = jnp.where(holds, total[spot % part:spot % part + 1], 0.0)
    n1_ref[a, 6:7, :] = jnp.sum(own * own, axis=0, keepdims=True)
    n1_ref[a, 7:8, :] = jnp.zeros((1, 128), F32)
    for k in range(1, d0):
        go(n1_ref.at[a], n1_ref.at[a], n1_send.at[k], n1_recv.at[a], {"fsdp": plan.block((a + k) % d0, b, c), "rep": core})
    for k in range(1, d0):
        got(n1_ref.at[(a + k) % d0], n1_recv.at[(a + k) % d0])
    tile = n1_ref[0]
    for k in range(1, d0):
        tile = tile + n1_ref[k]
    slot = (b * d2 + c) * 2 + core
    n2_ref[slot] = tile
    for n, (i, j, o, to) in enumerate(plane):
        go(n2_ref.at[slot], n2_ref.at[slot], n2_send.at[n], n2_recv.at[slot], to)
    got(total_ref.at[pl.ds(theirs, part)], t_recv.at[0])
    x = pltpu.roll(total_ref[...], (128 - off) % 128, 1)
    below = pltpu.roll(x, plan.rows - 1, 0)
    lane = lax.broadcasted_iota(jnp.int32, x.shape, 1)
    out_ref[...] = jnp.where(lane + off >= 128, below, x)
    for n, (i, j, o, to) in enumerate(plane):
        other = (((b + i) % d1) * d2 + (c + j) % d2) * 2 + (core + o) % 2
        got(n2_ref.at[other], n2_recv.at[other])
    tile = n2_ref[0]
    for n in range(1, 2 * d1 * d2):
        tile = tile + n2_ref[n]
    tile_ref[...] = tile
    for d in sent:
        d.wait_send()


def reduce_call(plan, *handed):
    whole = pl.BlockSpec(memory_space=pltpu.VMEM)
    d0, d1, d2 = plan.dims
    sems = pltpu.SemaphoreType.DMA
    low = lambda *shape: pltpu.VMEM(shape, BF)
    wide = lambda *shape: pltpu.VMEM(shape, F32)
    e1, e2 = max(d1 - 1, 1), max(d2 - 1, 1)
    rest = plan.part - plan.cut
    return pl.pallas_call(
        functools.partial(reduce_kernel, plan),
        out_shape=[jax.ShapeDtypeStruct((plan.rows, 128), F32), jax.ShapeDtypeStruct((8, 128), F32)],
        in_specs=[whole] * 4,
        out_specs=[whole] * 2,
        scratch_shapes=[
            low(2, 28 * 48, 256), wide(ROW_DOWN + plan.rows, 128),
            low(plan.n, plan.rows, 128), low(plan.n, plan.part, 128),
            low(d0, d2, e1, plan.cut, 128), low(d0, d1, e2, rest, 128),
            low(d0, e2, plan.cut, 128), low(d0, e1, rest, 128), low(max(d0 - 1, 1), plan.part, 128),
            low(plan.n, plan.part, 128),
            wide(plan.rows, 128), wide(d0, 8, 128), wide(2 * d1 * d2, 8, 128),
            sems((plan.n,)), sems((plan.n,)), sems((plan.n, 2)),
            sems((2, d0, max(d1, d2), max(e1, e2))), sems((2, d0, max(e1, e2))), sems((2, d0, max(e1, e2))),
            sems((d0,)), sems((d0,)), sems((1,)), sems((1,)),
            sems((d0,)), sems((d0,)), sems((2 * d1 * d2,)), sems((2 * d1 * d2,)),
        ],
        compiler_params=pltpu.CompilerParams(collective_id=1, has_side_effects=True, vmem_limit_bytes=20 * 2**20),
        name="reduce_gradients",
    )(*handed)


def update_kernel(
    plan,
    grad_ref, tile_ref, master_ref, first_ref, second_ref, average_ref,
    norm_ref, new_master_ref, new_first_ref, new_second_ref, new_average_ref, small_ref,
):
    grad_norm = jnp.sqrt(jnp.sum(tile_ref[6:7, :], axis=1, keepdims=True))
    factor = jnp.minimum(1.0, clip_norm / (grad_norm + 1e-06))
    norm_ref[...] = grad_norm
    for i in range(6):
        small_ref[pl.ds(128 * i, 128)] = (tile_ref[i : i + 1, :] * factor).reshape(128)
    full = plan.length // 128
    left = plan.length - 128 * full
    ema_rate = min(0.999, (1.0 + STEP) / (10.0 + STEP))

    def update(row, rows, lanes):
        at = pl.ds(128 * row, 128 * (rows - 1) + lanes)
        shape = (rows, lanes)
        clipped = grad_ref[row : row + rows, 0:lanes] * factor
        new_first = beta_one * first_ref[at].reshape(shape) + (1.0 - beta_one) * clipped
        new_second = beta_two * second_ref[at].reshape(shape) + (1.0 - beta_two) * clipped * clipped
        corrected_first = new_first / (1.0 - beta_one**STEP)
        corrected_second = new_second / (1.0 - beta_two**STEP)
        master = master_ref[at].reshape(shape)
        new_master = master - learn_rate * (
            corrected_first / (jnp.sqrt(corrected_second) + adam_eps) + decay_rate * master
        )
        new_average = ema_rate * average_ref[at].reshape(shape) + (1.0 - ema_rate) * new_master
        size = 128 * (rows - 1) + lanes
        new_master_ref[at] = new_master.reshape(size)
        new_first_ref[at] = new_first.reshape(size)
        new_second_ref[at] = new_second.reshape(size)
        new_average_ref[at] = new_average.reshape(size)

    update(0, full, 128)
    if left:
        update(full, 1, left)


def update_call(plan, *args):
    whole = pl.BlockSpec(memory_space=pltpu.VMEM)
    flat = jax.ShapeDtypeStruct((plan.length,), F32)
    return pl.pallas_call(
        functools.partial(update_kernel, plan),
        out_shape=[jax.ShapeDtypeStruct((1, 1), F32), flat, flat, flat, flat, jax.ShapeDtypeStruct((768,), F32)],
        in_specs=[whole] * 6,
        out_specs=[whole] * 6,
        compiler_params=pltpu.CompilerParams(vmem_limit_bytes=16 * 2**20),
        name="update",
    )(*args)


def per_device(
    input_fine, input_coarse, upstream_fine, upstream_coarse, extents, master, first_moment, second_moment, average
):
    plan = Plan(lax.axis_size("fsdp"), master.shape[0])
    vec, inp, upf, wu, wdn, wc6, wf = gather_call(
        plan, master, input_fine.reshape(PIX, C1), upstream_fine.reshape(PIX, C1)
    )
    out_fine, out_coarse, gi_fine, gi_coarse, *handed = layer_call(
        plan, extents, vec, inp, wu, wdn, wc6, wf, upf,
        input_coarse.reshape(CPIX, C2), upstream_coarse.reshape(CPIX, C2),
    )
    grad, tile = reduce_call(plan, *handed)
    grad_norm, new_master, new_first, new_second, new_average, norm_grads = update_call(
        plan, grad, tile, master, first_moment, second_moment, average
    )
    grad_norm = grad_norm.reshape(())
    return (
        out_fine.reshape(input_fine.shape),
        out_coarse.reshape(input_coarse.shape),
        gi_fine.reshape(input_fine.shape),
        gi_coarse.reshape(input_coarse.shape),
        grad_norm,
        new_master,
        new_first,
        new_second,
        new_average,
        norm_grads,
    )


def solution(mesh):
    images = P(("fsdp", "rep"), None, None, None)
    flat = P("fsdp")
    in_specs = (images,) * 4 + (P(("fsdp", "rep"), None),) + (flat,) * 4
    out_specs = (images,) * 4 + (P(),) + (flat,) * 4 + (P(),)
    return jax.shard_map(per_device, mesh=mesh, in_specs=in_specs, out_specs=out_specs, check_vma=False)
```

```python
import functools

import jax
import jax.numpy as jnp
from jax import lax
from jax.experimental import pallas as pl
from jax.experimental.pallas import tpu as pltpu
from jax.sharding import PartitionSpec as P

F32, BF = jnp.float32, jnp.bfloat16
C1, C2, GROUPS, ITERS, STEP = 256, 128, 8, 12, 10
HEIGHT, HALF = 48, 24
PIX, CPIX = HEIGHT * HEIGHT, HALF * HALF
FLAT_ROWS = 8326
ROW_DOWN, ROW_COARSE, ROW_UP, ROW_VEC = 4608, 6912, 8064, 8320

clip_norm = 1.0
learn_rate = 0.02
beta_one = 0.9
beta_two = 0.999
adam_eps = 1e-08
decay_rate = 0.1


def dot(a, b):
    return jnp.dot(a, b, preferred_element_type=F32)


def dot_rows(a, b):
    return lax.dot_general(a, b, (((0,), (0,)), ((), ())), preferred_element_type=F32)


def dot_lanes(a, b):
    return lax.dot_general(a, b, (((1,), (1,)), ((), ())), preferred_element_type=F32)


def run_sum(x, width):
    lane = lax.broadcasted_iota(jnp.int32, x.shape, 1)
    step = 1
    while step < width:
        up = pltpu.roll(x, 128 - step, 1)
        down = pltpu.roll(x, step, 1)
        x = x + jnp.where((lane & step) == 0, up, down)
        step *= 2
    return x


def shift_down(x):
    count = x.shape[0] // 8
    top = lax.broadcasted_iota(jnp.int32, (8, x.shape[1]), 0) == 0
    turned = [pltpu.roll(x[8 * i : 8 * i + 8], 1, 0) for i in range(count)]
    return jnp.concatenate(
        [jnp.where(top, turned[i - 1] if i else 0.0, turned[i]) for i in range(count)], axis=0
    )


def shift_up(x):
    count = x.shape[0] // 8
    end = lax.broadcasted_iota(jnp.int32, (8, x.shape[1]), 0) == 7
    turned = [pltpu.roll(x[8 * i : 8 * i + 8], 7, 0) for i in range(count)]
    return jnp.concatenate(
        [jnp.where(end, turned[i + 1] if i < count - 1 else 0.0, turned[i]) for i in range(count)], axis=0
    )


def rows_out(x):
    parts = [x[24 * i : 24 * i + 24] for i in range(24)]
    return parts[0::2] + parts[1::2]


def pair_order(rows):
    return jnp.concatenate([rows[i // 2 + 12 * (i % 2)] for i in range(24)], axis=0)


def image_order(x):
    return jnp.concatenate(rows_out(x), axis=0)


def in_rows(x, change):
    return jnp.concatenate([change(x[24 * r : 24 * r + 24]) for r in range(24)], axis=0)


def row_down(x):
    rows = rows_out(x)
    return pair_order([jnp.zeros_like(rows[0])] + rows[:-1])


def row_up(x):
    rows = rows_out(x)
    return pair_order(rows[1:] + [jnp.zeros_like(rows[0])])


def tile_sum(x):
    total = x[0:8]
    for i in range(1, x.shape[0] // 8):
        total = total + x[8 * i : 8 * i + 8]
    return total


def twice(m):
    return jnp.concatenate([m, m], axis=1)


def interleave(ref, r, even, odd):
    for p in range(2):
        at = slice(128 * p, 128 * p + 128)
        ref[p, pl.ds(r * 48, 24, stride=2), :] = even[:, at]
        ref[p, pl.ds(r * 48 + 1, 24, stride=2), :] = odd[:, at]


def rows_of(r, count, unit):
    start = r * unit
    return pl.ds(start if isinstance(r, int) else pl.multiple_of(start, unit if unit % 16 == 0 else 8), count)


STEPS = "E0 E1 E2 E3 C1-7 E4 E5 E6 C7-13 E7 E8 E9 E10 E11 C13-17 L C17-21 Z K C21-24,0-1 S F B"


def layer_kernel(
    plan,
    ext_ref, vec_ref, inp_in, wu_in, wdn_in, wc6_in, wf_in, upf_in, inc_hbm, upc_hbm,
    outf_ref, outc_ref, gif_ref, gic_ref, uo_ref, go_ref, join_ref, blocks_ref,
    g_ref, u_ref, upf_ref, inp_ref, wu_ref, wdn_ref, wc6_ref, wf_ref, inc_in, upc_ref, grad_ref, ph_ref, c_ref, x_ref, xc_ref, inc_ref, branch_ref, lift_ref, mf_ref, mb_ref, mc_ref,
    scf_ref, scc_ref, gl_ref, glo_ref, back_ref, gp_ref, row_ref, stage_ref, small_ref,
    in_sem, out_sem, small_sem,
):
    loads = [
        pltpu.make_async_copy(src, dst, in_sem.at[n])
        for n, (src, dst) in enumerate(
            ((inc_hbm, inc_in), (upc_hbm, upc_ref))
        )
    ]
    for load in loads:
        load.start()
    hh, ww = ext_ref[0, 0], ext_ref[0, 1]
    gain_f = jnp.concatenate([vec_ref[0:1, :], vec_ref[1:2, :]], axis=1)
    bias_f = jnp.concatenate([vec_ref[2:3, :], vec_ref[3:4, :]], axis=1)
    gain_c, bias_c = vec_ref[4:5, :], vec_ref[5:6, :]
    pos = lax.broadcasted_iota(jnp.int32, (24, 128), 0)
    even = jnp.where(2 * pos < ww, 1.0, 0.0).astype(F32)
    odd = jnp.where(2 * pos + 1 < ww, 1.0, 0.0).astype(F32)

    def setup(r, _):
        at = rows_of(r, 96, 96)
        low, high = r < hh, r + 24 < hh
        m = [jnp.where(here, v, 0.0) for v in (even, odd) for here in (low, high)]
        m = jnp.concatenate(m, axis=0)
        mf_ref[at, :] = m
        mb_ref[at, :] = m.astype(BF)
        x_ref[at, :] = jnp.zeros((96, 256), F32)
        return 0

    lax.fori_loop(0, 24, setup, 0)

    def setup_coarse(r, _):
        m = [jnp.where(2 * r < hh, even, 0.0), jnp.where(2 * r + 24 < hh, even, 0.0)]
        mc_ref[rows_of(r, 48, 48), :] = jnp.concatenate(m, axis=0)
        return 0

    lax.fori_loop(0, 12, setup_coarse, 0)
    nf = (hh * ww).astype(F32) * (C1 // GROUPS)
    nc = (((hh + 1) // 2) * ((ww + 1) // 2)).astype(F32) * (C2 // GROUPS)
    g_ref[:, 0:96, :] = jnp.zeros((2, 96, 256), BF)
    g_ref[:, 26 * 48 : 28 * 48, :] = jnp.zeros((2, 96, 256), BF)
    grad_ref[FLAT_ROWS:, :] = jnp.zeros((plan.tall - FLAT_ROWS, 128), F32)
    xc_ref[...] = jnp.zeros((576, 128), F32)
    scf_ref[...] = jnp.zeros((8, 256), F32)
    scc_ref[...] = jnp.zeros((8, 128), F32)
    scf_ref[1:2, :] = 0.5 * bias_f
    scc_ref[1:2, :] = 0.5 * bias_c
    for src, dst in (
        (inp_in, inp_ref), (wu_in, wu_ref), (wdn_in, wdn_ref), (wc6_in, wc6_ref), (wf_in, wf_ref)
    ):
        dst[...] = src[...]
    loads[0].wait()
    v = inc_in[...].astype(F32)
    inc_ref[...] = pair_order([v[24 * r : 24 * r + 24] for r in range(24)])

    def coarse_branch():
        h = xc_ref[...] * scc_ref[0:1, :] + scc_ref[1:2, :]
        y = h * jnp.tanh(h) + h
        branch = ((y + inc_ref[...]) * mc_ref[...]).astype(BF)
        branch_ref[...] = branch
        lift_ref[...] = dot(branch, wu_ref[...])

    def unit(r, final):
        scale, shift = scf_ref[0:1, :], scf_ref[1:2, :]
        half = rows_of(r // 2, 48, 48)
        lift = lift_ref[half, :]
        lift_low = lift.astype(BF)
        z = []
        for p in range(2):
            at = rows_of(2 * r + p, 48, 48)
            h = x_ref[at, :] * scale + shift
            if final:
                y = h * jnp.tanh(h) + h
            else:
                h = h.astype(BF)
                y = h * jnp.tanh(h) + h
            if final:
                m = twice(mf_ref[at, :])
                low = ((y + inp_ref[at, :].astype(F32)) * m).astype(BF)
                z.append((low.astype(F32) + lift) * m)
            else:
                m = twice(mb_ref[at, :])
                low = (y.astype(BF) + inp_ref[at, :]) * m
                z.append((low + lift_low) * m)
            ph_ref[2 * (r % 2) + p, half, :] = low
        even, odd = z
        if final:
            for i in range(2):
                at = slice(24 * i, 24 * i + 24)
                interleave(stage_ref.at[0], r + 24 * i, even[at], odd[at])
            return
        wide = odd.astype(F32)
        left = jnp.concatenate([shift_down(wide[0:24]), shift_down(wide[24:48])], axis=0).astype(BF)
        wide = even.astype(F32)
        right = jnp.concatenate([shift_up(wide[0:24]), shift_up(wide[24:48])], axis=0).astype(BF)
        for i, u in enumerate((left - odd, even + odd, odd - even, even - right)):
            u_ref[i, rows_of(r + 1, 48, 48), :] = u
            if r == 0:
                w = u.astype(F32)
                u_ref[i, 25 * 48 : 26 * 48, :] = jnp.concatenate([w[24:48], jnp.zeros_like(w[0:24])], axis=0).astype(BF)
            if r == 23:
                w = u.astype(F32)
                u_ref[i, 0:48, :] = jnp.concatenate([jnp.zeros_like(w[0:24]), w[0:24]], axis=0).astype(BF)

    def lowered_parts(first=0, last=CPIX):
        ee, eo, oe, oo = (ph_ref[i, first:last, :] for i in range(4))
        p = dot(eo, wdn_ref[:, 128:384]) + dot(oo, wdn_ref[:, 640:896])
        q = dot(oe, wdn_ref[:, 384:640])
        t = dot(oo, wdn_ref[:, 896:1152])
        return p, q, t, dot(ee, wdn_ref[:, 0:128])

    def lowered(parts):
        p, q, t, e = parts
        here = p[:, :128] + q[:, :128] + e
        return here + row_down(q[:, 128:] + t[:, :128]) + in_rows(p[:, 128:] + row_down(t[:, 128:]), shift_down)

    def coarse_state(parts):
        zc = (branch_ref[...].astype(F32) + lowered(parts)) * mc_ref[...]
        c_ref[:, 0:128] = in_rows(zc, shift_down).astype(BF)
        c_ref[:, 128:256] = zc.astype(BF)

    def coarse_sums(p):
        t = [p[:, 128 * i : 128 * i + 128] for i in range(6)]
        xc = row_down(t[0]) + t[1] + row_up(t[2]) + in_rows(row_down(t[3]) + t[4] + row_up(t[5]), shift_up)
        xc_ref[...] = xc
        xm = xc * mc_ref[...]
        return tile_sum(xm), tile_sum(xm * xm)

    def conv_units(units):
        products = []
        for i in range(4):
            total = None
            for dy in range(3):
                rows = [u_ref[i, 48 * (first + dy) : 48 * (last + dy), :] for first, last in units]
                rows = rows[0] if len(rows) == 1 else jnp.concatenate(rows, axis=0)
                at = 768 * i + 256 * dy
                p = dot(rows, wf_ref[at : at + 256, :])
                total = p if total is None else total + p
            products.append(total)
        m0, m1, m2, m3 = products
        even, odd = m0 + m1 + m2, m1 - m2 - m3
        s = q = None
        for n, r in enumerate(r for first, last in units for r in range(first, last)):
            for p, y in enumerate((even, odd)):
                y = y[48 * n : 48 * n + 48]
                at = slice(96 * r + 48 * p, 96 * r + 48 * p + 48)
                x_ref[at, :] = y
                ym = y * twice(mf_ref[at, :])
                ds, dq = tile_sum(ym), tile_sum(ym * ym)
                s, q = (ds, dq) if s is None else (s + ds, q + dq)
        return s, q

    def finish(s, q, width, n, gain, bias, to_ref):
        s, q = jnp.sum(s, axis=0, keepdims=True), jnp.sum(q, axis=0, keepdims=True)
        for p in range(s.shape[1] // 128):
            at = slice(128 * p, 128 * p + 128)
            mean = run_sum(s[:, at], width) / n
            var = jnp.maximum(run_sum(q[:, at], width) / n - mean * mean, 0.0)
            inv = lax.rsqrt(var + 1e-5)
            to_ref[0:1, at] = 0.5 * inv * gain[:, at]
            to_ref[1:2, at] = 0.5 * (bias[:, at] - mean * inv * gain[:, at])
            to_ref[2:3, at] = mean
            to_ref[3:4, at] = inv

    def iterate(t, _):
        s = q = parts = conv_c = sums_c = None
        for step in STEPS.split():
            if step[0] == "E":
                unit(2 * int(step[1:]), False)
                unit(2 * int(step[1:]) + 1, False)
            elif step[0] == "C":
                ds, dq = conv_units([tuple(map(int, piece.split("-"))) for piece in step[1:].split(",")])
                s, q = (ds, dq) if s is None else (s + ds, q + dq)
            elif step == "L":
                parts = lowered_parts()
            elif step == "L0":
                parts = lowered_parts(0, 288)
            elif step == "L1":
                parts = [jnp.concatenate(both, axis=0) for both in zip(parts, lowered_parts(288, 576))]
            elif step == "Z":
                coarse_state(parts)
            elif step == "K":
                conv_c = dot(c_ref[...], wc6_ref[...])
            elif step == "S":
                sums_c = coarse_sums(conv_c)
            elif step == "F":
                finish(*sums_c, C2 // GROUPS, nc, gain_c, bias_c, scc_ref)
            elif step == "B":
                coarse_branch()
        finish(s, q, C1 // GROUPS, nf, gain_f, bias_f, scf_ref)
        return 0

    coarse_branch()
    lax.fori_loop(0, ITERS, iterate, 0)

    sends = []

    def put(i, ref, half):
        for n in range(2):
            for p in range(2):
                at = pl.ds(48 * (12 * half + 24 * n), 576)
                send = pltpu.make_async_copy(
                    stage_ref.at[i, p, at], ref.at[at, 128 * p : 128 * p + 128], out_sem.at[i, half, n, p]
                )
                send.start()
                sends.append(send)

    def put_small(i, ref):
        send = pltpu.make_async_copy(small_ref.at[i], ref, small_sem.at[i])
        send.start()
        sends.append(send)

    for r in range(24):
        unit(r, True)
    upf_ref[...] = upf_in[...]
    put(0, outf_ref, 0)
    put(0, outf_ref, 1)
    small_ref[0] = image_order((branch_ref[...].astype(F32) + lowered(lowered_parts())) * mc_ref[...])
    put_small(0, outc_ref)
    loads[1].wait()

    v = upc_ref[...].astype(F32)
    seed_c = pair_order([v[24 * r : 24 * r + 24] for r in range(24)]) * mc_ref[...]
    right = in_rows(seed_c, shift_up)
    glo_ref[:, 0:128] = seed_c.astype(BF)
    glo_ref[:, 128:256] = right.astype(BF)
    glo_ref[:, 256:384] = row_up(seed_c).astype(BF)
    glo_ref[:, 384:512] = row_up(right).astype(BF)

    for j in range(12):
        total = None
        for i in range(4):
            at = rows_of(4 * j + i, 48, 48)
            seed = upf_ref[at, :].astype(F32) * twice(mf_ref[at, :])
            total = seed if total is None else total + seed
        gl_ref[rows_of(j, 48, 48), :] = total.astype(BF)
    g00, g01, g10, g11 = (glo_ref[:, 128 * i : 128 * i + 128] for i in range(4))

    back_c = (seed_c + dot_lanes(gl_ref[...], wu_ref[...])) * mc_ref[...]
    small_ref[1] = image_order(back_c)
    put_small(1, gic_ref)

    def pre_grad(gi, x, scale, shift, mean, inv):
        h = x * scale + shift
        t = jnp.tanh(h)
        sig = 0.5 * t + 0.5
        normed = (x - mean) * inv
        return gi * sig * (1.0 + 2.0 * h * (1.0 - sig)), normed

    def back_means(sum_bias, sum_gain, gain, width, n):
        return run_sum(sum_bias * gain, width) / n, run_sum(sum_gain * gain, width) / n

    gp_c, normed_c = pre_grad(
        back_c, xc_ref[...], scc_ref[0:1, :], scc_ref[1:2, :], scc_ref[2:3, :], scc_ref[3:4, :]
    )
    sum_gain = jnp.sum(gp_c * normed_c, axis=0, keepdims=True)
    sum_bias = jnp.sum(gp_c, axis=0, keepdims=True)
    grad_ref[ROW_VEC + 4 : ROW_VEC + 5, :] = sum_gain
    grad_ref[ROW_VEC + 5 : ROW_VEC + 6, :] = sum_bias
    mean_h, mean_hn = back_means(sum_bias, sum_gain, gain_c, C2 // GROUPS, nc)
    gconv = (gp_c * gain_c - mean_h - normed_c * mean_hn) * scc_ref[3:4, :] * mc_ref[...]
    around = jnp.concatenate([row_up(gconv), gconv, row_down(gconv)], axis=1)
    pair = dot_rows(c_ref[...], around.astype(BF))
    single = dot_rows(c_ref[:, 128:256], in_rows(around, shift_down).astype(BF))
    for dy in range(3):
        at = slice(128 * dy, 128 * dy + 128)
        grad_ref[pl.ds(ROW_COARSE + 3 * dy, 128, stride=9), :] = pair[0:128, at]
        grad_ref[pl.ds(ROW_COARSE + 3 * dy + 1, 128, stride=9), :] = pair[128:256, at]
        grad_ref[pl.ds(ROW_COARSE + 3 * dy + 2, 128, stride=9), :] = single[:, at]

    uo_ref[...] = u_ref[...]
    back_ref[0] = dot_lanes(g00, wdn_ref[:, 0:128])
    back_ref[1] = dot_lanes(jnp.concatenate([g00, g01], axis=1), wdn_ref[:, 128:384])
    back_ref[2] = dot_lanes(jnp.concatenate([g00, g10], axis=1), wdn_ref[:, 384:640])
    back_ref[3] = dot_lanes(glo_ref[...], wdn_ref[:, 640:1152])

    none8 = jnp.zeros((8, 256), F32)
    sums = [none8, none8]
    for j in range(12):
        for i in range(2):
            gi = []
            for p in range(2):
                at = rows_of(4 * j + 2 * i + p, 48, 48)
                back = back_ref[2 * i + p, rows_of(j, 48, 48), :]
                gi.append((upf_ref[at, :].astype(F32) + back) * twice(mf_ref[at, :]))
                gp, normed = pre_grad(
                    gi[p], x_ref[at, :], scf_ref[0:1, :], scf_ref[1:2, :], scf_ref[2:3, :], scf_ref[3:4, :]
                )
                gp_ref[at, :] = gp
                sums[0] = sums[0] + tile_sum(gp * normed)
                sums[1] = sums[1] + tile_sum(gp)
            for n in range(2):
                half = slice(24 * n, 24 * n + 24)
                interleave(stage_ref.at[1], 2 * j + i + 24 * n, gi[0][half], gi[1][half])
        if j % 6 == 5:
            put(1, gif_ref, j // 6)
    up_grad = dot_rows(branch_ref[...], gl_ref[...])
    for j in range(2):
        grad_ref[pl.ds(ROW_UP + j, 128, stride=2), :] = up_grad[:, 128 * j : 128 * j + 128]
    for i, (parts, taps) in enumerate(
        (((g00,), (4,)), ((g00, g01), (5, 3)), ((g00, g10), (7, 1)), ((g00, g01, g10, g11), (8, 6, 2, 0)))
    ):
        down = dot_rows(ph_ref[i], jnp.concatenate(parts, axis=1))
        for n, tap in enumerate(taps):
            grad_ref[pl.ds(ROW_DOWN + tap, 256, stride=9), :] = down[:, 128 * n : 128 * n + 128]
    sum_gain, sum_bias = (jnp.sum(v, axis=0, keepdims=True) for v in sums)
    for p in range(2):
        at = slice(128 * p, 128 * p + 128)
        grad_ref[ROW_VEC + p : ROW_VEC + p + 1, :] = sum_gain[:, at]
        grad_ref[ROW_VEC + 2 + p : ROW_VEC + 3 + p, :] = sum_bias[:, at]
        row_ref[0:1, at], row_ref[1:2, at] = back_means(
            sum_bias[:, at], sum_gain[:, at], gain_f[:, at], C1 // GROUPS, nf
        )

    for r in range(24):
        g = []
        for p in range(2):
            at = rows_of(2 * r + p, 48, 48)
            normed = (x_ref[at, :] - scf_ref[2:3, :]) * scf_ref[3:4, :]
            v = (gp_ref[at, :] * gain_f - row_ref[0:1, :] - normed * row_ref[1:2, :]) * scf_ref[3:4, :]
            g.append(v * twice(mf_ref[at, :]))
        for p in range(2):
            g_ref[p, rows_of(r + 2, 48, 48), :] = g[p].astype(BF)
    go_ref[...] = g_ref[...]
    join_ref[...] = grad_ref[ROW_DOWN : ROW_DOWN + plan.rows, :]
    for n, s in enumerate(plan.early):
        first = plan.first[s]
        blocks_ref[n] = grad_ref[first : first + plan.rows, :].astype(BF)
    for send in sends:
        send.wait()


def layer_call(plan, *args):
    there = pl.BlockSpec(memory_space=pltpu.HBM)
    whole = pl.BlockSpec(memory_space=pltpu.VMEM)
    low = lambda *shape: pltpu.VMEM(shape, BF)
    wide = lambda *shape: pltpu.VMEM(shape, F32)
    return pl.pallas_call(
        functools.partial(layer_kernel, plan),
        out_shape=[
            jax.ShapeDtypeStruct((PIX, 256), F32),
            jax.ShapeDtypeStruct((CPIX, 128), F32),
            jax.ShapeDtypeStruct((PIX, 256), F32),
            jax.ShapeDtypeStruct((CPIX, 128), F32),
            *(jax.ShapeDtypeStruct(shape, dtype) for shape, dtype in plan.handed),
        ],
        in_specs=[pl.BlockSpec(memory_space=pltpu.SMEM)] + [whole] * 7 + [there] * 2,
        out_specs=[there] * 4 + [whole] * 4,
        scratch_shapes=[
            low(2, 28 * 48, 256), low(4, 26 * 48, 256), low(PIX, 256), low(PIX, 256), low(128, 256), low(256, 1152), low(256, 768), low(12 * 256, 256),
            low(CPIX, 128), low(CPIX, 128),
            wide(plan.tall, 128), low(4, CPIX, 256), low(CPIX, 256),
            wide(PIX, 256), wide(CPIX, 128), wide(CPIX, 128), low(CPIX, 128), wide(CPIX, 256),
            wide(PIX, 128), low(PIX, 128), wide(CPIX, 128),
            wide(8, 256), wide(8, 128),
            low(CPIX, 256), low(CPIX, 512), wide(4, CPIX, 256), wide(PIX, 256), wide(8, 256),
            wide(2, 2, PIX, 128), wide(2, CPIX, 128),
            pltpu.SemaphoreType.DMA((2,)),
            pltpu.SemaphoreType.DMA((2, 2, 2, 2)),
            pltpu.SemaphoreType.DMA((2,)),
        ],
        compiler_params=pltpu.CompilerParams(vmem_limit_bytes=38 * 2**20),
        name="layer",
    )(*args)


class Plan:
    def __init__(self, shards, length):
        self.dims = {16: (4, 2, 2), 128: (4, 8, 4)}.get(shards, (shards, 1, 1))
        self.n, self.length = shards, length
        self.first = [s * length // 128 for s in range(shards)]
        self.rows = -(-(length + 127) // 128)
        self.rows = -(-self.rows // 32) * 32
        self.part = self.rows // 2
        self.cut = -(-self.part // 32) * 16
        self.tall = -(-(self.first[-1] + self.rows) // 16) * 16
        self.early = [s for s in range(shards) if self.first[s] >= ROW_DOWN]
        self.handed = (
            ((4, 26 * 48, 256), BF), ((2, 28 * 48, 256), BF), ((self.rows, 128), F32),
            ((len(self.early), self.rows, 128), BF),
        )

    def here(self):
        d0, d1, d2 = self.dims
        me = lax.axis_index("fsdp")
        return me, lax.axis_index("rep"), me // (d1 * d2), me // d2 % d1, me % d2

    def block(self, a, b, c):
        d0, d1, d2 = self.dims
        return (a * d1 + b) * d2 + c


def flip(a, k):
    bit = 1
    while bit <= k:
        if k & bit:
            a = a + bit - 2 * bit * (a // bit % 2)
        bit *= 2
    return a


def to_rows(plan, ref):
    full = plan.length // 128
    left = plan.length - 128 * full
    parts = [ref[pl.ds(0, 128 * full)].reshape(full, 128)]
    if left:
        tail = ref[pl.ds(128 * full, left)].reshape(1, left)
        parts.append(jnp.concatenate([tail, jnp.zeros((1, 128 - left), F32)], axis=1))
    have = full + (left > 0)
    parts.append(jnp.zeros((plan.rows - have, 128), F32))
    return jnp.concatenate(parts, axis=0)


def gather_kernel(
    plan,
    master_ref, inp_hbm, upf_hbm,
    vec_ref, inpo_ref, upfo_ref, wu_ref, wdn_ref, wc6_ref, wf_ref,
    inp_ref, upf_ref, g_ref, w_ref, tmp_ref, in_sem, send_sem, recv_sem, sib_send, sib_recv, far_send,
):
    d0, d1, d2 = plan.dims
    me, core, a, b, c = plan.here()
    part, cut = plan.part, plan.cut
    loads = [
        pltpu.make_async_copy(src, dst, in_sem.at[n])
        for n, (src, dst) in enumerate(((inp_hbm, inp_ref), (upf_hbm, upf_ref)))
    ]
    for load in loads:
        load.start()
    barrier = pltpu.get_barrier_semaphore()
    others = [plan.block((a + k) % d0, b, c) for k in range(1, d0)]
    others += [plan.block(a, (b + k) % d1, c) for k in range(1, d1)]
    others += [plan.block(a, b, (c + k) % d2) for k in range(1, d2)]
    others = [{"fsdp": other, "rep": core} for other in others] + [{"fsdp": me, "rep": 1 - core}]
    for other in others:
        pl.semaphore_signal(barrier, inc=1, device_id=other, device_id_type=pl.DeviceIdType.MESH)
    off = (me * plan.length) % 128
    x = pltpu.roll(to_rows(plan, master_ref), off, 1)
    row = lax.broadcasted_iota(jnp.int32, x.shape, 0)
    lane = lax.broadcasted_iota(jnp.int32, x.shape, 1)
    above = jnp.where(row == 0, 0.0, pltpu.roll(x, 1, 0))
    g_ref[me] = jnp.where(lane < off, above, x).astype(BF)
    pl.semaphore_wait(barrier, len(others))

    def span(half, which):
        start = which * part + (cut if half == 1 else 0)
        return pl.ds(pl.multiple_of(start, 16), (cut, part - cut)[half])

    def copy(block, half, fsdp, rep, send, recv, which):
        at = g_ref.at[block, span(half, which)]
        return pltpu.make_async_remote_copy(
            src_ref=at, dst_ref=at, send_sem=send, recv_sem=recv,
            device_id={"fsdp": fsdp, "rep": rep}, device_id_type=pl.DeviceIdType.MESH,
        )

    def arrive(block, half):
        copy(block, half, me, core, far_send.at[0, 0], recv_sem.at[block, half], core).wait_recv()

    sent = []

    def go(d):
        d.start()
        sent.append(d)

    def along1(block, half):
        for k in range(1, d1):
            go(copy(block, half, plan.block(a, (b + k) % d1, c), core,
                    send_sem.at[block, half, k - 1], recv_sem.at[block, half], core))

    def along2(block, half):
        for k in range(1, d2):
            go(copy(block, half, plan.block(a, b, (c + k) % d2), core,
                    send_sem.at[block, half, d1 + k - 2], recv_sem.at[block, half], core))

    def beside(block, half):
        go(copy(block, half, me, 1 - core, sib_send.at[block, half], sib_recv.at[block, half], core))

    def own_column(k):
        block = plan.block(flip(a, k), b, c)
        if k:
            arrive(block, 0)
        along2(block, 0)
        if k:
            arrive(block, 1)
        along1(block, 1)
        along2(block, 1)
        along1(block, 0)
        if k:
            beside(block, 0)
            beside(block, 1)

    def near(k):
        a2 = flip(a, k)
        ahead = [plan.block(a2, b, (c + i) % d2) for i in range(1, d2)]
        above = [plan.block(a2, (b + i) % d1, c) for i in range(1, d1)]
        for block in ahead:
            arrive(block, 0)
            along1(block, 0)
            beside(block, 0)
        for block in above:
            arrive(block, 1)
            along2(block, 1)
            beside(block, 1)
        for block in ahead:
            arrive(block, 1)
            beside(block, 1)
        for block in above:
            arrive(block, 0)
            beside(block, 0)

    def diagonal(k):
        a2 = flip(a, k)
        for i in range(1, d1):
            for j in range(1, d2):
                block = plan.block(a2, (b + i) % d1, (c + j) % d2)
                for half in (0, 1):
                    arrive(block, half)
                    beside(block, half)

    def parity(src, dst):
        def one(r, _):
            parts = []
            for n in range(2):
                at = rows_of(r + 24 * n, 48, 48)
                v = src[at, :].astype(F32)
                for p in range(2):
                    tmp_ref[p, at, :] = v[:, 128 * p : 128 * p + 128]
            for first in range(2):
                for n in range(2):
                    at = pl.ds((r + 24 * n) * 48 + first, 24, stride=2)
                    parts.append(jnp.concatenate([tmp_ref[p, at, :] for p in range(2)], axis=1))
            dst[rows_of(r, 96, 96), :] = jnp.concatenate(parts, axis=0).astype(BF)
            return 0

        lax.fori_loop(0, 24, one, 0, unroll=2)

    for k in range(1, d0):
        for half in (0, 1):
            go(copy(me, half, plan.block(flip(a, k), b, c), core, far_send.at[k, half], recv_sem.at[me, half], core))
    own_column(0)
    loads[0].wait()
    parity(inp_ref, inpo_ref)
    loads[1].wait()
    parity(upf_ref, upfo_ref)
    for k in range(1, d0):
        own_column(k)
    for k in range(d0):
        near(k)
    for k in range(d0):
        diagonal(k)
    for k in range(1, plan.n):
        block = (me + k) % plan.n
        for half in (0, 1):
            copy(block, half, me, core, far_send.at[0, 0], sib_recv.at[block, half], 1 - core).wait_recv()

    for s in range(plan.n):
        v = g_ref[s].astype(F32)
        at = plan.first[s]
        if s:
            low = w_ref[at : at + 1, :] + v[0:1]
            w_ref[at : at + plan.rows, :] = v
            w_ref[at : at + 1, :] = low
        else:
            w_ref[0 : plan.rows, :] = v
    vec_ref[...] = w_ref[ROW_VEC : ROW_VEC + 8, :]
    for dy in range(3):
        for h in range(2):
            g0, g1, g2 = (w_ref[pl.ds(2 * (3 * dy + dx) + h, 256, stride=18), :] for dx in range(3))
            outer = g0 + g2
            for i, v in enumerate((g0, 0.5 * (outer + g1), 0.5 * (outer - g1), g2)):
                at = 768 * i + 256 * dy
                wf_ref[at : at + 256, 128 * h : 128 * h + 128] = v.astype(BF)
    for h in range(2):
        wu_ref[:, 128 * h : 128 * h + 128] = w_ref[pl.ds(ROW_UP + h, 128, stride=2), :].astype(BF)
    for t in range(9):
        p = (4, 5, 3, 7, 1, 8, 6, 2, 0).index(t)
        wdn_ref[:, 128 * p : 128 * p + 128] = w_ref[pl.ds(ROW_DOWN + t, 256, stride=9), :].astype(BF)
    wc6_ref[0:128, 384:768] = jnp.zeros((128, 384), BF)
    for t in range(9):
        dy, dx = t // 3, t % 3
        at, p = 128 * (dx + 1) // 2 // 128 * 128, dy + 3 * (dx // 2)
        wc6_ref[at : at + 128, 128 * p : 128 * p + 128] = w_ref[pl.ds(ROW_COARSE + t, 128, stride=9), :].astype(BF)
    for d in sent:
        d.wait_send()


def gather_call(plan, master, inp, upf):
    there = pl.BlockSpec(memory_space=pltpu.HBM)
    whole = pl.BlockSpec(memory_space=pltpu.VMEM)
    low = lambda *shape: jax.ShapeDtypeStruct(shape, BF)
    outs = [
        jax.ShapeDtypeStruct((8, 128), F32), low(PIX, 256), low(PIX, 256), low(128, 256), low(256, 1152),
        low(256, 768), low(12 * 256, 256),
    ]
    d0, d1, d2 = plan.dims
    sems = pltpu.SemaphoreType.DMA
    return pl.pallas_call(
        functools.partial(gather_kernel, plan),
        out_shape=outs,
        in_specs=[whole, there, there],
        out_specs=[whole] * 7,
        scratch_shapes=[
            pltpu.VMEM((PIX, 256), BF), pltpu.VMEM((PIX, 256), BF),
            pltpu.VMEM((plan.n, plan.rows, 128), BF), pltpu.VMEM((plan.tall, 128), F32), pltpu.VMEM((2, PIX, 128), F32),
            sems((2,)), sems((plan.n, 2, max(d1 + d2 - 2, 1))), sems((plan.n, 2)), sems((plan.n, 2)),
            sems((plan.n, 2)), sems((d0, 2)),
        ],
        compiler_params=pltpu.CompilerParams(collective_id=0, has_side_effects=True, vmem_limit_bytes=20 * 2**20),
        name="gather_weights",
    )(master, *(pltpu.with_memory_space_constraint(x, pltpu.HBM) for x in (inp, upf)))


def reduce_kernel(
    plan,
    u_ref, g_ref, join_ref, blocks_ref,
    out_ref, tile_ref,
    sums_ref, grad_ref, p_ref, q_ref, ua_ref, ub_ref, va_ref, vb_ref, z_ref, sa_ref, total_ref,
    n1_ref, n2_ref,
    q_send, q_recv, s1_send, s1_recv, s2_send, s2_recv, s3_send, s3_recv, t_send, t_recv,
    n1_send, n1_recv, n2_send, n2_recv,
):
    d0, d1, d2 = plan.dims
    me, core, a, b, c = plan.here()
    part, cut = plan.part, plan.cut
    MESH = pl.DeviceIdType.MESH
    barrier = pltpu.get_barrier_semaphore()
    others = [{"fsdp": plan.block((a + k) % d0, b, c), "rep": core} for k in range(1, d0)]
    plane = []
    for i in range(d1):
        for j in range(d2):
            for o in range(2):
                if i or j or o:
                    plane.append((i, j, o, {"fsdp": plan.block(a, (b + i) % d1, (c + j) % d2), "rep": (core + o) % 2}))
    others += [p[3] for p in plane]
    for other in others:
        pl.semaphore_signal(barrier, inc=1, device_id=other, device_id_type=MESH)
    even, odd = g_ref[0], g_ref[1]
    sums_ref[0] = even + odd
    sums_ref[1] = even - odd
    products = []
    for i, ref in enumerate((g_ref.at[0], sums_ref.at[0], sums_ref.at[1], g_ref.at[1])):
        shifted = [ref[48 * (2 - dy) : 48 * (2 - dy) + 26 * 48, :] for dy in range(3)]
        products.append(dot_rows(u_ref[i], jnp.concatenate(shifted, axis=1)))
    p0, p1, p2, p3 = products
    both, apart = 0.5 * (p1 + p2), 0.5 * (p1 - p2)
    for dx, grad in enumerate((p0 + both, apart, both - p3)):
        for dy in range(3):
            for j in range(2):
                at = 256 * dy + 128 * j
                grad_ref[pl.ds(2 * (3 * dy + dx) + j, 256, stride=18), :] = grad[:, at : at + 128]
    count = len(plan.early)
    grad_ref[ROW_DOWN:, :] = join_ref[...]
    for s in range(plan.n - count):
        first = plan.first[s]
        p_ref[s] = grad_ref[first : first + plan.rows, :].astype(BF)
    p_ref[plan.n - count :] = blocks_ref[...]
    pl.semaphore_wait(barrier, len(others))

    sent = []

    def go(src, dst, send, recv, to):
        d = pltpu.make_async_remote_copy(
            src_ref=src, dst_ref=dst, send_sem=send, recv_sem=recv, device_id=to, device_id_type=MESH
        )
        d.start()
        sent.append(d)

    def got(ref, recv):
        pltpu.make_async_copy(ref, ref, recv).wait()

    mine = pl.multiple_of(core * part, 16)
    theirs = pl.multiple_of((1 - core) * part, 16)
    halves = ((0, cut), (cut, part - cut))
    order = [(k + 1) % d0 for k in range(d0)]
    for k in order:
        for i in list(range(1, d1)) + [0]:
            for j in list(range(1, d2)) + [0]:
                s = plan.block((a + k) % d0, (b + i) % d1, (c + j) % d2)
                go(
                    p_ref.at[s, pl.ds(theirs, part)], q_ref.at[s], q_send.at[s], q_recv.at[s],
                    {"fsdp": me, "rep": 1 - core},
                )

    def pair(s, half):
        start, size = halves[half]
        x = p_ref[s, pl.ds(pl.multiple_of(mine + start, 16), size), :].astype(F32)
        return x + q_ref[s, start : start + size, :].astype(F32)

    def step1(k):
        a2 = (a + k) % d0
        for i in range(1, d1):
            for j in list(range(1, d2)) + [0]:
                s = plan.block(a2, (b + i) % d1, (c + j) % d2)
                got(q_ref.at[s], q_recv.at[s])
                sa_ref[s, 0:cut, :] = pair(s, 0).astype(BF)
                go(sa_ref.at[s, 0:cut], ua_ref.at[a2, (c + j) % d2, i - 1], s1_send.at[s, 0], s1_recv.at[0, a2, (c + j) % d2, i - 1],
                   {"fsdp": plan.block(a, (b + i) % d1, c), "rep": core})
                if j:
                    step1b(s, a2, i, j)
        for j in range(1, d2):
            s = plan.block(a2, b, (c + j) % d2)
            got(q_ref.at[s], q_recv.at[s])
            step1b(s, a2, 0, j)

    def step1b(s, a2, i, j):
        sa_ref[s, cut:part, :] = pair(s, 1).astype(BF)
        go(sa_ref.at[s, cut:part], ub_ref.at[a2, (b + i) % d1, j - 1], s1_send.at[s, 1], s1_recv.at[1, a2, (b + i) % d1, j - 1],
           {"fsdp": plan.block(a, b, (c + j) % d2), "rep": core})

    def from1(half, a2, other):
        ref = ua_ref if half == 0 else ub_ref
        total = None
        for i in range((d1 if half == 0 else d2) - 1):
            got(ref.at[a2, other, i], s1_recv.at[half, a2, other, i])
            v = ref[a2, other, i].astype(F32)
            total = v if total is None else total + v
        return total

    def plus(x, y):
        return x if y is None else x + y

    def step2(k):
        a2 = (a + k) % d0
        for j in range(1, d2):
            c2 = (c + j) % d2
            s = plan.block(a2, b, c2)
            sa_ref[s, 0:cut, :] = plus(pair(s, 0), from1(0, a2, c2)).astype(BF)
            go(sa_ref.at[s, 0:cut], va_ref.at[a2, j - 1], s2_send.at[0, a2, j - 1], s2_recv.at[0, a2, j - 1],
               {"fsdp": plan.block(a, b, c2), "rep": core})
        for i in range(1, d1):
            b2 = (b + i) % d1
            s = plan.block(a2, b2, c)
            sa_ref[s, cut:part, :] = plus(pair(s, 1), from1(1, a2, b2)).astype(BF)
            go(sa_ref.at[s, cut:part], vb_ref.at[a2, i - 1], s2_send.at[1, a2, i - 1], s2_recv.at[1, a2, i - 1],
               {"fsdp": plan.block(a, b2, c), "rep": core})

    def column(k):
        a2 = (a + k) % d0
        s = plan.block(a2, b, c)
        got(q_ref.at[s], q_recv.at[s])
        x = plus(pair(s, 0), from1(0, a2, c))
        for j in range(1, d2):
            got(va_ref.at[a2, j - 1], s2_recv.at[0, a2, j - 1])
            x = x + va_ref[a2, j - 1].astype(F32)
        y = plus(pair(s, 1), from1(1, a2, b))
        for i in range(1, d1):
            got(vb_ref.at[a2, i - 1], s2_recv.at[1, a2, i - 1])
            y = y + vb_ref[a2, i - 1].astype(F32)
        return s, x, y

    def step3(k):
        s, x, y = column(k)
        sa_ref[s, 0:cut, :] = x.astype(BF)
        sa_ref[s, cut:part, :] = y.astype(BF)
        go(sa_ref.at[s], z_ref.at[k - 1], s3_send.at[k - 1], s3_recv.at[k - 1], {"fsdp": plan.block((a + k) % d0, b, c), "rep": core})

    for n in range(d0 + 2):
        if n < d0:
            step1(order[n])
        if 0 <= n - 1 < d0:
            step2(order[n - 1])
        if 0 <= n - 2 < d0 - 1:
            step3(order[n - 2])
    _, x, y = column(0)
    total = jnp.concatenate([x, y], axis=0)
    for k in range(1, d0):
        got(z_ref.at[k - 1], s3_recv.at[k - 1])
        total = total + z_ref[k - 1].astype(F32)
    total_ref[pl.ds(mine, part), :] = total
    go(total_ref.at[pl.ds(mine, part)], total_ref.at[pl.ds(mine, part)], t_send.at[0], t_recv.at[0], {"fsdp": me, "rep": 1 - core})

    off = (me * plan.length) % 128
    row = lax.broadcasted_iota(jnp.int32, (part, 128), 0) + mine
    at = row * 128 + lax.broadcasted_iota(jnp.int32, (part, 128), 1)
    own = jnp.where((at >= off) & (at < off + plan.length), total, 0.0)
    last = me == plan.n - 1
    for i in range(6):
        spot = ROW_VEC - plan.first[-1] + i
        holds = last & (core == spot // part)
        n1_ref[a, i:i + 1, :] = jnp.where(holds, total[spot % part:spot % part + 1], 0.0)
    n1_ref[a, 6:7, :] = jnp.sum(own * own, axis=0, keepdims=True)
    n1_ref[a, 7:8, :] = jnp.zeros((1, 128), F32)
    for k in range(1, d0):
        go(n1_ref.at[a], n1_ref.at[a], n1_send.at[k], n1_recv.at[a], {"fsdp": plan.block((a + k) % d0, b, c), "rep": core})
    for k in range(1, d0):
        got(n1_ref.at[(a + k) % d0], n1_recv.at[(a + k) % d0])
    tile = n1_ref[0]
    for k in range(1, d0):
        tile = tile + n1_ref[k]
    slot = (b * d2 + c) * 2 + core
    n2_ref[slot] = tile
    for n, (i, j, o, to) in enumerate(plane):
        go(n2_ref.at[slot], n2_ref.at[slot], n2_send.at[n], n2_recv.at[slot], to)
    got(total_ref.at[pl.ds(theirs, part)], t_recv.at[0])
    x = pltpu.roll(total_ref[...], (128 - off) % 128, 1)
    below = pltpu.roll(x, plan.rows - 1, 0)
    lane = lax.broadcasted_iota(jnp.int32, x.shape, 1)
    out_ref[...] = jnp.where(lane + off >= 128, below, x)
    for n, (i, j, o, to) in enumerate(plane):
        other = (((b + i) % d1) * d2 + (c + j) % d2) * 2 + (core + o) % 2
        got(n2_ref.at[other], n2_recv.at[other])
    tile = n2_ref[0]
    for n in range(1, 2 * d1 * d2):
        tile = tile + n2_ref[n]
    tile_ref[...] = tile
    for d in sent:
        d.wait_send()


def reduce_call(plan, *handed):
    whole = pl.BlockSpec(memory_space=pltpu.VMEM)
    d0, d1, d2 = plan.dims
    sems = pltpu.SemaphoreType.DMA
    low = lambda *shape: pltpu.VMEM(shape, BF)
    wide = lambda *shape: pltpu.VMEM(shape, F32)
    e1, e2 = max(d1 - 1, 1), max(d2 - 1, 1)
    rest = plan.part - plan.cut
    return pl.pallas_call(
        functools.partial(reduce_kernel, plan),
        out_shape=[jax.ShapeDtypeStruct((plan.rows, 128), F32), jax.ShapeDtypeStruct((8, 128), F32)],
        in_specs=[whole] * 4,
        out_specs=[whole] * 2,
        scratch_shapes=[
            low(2, 28 * 48, 256), wide(ROW_DOWN + plan.rows, 128),
            low(plan.n, plan.rows, 128), low(plan.n, plan.part, 128),
            low(d0, d2, e1, plan.cut, 128), low(d0, d1, e2, rest, 128),
            low(d0, e2, plan.cut, 128), low(d0, e1, rest, 128), low(max(d0 - 1, 1), plan.part, 128),
            low(plan.n, plan.part, 128),
            wide(plan.rows, 128), wide(d0, 8, 128), wide(2 * d1 * d2, 8, 128),
            sems((plan.n,)), sems((plan.n,)), sems((plan.n, 2)),
            sems((2, d0, max(d1, d2), max(e1, e2))), sems((2, d0, max(e1, e2))), sems((2, d0, max(e1, e2))),
            sems((d0,)), sems((d0,)), sems((1,)), sems((1,)),
            sems((d0,)), sems((d0,)), sems((2 * d1 * d2,)), sems((2 * d1 * d2,)),
        ],
        compiler_params=pltpu.CompilerParams(collective_id=1, has_side_effects=True, vmem_limit_bytes=20 * 2**20),
        name="reduce_gradients",
    )(*handed)


def update_kernel(
    plan,
    grad_ref, tile_ref, master_ref, first_ref, second_ref, average_ref,
    norm_ref, new_master_ref, new_first_ref, new_second_ref, new_average_ref, small_ref,
):
    grad_norm = jnp.sqrt(jnp.sum(tile_ref[6:7, :], axis=1, keepdims=True))
    factor = jnp.minimum(1.0, clip_norm / (grad_norm + 1e-06))
    norm_ref[...] = grad_norm
    for i in range(6):
        small_ref[pl.ds(128 * i, 128)] = (tile_ref[i : i + 1, :] * factor).reshape(128)
    full = plan.length // 128
    left = plan.length - 128 * full
    ema_rate = min(0.999, (1.0 + STEP) / (10.0 + STEP))

    def update(row, rows, lanes):
        at = pl.ds(128 * row, 128 * (rows - 1) + lanes)
        shape = (rows, lanes)
        clipped = grad_ref[row : row + rows, 0:lanes] * factor
        new_first = beta_one * first_ref[at].reshape(shape) + (1.0 - beta_one) * clipped
        new_second = beta_two * second_ref[at].reshape(shape) + (1.0 - beta_two) * clipped * clipped
        corrected_first = new_first / (1.0 - beta_one**STEP)
        corrected_second = new_second / (1.0 - beta_two**STEP)
        master = master_ref[at].reshape(shape)
        new_master = master - learn_rate * (
            corrected_first / (jnp.sqrt(corrected_second) + adam_eps) + decay_rate * master
        )
        new_average = ema_rate * average_ref[at].reshape(shape) + (1.0 - ema_rate) * new_master
        size = 128 * (rows - 1) + lanes
        new_master_ref[at] = new_master.reshape(size)
        new_first_ref[at] = new_first.reshape(size)
        new_second_ref[at] = new_second.reshape(size)
        new_average_ref[at] = new_average.reshape(size)

    update(0, full, 128)
    if left:
        update(full, 1, left)


def update_call(plan, *args):
    whole = pl.BlockSpec(memory_space=pltpu.VMEM)
    flat = jax.ShapeDtypeStruct((plan.length,), F32)
    return pl.pallas_call(
        functools.partial(update_kernel, plan),
        out_shape=[jax.ShapeDtypeStruct((1, 1), F32), flat, flat, flat, flat, jax.ShapeDtypeStruct((768,), F32)],
        in_specs=[whole] * 6,
        out_specs=[whole] * 6,
        compiler_params=pltpu.CompilerParams(vmem_limit_bytes=16 * 2**20),
        name="update",
    )(*args)


def per_device(
    input_fine, input_coarse, upstream_fine, upstream_coarse, extents, master, first_moment, second_moment, average
):
    plan = Plan(lax.axis_size("fsdp"), master.shape[0])
    vec, inp, upf, wu, wdn, wc6, wf = gather_call(
        plan, master, input_fine.reshape(PIX, C1), upstream_fine.reshape(PIX, C1)
    )
    out_fine, out_coarse, gi_fine, gi_coarse, *handed = layer_call(
        plan, extents, vec, inp, wu, wdn, wc6, wf, upf,
        input_coarse.reshape(CPIX, C2), upstream_coarse.reshape(CPIX, C2),
    )
    grad, tile = reduce_call(plan, *handed)
    grad_norm, new_master, new_first, new_second, new_average, norm_grads = update_call(
        plan, grad, tile, master, first_moment, second_moment, average
    )
    grad_norm = grad_norm.reshape(())
    return (
        out_fine.reshape(input_fine.shape),
        out_coarse.reshape(input_coarse.shape),
        gi_fine.reshape(input_fine.shape),
        gi_coarse.reshape(input_coarse.shape),
        grad_norm,
        new_master,
        new_first,
        new_second,
        new_average,
        norm_grads,
    )


def solution(mesh):
    images = P(("fsdp", "rep"), None, None, None)
    flat = P("fsdp")
    in_specs = (images,) * 4 + (P(("fsdp", "rep"), None),) + (flat,) * 4
    out_specs = (images,) * 4 + (P(),) + (flat,) * 4 + (P(),)
    return jax.shard_map(per_device, mesh=mesh, in_specs=in_specs, out_specs=out_specs, check_vma=False)
```

```python
import functools

import jax
import jax.numpy as jnp
from jax import lax
from jax.experimental import pallas as pl
from jax.experimental.pallas import tpu as pltpu
from jax.sharding import PartitionSpec as P

F32, BF = jnp.float32, jnp.bfloat16
C1, C2, GROUPS, ITERS, STEP = 256, 128, 8, 12, 10
HEIGHT, HALF = 48, 24
PIX, CPIX = HEIGHT * HEIGHT, HALF * HALF
FLAT_ROWS = 8326
ROW_DOWN, ROW_COARSE, ROW_UP, ROW_VEC = 4608, 6912, 8064, 8320

clip_norm = 1.0
learn_rate = 0.02
beta_one = 0.9
beta_two = 0.999
adam_eps = 1e-08
decay_rate = 0.1


def dot(a, b):
    return jnp.dot(a, b, preferred_element_type=F32)


def dot_rows(a, b):
    return lax.dot_general(a, b, (((0,), (0,)), ((), ())), preferred_element_type=F32)


def dot_lanes(a, b):
    return lax.dot_general(a, b, (((1,), (1,)), ((), ())), preferred_element_type=F32)


def run_sum(x, width):
    lane = lax.broadcasted_iota(jnp.int32, x.shape, 1)
    step = 1
    while step < width:
        up = pltpu.roll(x, 128 - step, 1)
        down = pltpu.roll(x, step, 1)
        x = x + jnp.where((lane & step) == 0, up, down)
        step *= 2
    return x


def shift_down(x):
    count = x.shape[0] // 8
    top = lax.broadcasted_iota(jnp.int32, (8, x.shape[1]), 0) == 0
    turned = [pltpu.roll(x[8 * i : 8 * i + 8], 1, 0) for i in range(count)]
    return jnp.concatenate(
        [jnp.where(top, turned[i - 1] if i else 0.0, turned[i]) for i in range(count)], axis=0
    )


def shift_up(x):
    count = x.shape[0] // 8
    end = lax.broadcasted_iota(jnp.int32, (8, x.shape[1]), 0) == 7
    turned = [pltpu.roll(x[8 * i : 8 * i + 8], 7, 0) for i in range(count)]
    return jnp.concatenate(
        [jnp.where(end, turned[i + 1] if i < count - 1 else 0.0, turned[i]) for i in range(count)], axis=0
    )


def rows_out(x):
    parts = [x[24 * i : 24 * i + 24] for i in range(24)]
    return parts[0::2] + parts[1::2]


def pair_order(rows):
    return jnp.concatenate([rows[i // 2 + 12 * (i % 2)] for i in range(24)], axis=0)


def image_order(x):
    return jnp.concatenate(rows_out(x), axis=0)


def in_rows(x, change):
    return jnp.concatenate([change(x[24 * r : 24 * r + 24]) for r in range(24)], axis=0)


def row_down(x):
    rows = rows_out(x)
    return pair_order([jnp.zeros_like(rows[0])] + rows[:-1])


def row_up(x):
    rows = rows_out(x)
    return pair_order(rows[1:] + [jnp.zeros_like(rows[0])])


def tile_sum(x):
    total = x[0:8]
    for i in range(1, x.shape[0] // 8):
        total = total + x[8 * i : 8 * i + 8]
    return total


def twice(m):
    return jnp.concatenate([m, m], axis=1)


def interleave(ref, r, even, odd):
    for p in range(2):
        at = slice(128 * p, 128 * p + 128)
        ref[p, pl.ds(r * 48, 24, stride=2), :] = even[:, at]
        ref[p, pl.ds(r * 48 + 1, 24, stride=2), :] = odd[:, at]


def rows_of(r, count, unit):
    start = r * unit
    return pl.ds(start if isinstance(r, int) else pl.multiple_of(start, unit if unit % 16 == 0 else 8), count)


STEPS = "E0 E1 E2 E3 C1-7 E4 E5 E6 C7-13 E7 E8 E9 E10 E11 C13-17 L C17-21 Z K C21-24,0-1 S F B"


def layer_kernel(
    plan,
    ext_ref, vec_ref, inp_in, wu_in, wdn_in, wc6_in, wf_in, upf_in, inc_hbm, upc_hbm,
    outf_ref, outc_ref, gif_ref, gic_ref, uo_ref, go_ref, join_ref, blocks_ref,
    g_ref, u_ref, upf_ref, inp_ref, wu_ref, wdn_ref, wc6_ref, wf_ref, inc_in, upc_ref, grad_ref, ph_ref, c_ref, x_ref, xc_ref, inc_ref, branch_ref, lift_ref, mf_ref, mb_ref, mc_ref,
    scf_ref, scc_ref, gl_ref, glo_ref, back_ref, gp_ref, row_ref, stage_ref, small_ref,
    in_sem, out_sem, small_sem,
):
    loads = [
        pltpu.make_async_copy(src, dst, in_sem.at[n])
        for n, (src, dst) in enumerate(
            ((inc_hbm, inc_in), (upc_hbm, upc_ref))
        )
    ]
    for load in loads:
        load.start()
    hh, ww = ext_ref[0, 0], ext_ref[0, 1]
    gain_f = jnp.concatenate([vec_ref[0:1, :], vec_ref[1:2, :]], axis=1)
    bias_f = jnp.concatenate([vec_ref[2:3, :], vec_ref[3:4, :]], axis=1)
    gain_c, bias_c = vec_ref[4:5, :], vec_ref[5:6, :]
    pos = lax.broadcasted_iota(jnp.int32, (24, 128), 0)
    even = jnp.where(2 * pos < ww, 1.0, 0.0).astype(F32)
    odd = jnp.where(2 * pos + 1 < ww, 1.0, 0.0).astype(F32)

    def setup(r, _):
        at = rows_of(r, 96, 96)
        low, high = r < hh, r + 24 < hh
        m = [jnp.where(here, v, 0.0) for v in (even, odd) for here in (low, high)]
        m = jnp.concatenate(m, axis=0)
        mf_ref[at, :] = m
        mb_ref[at, :] = m.astype(BF)
        x_ref[at, :] = jnp.zeros((96, 256), F32)
        return 0

    lax.fori_loop(0, 24, setup, 0)

    def setup_coarse(r, _):
        m = [jnp.where(2 * r < hh, even, 0.0), jnp.where(2 * r + 24 < hh, even, 0.0)]
        mc_ref[rows_of(r, 48, 48), :] = jnp.concatenate(m, axis=0)
        return 0

    lax.fori_loop(0, 12, setup_coarse, 0)
    nf = (hh * ww).astype(F32) * (C1 // GROUPS)
    nc = (((hh + 1) // 2) * ((ww + 1) // 2)).astype(F32) * (C2 // GROUPS)
    g_ref[:, 0:96, :] = jnp.zeros((2, 96, 256), BF)
    g_ref[:, 26 * 48 : 28 * 48, :] = jnp.zeros((2, 96, 256), BF)
    grad_ref[FLAT_ROWS:, :] = jnp.zeros((plan.tall - FLAT_ROWS, 128), F32)
    xc_ref[...] = jnp.zeros((576, 128), F32)
    scf_ref[...] = jnp.zeros((8, 256), F32)
    scc_ref[...] = jnp.zeros((8, 128), F32)
    scf_ref[1:2, :] = 0.5 * bias_f
    scc_ref[1:2, :] = 0.5 * bias_c
    for src, dst in (
        (inp_in, inp_ref), (wu_in, wu_ref), (wdn_in, wdn_ref), (wc6_in, wc6_ref), (wf_in, wf_ref)
    ):
        dst[...] = src[...]
    loads[0].wait()
    v = inc_in[...].astype(F32)
    inc_ref[...] = pair_order([v[24 * r : 24 * r + 24] for r in range(24)])

    def coarse_branch():
        h = xc_ref[...] * scc_ref[0:1, :] + scc_ref[1:2, :]
        y = h * jnp.tanh(h) + h
        branch = ((y + inc_ref[...]) * mc_ref[...]).astype(BF)
        branch_ref[...] = branch
        lift_ref[...] = dot(branch, wu_ref[...])

    def unit(r, final):
        scale, shift = scf_ref[0:1, :], scf_ref[1:2, :]
        half = rows_of(r // 2, 48, 48)
        lift = lift_ref[half, :]
        lift_low = lift.astype(BF)
        z = []
        for p in range(2):
            at = rows_of(2 * r + p, 48, 48)
            h = x_ref[at, :] * scale + shift
            if final:
                y = h * jnp.tanh(h) + h
            else:
                h = h.astype(BF)
                y = h * jnp.tanh(h) + h
            if final:
                m = twice(mf_ref[at, :])
                low = ((y + inp_ref[at, :].astype(F32)) * m).astype(BF)
                z.append((low.astype(F32) + lift) * m)
            else:
                m = twice(mb_ref[at, :])
                low = (y.astype(BF) + inp_ref[at, :]) * m
                z.append((low + lift_low) * m)
            ph_ref[2 * (r % 2) + p, half, :] = low
        even, odd = z
        if final:
            for i in range(2):
                at = slice(24 * i, 24 * i + 24)
                interleave(stage_ref.at[0], r + 24 * i, even[at], odd[at])
            return
        wide = odd.astype(F32)
        left = jnp.concatenate([shift_down(wide[0:24]), shift_down(wide[24:48])], axis=0).astype(BF)
        wide = even.astype(F32)
        right = jnp.concatenate([shift_up(wide[0:24]), shift_up(wide[24:48])], axis=0).astype(BF)
        for i, u in enumerate((left - odd, even + odd, odd - even, even - right)):
            u_ref[i, rows_of(r + 1, 48, 48), :] = u
            if r == 0:
                w = u.astype(F32)
                u_ref[i, 25 * 48 : 26 * 48, :] = jnp.concatenate([w[24:48], jnp.zeros_like(w[0:24])], axis=0).astype(BF)
            if r == 23:
                w = u.astype(F32)
                u_ref[i, 0:48, :] = jnp.concatenate([jnp.zeros_like(w[0:24]), w[0:24]], axis=0).astype(BF)

    def lowered_parts(first=0, last=CPIX):
        ee, eo, oe, oo = (ph_ref[i, first:last, :] for i in range(4))
        p = dot(eo, wdn_ref[:, 128:384]) + dot(oo, wdn_ref[:, 640:896])
        q = dot(oe, wdn_ref[:, 384:640])
        t = dot(oo, wdn_ref[:, 896:1152])
        return p, q, t, dot(ee, wdn_ref[:, 0:128])

    def lowered(parts):
        p, q, t, e = parts
        here = p[:, :128] + q[:, :128] + e
        return here + row_down(q[:, 128:] + t[:, :128]) + in_rows(p[:, 128:] + row_down(t[:, 128:]), shift_down)

    def coarse_state(parts):
        zc = (branch_ref[...].astype(F32) + lowered(parts)) * mc_ref[...]
        c_ref[:, 0:128] = in_rows(zc, shift_down).astype(BF)
        c_ref[:, 128:256] = zc.astype(BF)

    def coarse_sums(p):
        t = [p[:, 128 * i : 128 * i + 128] for i in range(6)]
        xc = row_down(t[0]) + t[1] + row_up(t[2]) + in_rows(row_down(t[3]) + t[4] + row_up(t[5]), shift_up)
        xc_ref[...] = xc
        xm = xc * mc_ref[...]
        return tile_sum(xm), tile_sum(xm * xm)

    def conv_units(units):
        products = []
        for i in range(4):
            total = None
            for dy in range(3):
                rows = [u_ref[i, 48 * (first + dy) : 48 * (last + dy), :] for first, last in units]
                rows = rows[0] if len(rows) == 1 else jnp.concatenate(rows, axis=0)
                at = 768 * i + 256 * dy
                p = dot(rows, wf_ref[at : at + 256, :])
                total = p if total is None else total + p
            products.append(total)
        m0, m1, m2, m3 = products
        even, odd = m0 + m1 + m2, m1 - m2 - m3
        s = q = None
        for n, r in enumerate(r for first, last in units for r in range(first, last)):
            for p, y in enumerate((even, odd)):
                y = y[48 * n : 48 * n + 48]
                at = slice(96 * r + 48 * p, 96 * r + 48 * p + 48)
                x_ref[at, :] = y
                ym = y * twice(mf_ref[at, :])
                ds, dq = tile_sum(ym), tile_sum(ym * ym)
                s, q = (ds, dq) if s is None else (s + ds, q + dq)
        return s, q

    def finish(s, q, width, n, gain, bias, to_ref):
        s, q = jnp.sum(s, axis=0, keepdims=True), jnp.sum(q, axis=0, keepdims=True)
        for p in range(s.shape[1] // 128):
            at = slice(128 * p, 128 * p + 128)
            mean = run_sum(s[:, at], width) / n
            var = jnp.maximum(run_sum(q[:, at], width) / n - mean * mean, 0.0)
            inv = lax.rsqrt(var + 1e-5)
            to_ref[0:1, at] = 0.5 * inv * gain[:, at]
            to_ref[1:2, at] = 0.5 * (bias[:, at] - mean * inv * gain[:, at])
            to_ref[2:3, at] = mean
            to_ref[3:4, at] = inv

    def iterate(t, _):
        s = q = parts = conv_c = sums_c = None
        for step in STEPS.split():
            if step[0] == "E":
                unit(2 * int(step[1:]), False)
                unit(2 * int(step[1:]) + 1, False)
            elif step[0] == "C":
                ds, dq = conv_units([tuple(map(int, piece.split("-"))) for piece in step[1:].split(",")])
                s, q = (ds, dq) if s is None else (s + ds, q + dq)
            elif step == "L":
                parts = lowered_parts()
            elif step == "L0":
                parts = lowered_parts(0, 288)
            elif step == "L1":
                parts = [jnp.concatenate(both, axis=0) for both in zip(parts, lowered_parts(288, 576))]
            elif step == "Z":
                coarse_state(parts)
            elif step == "K":
                conv_c = dot(c_ref[...], wc6_ref[...])
            elif step == "S":
                sums_c = coarse_sums(conv_c)
            elif step == "F":
                finish(*sums_c, C2 // GROUPS, nc, gain_c, bias_c, scc_ref)
            elif step == "B":
                coarse_branch()
        finish(s, q, C1 // GROUPS, nf, gain_f, bias_f, scf_ref)
        return 0

    coarse_branch()
    lax.fori_loop(0, ITERS, iterate, 0)

    sends = []

    def put(i, ref, half):
        for n in range(2):
            for p in range(2):
                at = pl.ds(48 * (12 * half + 24 * n), 576)
                send = pltpu.make_async_copy(
                    stage_ref.at[i, p, at], ref.at[at, 128 * p : 128 * p + 128], out_sem.at[i, half, n, p]
                )
                send.start()
                sends.append(send)

    def put_small(i, ref):
        send = pltpu.make_async_copy(small_ref.at[i], ref, small_sem.at[i])
        send.start()
        sends.append(send)

    for r in range(24):
        unit(r, True)
    upf_ref[...] = upf_in[...]
    put(0, outf_ref, 0)
    put(0, outf_ref, 1)
    small_ref[0] = image_order((branch_ref[...].astype(F32) + lowered(lowered_parts())) * mc_ref[...])
    put_small(0, outc_ref)
    loads[1].wait()

    v = upc_ref[...].astype(F32)
    seed_c = pair_order([v[24 * r : 24 * r + 24] for r in range(24)]) * mc_ref[...]
    right = in_rows(seed_c, shift_up)
    glo_ref[:, 0:128] = seed_c.astype(BF)
    glo_ref[:, 128:256] = right.astype(BF)
    glo_ref[:, 256:384] = row_up(seed_c).astype(BF)
    glo_ref[:, 384:512] = row_up(right).astype(BF)

    for j in range(12):
        total = None
        for i in range(4):
            at = rows_of(4 * j + i, 48, 48)
            seed = upf_ref[at, :].astype(F32) * twice(mf_ref[at, :])
            total = seed if total is None else total + seed
        gl_ref[rows_of(j, 48, 48), :] = total.astype(BF)
    g00, g01, g10, g11 = (glo_ref[:, 128 * i : 128 * i + 128] for i in range(4))

    back_c = (seed_c + dot_lanes(gl_ref[...], wu_ref[...])) * mc_ref[...]
    small_ref[1] = image_order(back_c)
    put_small(1, gic_ref)

    def pre_grad(gi, x, scale, shift, mean, inv):
        h = x * scale + shift
        t = jnp.tanh(h)
        sig = 0.5 * t + 0.5
        normed = (x - mean) * inv
        return gi * sig * (1.0 + 2.0 * h * (1.0 - sig)), normed

    def back_means(sum_bias, sum_gain, gain, width, n):
        return run_sum(sum_bias * gain, width) / n, run_sum(sum_gain * gain, width) / n

    gp_c, normed_c = pre_grad(
        back_c, xc_ref[...], scc_ref[0:1, :], scc_ref[1:2, :], scc_ref[2:3, :], scc_ref[3:4, :]
    )
    sum_gain = jnp.sum(gp_c * normed_c, axis=0, keepdims=True)
    sum_bias = jnp.sum(gp_c, axis=0, keepdims=True)
    grad_ref[ROW_VEC + 4 : ROW_VEC + 5, :] = sum_gain
    grad_ref[ROW_VEC + 5 : ROW_VEC + 6, :] = sum_bias
    mean_h, mean_hn = back_means(sum_bias, sum_gain, gain_c, C2 // GROUPS, nc)
    gconv = (gp_c * gain_c - mean_h - normed_c * mean_hn) * scc_ref[3:4, :] * mc_ref[...]
    around = jnp.concatenate([row_up(gconv), gconv, row_down(gconv)], axis=1)
    pair = dot_rows(c_ref[...], around.astype(BF))
    single = dot_rows(c_ref[:, 128:256], in_rows(around, shift_down).astype(BF))
    for dy in range(3):
        at = slice(128 * dy, 128 * dy + 128)
        grad_ref[pl.ds(ROW_COARSE + 3 * dy, 128, stride=9), :] = pair[0:128, at]
        grad_ref[pl.ds(ROW_COARSE + 3 * dy + 1, 128, stride=9), :] = pair[128:256, at]
        grad_ref[pl.ds(ROW_COARSE + 3 * dy + 2, 128, stride=9), :] = single[:, at]

    uo_ref[...] = u_ref[...]
    back_ref[0] = dot_lanes(g00, wdn_ref[:, 0:128])
    back_ref[1] = dot_lanes(jnp.concatenate([g00, g01], axis=1), wdn_ref[:, 128:384])
    back_ref[2] = dot_lanes(jnp.concatenate([g00, g10], axis=1), wdn_ref[:, 384:640])
    back_ref[3] = dot_lanes(glo_ref[...], wdn_ref[:, 640:1152])

    none8 = jnp.zeros((8, 256), F32)
    sums = [none8, none8]
    for j in range(12):
        for i in range(2):
            gi = []
            for p in range(2):
                at = rows_of(4 * j + 2 * i + p, 48, 48)
                back = back_ref[2 * i + p, rows_of(j, 48, 48), :]
                gi.append((upf_ref[at, :].astype(F32) + back) * twice(mf_ref[at, :]))
                gp, normed = pre_grad(
                    gi[p], x_ref[at, :], scf_ref[0:1, :], scf_ref[1:2, :], scf_ref[2:3, :], scf_ref[3:4, :]
                )
                gp_ref[at, :] = gp
                sums[0] = sums[0] + tile_sum(gp * normed)
                sums[1] = sums[1] + tile_sum(gp)
            for n in range(2):
                half = slice(24 * n, 24 * n + 24)
                interleave(stage_ref.at[1], 2 * j + i + 24 * n, gi[0][half], gi[1][half])
        if j % 6 == 5:
            put(1, gif_ref, j // 6)
    up_grad = dot_rows(branch_ref[...], gl_ref[...])
    for j in range(2):
        grad_ref[pl.ds(ROW_UP + j, 128, stride=2), :] = up_grad[:, 128 * j : 128 * j + 128]
    for i, (parts, taps) in enumerate(
        (((g00,), (4,)), ((g00, g01), (5, 3)), ((g00, g10), (7, 1)), ((g00, g01, g10, g11), (8, 6, 2, 0)))
    ):
        down = dot_rows(ph_ref[i], jnp.concatenate(parts, axis=1))
        for n, tap in enumerate(taps):
            grad_ref[pl.ds(ROW_DOWN + tap, 256, stride=9), :] = down[:, 128 * n : 128 * n + 128]
    sum_gain, sum_bias = (jnp.sum(v, axis=0, keepdims=True) for v in sums)
    for p in range(2):
        at = slice(128 * p, 128 * p + 128)
        grad_ref[ROW_VEC + p : ROW_VEC + p + 1, :] = sum_gain[:, at]
        grad_ref[ROW_VEC + 2 + p : ROW_VEC + 3 + p, :] = sum_bias[:, at]
        row_ref[0:1, at], row_ref[1:2, at] = back_means(
            sum_bias[:, at], sum_gain[:, at], gain_f[:, at], C1 // GROUPS, nf
        )

    for r in range(24):
        g = []
        for p in range(2):
            at = rows_of(2 * r + p, 48, 48)
            normed = (x_ref[at, :] - scf_ref[2:3, :]) * scf_ref[3:4, :]
            v = (gp_ref[at, :] * gain_f - row_ref[0:1, :] - normed * row_ref[1:2, :]) * scf_ref[3:4, :]
            g.append(v * twice(mf_ref[at, :]))
        for p in range(2):
            g_ref[p, rows_of(r + 2, 48, 48), :] = g[p].astype(BF)
    go_ref[...] = g_ref[...]
    join_ref[...] = grad_ref[ROW_DOWN : ROW_DOWN + plan.rows, :]
    for n, s in enumerate(plan.early):
        first = plan.first[s]
        blocks_ref[n] = grad_ref[first : first + plan.rows, :].astype(BF)
    for send in sends:
        send.wait()


def layer_call(plan, *args):
    there = pl.BlockSpec(memory_space=pltpu.HBM)
    whole = pl.BlockSpec(memory_space=pltpu.VMEM)
    low = lambda *shape: pltpu.VMEM(shape, BF)
    wide = lambda *shape: pltpu.VMEM(shape, F32)
    return pl.pallas_call(
        functools.partial(layer_kernel, plan),
        out_shape=[
            jax.ShapeDtypeStruct((PIX, 256), F32),
            jax.ShapeDtypeStruct((CPIX, 128), F32),
            jax.ShapeDtypeStruct((PIX, 256), F32),
            jax.ShapeDtypeStruct((CPIX, 128), F32),
            *(jax.ShapeDtypeStruct(shape, dtype) for shape, dtype in plan.handed),
        ],
        in_specs=[pl.BlockSpec(memory_space=pltpu.SMEM)] + [whole] * 7 + [there] * 2,
        out_specs=[there] * 4 + [whole] * 4,
        scratch_shapes=[
            low(2, 28 * 48, 256), low(4, 26 * 48, 256), low(PIX, 256), low(PIX, 256), low(128, 256), low(256, 1152), low(256, 768), low(12 * 256, 256),
            low(CPIX, 128), low(CPIX, 128),
            wide(plan.tall, 128), low(4, CPIX, 256), low(CPIX, 256),
            wide(PIX, 256), wide(CPIX, 128), wide(CPIX, 128), low(CPIX, 128), wide(CPIX, 256),
            wide(PIX, 128), low(PIX, 128), wide(CPIX, 128),
            wide(8, 256), wide(8, 128),
            low(CPIX, 256), low(CPIX, 512), wide(4, CPIX, 256), wide(PIX, 256), wide(8, 256),
            wide(2, 2, PIX + 8, 128), wide(2, CPIX, 128),
            pltpu.SemaphoreType.DMA((2,)),
            pltpu.SemaphoreType.DMA((2, 2, 2, 2)),
            pltpu.SemaphoreType.DMA((2,)),
        ],
        compiler_params=pltpu.CompilerParams(vmem_limit_bytes=38 * 2**20),
        name="layer",
    )(*args)


class Plan:
    def __init__(self, shards, length):
        self.dims = {16: (4, 2, 2), 128: (4, 8, 4)}.get(shards, (shards, 1, 1))
        self.n, self.length = shards, length
        self.tiled = length // 1024 * 1024
        self.first = [s * length // 128 for s in range(shards)]
        self.rows = -(-(length + 127) // 128)
        self.rows = -(-self.rows // 32) * 32
        self.part = self.rows // 2
        self.cut = -(-self.part // 32) * 16
        self.tall = -(-(self.first[-1] + self.rows) // 16) * 16
        self.early = [s for s in range(shards) if self.first[s] >= ROW_DOWN]
        self.handed = (
            ((4, 26 * 48, 256), BF), ((2, 28 * 48, 256), BF), ((self.rows, 128), F32),
            ((len(self.early), self.rows, 128), BF),
        )

    def here(self):
        d0, d1, d2 = self.dims
        me = lax.axis_index("fsdp")
        return me, lax.axis_index("rep"), me // (d1 * d2), me // d2 % d1, me % d2

    def block(self, a, b, c):
        d0, d1, d2 = self.dims
        return (a * d1 + b) * d2 + c


def flip(a, k):
    bit = 1
    while bit <= k:
        if k & bit:
            a = a + bit - 2 * bit * (a // bit % 2)
        bit *= 2
    return a


def to_rows(plan, ref, tail_ref):
    full = plan.tiled // 128
    left = plan.length - plan.tiled
    parts = [ref[...].reshape(full, 128)]
    whole = left // 128
    if whole:
        parts.append(tail_ref[pl.ds(0, 128 * whole)].reshape(whole, 128))
    left = left - 128 * whole
    if left:
        tail = tail_ref[pl.ds(128 * whole, left)].reshape(1, left)
        parts.append(jnp.concatenate([tail, jnp.zeros((1, 128 - left), F32)], axis=1))
    have = full + whole + (left > 0)
    parts.append(jnp.zeros((plan.rows - have, 128), F32))
    return jnp.concatenate(parts, axis=0)


def gather_kernel(
    plan,
    master_hbm, tail_ref, inp_hbm, upf_hbm,
    vec_ref, inpo_ref, upfo_ref, wu_ref, wdn_ref, wc6_ref, wf_ref,
    master_ref, inp_ref, upf_ref, g_ref, w_ref, tmp_ref, in_sem, send_sem, recv_sem, sib_send, sib_recv, far_send,
):
    d0, d1, d2 = plan.dims
    me, core, a, b, c = plan.here()
    part, cut = plan.part, plan.cut
    loads = [
        pltpu.make_async_copy(src, dst, in_sem.at[n])
        for n, (src, dst) in enumerate(
            ((master_hbm.at[pl.ds(0, plan.tiled)], master_ref), (inp_hbm, inp_ref), (upf_hbm, upf_ref))
        )
    ]
    for load in loads:
        load.start()
    barrier = pltpu.get_barrier_semaphore()
    others = [plan.block((a + k) % d0, b, c) for k in range(1, d0)]
    others += [plan.block(a, (b + k) % d1, c) for k in range(1, d1)]
    others += [plan.block(a, b, (c + k) % d2) for k in range(1, d2)]
    others = [{"fsdp": other, "rep": core} for other in others] + [{"fsdp": me, "rep": 1 - core}]
    for other in others:
        pl.semaphore_signal(barrier, inc=1, device_id=other, device_id_type=pl.DeviceIdType.MESH)
    off = (me * plan.length) % 128
    loads[0].wait()
    x = pltpu.roll(to_rows(plan, master_ref, tail_ref), off, 1)
    row = lax.broadcasted_iota(jnp.int32, x.shape, 0)
    lane = lax.broadcasted_iota(jnp.int32, x.shape, 1)
    above = jnp.where(row == 0, 0.0, pltpu.roll(x, 1, 0))
    g_ref[me] = jnp.where(lane < off, above, x).astype(BF)
    pl.semaphore_wait(barrier, len(others))

    def span(half, which):
        start = which * part + (cut if half == 1 else 0)
        return pl.ds(pl.multiple_of(start, 16), (cut, part - cut)[half])

    def copy(block, half, fsdp, rep, send, recv, which):
        at = g_ref.at[block, span(half, which)]
        return pltpu.make_async_remote_copy(
            src_ref=at, dst_ref=at, send_sem=send, recv_sem=recv,
            device_id={"fsdp": fsdp, "rep": rep}, device_id_type=pl.DeviceIdType.MESH,
        )

    def arrive(block, half):
        copy(block, half, me, core, far_send.at[0, 0], recv_sem.at[block, half], core).wait_recv()

    sent = []

    def go(d):
        d.start()
        sent.append(d)

    def along1(block, half):
        for k in range(1, d1):
            go(copy(block, half, plan.block(a, (b + k) % d1, c), core,
                    send_sem.at[block, half, k - 1], recv_sem.at[block, half], core))

    def along2(block, half):
        for k in range(1, d2):
            go(copy(block, half, plan.block(a, b, (c + k) % d2), core,
                    send_sem.at[block, half, d1 + k - 2], recv_sem.at[block, half], core))

    def beside(block, half):
        go(copy(block, half, me, 1 - core, sib_send.at[block, half], sib_recv.at[block, half], core))

    def own_column(k):
        block = plan.block(flip(a, k), b, c)
        if k:
            arrive(block, 0)
        along2(block, 0)
        if k:
            arrive(block, 1)
        along1(block, 1)
        along2(block, 1)
        along1(block, 0)
        if k:
            beside(block, 0)
            beside(block, 1)

    def near(k):
        a2 = flip(a, k)
        ahead = [plan.block(a2, b, (c + i) % d2) for i in range(1, d2)]
        above = [plan.block(a2, (b + i) % d1, c) for i in range(1, d1)]
        for block in ahead:
            arrive(block, 0)
            along1(block, 0)
            beside(block, 0)
        for block in above:
            arrive(block, 1)
            along2(block, 1)
            beside(block, 1)
        for block in ahead:
            arrive(block, 1)
            beside(block, 1)
        for block in above:
            arrive(block, 0)
            beside(block, 0)

    def diagonal(k):
        a2 = flip(a, k)
        for i in range(1, d1):
            for j in range(1, d2):
                block = plan.block(a2, (b + i) % d1, (c + j) % d2)
                for half in (0, 1):
                    arrive(block, half)
                    beside(block, half)

    def parity(src, dst):
        def one(r, _):
            parts = []
            for n in range(2):
                at = rows_of(r + 24 * n, 48, 48)
                v = src[at, :].astype(F32)
                for p in range(2):
                    tmp_ref[p, at, :] = v[:, 128 * p : 128 * p + 128]
            for first in range(2):
                for n in range(2):
                    at = pl.ds((r + 24 * n) * 48 + first, 24, stride=2)
                    parts.append(jnp.concatenate([tmp_ref[p, at, :] for p in range(2)], axis=1))
            dst[rows_of(r, 96, 96), :] = jnp.concatenate(parts, axis=0).astype(BF)
            return 0

        lax.fori_loop(0, 24, one, 0, unroll=2)

    for k in range(1, d0):
        for half in (0, 1):
            go(copy(me, half, plan.block(flip(a, k), b, c), core, far_send.at[k, half], recv_sem.at[me, half], core))
    own_column(0)
    loads[1].wait()
    parity(inp_ref, inpo_ref)
    loads[2].wait()
    parity(upf_ref, upfo_ref)
    for k in range(1, d0):
        own_column(k)
    for k in range(d0):
        near(k)
    for k in range(d0):
        diagonal(k)
    for k in range(1, plan.n):
        block = (me + k) % plan.n
        for half in (0, 1):
            copy(block, half, me, core, far_send.at[0, 0], sib_recv.at[block, half], 1 - core).wait_recv()

    for s in range(plan.n):
        v = g_ref[s].astype(F32)
        at = plan.first[s]
        if s:
            low = w_ref[at : at + 1, :] + v[0:1]
            w_ref[at : at + plan.rows, :] = v
            w_ref[at : at + 1, :] = low
        else:
            w_ref[0 : plan.rows, :] = v
    vec_ref[...] = w_ref[ROW_VEC : ROW_VEC + 8, :]
    for dy in range(3):
        for h in range(2):
            g0, g1, g2 = (w_ref[pl.ds(2 * (3 * dy + dx) + h, 256, stride=18), :] for dx in range(3))
            outer = g0 + g2
            for i, v in enumerate((g0, 0.5 * (outer + g1), 0.5 * (outer - g1), g2)):
                at = 768 * i + 256 * dy
                wf_ref[at : at + 256, 128 * h : 128 * h + 128] = v.astype(BF)
    for h in range(2):
        wu_ref[:, 128 * h : 128 * h + 128] = w_ref[pl.ds(ROW_UP + h, 128, stride=2), :].astype(BF)
    for t in range(9):
        p = (4, 5, 3, 7, 1, 8, 6, 2, 0).index(t)
        wdn_ref[:, 128 * p : 128 * p + 128] = w_ref[pl.ds(ROW_DOWN + t, 256, stride=9), :].astype(BF)
    wc6_ref[0:128, 384:768] = jnp.zeros((128, 384), BF)
    for t in range(9):
        dy, dx = t // 3, t % 3
        at, p = 128 * (dx + 1) // 2 // 128 * 128, dy + 3 * (dx // 2)
        wc6_ref[at : at + 128, 128 * p : 128 * p + 128] = w_ref[pl.ds(ROW_COARSE + t, 128, stride=9), :].astype(BF)
    for d in sent:
        d.wait_send()


def gather_call(plan, master, inp, upf):
    there = pl.BlockSpec(memory_space=pltpu.HBM)
    whole = pl.BlockSpec(memory_space=pltpu.VMEM)
    low = lambda *shape: jax.ShapeDtypeStruct(shape, BF)
    outs = [
        jax.ShapeDtypeStruct((8, 128), F32), low(PIX, 256), low(PIX, 256), low(128, 256), low(256, 1152),
        low(256, 768), low(12 * 256, 256),
    ]
    d0, d1, d2 = plan.dims
    sems = pltpu.SemaphoreType.DMA
    return pl.pallas_call(
        functools.partial(gather_kernel, plan),
        out_shape=outs,
        in_specs=[there, whole, there, there],
        out_specs=[whole] * 7,
        scratch_shapes=[
            pltpu.VMEM((plan.tiled,), F32), pltpu.VMEM((PIX, 256), BF), pltpu.VMEM((PIX, 256), BF),
            pltpu.VMEM((plan.n, plan.rows, 128), BF), pltpu.VMEM((plan.tall, 128), F32), pltpu.VMEM((2, PIX + 8, 128), F32),
            sems((3,)), sems((plan.n, 2, max(d1 + d2 - 2, 1))), sems((plan.n, 2)), sems((plan.n, 2)),
            sems((plan.n, 2)), sems((d0, 2)),
        ],
        compiler_params=pltpu.CompilerParams(collective_id=0, has_side_effects=True, vmem_limit_bytes=20 * 2**20),
        name="gather_weights",
    )(
        pltpu.with_memory_space_constraint(master, pltpu.HBM), master[plan.tiled :],
        *(pltpu.with_memory_space_constraint(x, pltpu.HBM) for x in (inp, upf)),
    )


def reduce_kernel(
    plan,
    u_ref, g_ref, join_ref, blocks_ref,
    out_ref, tile_ref,
    sums_ref, grad_ref, p_ref, q_ref, ua_ref, ub_ref, va_ref, vb_ref, z_ref, sa_ref, total_ref,
    n1_ref, n2_ref,
    q_send, q_recv, s1_send, s1_recv, s2_send, s2_recv, s3_send, s3_recv, t_send, t_recv,
    n1_send, n1_recv, n2_send, n2_recv,
):
    d0, d1, d2 = plan.dims
    me, core, a, b, c = plan.here()
    part, cut = plan.part, plan.cut
    MESH = pl.DeviceIdType.MESH
    barrier = pltpu.get_barrier_semaphore()
    others = [{"fsdp": plan.block((a + k) % d0, b, c), "rep": core} for k in range(1, d0)]
    plane = []
    for i in range(d1):
        for j in range(d2):
            for o in range(2):
                if i or j or o:
                    plane.append((i, j, o, {"fsdp": plan.block(a, (b + i) % d1, (c + j) % d2), "rep": (core + o) % 2}))
    others += [p[3] for p in plane]
    for other in others:
        pl.semaphore_signal(barrier, inc=1, device_id=other, device_id_type=MESH)
    even, odd = g_ref[0], g_ref[1]
    sums_ref[0] = even + odd
    sums_ref[1] = even - odd
    products = []
    for i, ref in enumerate((g_ref.at[0], sums_ref.at[0], sums_ref.at[1], g_ref.at[1])):
        shifted = [ref[48 * (2 - dy) : 48 * (2 - dy) + 26 * 48, :] for dy in range(3)]
        products.append(dot_rows(u_ref[i], jnp.concatenate(shifted, axis=1)))
    p0, p1, p2, p3 = products
    both, apart = 0.5 * (p1 + p2), 0.5 * (p1 - p2)
    for dx, grad in enumerate((p0 + both, apart, both - p3)):
        for dy in range(3):
            for j in range(2):
                at = 256 * dy + 128 * j
                grad_ref[pl.ds(2 * (3 * dy + dx) + j, 256, stride=18), :] = grad[:, at : at + 128]
    count = len(plan.early)
    grad_ref[ROW_DOWN:, :] = join_ref[...]
    for s in range(plan.n - count):
        first = plan.first[s]
        p_ref[s] = grad_ref[first : first + plan.rows, :].astype(BF)
    p_ref[plan.n - count :] = blocks_ref[...]
    pl.semaphore_wait(barrier, len(others))

    sent = []

    def go(src, dst, send, recv, to):
        d = pltpu.make_async_remote_copy(
            src_ref=src, dst_ref=dst, send_sem=send, recv_sem=recv, device_id=to, device_id_type=MESH
        )
        d.start()
        sent.append(d)

    def got(ref, recv):
        pltpu.make_async_copy(ref, ref, recv).wait()

    mine = pl.multiple_of(core * part, 16)
    theirs = pl.multiple_of((1 - core) * part, 16)
    halves = ((0, cut), (cut, part - cut))
    order = [(k + 1) % d0 for k in range(d0)]
    for k in order:
        for i in list(range(1, d1)) + [0]:
            for j in list(range(1, d2)) + [0]:
                s = plan.block((a + k) % d0, (b + i) % d1, (c + j) % d2)
                go(
                    p_ref.at[s, pl.ds(theirs, part)], q_ref.at[s], q_send.at[s], q_recv.at[s],
                    {"fsdp": me, "rep": 1 - core},
                )

    def pair(s, half):
        start, size = halves[half]
        x = p_ref[s, pl.ds(pl.multiple_of(mine + start, 16), size), :].astype(F32)
        return x + q_ref[s, start : start + size, :].astype(F32)

    def step1(k):
        a2 = (a + k) % d0
        for i in range(1, d1):
            for j in list(range(1, d2)) + [0]:
                s = plan.block(a2, (b + i) % d1, (c + j) % d2)
                got(q_ref.at[s], q_recv.at[s])
                sa_ref[s, 0:cut, :] = pair(s, 0).astype(BF)
                go(sa_ref.at[s, 0:cut], ua_ref.at[a2, (c + j) % d2, i - 1], s1_send.at[s, 0], s1_recv.at[0, a2, (c + j) % d2, i - 1],
                   {"fsdp": plan.block(a, (b + i) % d1, c), "rep": core})
                if j:
                    step1b(s, a2, i, j)
        for j in range(1, d2):
            s = plan.block(a2, b, (c + j) % d2)
            got(q_ref.at[s], q_recv.at[s])
            step1b(s, a2, 0, j)

    def step1b(s, a2, i, j):
        sa_ref[s, cut:part, :] = pair(s, 1).astype(BF)
        go(sa_ref.at[s, cut:part], ub_ref.at[a2, (b + i) % d1, j - 1], s1_send.at[s, 1], s1_recv.at[1, a2, (b + i) % d1, j - 1],
           {"fsdp": plan.block(a, b, (c + j) % d2), "rep": core})

    def from1(half, a2, other):
        ref = ua_ref if half == 0 else ub_ref
        total = None
        for i in range((d1 if half == 0 else d2) - 1):
            got(ref.at[a2, other, i], s1_recv.at[half, a2, other, i])
            v = ref[a2, other, i].astype(F32)
            total = v if total is None else total + v
        return total

    def plus(x, y):
        return x if y is None else x + y

    def step2(k):
        a2 = (a + k) % d0
        for j in range(1, d2):
            c2 = (c + j) % d2
            s = plan.block(a2, b, c2)
            sa_ref[s, 0:cut, :] = plus(pair(s, 0), from1(0, a2, c2)).astype(BF)
            go(sa_ref.at[s, 0:cut], va_ref.at[a2, j - 1], s2_send.at[0, a2, j - 1], s2_recv.at[0, a2, j - 1],
               {"fsdp": plan.block(a, b, c2), "rep": core})
        for i in range(1, d1):
            b2 = (b + i) % d1
            s = plan.block(a2, b2, c)
            sa_ref[s, cut:part, :] = plus(pair(s, 1), from1(1, a2, b2)).astype(BF)
            go(sa_ref.at[s, cut:part], vb_ref.at[a2, i - 1], s2_send.at[1, a2, i - 1], s2_recv.at[1, a2, i - 1],
               {"fsdp": plan.block(a, b2, c), "rep": core})

    def column(k):
        a2 = (a + k) % d0
        s = plan.block(a2, b, c)
        got(q_ref.at[s], q_recv.at[s])
        x = plus(pair(s, 0), from1(0, a2, c))
        for j in range(1, d2):
            got(va_ref.at[a2, j - 1], s2_recv.at[0, a2, j - 1])
            x = x + va_ref[a2, j - 1].astype(F32)
        y = plus(pair(s, 1), from1(1, a2, b))
        for i in range(1, d1):
            got(vb_ref.at[a2, i - 1], s2_recv.at[1, a2, i - 1])
            y = y + vb_ref[a2, i - 1].astype(F32)
        return s, x, y

    def step3(k):
        s, x, y = column(k)
        sa_ref[s, 0:cut, :] = x.astype(BF)
        sa_ref[s, cut:part, :] = y.astype(BF)
        go(sa_ref.at[s], z_ref.at[k - 1], s3_send.at[k - 1], s3_recv.at[k - 1], {"fsdp": plan.block((a + k) % d0, b, c), "rep": core})

    for n in range(d0 + 2):
        if n < d0:
            step1(order[n])
        if 0 <= n - 1 < d0:
            step2(order[n - 1])
        if 0 <= n - 2 < d0 - 1:
            step3(order[n - 2])
    _, x, y = column(0)
    total = jnp.concatenate([x, y], axis=0)
    for k in range(1, d0):
        got(z_ref.at[k - 1], s3_recv.at[k - 1])
        total = total + z_ref[k - 1].astype(F32)
    total_ref[pl.ds(mine, part), :] = total
    go(total_ref.at[pl.ds(mine, part)], total_ref.at[pl.ds(mine, part)], t_send.at[0], t_recv.at[0], {"fsdp": me, "rep": 1 - core})

    off = (me * plan.length) % 128
    row = lax.broadcasted_iota(jnp.int32, (part, 128), 0) + mine
    at = row * 128 + lax.broadcasted_iota(jnp.int32, (part, 128), 1)
    own = jnp.where((at >= off) & (at < off + plan.length), total, 0.0)
    last = me == plan.n - 1
    for i in range(6):
        spot = ROW_VEC - plan.first[-1] + i
        holds = last & (core == spot // part)
        n1_ref[a, i:i + 1, :] = jnp.where(holds, total[spot % part:spot % part + 1], 0.0)
    n1_ref[a, 6:7, :] = jnp.sum(own * own, axis=0, keepdims=True)
    n1_ref[a, 7:8, :] = jnp.zeros((1, 128), F32)
    for k in range(1, d0):
        go(n1_ref.at[a], n1_ref.at[a], n1_send.at[k], n1_recv.at[a], {"fsdp": plan.block((a + k) % d0, b, c), "rep": core})
    for k in range(1, d0):
        got(n1_ref.at[(a + k) % d0], n1_recv.at[(a + k) % d0])
    tile = n1_ref[0]
    for k in range(1, d0):
        tile = tile + n1_ref[k]
    slot = (b * d2 + c) * 2 + core
    n2_ref[slot] = tile
    for n, (i, j, o, to) in enumerate(plane):
        go(n2_ref.at[slot], n2_ref.at[slot], n2_send.at[n], n2_recv.at[slot], to)
    got(total_ref.at[pl.ds(theirs, part)], t_recv.at[0])
    x = pltpu.roll(total_ref[...], (128 - off) % 128, 1)
    below = pltpu.roll(x, plan.rows - 1, 0)
    lane = lax.broadcasted_iota(jnp.int32, x.shape, 1)
    out_ref[...] = jnp.where(lane + off >= 128, below, x)
    for n, (i, j, o, to) in enumerate(plane):
        other = (((b + i) % d1) * d2 + (c + j) % d2) * 2 + (core + o) % 2
        got(n2_ref.at[other], n2_recv.at[other])
    tile = n2_ref[0]
    for n in range(1, 2 * d1 * d2):
        tile = tile + n2_ref[n]
    tile_ref[...] = tile
    for d in sent:
        d.wait_send()


def reduce_call(plan, *handed):
    whole = pl.BlockSpec(memory_space=pltpu.VMEM)
    d0, d1, d2 = plan.dims
    sems = pltpu.SemaphoreType.DMA
    low = lambda *shape: pltpu.VMEM(shape, BF)
    wide = lambda *shape: pltpu.VMEM(shape, F32)
    e1, e2 = max(d1 - 1, 1), max(d2 - 1, 1)
    rest = plan.part - plan.cut
    return pl.pallas_call(
        functools.partial(reduce_kernel, plan),
        out_shape=[jax.ShapeDtypeStruct((plan.rows, 128), F32), jax.ShapeDtypeStruct((8, 128), F32)],
        in_specs=[whole] * 4,
        out_specs=[whole] * 2,
        scratch_shapes=[
            low(2, 28 * 48, 256), wide(ROW_DOWN + plan.rows, 128),
            low(plan.n, plan.rows, 128), low(plan.n, plan.part, 128),
            low(d0, d2, e1, plan.cut, 128), low(d0, d1, e2, rest, 128),
            low(d0, e2, plan.cut, 128), low(d0, e1, rest, 128), low(max(d0 - 1, 1), plan.part, 128),
            low(plan.n, plan.part, 128),
            wide(plan.rows, 128), wide(d0, 8, 128), wide(2 * d1 * d2, 8, 128),
            sems((plan.n,)), sems((plan.n,)), sems((plan.n, 2)),
            sems((2, d0, max(d1, d2), max(e1, e2))), sems((2, d0, max(e1, e2))), sems((2, d0, max(e1, e2))),
            sems((d0,)), sems((d0,)), sems((1,)), sems((1,)),
            sems((d0,)), sems((d0,)), sems((2 * d1 * d2,)), sems((2 * d1 * d2,)),
        ],
        compiler_params=pltpu.CompilerParams(collective_id=1, has_side_effects=True, vmem_limit_bytes=20 * 2**20),
        name="reduce_gradients",
    )(*handed)


def update_kernel(
    plan,
    grad_ref, tile_ref, master_ref, first_ref, second_ref, average_ref,
    norm_ref, new_master_ref, new_first_ref, new_second_ref, new_average_ref, small_ref,
):
    grad_norm = jnp.sqrt(jnp.sum(tile_ref[6:7, :], axis=1, keepdims=True))
    factor = jnp.minimum(1.0, clip_norm / (grad_norm + 1e-06))
    norm_ref[...] = grad_norm
    for i in range(6):
        small_ref[pl.ds(128 * i, 128)] = (tile_ref[i : i + 1, :] * factor).reshape(128)
    full = plan.length // 128
    left = plan.length - 128 * full
    ema_rate = min(0.999, (1.0 + STEP) / (10.0 + STEP))

    def update(row, rows, lanes):
        at = pl.ds(128 * row, 128 * (rows - 1) + lanes)
        shape = (rows, lanes)
        clipped = grad_ref[row : row + rows, 0:lanes] * factor
        new_first = beta_one * first_ref[at].reshape(shape) + (1.0 - beta_one) * clipped
        new_second = beta_two * second_ref[at].reshape(shape) + (1.0 - beta_two) * clipped * clipped
        corrected_first = new_first / (1.0 - beta_one**STEP)
        corrected_second = new_second / (1.0 - beta_two**STEP)
        master = master_ref[at].reshape(shape)
        new_master = master - learn_rate * (
            corrected_first / (jnp.sqrt(corrected_second) + adam_eps) + decay_rate * master
        )
        new_average = ema_rate * average_ref[at].reshape(shape) + (1.0 - ema_rate) * new_master
        size = 128 * (rows - 1) + lanes
        new_master_ref[at] = new_master.reshape(size)
        new_first_ref[at] = new_first.reshape(size)
        new_second_ref[at] = new_second.reshape(size)
        new_average_ref[at] = new_average.reshape(size)

    update(0, full, 128)
    if left:
        update(full, 1, left)


def update_call(plan, *args):
    whole = pl.BlockSpec(memory_space=pltpu.VMEM)
    flat = jax.ShapeDtypeStruct((plan.length,), F32)
    return pl.pallas_call(
        functools.partial(update_kernel, plan),
        out_shape=[jax.ShapeDtypeStruct((1, 1), F32), flat, flat, flat, flat, jax.ShapeDtypeStruct((768,), F32)],
        in_specs=[whole] * 6,
        out_specs=[whole] * 6,
        compiler_params=pltpu.CompilerParams(vmem_limit_bytes=16 * 2**20),
        name="update",
    )(*args)


def per_device(
    input_fine, input_coarse, upstream_fine, upstream_coarse, extents, master, first_moment, second_moment, average
):
    plan = Plan(lax.axis_size("fsdp"), master.shape[0])
    vec, inp, upf, wu, wdn, wc6, wf = gather_call(
        plan, master, input_fine.reshape(PIX, C1), upstream_fine.reshape(PIX, C1)
    )
    out_fine, out_coarse, gi_fine, gi_coarse, *handed = layer_call(
        plan, extents, vec, inp, wu, wdn, wc6, wf, upf,
        input_coarse.reshape(CPIX, C2), upstream_coarse.reshape(CPIX, C2),
    )
    grad, tile = reduce_call(plan, *handed)
    grad_norm, new_master, new_first, new_second, new_average, norm_grads = update_call(
        plan, grad, tile, master, first_moment, second_moment, average
    )
    grad_norm = grad_norm.reshape(())
    return (
        out_fine.reshape(input_fine.shape),
        out_coarse.reshape(input_coarse.shape),
        gi_fine.reshape(input_fine.shape),
        gi_coarse.reshape(input_coarse.shape),
        grad_norm,
        new_master,
        new_first,
        new_second,
        new_average,
        norm_grads,
    )


def solution(mesh):
    images = P(("fsdp", "rep"), None, None, None)
    flat = P("fsdp")
    in_specs = (images,) * 4 + (P(("fsdp", "rep"), None),) + (flat,) * 4
    out_specs = (images,) * 4 + (P(),) + (flat,) * 4 + (P(),)
    return jax.shard_map(per_device, mesh=mesh, in_specs=in_specs, out_specs=out_specs, check_vma=False)
```

```python
import functools

import jax
import jax.numpy as jnp
from jax import lax
from jax.experimental import pallas as pl
from jax.experimental.pallas import tpu as pltpu
from jax.sharding import PartitionSpec as P

F32, BF = jnp.float32, jnp.bfloat16
C1, C2, GROUPS, ITERS, STEP = 256, 128, 8, 12, 10
HEIGHT, HALF = 48, 24
PIX, CPIX = HEIGHT * HEIGHT, HALF * HALF
FLAT_ROWS = 8326
ROW_DOWN, ROW_COARSE, ROW_UP, ROW_VEC = 4608, 6912, 8064, 8320

clip_norm = 1.0
learn_rate = 0.02
beta_one = 0.9
beta_two = 0.999
adam_eps = 1e-08
decay_rate = 0.1


def dot(a, b):
    return jnp.dot(a, b, preferred_element_type=F32)


def dot_rows(a, b):
    return lax.dot_general(a, b, (((0,), (0,)), ((), ())), preferred_element_type=F32)


def dot_lanes(a, b):
    return lax.dot_general(a, b, (((1,), (1,)), ((), ())), preferred_element_type=F32)


def run_sum(x, width):
    lane = lax.broadcasted_iota(jnp.int32, x.shape, 1)
    step = 1
    while step < width:
        up = pltpu.roll(x, 128 - step, 1)
        down = pltpu.roll(x, step, 1)
        x = x + jnp.where((lane & step) == 0, up, down)
        step *= 2
    return x


def shift_down(x):
    count = x.shape[0] // 8
    top = lax.broadcasted_iota(jnp.int32, (8, x.shape[1]), 0) == 0
    turned = [pltpu.roll(x[8 * i : 8 * i + 8], 1, 0) for i in range(count)]
    return jnp.concatenate(
        [jnp.where(top, turned[i - 1] if i else 0.0, turned[i]) for i in range(count)], axis=0
    )


def shift_up(x):
    count = x.shape[0] // 8
    end = lax.broadcasted_iota(jnp.int32, (8, x.shape[1]), 0) == 7
    turned = [pltpu.roll(x[8 * i : 8 * i + 8], 7, 0) for i in range(count)]
    return jnp.concatenate(
        [jnp.where(end, turned[i + 1] if i < count - 1 else 0.0, turned[i]) for i in range(count)], axis=0
    )


def rows_out(x):
    parts = [x[24 * i : 24 * i + 24] for i in range(24)]
    return parts[0::2] + parts[1::2]


def pair_order(rows):
    return jnp.concatenate([rows[i // 2 + 12 * (i % 2)] for i in range(24)], axis=0)


def image_order(x):
    return jnp.concatenate(rows_out(x), axis=0)


def in_rows(x, change):
    return jnp.concatenate([change(x[24 * r : 24 * r + 24]) for r in range(24)], axis=0)


def row_down(x):
    rows = rows_out(x)
    return pair_order([jnp.zeros_like(rows[0])] + rows[:-1])


def row_up(x):
    rows = rows_out(x)
    return pair_order(rows[1:] + [jnp.zeros_like(rows[0])])


def tile_sum(x):
    total = x[0:8]
    for i in range(1, x.shape[0] // 8):
        total = total + x[8 * i : 8 * i + 8]
    return total


def twice(m):
    return jnp.concatenate([m, m], axis=1)


def interleave(ref, r, even, odd):
    for p in range(2):
        at = slice(128 * p, 128 * p + 128)
        ref[p, pl.ds(r * 48, 24, stride=2), :] = even[:, at]
        ref[p, pl.ds(r * 48 + 1, 24, stride=2), :] = odd[:, at]


def rows_of(r, count, unit):
    start = r * unit
    return pl.ds(start if isinstance(r, int) else pl.multiple_of(start, unit if unit % 16 == 0 else 8), count)


STEPS = "E0 E1 E2 E3 C1-7 E4 E5 E6 C7-13 E7 E8 E9 E10 E11 C13-17 L C17-21 Z K C21-24,0-1 S F B"


def layer_kernel(
    plan,
    ext_ref, vec_ref, inp_in, w_ref, upf_in, inc_hbm, upc_hbm,
    outf_ref, outc_ref, gif_ref, gic_ref, uo_ref, go_ref, join_ref, blocks_ref,
    g_ref, u_ref, upf_ref, inp_ref, wu_ref, wdn_ref, wc6_ref, wf_ref, inc_in, upc_ref, grad_ref, ph_ref, c_ref, x_ref, xc_ref, inc_ref, branch_ref, lift_ref, mf_ref, mb_ref, mc_ref,
    scf_ref, scc_ref, gl_ref, glo_ref, back_ref, gp_ref, row_ref, stage_ref, small_ref,
    in_sem, out_sem, small_sem,
):
    loads = [
        pltpu.make_async_copy(src, dst, in_sem.at[n])
        for n, (src, dst) in enumerate(
            ((inc_hbm, inc_in), (upc_hbm, upc_ref))
        )
    ]
    for load in loads:
        load.start()
    hh, ww = ext_ref[0, 0], ext_ref[0, 1]
    gain_f = jnp.concatenate([vec_ref[0:1, :], vec_ref[1:2, :]], axis=1)
    bias_f = jnp.concatenate([vec_ref[2:3, :], vec_ref[3:4, :]], axis=1)
    gain_c, bias_c = vec_ref[4:5, :], vec_ref[5:6, :]
    pos = lax.broadcasted_iota(jnp.int32, (24, 128), 0)
    even = jnp.where(2 * pos < ww, 1.0, 0.0).astype(F32)
    odd = jnp.where(2 * pos + 1 < ww, 1.0, 0.0).astype(F32)

    def setup(r, _):
        at = rows_of(r, 96, 96)
        low, high = r < hh, r + 24 < hh
        m = [jnp.where(here, v, 0.0) for v in (even, odd) for here in (low, high)]
        m = jnp.concatenate(m, axis=0)
        mf_ref[at, :] = m
        mb_ref[at, :] = m.astype(BF)
        x_ref[at, :] = jnp.zeros((96, 256), F32)
        return 0

    lax.fori_loop(0, 24, setup, 0)

    def setup_coarse(r, _):
        m = [jnp.where(2 * r < hh, even, 0.0), jnp.where(2 * r + 24 < hh, even, 0.0)]
        mc_ref[rows_of(r, 48, 48), :] = jnp.concatenate(m, axis=0)
        return 0

    lax.fori_loop(0, 12, setup_coarse, 0)
    nf = (hh * ww).astype(F32) * (C1 // GROUPS)
    nc = (((hh + 1) // 2) * ((ww + 1) // 2)).astype(F32) * (C2 // GROUPS)
    g_ref[:, 0:96, :] = jnp.zeros((2, 96, 256), BF)
    g_ref[:, 26 * 48 : 28 * 48, :] = jnp.zeros((2, 96, 256), BF)
    grad_ref[FLAT_ROWS:, :] = jnp.zeros((plan.tall - FLAT_ROWS, 128), F32)
    xc_ref[...] = jnp.zeros((576, 128), F32)
    scf_ref[...] = jnp.zeros((8, 256), F32)
    scc_ref[...] = jnp.zeros((8, 128), F32)
    scf_ref[1:2, :] = 0.5 * bias_f
    scc_ref[1:2, :] = 0.5 * bias_c
    for dy in range(3):
        for h in range(2):
            g0, g1, g2 = (w_ref[pl.ds(2 * (3 * dy + dx) + h, 256, stride=18), :] for dx in range(3))
            outer = g0 + g2
            for i, v in enumerate((g0, 0.5 * (outer + g1), 0.5 * (outer - g1), g2)):
                at = 768 * i + 256 * dy
                wf_ref[at : at + 256, 128 * h : 128 * h + 128] = v.astype(BF)
    for h in range(2):
        wu_ref[:, 128 * h : 128 * h + 128] = w_ref[pl.ds(ROW_UP + h, 128, stride=2), :].astype(BF)
    for t in range(9):
        p = (4, 5, 3, 7, 1, 8, 6, 2, 0).index(t)
        wdn_ref[:, 128 * p : 128 * p + 128] = w_ref[pl.ds(ROW_DOWN + t, 256, stride=9), :].astype(BF)
    wc6_ref[0:128, 384:768] = jnp.zeros((128, 384), BF)
    for t in range(9):
        dy, dx = t // 3, t % 3
        at, p = 128 * (dx + 1) // 2 // 128 * 128, dy + 3 * (dx // 2)
        wc6_ref[at : at + 128, 128 * p : 128 * p + 128] = w_ref[pl.ds(ROW_COARSE + t, 128, stride=9), :].astype(BF)
    inp_ref[...] = inp_in[...]
    loads[0].wait()
    v = inc_in[...].astype(F32)
    inc_ref[...] = pair_order([v[24 * r : 24 * r + 24] for r in range(24)])

    def coarse_branch():
        h = xc_ref[...] * scc_ref[0:1, :] + scc_ref[1:2, :]
        y = h * jnp.tanh(h) + h
        branch = ((y + inc_ref[...]) * mc_ref[...]).astype(BF)
        branch_ref[...] = branch
        lift_ref[...] = dot(branch, wu_ref[...])

    def unit(r, final):
        scale, shift = scf_ref[0:1, :], scf_ref[1:2, :]
        half = rows_of(r // 2, 48, 48)
        lift = lift_ref[half, :]
        lift_low = lift.astype(BF)
        z = []
        for p in range(2):
            at = rows_of(2 * r + p, 48, 48)
            h = x_ref[at, :] * scale + shift
            if final:
                y = h * jnp.tanh(h) + h
            else:
                h = h.astype(BF)
                y = h * jnp.tanh(h) + h
            if final:
                m = twice(mf_ref[at, :])
                low = ((y + inp_ref[at, :].astype(F32)) * m).astype(BF)
                z.append((low.astype(F32) + lift) * m)
            else:
                m = twice(mb_ref[at, :])
                low = (y.astype(BF) + inp_ref[at, :]) * m
                z.append((low + lift_low) * m)
            ph_ref[2 * (r % 2) + p, half, :] = low
        even, odd = z
        if final:
            for i in range(2):
                at = slice(24 * i, 24 * i + 24)
                interleave(stage_ref.at[0], r + 24 * i, even[at], odd[at])
            return
        wide = odd.astype(F32)
        left = jnp.concatenate([shift_down(wide[0:24]), shift_down(wide[24:48])], axis=0).astype(BF)
        wide = even.astype(F32)
        right = jnp.concatenate([shift_up(wide[0:24]), shift_up(wide[24:48])], axis=0).astype(BF)
        for i, u in enumerate((left - odd, even + odd, odd - even, even - right)):
            u_ref[i, rows_of(r + 1, 48, 48), :] = u
            if r == 0:
                w = u.astype(F32)
                u_ref[i, 25 * 48 : 26 * 48, :] = jnp.concatenate([w[24:48], jnp.zeros_like(w[0:24])], axis=0).astype(BF)
            if r == 23:
                w = u.astype(F32)
                u_ref[i, 0:48, :] = jnp.concatenate([jnp.zeros_like(w[0:24]), w[0:24]], axis=0).astype(BF)

    def lowered_parts(first=0, last=CPIX):
        ee, eo, oe, oo = (ph_ref[i, first:last, :] for i in range(4))
        p = dot(eo, wdn_ref[:, 128:384]) + dot(oo, wdn_ref[:, 640:896])
        q = dot(oe, wdn_ref[:, 384:640])
        t = dot(oo, wdn_ref[:, 896:1152])
        return p, q, t, dot(ee, wdn_ref[:, 0:128])

    def lowered(parts):
        p, q, t, e = parts
        here = p[:, :128] + q[:, :128] + e
        return here + row_down(q[:, 128:] + t[:, :128]) + in_rows(p[:, 128:] + row_down(t[:, 128:]), shift_down)

    def coarse_state(parts):
        zc = (branch_ref[...].astype(F32) + lowered(parts)) * mc_ref[...]
        c_ref[:, 0:128] = in_rows(zc, shift_down).astype(BF)
        c_ref[:, 128:256] = zc.astype(BF)

    def coarse_sums(p):
        t = [p[:, 128 * i : 128 * i + 128] for i in range(6)]
        xc = row_down(t[0]) + t[1] + row_up(t[2]) + in_rows(row_down(t[3]) + t[4] + row_up(t[5]), shift_up)
        xc_ref[...] = xc
        xm = xc * mc_ref[...]
        return tile_sum(xm), tile_sum(xm * xm)

    def conv_units(units):
        products = []
        for i in range(4):
            total = None
            for dy in range(3):
                rows = [u_ref[i, 48 * (first + dy) : 48 * (last + dy), :] for first, last in units]
                rows = rows[0] if len(rows) == 1 else jnp.concatenate(rows, axis=0)
                at = 768 * i + 256 * dy
                p = dot(rows, wf_ref[at : at + 256, :])
                total = p if total is None else total + p
            products.append(total)
        m0, m1, m2, m3 = products
        even, odd = m0 + m1 + m2, m1 - m2 - m3
        s = q = None
        for n, r in enumerate(r for first, last in units for r in range(first, last)):
            for p, y in enumerate((even, odd)):
                y = y[48 * n : 48 * n + 48]
                at = slice(96 * r + 48 * p, 96 * r + 48 * p + 48)
                x_ref[at, :] = y
                ym = y * twice(mf_ref[at, :])
                ds, dq = tile_sum(ym), tile_sum(ym * ym)
                s, q = (ds, dq) if s is None else (s + ds, q + dq)
        return s, q

    def finish(s, q, width, n, gain, bias, to_ref):
        s, q = jnp.sum(s, axis=0, keepdims=True), jnp.sum(q, axis=0, keepdims=True)
        for p in range(s.shape[1] // 128):
            at = slice(128 * p, 128 * p + 128)
            mean = run_sum(s[:, at], width) / n
            var = jnp.maximum(run_sum(q[:, at], width) / n - mean * mean, 0.0)
            inv = lax.rsqrt(var + 1e-5)
            to_ref[0:1, at] = 0.5 * inv * gain[:, at]
            to_ref[1:2, at] = 0.5 * (bias[:, at] - mean * inv * gain[:, at])
            to_ref[2:3, at] = mean
            to_ref[3:4, at] = inv

    def iterate(t, _):
        s = q = parts = conv_c = sums_c = None
        for step in STEPS.split():
            if step[0] == "E":
                unit(2 * int(step[1:]), False)
                unit(2 * int(step[1:]) + 1, False)
            elif step[0] == "C":
                ds, dq = conv_units([tuple(map(int, piece.split("-"))) for piece in step[1:].split(",")])
                s, q = (ds, dq) if s is None else (s + ds, q + dq)
            elif step == "L":
                parts = lowered_parts()
            elif step == "L0":
                parts = lowered_parts(0, 288)
            elif step == "L1":
                parts = [jnp.concatenate(both, axis=0) for both in zip(parts, lowered_parts(288, 576))]
            elif step == "Z":
                coarse_state(parts)
            elif step == "K":
                conv_c = dot(c_ref[...], wc6_ref[...])
            elif step == "S":
                sums_c = coarse_sums(conv_c)
            elif step == "F":
                finish(*sums_c, C2 // GROUPS, nc, gain_c, bias_c, scc_ref)
            elif step == "B":
                coarse_branch()
        finish(s, q, C1 // GROUPS, nf, gain_f, bias_f, scf_ref)
        return 0

    coarse_branch()
    lax.fori_loop(0, ITERS, iterate, 0)

    sends = []

    def put(i, ref, half):
        for n in range(2):
            for p in range(2):
                at = pl.ds(48 * (12 * half + 24 * n), 576)
                send = pltpu.make_async_copy(
                    stage_ref.at[i, p, at], ref.at[at, 128 * p : 128 * p + 128], out_sem.at[i, half, n, p]
                )
                send.start()
                sends.append(send)

    def put_small(i, ref):
        send = pltpu.make_async_copy(small_ref.at[i], ref, small_sem.at[i])
        send.start()
        sends.append(send)

    for r in range(24):
        unit(r, True)
    upf_ref[...] = upf_in[...]
    put(0, outf_ref, 0)
    put(0, outf_ref, 1)
    small_ref[0] = image_order((branch_ref[...].astype(F32) + lowered(lowered_parts())) * mc_ref[...])
    put_small(0, outc_ref)
    loads[1].wait()

    v = upc_ref[...].astype(F32)
    seed_c = pair_order([v[24 * r : 24 * r + 24] for r in range(24)]) * mc_ref[...]
    right = in_rows(seed_c, shift_up)
    glo_ref[:, 0:128] = seed_c.astype(BF)
    glo_ref[:, 128:256] = right.astype(BF)
    glo_ref[:, 256:384] = row_up(seed_c).astype(BF)
    glo_ref[:, 384:512] = row_up(right).astype(BF)

    for j in range(12):
        total = None
        for i in range(4):
            at = rows_of(4 * j + i, 48, 48)
            seed = upf_ref[at, :].astype(F32) * twice(mf_ref[at, :])
            total = seed if total is None else total + seed
        gl_ref[rows_of(j, 48, 48), :] = total.astype(BF)
    g00, g01, g10, g11 = (glo_ref[:, 128 * i : 128 * i + 128] for i in range(4))

    back_c = (seed_c + dot_lanes(gl_ref[...], wu_ref[...])) * mc_ref[...]
    small_ref[1] = image_order(back_c)
    put_small(1, gic_ref)

    def pre_grad(gi, x, scale, shift, mean, inv):
        h = x * scale + shift
        t = jnp.tanh(h)
        sig = 0.5 * t + 0.5
        normed = (x - mean) * inv
        return gi * sig * (1.0 + 2.0 * h * (1.0 - sig)), normed

    def back_means(sum_bias, sum_gain, gain, width, n):
        return run_sum(sum_bias * gain, width) / n, run_sum(sum_gain * gain, width) / n

    gp_c, normed_c = pre_grad(
        back_c, xc_ref[...], scc_ref[0:1, :], scc_ref[1:2, :], scc_ref[2:3, :], scc_ref[3:4, :]
    )
    sum_gain = jnp.sum(gp_c * normed_c, axis=0, keepdims=True)
    sum_bias = jnp.sum(gp_c, axis=0, keepdims=True)
    grad_ref[ROW_VEC + 4 : ROW_VEC + 5, :] = sum_gain
    grad_ref[ROW_VEC + 5 : ROW_VEC + 6, :] = sum_bias
    mean_h, mean_hn = back_means(sum_bias, sum_gain, gain_c, C2 // GROUPS, nc)
    gconv = (gp_c * gain_c - mean_h - normed_c * mean_hn) * scc_ref[3:4, :] * mc_ref[...]
    around = jnp.concatenate([row_up(gconv), gconv, row_down(gconv)], axis=1)
    pair = dot_rows(c_ref[...], around.astype(BF))
    single = dot_rows(c_ref[:, 128:256], in_rows(around, shift_down).astype(BF))
    for dy in range(3):
        at = slice(128 * dy, 128 * dy + 128)
        grad_ref[pl.ds(ROW_COARSE + 3 * dy, 128, stride=9), :] = pair[0:128, at]
        grad_ref[pl.ds(ROW_COARSE + 3 * dy + 1, 128, stride=9), :] = pair[128:256, at]
        grad_ref[pl.ds(ROW_COARSE + 3 * dy + 2, 128, stride=9), :] = single[:, at]

    uo_ref[...] = u_ref[...]
    back_ref[0] = dot_lanes(g00, wdn_ref[:, 0:128])
    back_ref[1] = dot_lanes(jnp.concatenate([g00, g01], axis=1), wdn_ref[:, 128:384])
    back_ref[2] = dot_lanes(jnp.concatenate([g00, g10], axis=1), wdn_ref[:, 384:640])
    back_ref[3] = dot_lanes(glo_ref[...], wdn_ref[:, 640:1152])

    none8 = jnp.zeros((8, 256), F32)
    sums = [none8, none8]
    for j in range(12):
        for i in range(2):
            gi = []
            for p in range(2):
                at = rows_of(4 * j + 2 * i + p, 48, 48)
                back = back_ref[2 * i + p, rows_of(j, 48, 48), :]
                gi.append((upf_ref[at, :].astype(F32) + back) * twice(mf_ref[at, :]))
                gp, normed = pre_grad(
                    gi[p], x_ref[at, :], scf_ref[0:1, :], scf_ref[1:2, :], scf_ref[2:3, :], scf_ref[3:4, :]
                )
                gp_ref[at, :] = gp
                sums[0] = sums[0] + tile_sum(gp * normed)
                sums[1] = sums[1] + tile_sum(gp)
            for n in range(2):
                half = slice(24 * n, 24 * n + 24)
                interleave(stage_ref.at[1], 2 * j + i + 24 * n, gi[0][half], gi[1][half])
        if j % 6 == 5:
            put(1, gif_ref, j // 6)
    up_grad = dot_rows(branch_ref[...], gl_ref[...])
    for j in range(2):
        grad_ref[pl.ds(ROW_UP + j, 128, stride=2), :] = up_grad[:, 128 * j : 128 * j + 128]
    for i, (parts, taps) in enumerate(
        (((g00,), (4,)), ((g00, g01), (5, 3)), ((g00, g10), (7, 1)), ((g00, g01, g10, g11), (8, 6, 2, 0)))
    ):
        down = dot_rows(ph_ref[i], jnp.concatenate(parts, axis=1))
        for n, tap in enumerate(taps):
            grad_ref[pl.ds(ROW_DOWN + tap, 256, stride=9), :] = down[:, 128 * n : 128 * n + 128]
    sum_gain, sum_bias = (jnp.sum(v, axis=0, keepdims=True) for v in sums)
    for p in range(2):
        at = slice(128 * p, 128 * p + 128)
        grad_ref[ROW_VEC + p : ROW_VEC + p + 1, :] = sum_gain[:, at]
        grad_ref[ROW_VEC + 2 + p : ROW_VEC + 3 + p, :] = sum_bias[:, at]
        row_ref[0:1, at], row_ref[1:2, at] = back_means(
            sum_bias[:, at], sum_gain[:, at], gain_f[:, at], C1 // GROUPS, nf
        )

    for r in range(24):
        g = []
        for p in range(2):
            at = rows_of(2 * r + p, 48, 48)
            normed = (x_ref[at, :] - scf_ref[2:3, :]) * scf_ref[3:4, :]
            v = (gp_ref[at, :] * gain_f - row_ref[0:1, :] - normed * row_ref[1:2, :]) * scf_ref[3:4, :]
            g.append(v * twice(mf_ref[at, :]))
        for p in range(2):
            g_ref[p, rows_of(r + 2, 48, 48), :] = g[p].astype(BF)
    go_ref[...] = g_ref[...]
    join_ref[...] = grad_ref[ROW_DOWN : ROW_DOWN + plan.rows, :]
    for n, s in enumerate(plan.early):
        first = plan.first[s]
        blocks_ref[n] = grad_ref[first : first + plan.rows, :].astype(BF)
    for send in sends:
        send.wait()


def layer_call(plan, *args):
    there = pl.BlockSpec(memory_space=pltpu.HBM)
    whole = pl.BlockSpec(memory_space=pltpu.VMEM)
    low = lambda *shape: pltpu.VMEM(shape, BF)
    wide = lambda *shape: pltpu.VMEM(shape, F32)
    return pl.pallas_call(
        functools.partial(layer_kernel, plan),
        out_shape=[
            jax.ShapeDtypeStruct((PIX, 256), F32),
            jax.ShapeDtypeStruct((CPIX, 128), F32),
            jax.ShapeDtypeStruct((PIX, 256), F32),
            jax.ShapeDtypeStruct((CPIX, 128), F32),
            *(jax.ShapeDtypeStruct(shape, dtype) for shape, dtype in plan.handed),
        ],
        in_specs=[pl.BlockSpec(memory_space=pltpu.SMEM)] + [whole] * 4 + [there] * 2,
        out_specs=[there] * 4 + [whole] * 4,
        scratch_shapes=[
            low(2, 28 * 48, 256), low(4, 26 * 48, 256), low(PIX, 256), low(PIX, 256), low(128, 256), low(256, 1152), low(256, 768), low(12 * 256, 256),
            low(CPIX, 128), low(CPIX, 128),
            wide(plan.tall, 128), low(4, CPIX, 256), low(CPIX, 256),
            wide(PIX, 256), wide(CPIX, 128), wide(CPIX, 128), low(CPIX, 128), wide(CPIX, 256),
            wide(PIX, 128), low(PIX, 128), wide(CPIX, 128),
            wide(8, 256), wide(8, 128),
            low(CPIX, 256), low(CPIX, 512), wide(4, CPIX, 256), wide(PIX, 256), wide(8, 256),
            wide(2, 2, PIX + 8, 128), wide(2, CPIX, 128),
            pltpu.SemaphoreType.DMA((2,)),
            pltpu.SemaphoreType.DMA((2, 2, 2, 2)),
            pltpu.SemaphoreType.DMA((2,)),
        ],
        compiler_params=pltpu.CompilerParams(vmem_limit_bytes=38 * 2**20),
        name="layer",
    )(*args)


class Plan:
    def __init__(self, shards, length):
        self.dims = {16: (4, 2, 2), 128: (4, 8, 4)}.get(shards, (shards, 1, 1))
        self.n, self.length = shards, length
        self.tiled = length // 1024 * 1024
        self.first = [s * length // 128 for s in range(shards)]
        self.rows = -(-(length + 127) // 128)
        self.rows = -(-self.rows // 32) * 32
        self.part = self.rows // 2
        self.cut = -(-self.part // 32) * 16
        self.tall = -(-(self.first[-1] + self.rows) // 16) * 16
        self.early = [s for s in range(shards) if self.first[s] >= ROW_DOWN]
        self.handed = (
            ((4, 26 * 48, 256), BF), ((2, 28 * 48, 256), BF), ((self.rows, 128), F32),
            ((len(self.early), self.rows, 128), BF),
        )

    def here(self):
        d0, d1, d2 = self.dims
        me = lax.axis_index("fsdp")
        return me, lax.axis_index("rep"), me // (d1 * d2), me // d2 % d1, me % d2

    def block(self, a, b, c):
        d0, d1, d2 = self.dims
        return (a * d1 + b) * d2 + c


def flip(a, k):
    bit = 1
    while bit <= k:
        if k & bit:
            a = a + bit - 2 * bit * (a // bit % 2)
        bit *= 2
    return a


def to_rows(plan, ref, tail_ref):
    full = plan.tiled // 128
    left = plan.length - plan.tiled
    parts = [ref[...].reshape(full, 128)]
    whole = left // 128
    if whole:
        parts.append(tail_ref[pl.ds(0, 128 * whole)].reshape(whole, 128))
    left = left - 128 * whole
    if left:
        tail = tail_ref[pl.ds(128 * whole, left)].reshape(1, left)
        parts.append(jnp.concatenate([tail, jnp.zeros((1, 128 - left), F32)], axis=1))
    have = full + whole + (left > 0)
    parts.append(jnp.zeros((plan.rows - have, 128), F32))
    return jnp.concatenate(parts, axis=0)


def gather_kernel(
    plan,
    master_hbm, tail_ref, inp_hbm, upf_hbm,
    vec_ref, inpo_ref, upfo_ref, w_ref,
    master_ref, inp_ref, upf_ref, g_ref, tmp_ref, in_sem, send_sem, recv_sem, sib_send, sib_recv, far_send,
):
    d0, d1, d2 = plan.dims
    me, core, a, b, c = plan.here()
    part, cut = plan.part, plan.cut
    loads = [
        pltpu.make_async_copy(src, dst, in_sem.at[n])
        for n, (src, dst) in enumerate(
            ((master_hbm.at[pl.ds(0, plan.tiled)], master_ref), (inp_hbm, inp_ref), (upf_hbm, upf_ref))
        )
    ]
    for load in loads:
        load.start()
    barrier = pltpu.get_barrier_semaphore()
    others = [plan.block((a + k) % d0, b, c) for k in range(1, d0)]
    others += [plan.block(a, (b + k) % d1, c) for k in range(1, d1)]
    others += [plan.block(a, b, (c + k) % d2) for k in range(1, d2)]
    others = [{"fsdp": other, "rep": core} for other in others] + [{"fsdp": me, "rep": 1 - core}]
    for other in others:
        pl.semaphore_signal(barrier, inc=1, device_id=other, device_id_type=pl.DeviceIdType.MESH)
    off = (me * plan.length) % 128
    loads[0].wait()
    x = pltpu.roll(to_rows(plan, master_ref, tail_ref), off, 1)
    row = lax.broadcasted_iota(jnp.int32, x.shape, 0)
    lane = lax.broadcasted_iota(jnp.int32, x.shape, 1)
    above = jnp.where(row == 0, 0.0, pltpu.roll(x, 1, 0))
    g_ref[me] = jnp.where(lane < off, above, x).astype(BF)
    pl.semaphore_wait(barrier, len(others))

    def span(half, which):
        start = which * part + (cut if half == 1 else 0)
        return pl.ds(pl.multiple_of(start, 16), (cut, part - cut)[half])

    def copy(block, half, fsdp, rep, send, recv, which):
        at = g_ref.at[block, span(half, which)]
        return pltpu.make_async_remote_copy(
            src_ref=at, dst_ref=at, send_sem=send, recv_sem=recv,
            device_id={"fsdp": fsdp, "rep": rep}, device_id_type=pl.DeviceIdType.MESH,
        )

    def arrive(block, half):
        copy(block, half, me, core, far_send.at[0, 0], recv_sem.at[block, half], core).wait_recv()

    sent = []

    def go(d):
        d.start()
        sent.append(d)

    def along1(block, half):
        for k in range(1, d1):
            go(copy(block, half, plan.block(a, (b + k) % d1, c), core,
                    send_sem.at[block, half, k - 1], recv_sem.at[block, half], core))

    def along2(block, half):
        for k in range(1, d2):
            go(copy(block, half, plan.block(a, b, (c + k) % d2), core,
                    send_sem.at[block, half, d1 + k - 2], recv_sem.at[block, half], core))

    def beside(block, half):
        go(copy(block, half, me, 1 - core, sib_send.at[block, half], sib_recv.at[block, half], core))

    def own_column(k):
        block = plan.block(flip(a, k), b, c)
        if k:
            arrive(block, 0)
        along2(block, 0)
        if k:
            arrive(block, 1)
        along1(block, 1)
        along2(block, 1)
        along1(block, 0)
        if k:
            beside(block, 0)
            beside(block, 1)

    def near(k):
        a2 = flip(a, k)
        ahead = [plan.block(a2, b, (c + i) % d2) for i in range(1, d2)]
        above = [plan.block(a2, (b + i) % d1, c) for i in range(1, d1)]
        for block in ahead:
            arrive(block, 0)
            along1(block, 0)
            beside(block, 0)
        for block in above:
            arrive(block, 1)
            along2(block, 1)
            beside(block, 1)
        for block in ahead:
            arrive(block, 1)
            beside(block, 1)
        for block in above:
            arrive(block, 0)
            beside(block, 0)

    def diagonal(k):
        a2 = flip(a, k)
        for i in range(1, d1):
            for j in range(1, d2):
                block = plan.block(a2, (b + i) % d1, (c + j) % d2)
                for half in (0, 1):
                    arrive(block, half)
                    beside(block, half)

    def parity(src, dst):
        def one(r, _):
            parts = []
            for n in range(2):
                at = rows_of(r + 24 * n, 48, 48)
                v = src[at, :].astype(F32)
                for p in range(2):
                    tmp_ref[p, at, :] = v[:, 128 * p : 128 * p + 128]
            for first in range(2):
                for n in range(2):
                    at = pl.ds((r + 24 * n) * 48 + first, 24, stride=2)
                    parts.append(jnp.concatenate([tmp_ref[p, at, :] for p in range(2)], axis=1))
            dst[rows_of(r, 96, 96), :] = jnp.concatenate(parts, axis=0).astype(BF)
            return 0

        lax.fori_loop(0, 24, one, 0, unroll=2)

    for k in range(1, d0):
        for half in (0, 1):
            go(copy(me, half, plan.block(flip(a, k), b, c), core, far_send.at[k, half], recv_sem.at[me, half], core))
    own_column(0)
    loads[1].wait()
    parity(inp_ref, inpo_ref)
    loads[2].wait()
    parity(upf_ref, upfo_ref)
    for k in range(1, d0):
        own_column(k)
    for k in range(d0):
        near(k)
    for k in range(d0):
        diagonal(k)
    for k in range(1, plan.n):
        block = (me + k) % plan.n
        for half in (0, 1):
            copy(block, half, me, core, far_send.at[0, 0], sib_recv.at[block, half], 1 - core).wait_recv()

    for s in range(plan.n):
        v = g_ref[s].astype(F32)
        at = plan.first[s]
        if s:
            low = w_ref[at : at + 1, :] + v[0:1]
            w_ref[at : at + plan.rows, :] = v
            w_ref[at : at + 1, :] = low
        else:
            w_ref[0 : plan.rows, :] = v
    vec_ref[...] = w_ref[ROW_VEC : ROW_VEC + 8, :]
    for d in sent:
        d.wait_send()


def gather_call(plan, master, inp, upf):
    there = pl.BlockSpec(memory_space=pltpu.HBM)
    whole = pl.BlockSpec(memory_space=pltpu.VMEM)
    low = lambda *shape: jax.ShapeDtypeStruct(shape, BF)
    outs = [
        jax.ShapeDtypeStruct((8, 128), F32), low(PIX, 256), low(PIX, 256),
        jax.ShapeDtypeStruct((plan.tall, 128), F32),
    ]
    d0, d1, d2 = plan.dims
    sems = pltpu.SemaphoreType.DMA
    return pl.pallas_call(
        functools.partial(gather_kernel, plan),
        out_shape=outs,
        in_specs=[there, whole, there, there],
        out_specs=[whole] * 4,
        scratch_shapes=[
            pltpu.VMEM((plan.tiled,), F32), pltpu.VMEM((PIX, 256), BF), pltpu.VMEM((PIX, 256), BF),
            pltpu.VMEM((plan.n, plan.rows, 128), BF), pltpu.VMEM((2, PIX + 8, 128), F32),
            sems((3,)), sems((plan.n, 2, max(d1 + d2 - 2, 1))), sems((plan.n, 2)), sems((plan.n, 2)),
            sems((plan.n, 2)), sems((d0, 2)),
        ],
        compiler_params=pltpu.CompilerParams(collective_id=0, has_side_effects=True, vmem_limit_bytes=20 * 2**20),
        name="gather_weights",
    )(
        pltpu.with_memory_space_constraint(master, pltpu.HBM), master[plan.tiled :],
        *(pltpu.with_memory_space_constraint(x, pltpu.HBM) for x in (inp, upf)),
    )


def reduce_kernel(
    plan,
    u_ref, g_ref, join_ref, blocks_ref,
    out_ref, tile_ref,
    sums_ref, grad_ref, p_ref, q_ref, ua_ref, ub_ref, va_ref, vb_ref, z_ref, sa_ref, total_ref,
    n1_ref, n2_ref,
    q_send, q_recv, s1_send, s1_recv, s2_send, s2_recv, s3_send, s3_recv, t_send, t_recv,
    n1_send, n1_recv, n2_send, n2_recv,
):
    d0, d1, d2 = plan.dims
    me, core, a, b, c = plan.here()
    part, cut = plan.part, plan.cut
    MESH = pl.DeviceIdType.MESH
    barrier = pltpu.get_barrier_semaphore()
    others = [{"fsdp": plan.block((a + k) % d0, b, c), "rep": core} for k in range(1, d0)]
    plane = []
    for i in range(d1):
        for j in range(d2):
            for o in range(2):
                if i or j or o:
                    plane.append((i, j, o, {"fsdp": plan.block(a, (b + i) % d1, (c + j) % d2), "rep": (core + o) % 2}))
    others += [p[3] for p in plane]
    for other in others:
        pl.semaphore_signal(barrier, inc=1, device_id=other, device_id_type=MESH)
    even, odd = g_ref[0], g_ref[1]
    sums_ref[0] = even + odd
    sums_ref[1] = even - odd
    products = []
    for i, ref in enumerate((g_ref.at[0], sums_ref.at[0], sums_ref.at[1], g_ref.at[1])):
        shifted = [ref[48 * (2 - dy) : 48 * (2 - dy) + 26 * 48, :] for dy in range(3)]
        products.append(dot_rows(u_ref[i], jnp.concatenate(shifted, axis=1)))
    p0, p1, p2, p3 = products
    both, apart = 0.5 * (p1 + p2), 0.5 * (p1 - p2)
    for dx, grad in enumerate((p0 + both, apart, both - p3)):
        for dy in range(3):
            for j in range(2):
                at = 256 * dy + 128 * j
                grad_ref[pl.ds(2 * (3 * dy + dx) + j, 256, stride=18), :] = grad[:, at : at + 128]
    count = len(plan.early)
    grad_ref[ROW_DOWN:, :] = join_ref[...]
    for s in range(plan.n - count):
        first = plan.first[s]
        p_ref[s] = grad_ref[first : first + plan.rows, :].astype(BF)
    p_ref[plan.n - count :] = blocks_ref[...]
    pl.semaphore_wait(barrier, len(others))

    sent = []

    def go(src, dst, send, recv, to):
        d = pltpu.make_async_remote_copy(
            src_ref=src, dst_ref=dst, send_sem=send, recv_sem=recv, device_id=to, device_id_type=MESH
        )
        d.start()
        sent.append(d)

    def got(ref, recv):
        pltpu.make_async_copy(ref, ref, recv).wait()

    mine = pl.multiple_of(core * part, 16)
    theirs = pl.multiple_of((1 - core) * part, 16)
    halves = ((0, cut), (cut, part - cut))
    order = [(k + 1) % d0 for k in range(d0)]
    for k in order:
        for i in list(range(1, d1)) + [0]:
            for j in list(range(1, d2)) + [0]:
                s = plan.block((a + k) % d0, (b + i) % d1, (c + j) % d2)
                go(
                    p_ref.at[s, pl.ds(theirs, part)], q_ref.at[s], q_send.at[s], q_recv.at[s],
                    {"fsdp": me, "rep": 1 - core},
                )

    def pair(s, half):
        start, size = halves[half]
        x = p_ref[s, pl.ds(pl.multiple_of(mine + start, 16), size), :].astype(F32)
        return x + q_ref[s, start : start + size, :].astype(F32)

    def step1(k):
        a2 = (a + k) % d0
        for i in range(1, d1):
            for j in list(range(1, d2)) + [0]:
                s = plan.block(a2, (b + i) % d1, (c + j) % d2)
                got(q_ref.at[s], q_recv.at[s])
                sa_ref[s, 0:cut, :] = pair(s, 0).astype(BF)
                go(sa_ref.at[s, 0:cut], ua_ref.at[a2, (c + j) % d2, i - 1], s1_send.at[s, 0], s1_recv.at[0, a2, (c + j) % d2, i - 1],
                   {"fsdp": plan.block(a, (b + i) % d1, c), "rep": core})
                if j:
                    step1b(s, a2, i, j)
        for j in range(1, d2):
            s = plan.block(a2, b, (c + j) % d2)
            got(q_ref.at[s], q_recv.at[s])
            step1b(s, a2, 0, j)

    def step1b(s, a2, i, j):
        sa_ref[s, cut:part, :] = pair(s, 1).astype(BF)
        go(sa_ref.at[s, cut:part], ub_ref.at[a2, (b + i) % d1, j - 1], s1_send.at[s, 1], s1_recv.at[1, a2, (b + i) % d1, j - 1],
           {"fsdp": plan.block(a, b, (c + j) % d2), "rep": core})

    def from1(half, a2, other):
        ref = ua_ref if half == 0 else ub_ref
        total = None
        for i in range((d1 if half == 0 else d2) - 1):
            got(ref.at[a2, other, i], s1_recv.at[half, a2, other, i])
            v = ref[a2, other, i].astype(F32)
            total = v if total is None else total + v
        return total

    def plus(x, y):
        return x if y is None else x + y

    def step2(k):
        a2 = (a + k) % d0
        for j in range(1, d2):
            c2 = (c + j) % d2
            s = plan.block(a2, b, c2)
            sa_ref[s, 0:cut, :] = plus(pair(s, 0), from1(0, a2, c2)).astype(BF)
            go(sa_ref.at[s, 0:cut], va_ref.at[a2, j - 1], s2_send.at[0, a2, j - 1], s2_recv.at[0, a2, j - 1],
               {"fsdp": plan.block(a, b, c2), "rep": core})
        for i in range(1, d1):
            b2 = (b + i) % d1
            s = plan.block(a2, b2, c)
            sa_ref[s, cut:part, :] = plus(pair(s, 1), from1(1, a2, b2)).astype(BF)
            go(sa_ref.at[s, cut:part], vb_ref.at[a2, i - 1], s2_send.at[1, a2, i - 1], s2_recv.at[1, a2, i - 1],
               {"fsdp": plan.block(a, b2, c), "rep": core})

    def column(k, half):
        a2 = (a + k) % d0
        s = plan.block(a2, b, c)
        if half == 0:
            got(q_ref.at[s], q_recv.at[s])
        total = plus(pair(s, half), from1(half, a2, (c, b)[half]))
        ref = (va_ref, vb_ref)[half]
        for i in range(1, (d2, d1)[half]):
            got(ref.at[a2, i - 1], s2_recv.at[half, a2, i - 1])
            total = total + ref[a2, i - 1].astype(F32)
        return s, total

    def step3(k):
        for half, (start, size) in enumerate(halves):
            s, total = column(k, half)
            sa_ref[s, start:start + size, :] = total.astype(BF)
            go(
                sa_ref.at[s, start:start + size], z_ref.at[k - 1, start:start + size], s3_send.at[k - 1, half],
                s3_recv.at[k - 1, half], {"fsdp": s, "rep": core},
            )

    for n in range(d0 + 2):
        if n < d0:
            step1(order[n])
        if 0 <= n - 1 < d0:
            step2(order[n - 1])
        if 0 <= n - 2 < d0 - 1:
            step3(order[n - 2])
    sums = []
    for half, (start, size) in enumerate(halves):
        _, total = column(0, half)
        for k in range(1, d0):
            got(z_ref.at[k - 1, start:start + size], s3_recv.at[k - 1, half])
            total = total + z_ref[k - 1, start:start + size, :].astype(F32)
        sums.append(total)
    total = jnp.concatenate(sums, axis=0)
    total_ref[pl.ds(mine, part), :] = total
    go(total_ref.at[pl.ds(mine, part)], total_ref.at[pl.ds(mine, part)], t_send.at[0], t_recv.at[0], {"fsdp": me, "rep": 1 - core})

    off = (me * plan.length) % 128
    row = lax.broadcasted_iota(jnp.int32, (part, 128), 0) + mine
    at = row * 128 + lax.broadcasted_iota(jnp.int32, (part, 128), 1)
    own = jnp.where((at >= off) & (at < off + plan.length), total, 0.0)
    last = me == plan.n - 1
    for i in range(6):
        spot = ROW_VEC - plan.first[-1] + i
        holds = last & (core == spot // part)
        n1_ref[a, i:i + 1, :] = jnp.where(holds, total[spot % part:spot % part + 1], 0.0)
    n1_ref[a, 6:7, :] = jnp.sum(own * own, axis=0, keepdims=True)
    n1_ref[a, 7:8, :] = jnp.zeros((1, 128), F32)
    for k in range(1, d0):
        go(n1_ref.at[a], n1_ref.at[a], n1_send.at[k], n1_recv.at[a], {"fsdp": plan.block((a + k) % d0, b, c), "rep": core})
    for k in range(1, d0):
        got(n1_ref.at[(a + k) % d0], n1_recv.at[(a + k) % d0])
    tile = n1_ref[0]
    for k in range(1, d0):
        tile = tile + n1_ref[k]
    slot = (b * d2 + c) * 2 + core
    n2_ref[slot] = tile
    for n, (i, j, o, to) in enumerate(plane):
        go(n2_ref.at[slot], n2_ref.at[slot], n2_send.at[n], n2_recv.at[slot], to)
    got(total_ref.at[pl.ds(theirs, part)], t_recv.at[0])
    x = pltpu.roll(total_ref[...], (128 - off) % 128, 1)
    below = pltpu.roll(x, plan.rows - 1, 0)
    lane = lax.broadcasted_iota(jnp.int32, x.shape, 1)
    out_ref[...] = jnp.where(lane + off >= 128, below, x)
    for n, (i, j, o, to) in enumerate(plane):
        other = (((b + i) % d1) * d2 + (c + j) % d2) * 2 + (core + o) % 2
        got(n2_ref.at[other], n2_recv.at[other])
    tile = n2_ref[0]
    for n in range(1, 2 * d1 * d2):
        tile = tile + n2_ref[n]
    tile_ref[...] = tile
    for d in sent:
        d.wait_send()


def reduce_call(plan, *handed):
    whole = pl.BlockSpec(memory_space=pltpu.VMEM)
    d0, d1, d2 = plan.dims
    sems = pltpu.SemaphoreType.DMA
    low = lambda *shape: pltpu.VMEM(shape, BF)
    wide = lambda *shape: pltpu.VMEM(shape, F32)
    e1, e2 = max(d1 - 1, 1), max(d2 - 1, 1)
    rest = plan.part - plan.cut
    return pl.pallas_call(
        functools.partial(reduce_kernel, plan),
        out_shape=[jax.ShapeDtypeStruct((plan.rows, 128), F32), jax.ShapeDtypeStruct((8, 128), F32)],
        in_specs=[whole] * 4,
        out_specs=[whole] * 2,
        scratch_shapes=[
            low(2, 28 * 48, 256), wide(ROW_DOWN + plan.rows, 128),
            low(plan.n, plan.rows, 128), low(plan.n, plan.part, 128),
            low(d0, d2, e1, plan.cut, 128), low(d0, d1, e2, rest, 128),
            low(d0, e2, plan.cut, 128), low(d0, e1, rest, 128), low(max(d0 - 1, 1), plan.part, 128),
            low(plan.n, plan.part, 128),
            wide(plan.rows, 128), wide(d0, 8, 128), wide(2 * d1 * d2, 8, 128),
            sems((plan.n,)), sems((plan.n,)), sems((plan.n, 2)),
            sems((2, d0, max(d1, d2), max(e1, e2))), sems((2, d0, max(e1, e2))), sems((2, d0, max(e1, e2))),
            sems((d0, 2)), sems((d0, 2)), sems((1,)), sems((1,)),
            sems((d0,)), sems((d0,)), sems((2 * d1 * d2,)), sems((2 * d1 * d2,)),
        ],
        compiler_params=pltpu.CompilerParams(collective_id=1, has_side_effects=True, vmem_limit_bytes=20 * 2**20),
        name="reduce_gradients",
    )(*handed)


def update_kernel(
    plan,
    grad_ref, tile_ref, master_ref, first_ref, second_ref, average_ref,
    norm_ref, new_master_ref, new_first_ref, new_second_ref, new_average_ref, small_ref,
):
    grad_norm = jnp.sqrt(jnp.sum(tile_ref[6:7, :], axis=1, keepdims=True))
    factor = jnp.minimum(1.0, clip_norm / (grad_norm + 1e-06))
    norm_ref[...] = grad_norm
    for i in range(6):
        small_ref[pl.ds(128 * i, 128)] = (tile_ref[i : i + 1, :] * factor).reshape(128)
    full = plan.length // 128
    left = plan.length - 128 * full
    ema_rate = min(0.999, (1.0 + STEP) / (10.0 + STEP))

    def update(row, rows, lanes):
        at = pl.ds(128 * row, 128 * (rows - 1) + lanes)
        shape = (rows, lanes)
        clipped = grad_ref[row : row + rows, 0:lanes] * factor
        new_first = beta_one * first_ref[at].reshape(shape) + (1.0 - beta_one) * clipped
        new_second = beta_two * second_ref[at].reshape(shape) + (1.0 - beta_two) * clipped * clipped
        corrected_first = new_first / (1.0 - beta_one**STEP)
        corrected_second = new_second / (1.0 - beta_two**STEP)
        master = master_ref[at].reshape(shape)
        new_master = master - learn_rate * (
            corrected_first / (jnp.sqrt(corrected_second) + adam_eps) + decay_rate * master
        )
        new_average = ema_rate * average_ref[at].reshape(shape) + (1.0 - ema_rate) * new_master
        size = 128 * (rows - 1) + lanes
        new_master_ref[at] = new_master.reshape(size)
        new_first_ref[at] = new_first.reshape(size)
        new_second_ref[at] = new_second.reshape(size)
        new_average_ref[at] = new_average.reshape(size)

    update(0, full, 128)
    if left:
        update(full, 1, left)


def update_call(plan, *args):
    whole = pl.BlockSpec(memory_space=pltpu.VMEM)
    flat = jax.ShapeDtypeStruct((plan.length,), F32)
    return pl.pallas_call(
        functools.partial(update_kernel, plan),
        out_shape=[jax.ShapeDtypeStruct((1, 1), F32), flat, flat, flat, flat, jax.ShapeDtypeStruct((768,), F32)],
        in_specs=[whole] * 6,
        out_specs=[whole] * 6,
        compiler_params=pltpu.CompilerParams(vmem_limit_bytes=16 * 2**20),
        name="update",
    )(*args)


def per_device(
    input_fine, input_coarse, upstream_fine, upstream_coarse, extents, master, first_moment, second_moment, average
):
    plan = Plan(lax.axis_size("fsdp"), master.shape[0])
    vec, inp, upf, rows = gather_call(
        plan, master, input_fine.reshape(PIX, C1), upstream_fine.reshape(PIX, C1)
    )
    out_fine, out_coarse, gi_fine, gi_coarse, *handed = layer_call(
        plan, extents, vec, inp, rows, upf,
        input_coarse.reshape(CPIX, C2), upstream_coarse.reshape(CPIX, C2),
    )
    grad, tile = reduce_call(plan, *handed)
    grad_norm, new_master, new_first, new_second, new_average, norm_grads = update_call(
        plan, grad, tile, master, first_moment, second_moment, average
    )
    grad_norm = grad_norm.reshape(())
    return (
        out_fine.reshape(input_fine.shape),
        out_coarse.reshape(input_coarse.shape),
        gi_fine.reshape(input_fine.shape),
        gi_coarse.reshape(input_coarse.shape),
        grad_norm,
        new_master,
        new_first,
        new_second,
        new_average,
        norm_grads,
    )


def solution(mesh):
    images = P(("fsdp", "rep"), None, None, None)
    flat = P("fsdp")
    in_specs = (images,) * 4 + (P(("fsdp", "rep"), None),) + (flat,) * 4
    out_specs = (images,) * 4 + (P(),) + (flat,) * 4 + (P(),)
    return jax.shard_map(per_device, mesh=mesh, in_specs=in_specs, out_specs=out_specs, check_vma=False)
```
